32 devices in a mesh: groups: 2 (over y), loop: 4 (over z), far: 4 (over x, core).
Axes of the slice: x: 2, y: 2, z: 4, core: 2. Of those that a mesh axis runs over, the one named last changes fastest.
Arguments:
- block: bfloat16 [64, 32768], P(None, ('groups', 'loop', 'far')), parts along dimension 1, may hold values from -6 to 6
- near_tiles: bfloat16 [1024, 256, 256], P(('groups', 'loop', 'far')), parts along dimension 0, may hold values from -0.125 to 0.125
- near_rows: int32 [1024], P(('groups', 'loop', 'far')), parts along dimension 0, may hold values from 0 to 3, as said below
- near_offsets: int32 [1024], P(('groups', 'loop', 'far')), parts along dimension 0, may hold values from -4 to 4, as said below
- col_basis: bfloat16 [128, 32, 256], P(('groups', 'loop', 'far')), parts along dimension 0, may hold values from -0.375 to 0.375
- couplings: bfloat16 [1024, 32, 32], P(('groups', 'loop', 'far')), parts along dimension 0, may hold values from -0.375 to 0.375
- far_rows: int32 [1024], P(('groups', 'loop', 'far')), parts along dimension 0, may hold values from 0 to 47, as said below
- far_cols: int32 [1024], P(('groups', 'loop', 'far')), parts along dimension 0, may hold values from 0 to 3
- row_basis: bfloat16 [128, 32, 256], P(('groups', 'loop', 'far')), parts along dimension 0, may hold values from -1 to 1
Outputs:
- krylov: bfloat16 [4, 64, 32768], P(None, None, ('groups', 'loop', 'far')), parts along dimension 2
The draws below stay inside these ranges and needn't reach their ends.
There are 2 independent parts, one for each index of `groups`. The reference program is written for one: setup_inputs(seed, part) draws one part's arguments, and reference() takes and returns one part's arrays. A program takes and returns all parts, laid end to end along the dimension named above; each array names one. Nothing has to cross between parts.
Inputs may be any that keep to these rules, and one draw needn't show every extreme that they name: Within each device block of 32 near slots no pair of near_rows and near_offsets repeats; every device block has a slot with row 0 and offset -4. `near_offsets`: every device block has a slot with offset 4 on row 3. Within each device block of 32 far slots no pair of far_rows and far_cols repeats.
All inputs are finite; a program needn't handle non-finite values.
Results may differ from the reference program's by a relative error of at most 0.0071.
Values may be sent and summed in bfloat16 or wider, within the bound.
No kernel may reach another device: no remote copies, remote signals or barrier semaphores. Data moves between devices by JAX's collectives and lax.ppermute only.
A program may use at most 64 MiB of HBM per device.

```python
import jax
import jax.numpy as jnp
from jax import lax

BS = 256
RHS = 64
RANK = 32
PRODUCTS = 4
LEVELS = 3
CPD = 4
CPL = 16
REACH = 4
NEAR_DEV = 32
FAR_DEV = 32
CLUSTERS = 64
N = 16384
N_LOOP = 4
N_FAR = 4


def near_pattern(key):
    key = jax.random.fold_in(key, 5)
    devices = N_LOOP * N_FAR
    span = 2 * REACH + 1
    cells = CPD * span
    keys = jax.random.split(key, devices)

    def one_device(dev_key):
        middle = jax.random.permutation(dev_key, cells - 2).astype(jnp.int32) + 1
        ends = jnp.array([0, cells - 1], dtype=jnp.int32)
        picked = jnp.concatenate([ends, middle[:NEAR_DEV - 2]])
        return (picked // span, picked % span - REACH)
    rows_all, offsets_all = jax.vmap(one_device)(keys)
    return (rows_all.reshape(-1), offsets_all.reshape(-1))


def far_pattern(key):
    key = jax.random.fold_in(key, 7)
    devices = N_LOOP * N_FAR
    cells = LEVELS * CPL * CPD
    keys = jax.random.split(key, devices)

    def one_device(dev_key):
        middle = jax.random.permutation(dev_key, cells - 2).astype(jnp.int32) + 1
        ends = jnp.array([0, cells - 1], dtype=jnp.int32)
        picked = jnp.concatenate([ends, middle[:FAR_DEV - 2]])
        return (picked // CPD, picked % CPD)
    rows_all, cols_all = jax.vmap(one_device)(keys)
    return (rows_all.reshape(-1), cols_all.reshape(-1))


def draw_near_rows(key, part):
    return near_pattern(key)[0]


def draw_near_offsets(key, part):
    return near_pattern(key)[1]


def draw_far_rows(key, part):
    return far_pattern(key)[0]


def draw_far_cols(key, part):
    return far_pattern(key)[1]


def block_levels(rng, extent, cuts, least, high):
    factor_of = 1.0
    for position, blocks in cuts:
        steps = jax.random.uniform(jax.random.fold_in(jax.random.fold_in(rng, 6), position), (blocks,), jnp.float32, least / len(cuts), high / len(cuts))
        factor_of = factor_of * jnp.repeat(jnp.exp(steps), extent[position] // blocks).reshape((-1,) + (1,) * (len(extent) - 1 - position))
    return factor_of


def bell_draw(key, extent, deviation, most, pieces=(), held_as=jnp.bfloat16):
    values = deviation * jax.random.normal(key, extent, jnp.float32)
    if pieces:
        values = values * block_levels(key, extent, pieces, -0.22, 0.18)
    return jnp.clip(values, -most, most).astype(held_as)


def setup_inputs(seed: int = 0, part: int = 0) -> dict:
    key_of = jax.random.split(jax.random.key(seed), 10)
    part_splits = jax.random.split(jax.random.fold_in(key_of[9], part), 10)
    block = bell_draw(part_splits[0], (RHS, N), 1.0, 6.0, ((1, 16),))
    near_tiles = bell_draw(part_splits[1], (N_LOOP * N_FAR * NEAR_DEV, BS, BS), (8 * BS) ** -0.5, 0.125, ((0, 16),))
    near_rows = draw_near_rows(jax.random.fold_in(jax.random.fold_in(key_of[9], part), 71), part)
    near_offsets = draw_near_offsets(jax.random.fold_in(jax.random.fold_in(key_of[9], part), 71), part)
    col_basis = bell_draw(part_splits[4], (CLUSTERS, RANK, BS), BS ** -0.5, 0.375, ((0, 16),))
    couplings = bell_draw(part_splits[5], (N_LOOP * N_FAR * FAR_DEV, RANK, RANK), (RANK * 8) ** -0.5, 0.375, ((0, 16),))
    far_rows = draw_far_rows(jax.random.fold_in(jax.random.fold_in(key_of[9], part), 71), part)
    far_cols = draw_far_cols(jax.random.fold_in(jax.random.fold_in(key_of[9], part), 71), part)
    row_basis = bell_draw(part_splits[8], (CLUSTERS, RANK, BS), RANK ** -0.5, 1.0, ((0, 16),))
    return dict(block=block, near_tiles=near_tiles, near_rows=near_rows, near_offsets=near_offsets, col_basis=col_basis, couplings=couplings, far_rows=far_rows, far_cols=far_cols, row_basis=row_basis)


def product(current, near_tiles, near_rows, near_offsets, col_basis, couplings, far_rows, far_cols, row_basis):
    highest = lax.Precision.HIGHEST
    clusters_view = current.reshape(RHS, CLUSTERS, BS)
    extended = jnp.concatenate([clusters_view[:, CLUSTERS - REACH:], clusters_view, clusters_view[:, :REACH]], axis=1)
    member = jnp.arange(N_FAR, dtype=jnp.int32)[:, None]
    near_r = near_rows.reshape(N_LOOP, N_FAR, NEAR_DEV)
    near_o = near_offsets.reshape(N_LOOP, N_FAR, NEAR_DEV)
    window_pos = (REACH + member * CPD + near_r + near_o).reshape(N_LOOP, N_FAR * NEAR_DEV)
    local_rows = (member * CPD + near_r).reshape(N_LOOP, N_FAR * NEAR_DEV)
    tiles = near_tiles.reshape(N_LOOP, N_FAR * NEAR_DEV, BS, BS)

    def one_block(args):
        loop_idx, tile_set, positions, rows_here = args
        start = (loop_idx * CPL).astype(jnp.int32)
        window = lax.dynamic_slice_in_dim(extended, start, CPL + 2 * REACH, axis=1)
        chosen = jnp.take(window, positions, axis=1)
        contrib = jnp.einsum('esq,spq->sep', chosen.astype(jnp.float32), tile_set.astype(jnp.float32), precision=highest)
        onehot = (rows_here[:, None] == jnp.arange(CPL, dtype=jnp.int32)[None, :]).astype(jnp.float32)
        return jnp.einsum('sr,sep->rep', onehot, contrib, precision=highest)

    near_part = lax.map(one_block, (jnp.arange(N_LOOP, dtype=jnp.int32), tiles, window_pos, local_rows))
    near_part = jnp.transpose(near_part, (2, 0, 1, 3)).reshape(RHS, CLUSTERS, BS)
    coeffs = jnp.einsum('ckq,ecq->cke', col_basis.astype(jnp.float32), clusters_view.astype(jnp.float32), precision=highest).astype(jnp.bfloat16)
    hop_table = jnp.array([2, N_LOOP - 2, N_LOOP // 2], dtype=jnp.int32)
    loop_ids = jnp.arange(N_LOOP, dtype=jnp.int32)[:, None, None]
    far_all = far_rows.reshape(N_LOOP, N_FAR, FAR_DEV)
    far_l = far_all // CPL
    far_r = far_all % CPL
    far_c = far_cols.reshape(N_LOOP, N_FAR, FAR_DEV)
    col_cluster = (loop_ids * CPL + member[None] * CPD + far_c).reshape(-1)
    row_block = (loop_ids + hop_table[far_l]) % N_LOOP
    row_cluster = (row_block * CPL + far_r).reshape(-1).astype(jnp.int32)
    far_terms = jnp.einsum('skq,sqe->ske', couplings.astype(jnp.float32), coeffs[col_cluster].astype(jnp.float32), precision=highest)
    far_sum = jax.ops.segment_sum(far_terms, row_cluster, num_segments=CLUSTERS)
    far_part = jnp.einsum('ckp,cke->ecp', row_basis.astype(jnp.float32), far_sum, precision=highest)
    return (near_part + far_part).reshape(RHS, N).astype(jnp.bfloat16)


def reference(block, near_tiles, near_rows, near_offsets, col_basis, couplings, far_rows, far_cols, row_basis):
    current = block
    results = []
    for index in range(PRODUCTS):
        current = product(current, near_tiles, near_rows, near_offsets, col_basis, couplings, far_rows, far_cols, row_basis)
        results.append(current)
    return jnp.stack(results)
```

```python
import functools

import jax
import jax.numpy as jnp
from jax import lax
from jax.experimental import pallas as pl
from jax.experimental.pallas import tpu as pltpu
from jax.sharding import PartitionSpec as P

PRODUCTS = 4
REACH = 4
LEVELS = 3
SPAN = 2 * REACH + 1

F32 = jnp.float32
BF16 = jnp.bfloat16
IN_VMEM = pl.BlockSpec(memory_space=pltpu.VMEM)
IN_SMEM = pl.BlockSpec(memory_space=pltpu.SMEM)
ANYWHERE = pl.BlockSpec(memory_space=pl.ANY)


def dot_nt(a, b):
    return lax.dot_general(a, b, (((1,), (1,)), ((), ())), preferred_element_type=F32)


def dot_nn(a, b):
    return lax.dot_general(a, b, (((1,), (0,)), ((), ())), preferred_element_type=F32)


def held(value):
    return pltpu.with_memory_space_constraint(value, pltpu.VMEM)


def far_pieces(x, cb_ref, g_ref, sets, send_refs):
    coeffs = dot_nt(x, cb_ref[...]).astype(BF16)
    width = cb_ref.shape[0]
    steps = len(send_refs) // len(sets)
    for index, levels in enumerate(sets):
        total = sum(dot_nt(coeffs, g_ref[level]) for level in levels).astype(BF16)
        for step in range(steps):
            send_refs[index * steps + step][...] = total[:, step * width : (step + 1) * width]


def prepare_kernel(
    per_device, members, sets, rows_ref, cols_ref, member_ref, x_ref, col_ref, coup_ref, row_ref, *outs
):
    g_ref, cb_ref, rb_ref, *sends = outs
    slots, rank, _ = coup_ref.shape
    size = col_ref.shape[2]
    width = per_device * rank
    block_clusters = per_device * members
    member = member_ref[0]
    cb_ref[...] = jnp.zeros_like(cb_ref)
    rb_ref[...] = jnp.zeros_like(rb_ref)
    for c in range(per_device):
        cb_ref[c * rank : (c + 1) * rank, c * size : (c + 1) * size] = col_ref[c]
        for half in range(2):
            start = half * width + c * rank
            rb_ref[start : start + rank, c * size : (c + 1) * size] = row_ref[c]
    g_ref[...] = jnp.zeros_like(g_ref)
    column = lax.broadcasted_iota(jnp.int32, (rank, width), 1) // rank
    for s in range(slots):
        level = rows_ref[s] // block_clusters
        row = rows_ref[s] % block_clusters
        step = lax.rem(row // per_device - member + members, members)
        start = pl.multiple_of((step * per_device + row % per_device) * rank, rank)
        tile = coup_ref[s].astype(F32)
        wide = jnp.where(column == cols_ref[s], jnp.concatenate([tile] * per_device, axis=1), 0.0)
        where = (level, pl.ds(start, rank), slice(None))
        g_ref[where] = g_ref[where] + wide.astype(BF16)
    far_pieces(x_ref[...], cb_ref, g_ref, sets, sends)


def own_sums(x_ref, d_ref, acc_ref, per_device):
    size = d_ref.shape[1]
    panels = [x_ref[:, c * size : (c + 1) * size] for c in range(per_device)]
    for r in range(per_device):
        acc_ref[:, r * size : (r + 1) * size] = sum(
            dot_nt(panels[c], d_ref[r * SPAN + c - r + REACH]) for c in range(per_device)
        )


def first_own_kernel(per_device, rows_ref, offsets_ref, x_ref, tiles_ref, d_ref, acc_ref, present, sems):
    slots = tiles_ref.shape[0]
    for cell in range(per_device * SPAN):
        present[cell] = 0
    for s in range(slots):
        cell = rows_ref[s] * SPAN + offsets_ref[s] + REACH
        present[cell] = 1
        pltpu.make_async_copy(tiles_ref.at[s], d_ref.at[cell], sems.at[s]).start()
    for s in range(slots):
        cell = rows_ref[s] * SPAN + offsets_ref[s] + REACH
        pltpu.make_async_copy(tiles_ref.at[s], d_ref.at[cell], sems.at[s]).wait()

    @pl.loop(0, per_device * SPAN)
    def _(cell):
        @pl.when(present[cell] == 0)
        def _():
            d_ref[cell] = jnp.zeros(d_ref.shape[1:], d_ref.dtype)

    own_sums(x_ref, d_ref, acc_ref, per_device)


def own_kernel(per_device, slot, x_ref, d_ref, *refs):
    krylov_ref, acc_ref, sem = refs[-3:]
    copy = pltpu.make_async_copy(x_ref, krylov_ref.at[slot], sem)
    copy.start()
    own_sums(x_ref, d_ref, acc_ref, per_device)
    copy.wait()


def next_block(per_device, acc_ref, low_ref, high_ref, d_ref, rb_ref, piece_refs):
    size = d_ref.shape[1]
    total = sum(piece[...].astype(F32) for piece in piece_refs)
    upper = total.astype(BF16)
    lower = (total - upper.astype(F32)).astype(BF16)
    both = jnp.concatenate([upper, lower], axis=1)
    low = [low_ref[:, c * size : (c + 1) * size] for c in range(per_device)]
    high = [high_ref[:, c * size : (c + 1) * size] for c in range(per_device)]
    parts = []
    for r in range(per_device):
        columns = slice(r * size, (r + 1) * size)
        value = acc_ref[:, columns] + dot_nn(both, rb_ref[:, columns])
        for c in range(per_device):
            for panel, place in ((low[c], c - per_device), (high[c], c + per_device)):
                offset = place - r
                if -REACH <= offset <= REACH:
                    value = value + dot_nt(panel, d_ref[r * SPAN + offset + REACH])
        parts.append(value.astype(BF16))
    return jnp.concatenate(parts, axis=1)


def finish_kernel(per_device, sets, pieces, *refs):
    acc_ref, low_ref, high_ref, d_ref, rb_ref, cb_ref, g_ref = refs[:7]
    piece_refs = refs[7 : 7 + pieces]
    x_ref, *sends = refs[7 + pieces :]
    x = next_block(per_device, acc_ref, low_ref, high_ref, d_ref, rb_ref, piece_refs)
    x_ref[...] = x
    far_pieces(x, cb_ref, g_ref, sets, sends)


def last_kernel(per_device, slot, pieces, *refs):
    acc_ref, low_ref, high_ref, d_ref, rb_ref = refs[:5]
    piece_refs = refs[5 : 5 + pieces]
    _, krylov_ref, x_ref, sem = refs[5 + pieces :]
    x_ref[...] = next_block(per_device, acc_ref, low_ref, high_ref, d_ref, rb_ref, piece_refs)
    copy = pltpu.make_async_copy(x_ref, krylov_ref.at[slot], sem)
    copy.start()
    copy.wait()


def on_device(
    block, near_tiles, near_rows, near_offsets, col_basis, couplings, far_rows, far_cols, row_basis
):
    rhs, shard_len = block.shape
    size = near_tiles.shape[1]
    rank = couplings.shape[1]
    per_device = shard_len // size
    members = lax.axis_size("far")
    loop_size = lax.axis_size("loop")
    devices = members * loop_size
    width = per_device * rank
    distances = [d % loop_size for d in (2, loop_size - 2, loop_size // 2)]
    hops = sorted(set(distances))
    sets = tuple(tuple(i for i, d in enumerate(distances) if d == hop) for hop in hops)
    pieces = len(hops) * members
    ring = [(i, (i + 1) % devices) for i in range(devices)]
    back = [(target, source) for source, target in ring]
    routes = []
    for hop in hops:
        for step in range(members):
            routes.append(
                [
                    (l * members + m, (l + hop) % loop_size * members + (m + step) % members)
                    for l in range(loop_size)
                    for m in range(members)
                ]
            )
    both_axes = ("loop", "far")
    params = pltpu.CompilerParams(vmem_limit_bytes=16 * 2**20)

    def call(kernel, ins, specs, outs, out_specs, scratch=(), aliases=None, flops=0, name=None):
        ins = [held(v) if spec is IN_VMEM else v for v, spec in zip(ins, specs)]
        return pl.pallas_call(
            kernel,
            in_specs=list(specs),
            out_specs=list(out_specs),
            out_shape=list(outs),
            scratch_shapes=list(scratch),
            input_output_aliases=aliases or {},
            compiler_params=params,
            cost_estimate=pl.CostEstimate(flops=flops, bytes_accessed=2**22, transcendentals=0),
            name=name,
        )(*ins)

    def vmem(shape, dtype):
        return pltpu.VMEM(shape, dtype)

    block_out = vmem((rhs, shard_len), BF16)
    acc_out = vmem((rhs, shard_len), F32)
    piece_outs = [vmem((rhs, width), BF16)] * pieces
    krylov_out = jax.ShapeDtypeStruct((PRODUCTS, rhs, shard_len), BF16)
    cells = per_device * SPAN

    current = block
    krylov = None
    sends = None
    for index in range(PRODUCTS):
        low = lax.ppermute(current, both_axes, ring)
        high = lax.ppermute(current, both_axes, back)
        if index == 0:
            member = lax.axis_index("far").astype(jnp.int32).reshape(1)
            coupled, col_wide, row_wide, *sends = call(
                functools.partial(prepare_kernel, per_device, members, sets),
                [far_rows, far_cols, member, block, col_basis, couplings, row_basis],
                [IN_SMEM] * 3 + [IN_VMEM] * 4,
                [
                    vmem((LEVELS, members * width, width), BF16),
                    vmem((width, shard_len), BF16),
                    vmem((2 * width, shard_len), BF16),
                    *piece_outs,
                ],
                [IN_VMEM] * (3 + pieces),
                flops=10**8,
                name="prepare",
            )
        received = [lax.ppermute(s, both_axes, route) for s, route in zip(sends, routes)]
        if index == 0:
            dense, acc = call(
                functools.partial(first_own_kernel, per_device),
                [near_rows, near_offsets, current, near_tiles],
                [IN_SMEM, IN_SMEM, IN_VMEM, ANYWHERE],
                [vmem((cells, size, size), BF16), acc_out],
                [IN_VMEM] * 2,
                [pltpu.SMEM((cells,), jnp.int32), pltpu.SemaphoreType.DMA((near_tiles.shape[0],))],
                flops=10**9,
                name="first_own",
            )
        else:
            ins, specs, aliases = [current, dense], [IN_VMEM] * 2, None
            if krylov is not None:
                ins, specs, aliases = ins + [krylov], specs + [ANYWHERE], {2: 0}
            krylov, acc = call(
                functools.partial(own_kernel, per_device, index - 1),
                ins,
                specs,
                [krylov_out, acc_out],
                [ANYWHERE, IN_VMEM],
                [pltpu.SemaphoreType.DMA],
                aliases,
                flops=10**9,
                name="own",
            )
        if index < PRODUCTS - 1:
            ins = [acc, low, high, dense, row_wide, col_wide, coupled, *received]
            current, *sends = call(
                functools.partial(finish_kernel, per_device, sets, pieces),
                ins,
                [IN_VMEM] * len(ins),
                [block_out, *piece_outs],
                [IN_VMEM] * (1 + pieces),
                flops=10**9,
                name="finish",
            )
        else:
            ins = [acc, low, high, dense, row_wide, *received, krylov]
            (krylov,) = call(
                functools.partial(last_kernel, per_device, index, pieces),
                ins,
                [IN_VMEM] * (len(ins) - 1) + [ANYWHERE],
                [krylov_out],
                [ANYWHERE],
                [pltpu.VMEM((rhs, shard_len), BF16), pltpu.SemaphoreType.DMA],
                {len(ins) - 1: 0},
                flops=10**9,
                name="last",
            )
    return krylov


def solution(mesh):
    split = ("groups", "loop", "far")
    in_specs = (
        P(None, split),
        P(split, None, None),
        P(split),
        P(split),
        P(split, None, None),
        P(split, None, None),
        P(split),
        P(split),
        P(split, None, None),
    )
    return jax.shard_map(
        on_device, mesh=mesh, in_specs=in_specs, out_specs=P(None, None, split), check_vma=False
    )
```

```python
import functools

import jax
import jax.numpy as jnp
from jax import lax
from jax.experimental import pallas as pl
from jax.experimental.pallas import tpu as pltpu
from jax.sharding import PartitionSpec as P

PRODUCTS = 4
REACH = 4
LEVELS = 3
SPAN = 2 * REACH + 1

F32 = jnp.float32
BF16 = jnp.bfloat16
IN_VMEM = pl.BlockSpec(memory_space=pltpu.VMEM)
IN_SMEM = pl.BlockSpec(memory_space=pltpu.SMEM)
IN_HBM = pl.BlockSpec(memory_space=pltpu.HBM)
ANYWHERE = pl.BlockSpec(memory_space=pl.ANY)


def dot_nt(a, b):
    return lax.dot_general(a, b, (((1,), (1,)), ((), ())), preferred_element_type=F32)


def dot_nn(a, b):
    return lax.dot_general(a, b, (((1,), (0,)), ((), ())), preferred_element_type=F32)


def far_pieces(x, cb_ref, g_ref, sets, members, place, send_refs):
    coeffs = dot_nt(x, cb_ref[...]).astype(BF16)
    width = cb_ref.shape[0]
    for index, levels in enumerate(sets):
        total = sum(dot_nt(coeffs, g_ref[level]) for level in levels).astype(BF16)
        for step in range(members):
            piece = total[:, step * width : (step + 1) * width]
            if place is None:
                send_refs[index * members + step][...] = piece
            else:
                send_refs[0][place + step] = piece


def prepare_kernel(
    per_device, members, sets, paired, index_ref, rows_hbm, cols_hbm, near_rows_hbm, offsets_hbm,
    x_hbm, col_hbm, coup_hbm, row_hbm, tiles_hbm, x_ref, d_ref, g_ref, cb_ref, rb_ref, *rest
):
    *sends, rows_ref, cols_ref, near_rows_ref, offsets_ref, col_ref, coup_ref, row_ref, present, sems, tile_sems = rest
    pairs = (
        (near_rows_hbm, near_rows_ref),
        (offsets_hbm, offsets_ref),
        (rows_hbm, rows_ref),
        (cols_hbm, cols_ref),
        (x_hbm, x_ref),
        (col_hbm, col_ref),
        (coup_hbm, coup_ref),
        (row_hbm, row_ref),
    )
    copies = [pltpu.make_async_copy(src, dst, sems.at[i]) for i, (src, dst) in enumerate(pairs)]
    for copy in copies:
        copy.start()
    slots, rank, _ = coup_ref.shape
    size = col_ref.shape[2]
    width = per_device * rank
    block_clusters = per_device * members
    cb_ref[...] = jnp.zeros_like(cb_ref)
    rb_ref[...] = jnp.zeros_like(rb_ref)
    g_ref[...] = jnp.zeros_like(g_ref)
    for cell in range(per_device * SPAN):
        present[cell] = 0
    copies[0].wait()
    copies[1].wait()
    tiles = []
    for s in range(tiles_hbm.shape[0]):
        cell = near_rows_ref[s] * SPAN + offsets_ref[s] + REACH
        present[cell] = 1
        tiles.append(pltpu.make_async_copy(tiles_hbm.at[s], d_ref.at[cell], tile_sems.at[s]))
        tiles[-1].start()
    for copy in copies[2:]:
        copy.wait()
    for c in range(per_device):
        cb_ref[c * rank : (c + 1) * rank, c * size : (c + 1) * size] = col_ref[c]
        for half in range(2):
            start = half * width + c * rank
            rb_ref[start : start + rank, c * size : (c + 1) * size] = row_ref[c]
    column = lax.broadcasted_iota(jnp.int32, (rank, width), 1) // rank
    shift = 0 if paired else lax.rem(index_ref[0], members)
    for s in range(slots):
        level = rows_ref[s] // block_clusters
        row = rows_ref[s] % block_clusters
        step = lax.rem(row // per_device - shift + members, members)
        start = pl.multiple_of((step * per_device + row % per_device) * rank, rank)
        tile = coup_ref[s].astype(F32)
        wide = jnp.where(column == cols_ref[s], jnp.concatenate([tile] * per_device, axis=1), 0.0)
        where = (level, pl.ds(start, rank), slice(None))
        g_ref[where] = g_ref[where] + wide.astype(BF16)
    far_pieces(x_ref[...], cb_ref, g_ref, sets, members, other_half(index_ref, members, paired), sends)
    for copy in tiles:
        copy.wait()

    @pl.loop(0, per_device * SPAN)
    def _(cell):
        @pl.when(present[cell] == 0)
        def _():
            d_ref[cell] = jnp.zeros(d_ref.shape[1:], d_ref.dtype)


def other_half(index_ref, members, paired):
    if not paired:
        return None
    return jnp.where(lax.div(index_ref[0], members) >= paired, 0, members)


def own_sums(x_ref, d_ref, acc_ref, per_device):
    size = d_ref.shape[1]
    panels = [x_ref[:, c * size : (c + 1) * size] for c in range(per_device)]
    for r in range(per_device):
        acc_ref[:, r * size : (r + 1) * size] = sum(
            dot_nt(panels[c], d_ref[r * SPAN + c - r + REACH]) for c in range(per_device)
        )


def own_kernel(per_device, x_ref, d_ref, acc_ref):
    own_sums(x_ref, d_ref, acc_ref, per_device)


def later_own_kernel(per_device, slot, x_ref, d_ref, *refs):
    krylov_ref, acc_ref, sem = refs[-3:]
    copy = pltpu.make_async_copy(x_ref, krylov_ref.at[slot], sem)
    copy.start()
    own_sums(x_ref, d_ref, acc_ref, per_device)
    copy.wait()


def next_block(per_device, members, paired, index_ref, acc_ref, near_ref, over_ref, d_ref, rb_ref, piece_refs):
    size = d_ref.shape[1]
    if paired:
        place = other_half(index_ref, members, paired)
        pieces = [piece_refs[0][place + step] for step in range(members)]
    else:
        pieces = [piece[...] for piece in piece_refs]
    total = sum(piece.astype(F32) for piece in pieces)
    upper = total.astype(BF16)
    lower = (total - upper.astype(F32)).astype(BF16)
    both = jnp.concatenate([upper, lower], axis=1)
    odd = lax.rem(index_ref[0], 2) == 1
    low, high = [], []
    for c in range(per_device):
        near, over = (ref[:, c * size : (c + 1) * size] for ref in (near_ref, over_ref))
        low.append(jnp.where(odd, near, over))
        high.append(jnp.where(odd, over, near))
    parts = []
    for r in range(per_device):
        columns = slice(r * size, (r + 1) * size)
        value = acc_ref[:, columns] + dot_nn(both, rb_ref[:, columns])
        for c in range(per_device):
            for panel, place in ((low[c], c - per_device), (high[c], c + per_device)):
                offset = place - r
                if -REACH <= offset <= REACH:
                    value = value + dot_nt(panel, d_ref[r * SPAN + offset + REACH])
        parts.append(value.astype(BF16))
    return jnp.concatenate(parts, axis=1)


def finish_kernel(per_device, members, sets, paired, pieces, *refs):
    index_ref, acc_ref, near_ref, over_ref, d_ref, rb_ref, cb_ref, g_ref = refs[:8]
    piece_refs = refs[8 : 8 + pieces]
    x_ref, *sends = refs[8 + pieces :]
    x = next_block(
        per_device, members, paired, index_ref, acc_ref, near_ref, over_ref, d_ref, rb_ref, piece_refs
    )
    x_ref[...] = x
    far_pieces(x, cb_ref, g_ref, sets, members, other_half(index_ref, members, paired), sends)


def last_kernel(per_device, members, paired, slot, pieces, *refs):
    index_ref, acc_ref, near_ref, over_ref, d_ref, rb_ref = refs[:6]
    piece_refs = refs[6 : 6 + pieces]
    _, krylov_ref, x_ref, sem = refs[6 + pieces :]
    x_ref[...] = next_block(
        per_device, members, paired, index_ref, acc_ref, near_ref, over_ref, d_ref, rb_ref, piece_refs
    )
    copy = pltpu.make_async_copy(x_ref, krylov_ref.at[slot], sem)
    copy.start()
    copy.wait()


def on_device(
    block, near_tiles, near_rows, near_offsets, col_basis, couplings, far_rows, far_cols, row_basis
):
    rhs, shard_len = block.shape
    size = near_tiles.shape[1]
    rank = couplings.shape[1]
    per_device = shard_len // size
    members = lax.axis_size("far")
    loop_size = lax.axis_size("loop")
    devices = members * loop_size
    width = per_device * rank
    distances = [d % loop_size for d in (2, loop_size - 2, loop_size // 2)]
    hops = sorted(set(distances))
    sets = tuple(tuple(i for i, d in enumerate(distances) if d == hop) for hop in hops)
    both_axes = ("loop", "far")
    paired = hops[0] if len(hops) == 1 and 2 * hops[0] == loop_size else 0
    pieces = 1 if paired else len(hops) * members
    swap = [(i, i ^ 1) for i in range(devices)]
    over = [(i, (i + 1 if i % 2 else i - 1) % devices) for i in range(devices)]

    def exchanged(sends):
        if paired:
            groups = [
                [(l + half * paired) * members + m for half in range(2) for m in range(members)]
                for l in range(paired)
            ]
            return [
                lax.all_to_all(sends[0], both_axes, 0, 0, axis_index_groups=groups, tiled=True)
            ]
        received = []
        for i, send in enumerate(sends):
            hop, step = hops[i // members], i % members
            route = [
                (l * members + m, (l + hop) % loop_size * members + (m + step) % members)
                for l in range(loop_size)
                for m in range(members)
            ]
            received.append(lax.ppermute(send, both_axes, route))
        return received

    params = pltpu.CompilerParams(vmem_limit_bytes=16 * 2**20)

    def call(kernel, ins, specs, outs, out_specs, scratch=(), aliases=None, flops=0, name=None):
        constraint = {id(IN_VMEM): pltpu.VMEM, id(IN_HBM): pltpu.HBM}
        ins = [
            pltpu.with_memory_space_constraint(v, constraint[id(spec)]) if id(spec) in constraint else v
            for v, spec in zip(ins, specs)
        ]
        return pl.pallas_call(
            kernel,
            in_specs=list(specs),
            out_specs=list(out_specs),
            out_shape=list(outs),
            scratch_shapes=list(scratch),
            input_output_aliases=aliases or {},
            compiler_params=params,
            cost_estimate=pl.CostEstimate(flops=flops, bytes_accessed=2**22, transcendentals=0),
            name=name,
        )(*ins)

    block_out = pltpu.VMEM((rhs, shard_len), BF16)
    acc_out = pltpu.VMEM((rhs, shard_len), F32)
    if paired:
        piece_outs = [pltpu.VMEM((2 * members, rhs, width), BF16)]
    else:
        piece_outs = [pltpu.VMEM((rhs, width), BF16)] * pieces
    krylov_out = jax.ShapeDtypeStruct((PRODUCTS, rhs, shard_len), BF16)
    cells = per_device * SPAN
    slots = near_tiles.shape[0]
    index = lax.axis_index(both_axes).astype(jnp.int32).reshape(1)

    current = block
    krylov = None
    for product in range(PRODUCTS):
        near = lax.ppermute(current, both_axes, swap)
        far = lax.ppermute(current, both_axes, over)
        if product == 0:
            current, dense, coupled, col_wide, row_wide, *sends = call(
                functools.partial(prepare_kernel, per_device, members, sets, paired),
                [index, far_rows, far_cols, near_rows, near_offsets]
                + [block, col_basis, couplings, row_basis, near_tiles],
                [IN_SMEM] + [IN_HBM] * 9,
                [
                    block_out,
                    pltpu.VMEM((cells, size, size), BF16),
                    pltpu.VMEM((LEVELS, members * width, width), BF16),
                    pltpu.VMEM((width, shard_len), BF16),
                    pltpu.VMEM((2 * width, shard_len), BF16),
                    *piece_outs,
                ],
                [IN_VMEM] * (5 + pieces),
                [
                    pltpu.SMEM(far_rows.shape, jnp.int32),
                    pltpu.SMEM(far_cols.shape, jnp.int32),
                    pltpu.SMEM(near_rows.shape, jnp.int32),
                    pltpu.SMEM(near_offsets.shape, jnp.int32),
                    pltpu.VMEM(col_basis.shape, BF16),
                    pltpu.VMEM(couplings.shape, BF16),
                    pltpu.VMEM(row_basis.shape, BF16),
                    pltpu.SMEM((cells,), jnp.int32),
                    pltpu.SemaphoreType.DMA((8,)),
                    pltpu.SemaphoreType.DMA((slots,)),
                ],
                flops=10**8,
                name="prepare",
            )
        received = exchanged(sends)
        if product == 0:
            (acc,) = call(
                functools.partial(own_kernel, per_device),
                [current, dense],
                [IN_VMEM] * 2,
                [acc_out],
                [IN_VMEM],
                flops=10**9,
                name="own",
            )
        else:
            ins, specs, aliases = [current, dense], [IN_VMEM] * 2, None
            if krylov is not None:
                ins, specs, aliases = ins + [krylov], specs + [ANYWHERE], {2: 0}
            krylov, acc = call(
                functools.partial(later_own_kernel, per_device, product - 1),
                ins,
                specs,
                [krylov_out, acc_out],
                [ANYWHERE, IN_VMEM],
                [pltpu.SemaphoreType.DMA],
                aliases,
                flops=10**9,
                name="own",
            )
        if product < PRODUCTS - 1:
            ins = [index, acc, near, far, dense, row_wide, col_wide, coupled, *received]
            current, *sends = call(
                functools.partial(finish_kernel, per_device, members, sets, paired, pieces),
                ins,
                [IN_SMEM] + [IN_VMEM] * (len(ins) - 1),
                [block_out, *piece_outs],
                [IN_VMEM] * (1 + pieces),
                flops=10**9,
                name="finish",
            )
        else:
            ins = [index, acc, near, far, dense, row_wide, *received, krylov]
            (krylov,) = call(
                functools.partial(last_kernel, per_device, members, paired, product, pieces),
                ins,
                [IN_SMEM] + [IN_VMEM] * (len(ins) - 2) + [ANYWHERE],
                [krylov_out],
                [ANYWHERE],
                [pltpu.VMEM((rhs, shard_len), BF16), pltpu.SemaphoreType.DMA],
                {len(ins) - 1: 0},
                flops=10**9,
                name="last",
            )
    return krylov


def solution(mesh):
    split = ("groups", "loop", "far")
    in_specs = (
        P(None, split),
        P(split, None, None),
        P(split),
        P(split),
        P(split, None, None),
        P(split, None, None),
        P(split),
        P(split),
        P(split, None, None),
    )
    return jax.shard_map(
        on_device, mesh=mesh, in_specs=in_specs, out_specs=P(None, None, split), check_vma=False
    )
```

```python
import functools

import jax
import jax.numpy as jnp
from jax import lax
from jax.experimental import pallas as pl
from jax.experimental.pallas import tpu as pltpu
from jax.sharding import PartitionSpec as P

PRODUCTS = 4
REACH = 4
LEVELS = 3
SPAN = 2 * REACH + 1

F32 = jnp.float32
BF16 = jnp.bfloat16
IN_VMEM = pl.BlockSpec(memory_space=pltpu.VMEM)
IN_SMEM = pl.BlockSpec(memory_space=pltpu.SMEM)
IN_HBM = pl.BlockSpec(memory_space=pltpu.HBM)
ANYWHERE = pl.BlockSpec(memory_space=pl.ANY)


def dot_nt(a, b):
    return lax.dot_general(a, b, (((1,), (1,)), ((), ())), preferred_element_type=F32)


def dot_nn(a, b):
    return lax.dot_general(a, b, (((1,), (0,)), ((), ())), preferred_element_type=F32)


def halves(value):
    upper = value.astype(BF16)
    return upper, (value - upper.astype(F32)).astype(BF16)


class Plan:
    def __init__(self, block_shape, tile_shape, coupling_shape, members, loop_size):
        self.rhs, self.shard_len = block_shape
        self.tiles, self.size, _ = tile_shape
        self.slots, self.rank, _ = coupling_shape
        self.members, self.loop_size = members, loop_size
        self.per_device = self.shard_len // self.size
        self.width = self.per_device * self.rank
        self.cells = self.per_device * SPAN
        self.block_clusters = self.per_device * members
        distances = [d % loop_size for d in (2, loop_size - 2, loop_size // 2)]
        self.hops = sorted(set(distances))
        self.sets = [[i for i, d in enumerate(distances) if d == hop] for hop in self.hops]
        self.paired = len(self.hops) == 1 and 2 * self.hops[0] == loop_size and members == 4
        devices = members * loop_size
        self.near = [(i, i ^ 1) for i in range(devices)]
        self.over = [(i, (i + 1 if i % 2 else i - 1) % devices) for i in range(devices)]
        places = [(l, m) for l in range(loop_size) for m in range(members)]
        self.across = [
            (l * members + m, (l + self.hops[0]) % loop_size * members + (m ^ (m % 2 * 2)))
            for l, m in places
        ]
        self.routes = [
            [(l * members + m, (l + hop) % loop_size * members + (m + step) % members) for l, m in places]
            for hop in self.hops
            for step in range(members)
        ]

    def panel(self, ref, c):
        return ref[:, c * self.size : (c + 1) * self.size]

    def member(self, index_ref):
        return lax.rem(index_ref[0], self.members)

    def send_far(self, index_ref, x, cb_ref, g_ref, out_refs):
        coeffs = dot_nt(x, cb_ref[...]).astype(BF16)
        totals = [sum(dot_nt(coeffs, g_ref[level]) for level in levels) for levels in self.sets]
        if not self.paired:
            for i, out_ref in enumerate(out_refs):
                step = i % self.members * self.width
                out_ref[...] = totals[i // self.members][:, step : step + self.width].astype(BF16)
            return
        message_ref, keep_ref = out_refs
        (total,) = totals
        member = self.member(index_ref)
        second = lax.rem(member, 2) != lax.div(member, 2)
        first, last = total[:, : 2 * self.width], total[:, 2 * self.width :]
        keep_ref[...] = jnp.where(second, last, first)
        upper, lower = halves(jnp.where(second, first, last))
        message_ref[:, : self.shard_len] = x
        message_ref[:, self.shard_len : self.shard_len + 2 * self.width] = upper
        message_ref[:, self.shard_len + 2 * self.width :] = lower

    def relay_far(self, keep_ref, message_ref, out_ref):
        upper = message_ref[:, self.shard_len : self.shard_len + 2 * self.width].astype(F32)
        lower = message_ref[:, self.shard_len + 2 * self.width :].astype(F32)
        out_ref[...] = (keep_ref[...] + (upper + lower)).astype(BF16)

    def far_sum(self, index_ref, far_refs):
        if not self.paired:
            return sum(ref[...].astype(F32) for ref in far_refs)
        both = far_refs[0][...].astype(F32) + far_refs[1][...].astype(F32)
        second = lax.rem(index_ref[0], 2) == 1
        return jnp.where(second, both[:, self.width :], both[:, : self.width])

    def own_sums(self, x_ref, d_ref, acc_ref):
        panels = [self.panel(x_ref, c) for c in range(self.per_device)]
        for r in range(self.per_device):
            acc_ref[:, r * self.size : (r + 1) * self.size] = sum(
                dot_nt(panels[c], d_ref[r * SPAN + c - r + REACH]) for c in range(self.per_device)
            )

    def next_block(self, index_ref, acc_ref, near_ref, over_ref, d_ref, rb_ref, far_refs):
        both = jnp.concatenate(halves(self.far_sum(index_ref, far_refs)), axis=1)
        odd = lax.rem(index_ref[0], 2) == 1
        low, high = [], []
        for c in range(self.per_device):
            near, over = self.panel(near_ref, c), self.panel(over_ref, c)
            low.append(jnp.where(odd, near, over))
            high.append(jnp.where(odd, over, near))
        parts = []
        for r in range(self.per_device):
            value = self.panel(acc_ref, r) + dot_nn(both, self.panel(rb_ref, r))
            for c in range(self.per_device):
                for panel, place in ((low[c], c - self.per_device), (high[c], c + self.per_device)):
                    offset = place - r
                    if -REACH <= offset <= REACH:
                        value = value + dot_nt(panel, d_ref[r * SPAN + offset + REACH])
            parts.append(value.astype(BF16))
        return jnp.concatenate(parts, axis=1)


def prepare_kernel(plan, index_ref, *refs):
    sources, refs = refs[:9], refs[9:]
    x_ref, d_ref, g_ref, cb_ref, rb_ref = refs[:5]
    sends, held, (present, sems, tile_sems) = refs[5:-10], refs[-10:-3], refs[-3:]
    rows_ref, cols_ref, near_rows_ref, offsets_ref, col_ref, coup_ref, row_ref = held
    tiles_hbm = sources[8]
    targets = (near_rows_ref, offsets_ref, rows_ref, cols_ref, x_ref, col_ref, coup_ref, row_ref)
    copies = [
        pltpu.make_async_copy(source, target, sems.at[i])
        for i, (source, target) in enumerate(zip(sources[:8], targets))
    ]
    for copy in copies:
        copy.start()
    rank, size = plan.rank, plan.size
    cb_ref[...] = jnp.zeros_like(cb_ref)
    rb_ref[...] = jnp.zeros_like(rb_ref)
    g_ref[...] = jnp.zeros_like(g_ref)
    for cell in range(plan.cells):
        present[cell] = 0
    copies[0].wait()
    copies[1].wait()
    tiles = []
    for s in range(plan.tiles):
        cell = near_rows_ref[s] * SPAN + offsets_ref[s] + REACH
        present[cell] = 1
        tiles.append(pltpu.make_async_copy(tiles_hbm.at[s], d_ref.at[cell], tile_sems.at[s]))
        tiles[-1].start()
    for copy in copies[2:]:
        copy.wait()
    for c in range(plan.per_device):
        columns = slice(c * size, (c + 1) * size)
        cb_ref[c * rank : (c + 1) * rank, columns] = col_ref[c]
        for start in (c * rank, plan.width + c * rank):
            rb_ref[start : start + rank, columns] = row_ref[c]
    column = lax.broadcasted_iota(jnp.int32, (rank, plan.width), 1) // rank
    shift = 0 if plan.paired else plan.member(index_ref)
    for s in range(plan.slots):
        level = lax.div(rows_ref[s], plan.block_clusters)
        row = lax.rem(rows_ref[s], plan.block_clusters)
        step = lax.rem(lax.div(row, plan.per_device) - shift + plan.members, plan.members)
        place = step * plan.per_device + lax.rem(row, plan.per_device)
        where = (level, pl.ds(pl.multiple_of(place * rank, rank), rank), slice(None))
        tile = coup_ref[s].astype(F32)
        wide = jnp.where(column == cols_ref[s], jnp.concatenate([tile] * plan.per_device, axis=1), 0.0)
        g_ref[where] = g_ref[where] + wide.astype(BF16)
    plan.send_far(index_ref, x_ref[...], cb_ref, g_ref, sends)
    for copy in tiles:
        copy.wait()

    @pl.loop(0, plan.cells)
    def _(cell):
        @pl.when(present[cell] == 0)
        def _():
            d_ref[cell] = jnp.zeros(d_ref.shape[1:], d_ref.dtype)


def own_kernel(plan, slot, *refs):
    x_ref, d_ref, *refs = refs
    if plan.paired:
        keep_ref, message_ref, *refs = refs
    if slot is not None:
        *refs, sem = refs
        krylov_ref = refs[-1]
        copy = pltpu.make_async_copy(x_ref, krylov_ref.at[slot], sem)
        copy.start()
        refs = refs[1:-1] if slot else refs[:-1]
    if plan.paired:
        plan.relay_far(keep_ref, message_ref, refs[1])
    plan.own_sums(x_ref, d_ref, refs[0])
    if slot is not None:
        copy.wait()


def finish_kernel(plan, fars, *refs):
    index_ref, acc_ref, near_ref, over_ref, d_ref, rb_ref, cb_ref, g_ref = refs[:8]
    far_refs, (x_ref, *sends) = refs[8 : 8 + fars], refs[8 + fars :]
    x = plan.next_block(index_ref, acc_ref, near_ref, over_ref, d_ref, rb_ref, far_refs)
    x_ref[...] = x
    plan.send_far(index_ref, x, cb_ref, g_ref, sends)


def last_kernel(plan, fars, slot, *refs):
    index_ref, acc_ref, near_ref, over_ref, d_ref, rb_ref = refs[:6]
    far_refs, (_, krylov_ref, x_ref, sem) = refs[6 : 6 + fars], refs[6 + fars :]
    x_ref[...] = plan.next_block(index_ref, acc_ref, near_ref, over_ref, d_ref, rb_ref, far_refs)
    copy = pltpu.make_async_copy(x_ref, krylov_ref.at[slot], sem)
    copy.start()
    copy.wait()


def call(kernel, name, ins, specs, outs, out_specs=None, scratch=(), aliases=None):
    spaces = {id(IN_VMEM): pltpu.VMEM, id(IN_HBM): pltpu.HBM}
    ins = [
        pltpu.with_memory_space_constraint(v, spaces[id(spec)]) if id(spec) in spaces else v
        for v, spec in zip(ins, specs)
    ]
    return pl.pallas_call(
        kernel,
        in_specs=list(specs),
        out_specs=out_specs or [IN_VMEM] * len(outs),
        out_shape=list(outs),
        scratch_shapes=list(scratch),
        input_output_aliases=aliases or {},
        compiler_params=pltpu.CompilerParams(vmem_limit_bytes=16 * 2**20),
        cost_estimate=pl.CostEstimate(flops=10**9, bytes_accessed=2**22, transcendentals=0),
        name=name,
    )(*ins)


def on_device(
    block, near_tiles, near_rows, near_offsets, col_basis, couplings, far_rows, far_cols, row_basis
):
    axes = ("loop", "far")
    plan = Plan(
        block.shape, near_tiles.shape, couplings.shape, lax.axis_size("far"), lax.axis_size("loop")
    )
    rhs, shard_len, width = plan.rhs, plan.shard_len, plan.width
    block_out = pltpu.VMEM((rhs, shard_len), BF16)
    acc_out = pltpu.VMEM((rhs, shard_len), F32)
    relay_out = pltpu.VMEM((rhs, 2 * width), BF16)
    krylov_out = jax.ShapeDtypeStruct((PRODUCTS, rhs, shard_len), BF16)
    if plan.paired:
        sends_out = [
            pltpu.VMEM((rhs, shard_len + 4 * width), BF16),
            pltpu.VMEM((rhs, 2 * width), F32),
        ]
    else:
        sends_out = [pltpu.VMEM((rhs, width), BF16)] * len(plan.routes)
    index = lax.axis_index(axes).astype(jnp.int32).reshape(1)
    smem = [pltpu.SMEM(v.shape, jnp.int32) for v in (far_rows, far_cols, near_rows, near_offsets)]
    vmem = [pltpu.VMEM(v.shape, BF16) for v in (col_basis, couplings, row_basis)]

    current = block
    krylov = None
    for product in range(PRODUCTS):
        over = lax.ppermute(current, axes, plan.over)
        if product == 0:
            ins = [near_rows, near_offsets, far_rows, far_cols]
            ins += [block, col_basis, couplings, row_basis, near_tiles]
            current, dense, coupled, col_wide, row_wide, *sends = call(
                functools.partial(prepare_kernel, plan),
                "prepare",
                [index, *ins],
                [IN_SMEM] + [IN_HBM] * 9,
                [
                    block_out,
                    pltpu.VMEM((plan.cells, plan.size, plan.size), BF16),
                    pltpu.VMEM((LEVELS, plan.members * width, width), BF16),
                    pltpu.VMEM((width, shard_len), BF16),
                    pltpu.VMEM((2 * width, shard_len), BF16),
                    *sends_out,
                ],
                scratch=[
                    *smem,
                    *vmem,
                    pltpu.SMEM((plan.cells,), jnp.int32),
                    pltpu.SemaphoreType.DMA((8,)),
                    pltpu.SemaphoreType.DMA((plan.tiles,)),
                ],
            )
        ins, outs = [current, dense], [acc_out]
        if plan.paired:
            message, keep = sends
            near = lax.ppermute(message, axes, plan.near)
            ins, outs = ins + [keep, near], outs + [relay_out]
        else:
            near = lax.ppermute(current, axes, plan.near)
            fars = [lax.ppermute(s, axes, route) for s, route in zip(sends, plan.routes)]
        specs, out_specs, scratch, aliases = [IN_VMEM] * len(ins), [IN_VMEM] * len(outs), [], None
        if product > 0:
            scratch, out_specs, outs = [pltpu.SemaphoreType.DMA], out_specs + [ANYWHERE], outs + [krylov_out]
        if product > 1:
            aliases = {len(ins): len(outs) - 1}
            ins, specs = ins + [krylov], specs + [ANYWHERE]
        slot = product - 1 if product else None
        acc, *rest = call(
            functools.partial(own_kernel, plan, slot), "own", ins, specs, outs, out_specs, scratch, aliases
        )
        if product > 0:
            *rest, krylov = rest
        if plan.paired:
            received = lax.ppermute(rest[0], axes, plan.across)
            fars = [received, lax.ppermute(received, axes, plan.near)]
        ins = [index, acc, near, over, dense, row_wide]
        if product < PRODUCTS - 1:
            ins += [col_wide, coupled, *fars]
            current, *sends = call(
                functools.partial(finish_kernel, plan, len(fars)),
                "finish",
                ins,
                [IN_SMEM] + [IN_VMEM] * (len(ins) - 1),
                [block_out, *sends_out],
            )
        else:
            ins += [*fars, krylov]
            (krylov,) = call(
                functools.partial(last_kernel, plan, len(fars), product),
                "last",
                ins,
                [IN_SMEM] + [IN_VMEM] * (len(ins) - 2) + [ANYWHERE],
                [krylov_out],
                [ANYWHERE],
                [pltpu.VMEM((rhs, shard_len), BF16), pltpu.SemaphoreType.DMA],
                {len(ins) - 1: 0},
            )
    return krylov


def solution(mesh):
    split = ("groups", "loop", "far")
    wide, narrow = P(split, None, None), P(split)
    in_specs = (P(None, split), wide, narrow, narrow, wide, wide, narrow, narrow, wide)
    return jax.shard_map(
        on_device, mesh=mesh, in_specs=in_specs, out_specs=P(None, None, split), check_vma=False
    )
```

```python
import functools

import jax
import jax.numpy as jnp
from jax import lax
from jax.experimental import pallas as pl
from jax.experimental.pallas import tpu as pltpu
from jax.sharding import PartitionSpec as P

PRODUCTS = 4
REACH = 4
LEVELS = 3
SPAN = 2 * REACH + 1

F32 = jnp.float32
BF16 = jnp.bfloat16
IN_VMEM = pl.BlockSpec(memory_space=pltpu.VMEM)
IN_SMEM = pl.BlockSpec(memory_space=pltpu.SMEM)
IN_HBM = pl.BlockSpec(memory_space=pltpu.HBM)
ANYWHERE = pl.BlockSpec(memory_space=pl.ANY)


def dot_nt(a, b):
    return lax.dot_general(a, b, (((1,), (1,)), ((), ())), preferred_element_type=F32)


def dot_nn(a, b):
    return lax.dot_general(a, b, (((1,), (0,)), ((), ())), preferred_element_type=F32)


def halves(value):
    upper = value.astype(BF16)
    return upper, (value - upper.astype(F32)).astype(BF16)


class Plan:
    def __init__(self, block_shape, tile_shape, coupling_shape, members, loop_size):
        self.rhs, self.shard_len = block_shape
        self.tiles, self.size, _ = tile_shape
        self.slots, self.rank, _ = coupling_shape
        self.members, self.loop_size = members, loop_size
        self.per_device = self.shard_len // self.size
        self.width = self.per_device * self.rank
        self.cells = self.per_device * SPAN
        self.block_clusters = self.per_device * members
        distances = [d % loop_size for d in (2, loop_size - 2, loop_size // 2)]
        self.hops = sorted(set(distances))
        self.sets = [[i for i, d in enumerate(distances) if d == hop] for hop in self.hops]
        self.paired = len(self.hops) == 1 and 2 * self.hops[0] == loop_size and members == 4
        devices = members * loop_size
        self.near = [(i, i ^ 1) for i in range(devices)]
        self.over = [(i, (i + 1 if i % 2 else i - 1) % devices) for i in range(devices)]
        places = [(l, m) for l in range(loop_size) for m in range(members)]
        self.across = [
            (l * members + m, (l + self.hops[0]) % loop_size * members + (m ^ (m % 2 * 2)))
            for l, m in places
        ]
        self.routes = [
            [(l * members + m, (l + hop) % loop_size * members + (m + step) % members) for l, m in places]
            for hop in self.hops
            for step in range(members)
        ]

    def panel(self, ref, c):
        return ref[:, c * self.size : (c + 1) * self.size]

    def member(self, index_ref):
        return lax.rem(index_ref[0], self.members)

    def send_far(self, index_ref, x, cb_ref, g_ref, out_refs):
        coeffs = dot_nt(x, cb_ref[...]).astype(BF16)
        totals = [sum(dot_nt(coeffs, g_ref[level]) for level in levels) for levels in self.sets]
        if not self.paired:
            for i, out_ref in enumerate(out_refs):
                step = i % self.members * self.width
                out_ref[...] = totals[i // self.members][:, step : step + self.width].astype(BF16)
            return
        message_ref, keep_ref = out_refs
        (total,) = totals
        member = self.member(index_ref)
        second = lax.rem(member, 2) != lax.div(member, 2)
        first, last = total[:, : 2 * self.width], total[:, 2 * self.width :]
        keep_ref[...] = jnp.where(second, last, first)
        upper, lower = halves(jnp.where(second, first, last))
        message_ref[:, : self.shard_len] = x
        message_ref[:, self.shard_len : self.shard_len + 2 * self.width] = upper
        message_ref[:, self.shard_len + 2 * self.width :] = lower

    def relay_far(self, keep_ref, message_ref, out_ref):
        upper = message_ref[:, self.shard_len : self.shard_len + 2 * self.width].astype(F32)
        lower = message_ref[:, self.shard_len + 2 * self.width :].astype(F32)
        out_ref[...] = (keep_ref[...] + (upper + lower)).astype(BF16)

    def far_sum(self, index_ref, far_refs):
        if not self.paired:
            return sum(ref[...].astype(F32) for ref in far_refs)
        both = far_refs[0][...].astype(F32) + far_refs[1][...].astype(F32)
        second = lax.rem(index_ref[0], 2) == 1
        return jnp.where(second, both[:, self.width :], both[:, : self.width])

    def own_sums(self, x_ref, d_ref, acc_ref):
        panels = [self.panel(x_ref, c) for c in range(self.per_device)]
        for r in range(self.per_device):
            acc_ref[:, r * self.size : (r + 1) * self.size] = sum(
                dot_nt(panels[c], d_ref[r * SPAN + c - r + REACH]) for c in range(self.per_device)
            )

    def halo_sums(self, index_ref, acc_ref, near_ref, over_ref, d_ref, out_ref):
        odd = lax.rem(index_ref[0], 2) == 1
        low, high = [], []
        for c in range(self.per_device):
            near, over = self.panel(near_ref, c), self.panel(over_ref, c)
            low.append(jnp.where(odd, near, over))
            high.append(jnp.where(odd, over, near))
        for r in range(self.per_device):
            value = self.panel(acc_ref, r)
            for c in range(self.per_device):
                for panel, place in ((low[c], c - self.per_device), (high[c], c + self.per_device)):
                    offset = place - r
                    if -REACH <= offset <= REACH:
                        value = value + dot_nt(panel, d_ref[r * SPAN + offset + REACH])
            out_ref[:, r * self.size : (r + 1) * self.size] = value

    def next_block(self, index_ref, acc_ref, rb_ref, far_refs):
        both = jnp.concatenate(halves(self.far_sum(index_ref, far_refs)), axis=1)
        return (acc_ref[...] + dot_nn(both, rb_ref[...])).astype(BF16)


def prepare_kernel(plan, index_ref, *refs):
    sources, refs = refs[:5], refs[5:]
    x_ref, g_ref, cb_ref = refs[:3]
    sends, (rows_ref, cols_ref, col_ref, coup_ref, sems) = refs[3:-5], refs[-5:]
    targets = (rows_ref, cols_ref, x_ref, col_ref, coup_ref)
    copies = [
        pltpu.make_async_copy(source, target, sems.at[i])
        for i, (source, target) in enumerate(zip(sources, targets))
    ]
    for copy in copies:
        copy.start()
    rank, size = plan.rank, plan.size
    cb_ref[...] = jnp.zeros_like(cb_ref)
    g_ref[...] = jnp.zeros_like(g_ref)
    for copy in copies:
        copy.wait()
    for c in range(plan.per_device):
        cb_ref[c * rank : (c + 1) * rank, c * size : (c + 1) * size] = col_ref[c]
    column = lax.broadcasted_iota(jnp.int32, (rank, plan.width), 1) // rank
    shift = 0 if plan.paired else plan.member(index_ref)
    for s in range(plan.slots):
        level = lax.div(rows_ref[s], plan.block_clusters)
        row = lax.rem(rows_ref[s], plan.block_clusters)
        step = lax.rem(lax.div(row, plan.per_device) - shift + plan.members, plan.members)
        place = step * plan.per_device + lax.rem(row, plan.per_device)
        where = (level, pl.ds(pl.multiple_of(place * rank, rank), rank), slice(None))
        tile = coup_ref[s].astype(F32)
        wide = jnp.where(column == cols_ref[s], jnp.concatenate([tile] * plan.per_device, axis=1), 0.0)
        g_ref[where] = g_ref[where] + wide.astype(BF16)
    plan.send_far(index_ref, x_ref[...], cb_ref, g_ref, sends)


def relay_kernel(plan, keep_ref, message_ref, out_ref):
    plan.relay_far(keep_ref, message_ref, out_ref)


def first_own_kernel(plan, *refs):
    x_ref, rows_hbm, offsets_hbm, row_hbm, tiles_hbm = refs[:5]
    acc_ref, d_ref, rb_ref, rows_ref, offsets_ref, row_ref, present, sems, tile_sems = refs[-9:]
    pairs = ((rows_hbm, rows_ref), (offsets_hbm, offsets_ref), (row_hbm, row_ref))
    copies = [pltpu.make_async_copy(*pair, sems.at[i]) for i, pair in enumerate(pairs)]
    for copy in copies:
        copy.start()
    rb_ref[...] = jnp.zeros_like(rb_ref)
    for cell in range(plan.cells):
        present[cell] = 0
    copies[0].wait()
    copies[1].wait()
    tiles = []
    for s in range(plan.tiles):
        cell = rows_ref[s] * SPAN + offsets_ref[s] + REACH
        present[cell] = 1
        tiles.append(pltpu.make_async_copy(tiles_hbm.at[s], d_ref.at[cell], tile_sems.at[s]))
        tiles[-1].start()
    copies[2].wait()
    rank, size = plan.rank, plan.size
    for c in range(plan.per_device):
        for start in (c * rank, plan.width + c * rank):
            rb_ref[start : start + rank, c * size : (c + 1) * size] = row_ref[c]
    for copy in tiles:
        copy.wait()

    @pl.loop(0, plan.cells)
    def _(cell):
        @pl.when(present[cell] == 0)
        def _():
            d_ref[cell] = jnp.zeros(d_ref.shape[1:], d_ref.dtype)

    plan.own_sums(x_ref, d_ref, acc_ref)


def own_kernel(plan, slot, *refs):
    x_ref, d_ref = refs[:2]
    acc_ref, krylov_ref, sem = refs[-3:]
    copy = pltpu.make_async_copy(x_ref, krylov_ref.at[slot], sem)
    copy.start()
    plan.own_sums(x_ref, d_ref, acc_ref)
    copy.wait()


def halo_kernel(plan, index_ref, acc_ref, near_ref, over_ref, d_ref, *refs):
    plan.halo_sums(index_ref, acc_ref, near_ref, over_ref, d_ref, refs[-1])


def finish_kernel(plan, fars, *refs):
    index_ref, acc_ref, rb_ref, cb_ref, g_ref = refs[:5]
    far_refs, (x_ref, *sends) = refs[5 : 5 + fars], refs[5 + fars :]
    x = plan.next_block(index_ref, acc_ref, rb_ref, far_refs)
    x_ref[...] = x
    plan.send_far(index_ref, x, cb_ref, g_ref, sends)


def last_kernel(plan, fars, slot, *refs):
    index_ref, acc_ref, rb_ref = refs[:3]
    far_refs, (_, krylov_ref, x_ref, sem) = refs[3 : 3 + fars], refs[3 + fars :]
    x_ref[...] = plan.next_block(index_ref, acc_ref, rb_ref, far_refs)
    copy = pltpu.make_async_copy(x_ref, krylov_ref.at[slot], sem)
    copy.start()
    copy.wait()


def call(kernel, name, ins, specs, outs, out_specs=None, scratch=(), aliases=None):
    spaces = {id(IN_VMEM): pltpu.VMEM, id(IN_HBM): pltpu.HBM}
    ins = [
        pltpu.with_memory_space_constraint(v, spaces[id(spec)]) if id(spec) in spaces else v
        for v, spec in zip(ins, specs)
    ]
    return pl.pallas_call(
        kernel,
        in_specs=list(specs),
        out_specs=out_specs or [IN_VMEM] * len(outs),
        out_shape=list(outs),
        scratch_shapes=list(scratch),
        input_output_aliases=aliases or {},
        compiler_params=pltpu.CompilerParams(vmem_limit_bytes=16 * 2**20),
        cost_estimate=pl.CostEstimate(flops=10**9, bytes_accessed=2**22, transcendentals=0),
        name=name,
    )(*ins)


def on_device(
    block, near_tiles, near_rows, near_offsets, col_basis, couplings, far_rows, far_cols, row_basis
):
    axes = ("loop", "far")
    plan = Plan(
        block.shape, near_tiles.shape, couplings.shape, lax.axis_size("far"), lax.axis_size("loop")
    )
    rhs, shard_len, width = plan.rhs, plan.shard_len, plan.width
    block_out = pltpu.VMEM((rhs, shard_len), BF16)
    acc_out = pltpu.VMEM((rhs, shard_len), F32)
    relay_out = pltpu.VMEM((rhs, 2 * width), BF16)
    krylov_out = jax.ShapeDtypeStruct((PRODUCTS, rhs, shard_len), BF16)
    if plan.paired:
        sends_out = [
            pltpu.VMEM((rhs, shard_len + 4 * width), BF16),
            pltpu.VMEM((rhs, 2 * width), F32),
        ]
    else:
        sends_out = [pltpu.VMEM((rhs, width), BF16)] * len(plan.routes)
    index = lax.axis_index(axes).astype(jnp.int32).reshape(1)

    def scratch_for(*arrays):
        return [
            pltpu.SMEM(v.shape, v.dtype) if v.dtype == jnp.int32 else pltpu.VMEM(v.shape, v.dtype)
            for v in arrays
        ]

    current, sends, krylov = block, None, None
    for product in range(PRODUCTS):
        if product == 0:
            ins = [far_rows, far_cols, block, col_basis, couplings]
            current, coupled, col_wide, *sends = call(
                functools.partial(prepare_kernel, plan),
                "prepare",
                [index, *ins],
                [IN_SMEM] + [IN_HBM] * 5,
                [
                    block_out,
                    pltpu.VMEM((LEVELS, plan.members * width, width), BF16),
                    pltpu.VMEM((width, shard_len), BF16),
                    *sends_out,
                ],
                scratch=scratch_for(far_rows, far_cols, col_basis, couplings)
                + [pltpu.SemaphoreType.DMA((5,))],
            )
        near = lax.ppermute(sends[0] if plan.paired else current, axes, plan.near)
        over = lax.ppermute(block if product == 0 else current, axes, plan.over)
        if plan.paired:
            (relayed,) = call(
                functools.partial(relay_kernel, plan), "relay", [sends[1], near], [IN_VMEM] * 2, [relay_out]
            )
            fars = [lax.ppermute(relayed, axes, plan.across)]
        else:
            fars = [lax.ppermute(s, axes, route) for s, route in zip(sends, plan.routes)]
        after = [relayed] if plan.paired else []
        if product == 0:
            acc, dense, row_wide = call(
                functools.partial(first_own_kernel, plan),
                "first_own",
                [current, near_rows, near_offsets, row_basis, near_tiles, *after],
                [IN_VMEM] + [IN_HBM] * 4 + [ANYWHERE] * len(after),
                [
                    acc_out,
                    pltpu.VMEM((plan.cells, plan.size, plan.size), BF16),
                    pltpu.VMEM((2 * width, shard_len), BF16),
                ],
                scratch=scratch_for(near_rows, near_offsets, row_basis)
                + [
                    pltpu.SMEM((plan.cells,), jnp.int32),
                    pltpu.SemaphoreType.DMA((3,)),
                    pltpu.SemaphoreType.DMA((plan.tiles,)),
                ],
            )
        else:
            ins = [current, dense, *after] + ([krylov] if product > 1 else [])
            acc, krylov = call(
                functools.partial(own_kernel, plan, product - 1),
                "own",
                ins,
                [IN_VMEM] * 2 + [ANYWHERE] * (len(ins) - 2),
                [acc_out, krylov_out],
                [IN_VMEM, ANYWHERE],
                [pltpu.SemaphoreType.DMA],
                {len(ins) - 1: 1} if product > 1 else None,
            )
        after = list(fars) if plan.paired else []
        if plan.paired:
            fars.append(lax.ppermute(fars[0], axes, plan.near))
        (acc,) = call(
            functools.partial(halo_kernel, plan),
            "halo",
            [index, acc, near, over, dense, *after],
            [IN_SMEM] + [IN_VMEM] * 4 + [ANYWHERE] * len(after),
            [acc_out],
        )
        if product < PRODUCTS - 1:
            ins = [index, acc, row_wide, col_wide, coupled, *fars]
            current, *sends = call(
                functools.partial(finish_kernel, plan, len(fars)),
                "finish",
                ins,
                [IN_SMEM] + [IN_VMEM] * (len(ins) - 1),
                [block_out, *sends_out],
            )
        else:
            ins = [index, acc, row_wide, *fars, krylov]
            (krylov,) = call(
                functools.partial(last_kernel, plan, len(fars), product),
                "last",
                ins,
                [IN_SMEM] + [IN_VMEM] * (len(ins) - 2) + [ANYWHERE],
                [krylov_out],
                [ANYWHERE],
                [pltpu.VMEM((rhs, shard_len), BF16), pltpu.SemaphoreType.DMA],
                {len(ins) - 1: 0},
            )
    return krylov


def solution(mesh):
    split = ("groups", "loop", "far")
    wide, narrow = P(split, None, None), P(split)
    in_specs = (P(None, split), wide, narrow, narrow, wide, wide, narrow, narrow, wide)
    return jax.shard_map(
        on_device, mesh=mesh, in_specs=in_specs, out_specs=P(None, None, split), check_vma=False
    )
```

```python
import functools

import jax
import jax.numpy as jnp
from jax import lax
from jax.experimental import pallas as pl
from jax.experimental.pallas import tpu as pltpu
from jax.sharding import PartitionSpec as P

PRODUCTS = 4
REACH = 4
LEVELS = 3
SPAN = 2 * REACH + 1

F32 = jnp.float32
BF16 = jnp.bfloat16
IN_VMEM = pl.BlockSpec(memory_space=pltpu.VMEM)
IN_SMEM = pl.BlockSpec(memory_space=pltpu.SMEM)
IN_HBM = pl.BlockSpec(memory_space=pltpu.HBM)
ANYWHERE = pl.BlockSpec(memory_space=pl.ANY)


def dot_nt(a, b):
    return lax.dot_general(a, b, (((1,), (1,)), ((), ())), preferred_element_type=F32)


def dot_nn(a, b):
    return lax.dot_general(a, b, (((1,), (0,)), ((), ())), preferred_element_type=F32)


def halves(value):
    upper = value.astype(BF16)
    return upper, (value - upper.astype(F32)).astype(BF16)


class Plan:
    def __init__(self, block_shape, tile_shape, coupling_shape, members, loop_size):
        self.rhs, self.shard_len = block_shape
        self.tiles, self.size, _ = tile_shape
        self.slots, self.rank, _ = coupling_shape
        self.members, self.loop_size = members, loop_size
        self.per_device = self.shard_len // self.size
        self.width = self.per_device * self.rank
        self.cells = self.per_device * SPAN
        self.block_clusters = self.per_device * members
        distances = [d % loop_size for d in (2, loop_size - 2, loop_size // 2)]
        self.hops = sorted(set(distances))
        self.sets = [[i for i, d in enumerate(distances) if d == hop] for hop in self.hops]
        self.paired = len(self.hops) == 1 and 2 * self.hops[0] == loop_size and members == 4
        devices = members * loop_size
        self.near = [(i, i ^ 1) for i in range(devices)]
        self.over = [(i, (i + 1 if i % 2 else i - 1) % devices) for i in range(devices)]
        places = [(l, m) for l in range(loop_size) for m in range(members)]
        self.across = [
            (l * members + m, (l + self.hops[0]) % loop_size * members + (m ^ (m % 2 * 2)))
            for l, m in places
        ]
        self.routes = [
            [(l * members + m, (l + hop) % loop_size * members + (m + step) % members) for l, m in places]
            for hop in self.hops
            for step in range(members)
        ]

    def panel(self, ref, c):
        return ref[:, c * self.size : (c + 1) * self.size]

    def member(self, index_ref):
        return lax.rem(index_ref[0], self.members)

    def send_far(self, index_ref, x, cb_ref, g_ref, out_refs):
        coeffs = dot_nt(x, cb_ref[...]).astype(BF16)
        totals = [sum(dot_nt(coeffs, g_ref[level]) for level in levels) for levels in self.sets]
        if not self.paired:
            for i, out_ref in enumerate(out_refs):
                step = i % self.members * self.width
                out_ref[...] = totals[i // self.members][:, step : step + self.width].astype(BF16)
            return
        message_ref, keep_ref = out_refs
        (total,) = totals
        member = self.member(index_ref)
        second = lax.rem(member, 2) != lax.div(member, 2)
        first, last = total[:, : 2 * self.width], total[:, 2 * self.width :]
        keep_ref[...] = jnp.where(second, last, first)
        upper, lower = halves(jnp.where(second, first, last))
        message_ref[:, : self.shard_len] = x
        message_ref[:, self.shard_len : self.shard_len + 2 * self.width] = upper
        message_ref[:, self.shard_len + 2 * self.width :] = lower

    def relay_far(self, keep_ref, message_ref, out_ref):
        upper = message_ref[:, self.shard_len : self.shard_len + 2 * self.width].astype(F32)
        lower = message_ref[:, self.shard_len + 2 * self.width :].astype(F32)
        out_ref[...] = (keep_ref[...] + (upper + lower)).astype(BF16)

    def far_sum(self, index_ref, far_refs):
        if not self.paired:
            return sum(ref[...].astype(F32) for ref in far_refs)
        both = far_refs[0][...].astype(F32) + far_refs[1][...].astype(F32)
        second = lax.rem(index_ref[0], 2) == 1
        return jnp.where(second, both[:, self.width :], both[:, : self.width])

    def near_sums(self, x_ref, d_ref, acc_ref, first, start_ref=None):
        panels = [self.panel(x_ref, c) for c in range(self.per_device)]
        for r in range(self.per_device):
            value = None if start_ref is None else self.panel(start_ref, r)
            for c in range(self.per_device):
                offset = first + c - r
                if -REACH <= offset <= REACH:
                    term = dot_nt(panels[c], d_ref[r * SPAN + offset + REACH])
                    value = term if value is None else value + term
            acc_ref[:, r * self.size : (r + 1) * self.size] = value

    def halo_sums(self, below, x_ref, d_ref, acc_ref, start_ref):
        @pl.when(below)
        def _():
            self.near_sums(x_ref, d_ref, acc_ref, -self.per_device, start_ref)

        @pl.when(jnp.logical_not(below))
        def _():
            self.near_sums(x_ref, d_ref, acc_ref, self.per_device, start_ref)

    def next_block(self, index_ref, acc_ref, rb_ref, far_refs):
        both = jnp.concatenate(halves(self.far_sum(index_ref, far_refs)), axis=1)
        return (acc_ref[...] + dot_nn(both, rb_ref[...])).astype(BF16)


def prepare_kernel(plan, index_ref, *refs):
    sources, refs = refs[:5], refs[5:]
    x_ref, g_ref, cb_ref = refs[:3]
    sends, (rows_ref, cols_ref, col_ref, coup_ref, sems) = refs[3:-5], refs[-5:]
    targets = (rows_ref, cols_ref, x_ref, col_ref, coup_ref)
    copies = [
        pltpu.make_async_copy(source, target, sems.at[i])
        for i, (source, target) in enumerate(zip(sources, targets))
    ]
    for copy in copies:
        copy.start()
    rank, size = plan.rank, plan.size
    cb_ref[...] = jnp.zeros_like(cb_ref)
    g_ref[...] = jnp.zeros_like(g_ref)
    for copy in copies:
        copy.wait()
    for c in range(plan.per_device):
        cb_ref[c * rank : (c + 1) * rank, c * size : (c + 1) * size] = col_ref[c]
    column = lax.broadcasted_iota(jnp.int32, (rank, plan.width), 1) // rank
    shift = 0 if plan.paired else plan.member(index_ref)
    for s in range(plan.slots):
        level = lax.div(rows_ref[s], plan.block_clusters)
        row = lax.rem(rows_ref[s], plan.block_clusters)
        step = lax.rem(lax.div(row, plan.per_device) - shift + plan.members, plan.members)
        place = step * plan.per_device + lax.rem(row, plan.per_device)
        where = (level, pl.ds(pl.multiple_of(place * rank, rank), rank), slice(None))
        tile = coup_ref[s].astype(F32)
        wide = jnp.where(column == cols_ref[s], jnp.concatenate([tile] * plan.per_device, axis=1), 0.0)
        g_ref[where] = g_ref[where] + wide.astype(BF16)
    plan.send_far(index_ref, x_ref[...], cb_ref, g_ref, sends)


def relay_kernel(plan, keep_ref, message_ref, out_ref):
    plan.relay_far(keep_ref, message_ref, out_ref)


def first_own_kernel(plan, *refs):
    index_ref, x_ref, near_ref, rows_hbm, offsets_hbm, row_hbm, tiles_hbm = refs[:7]
    acc_ref, d_ref, rb_ref, rows_ref, offsets_ref, row_ref, present, sems, tile_sems = refs[-9:]
    pairs = ((rows_hbm, rows_ref), (offsets_hbm, offsets_ref), (row_hbm, row_ref))
    copies = [pltpu.make_async_copy(*pair, sems.at[i]) for i, pair in enumerate(pairs)]
    for copy in copies:
        copy.start()
    rb_ref[...] = jnp.zeros_like(rb_ref)
    for cell in range(plan.cells):
        present[cell] = 0
    copies[0].wait()
    copies[1].wait()
    tiles = []
    for s in range(plan.tiles):
        cell = rows_ref[s] * SPAN + offsets_ref[s] + REACH
        present[cell] = 1
        tiles.append(pltpu.make_async_copy(tiles_hbm.at[s], d_ref.at[cell], tile_sems.at[s]))
        tiles[-1].start()
    copies[2].wait()
    rank, size = plan.rank, plan.size
    for c in range(plan.per_device):
        for start in (c * rank, plan.width + c * rank):
            rb_ref[start : start + rank, c * size : (c + 1) * size] = row_ref[c]
    for copy in tiles:
        copy.wait()

    @pl.loop(0, plan.cells)
    def _(cell):
        @pl.when(present[cell] == 0)
        def _():
            d_ref[cell] = jnp.zeros(d_ref.shape[1:], d_ref.dtype)

    plan.near_sums(x_ref, d_ref, acc_ref, 0)
    plan.halo_sums(lax.rem(index_ref[0], 2) == 1, near_ref, d_ref, acc_ref, acc_ref)


def own_kernel(plan, slot, *refs):
    index_ref, x_ref, near_ref, d_ref = refs[:4]
    acc_ref, krylov_ref, sem = refs[-3:]
    copy = pltpu.make_async_copy(x_ref, krylov_ref.at[slot], sem)
    copy.start()
    plan.near_sums(x_ref, d_ref, acc_ref, 0)
    plan.halo_sums(lax.rem(index_ref[0], 2) == 1, near_ref, d_ref, acc_ref, acc_ref)
    copy.wait()


def halo_kernel(plan, index_ref, acc_ref, over_ref, d_ref, *refs):
    plan.halo_sums(lax.rem(index_ref[0], 2) == 0, over_ref, d_ref, refs[-1], acc_ref)


def finish_kernel(plan, fars, *refs):
    index_ref, acc_ref, rb_ref, cb_ref, g_ref = refs[:5]
    far_refs, (x_ref, *sends) = refs[5 : 5 + fars], refs[5 + fars :]
    x = plan.next_block(index_ref, acc_ref, rb_ref, far_refs)
    x_ref[...] = x
    plan.send_far(index_ref, x, cb_ref, g_ref, sends)


def last_kernel(plan, fars, slot, *refs):
    index_ref, acc_ref, rb_ref = refs[:3]
    far_refs, (_, krylov_ref, x_ref, sem) = refs[3 : 3 + fars], refs[3 + fars :]
    x_ref[...] = plan.next_block(index_ref, acc_ref, rb_ref, far_refs)
    copy = pltpu.make_async_copy(x_ref, krylov_ref.at[slot], sem)
    copy.start()
    copy.wait()


def call(kernel, name, ins, specs, outs, out_specs=None, scratch=(), aliases=None):
    spaces = {id(IN_VMEM): pltpu.VMEM, id(IN_HBM): pltpu.HBM}
    ins = [
        pltpu.with_memory_space_constraint(v, spaces[id(spec)]) if id(spec) in spaces else v
        for v, spec in zip(ins, specs)
    ]
    return pl.pallas_call(
        kernel,
        in_specs=list(specs),
        out_specs=out_specs or [IN_VMEM] * len(outs),
        out_shape=list(outs),
        scratch_shapes=list(scratch),
        input_output_aliases=aliases or {},
        compiler_params=pltpu.CompilerParams(vmem_limit_bytes=16 * 2**20),
        cost_estimate=pl.CostEstimate(flops=10**9, bytes_accessed=2**22, transcendentals=0),
        name=name,
    )(*ins)


def on_device(
    block, near_tiles, near_rows, near_offsets, col_basis, couplings, far_rows, far_cols, row_basis
):
    axes = ("loop", "far")
    plan = Plan(
        block.shape, near_tiles.shape, couplings.shape, lax.axis_size("far"), lax.axis_size("loop")
    )
    rhs, shard_len, width = plan.rhs, plan.shard_len, plan.width
    block_out = pltpu.VMEM((rhs, shard_len), BF16)
    acc_out = pltpu.VMEM((rhs, shard_len), F32)
    relay_out = pltpu.VMEM((rhs, 2 * width), BF16)
    krylov_out = jax.ShapeDtypeStruct((PRODUCTS, rhs, shard_len), BF16)
    if plan.paired:
        sends_out = [
            pltpu.VMEM((rhs, shard_len + 4 * width), BF16),
            pltpu.VMEM((rhs, 2 * width), F32),
        ]
    else:
        sends_out = [pltpu.VMEM((rhs, width), BF16)] * len(plan.routes)
    index = lax.axis_index(axes).astype(jnp.int32).reshape(1)

    def scratch_for(*arrays):
        return [
            pltpu.SMEM(v.shape, v.dtype) if v.dtype == jnp.int32 else pltpu.VMEM(v.shape, v.dtype)
            for v in arrays
        ]

    current, sends, krylov = block, None, None
    for product in range(PRODUCTS):
        if product == 0:
            ins = [far_rows, far_cols, block, col_basis, couplings]
            current, coupled, col_wide, *sends = call(
                functools.partial(prepare_kernel, plan),
                "prepare",
                [index, *ins],
                [IN_SMEM] + [IN_HBM] * 5,
                [
                    block_out,
                    pltpu.VMEM((LEVELS, plan.members * width, width), BF16),
                    pltpu.VMEM((width, shard_len), BF16),
                    *sends_out,
                ],
                scratch=scratch_for(far_rows, far_cols, col_basis, couplings)
                + [pltpu.SemaphoreType.DMA((5,))],
            )
        near = lax.ppermute(sends[0] if plan.paired else current, axes, plan.near)
        over = lax.ppermute(block if product == 0 else current, axes, plan.over)
        if plan.paired:
            (relayed,) = call(
                functools.partial(relay_kernel, plan), "relay", [sends[1], near], [IN_VMEM] * 2, [relay_out]
            )
            fars = [lax.ppermute(relayed, axes, plan.across)]
        else:
            fars = [lax.ppermute(s, axes, route) for s, route in zip(sends, plan.routes)]
        after = [relayed] if plan.paired else []
        if product == 0:
            acc, dense, row_wide = call(
                functools.partial(first_own_kernel, plan),
                "first_own",
                [index, current, near, near_rows, near_offsets, row_basis, near_tiles, *after],
                [IN_SMEM] + [IN_VMEM] * 2 + [IN_HBM] * 4 + [ANYWHERE] * len(after),
                [
                    acc_out,
                    pltpu.VMEM((plan.cells, plan.size, plan.size), BF16),
                    pltpu.VMEM((2 * width, shard_len), BF16),
                ],
                scratch=scratch_for(near_rows, near_offsets, row_basis)
                + [
                    pltpu.SMEM((plan.cells,), jnp.int32),
                    pltpu.SemaphoreType.DMA((3,)),
                    pltpu.SemaphoreType.DMA((plan.tiles,)),
                ],
            )
        else:
            ins = [index, current, near, dense, *after] + ([krylov] if product > 1 else [])
            acc, krylov = call(
                functools.partial(own_kernel, plan, product - 1),
                "own",
                ins,
                [IN_SMEM] + [IN_VMEM] * 3 + [ANYWHERE] * (len(ins) - 4),
                [acc_out, krylov_out],
                [IN_VMEM, ANYWHERE],
                [pltpu.SemaphoreType.DMA],
                {len(ins) - 1: 1} if product > 1 else None,
            )
        after = list(fars) if plan.paired else []
        if plan.paired:
            fars.append(lax.ppermute(fars[0], axes, plan.near))
        (acc,) = call(
            functools.partial(halo_kernel, plan),
            "halo",
            [index, acc, over, dense, *after],
            [IN_SMEM] + [IN_VMEM] * 3 + [ANYWHERE] * len(after),
            [acc_out],
        )
        if product < PRODUCTS - 1:
            ins = [index, acc, row_wide, col_wide, coupled, *fars]
            current, *sends = call(
                functools.partial(finish_kernel, plan, len(fars)),
                "finish",
                ins,
                [IN_SMEM] + [IN_VMEM] * (len(ins) - 1),
                [block_out, *sends_out],
            )
        else:
            ins = [index, acc, row_wide, *fars, krylov]
            (krylov,) = call(
                functools.partial(last_kernel, plan, len(fars), product),
                "last",
                ins,
                [IN_SMEM] + [IN_VMEM] * (len(ins) - 2) + [ANYWHERE],
                [krylov_out],
                [ANYWHERE],
                [pltpu.VMEM((rhs, shard_len), BF16), pltpu.SemaphoreType.DMA],
                {len(ins) - 1: 0},
            )
    return krylov


def solution(mesh):
    split = ("groups", "loop", "far")
    wide, narrow = P(split, None, None), P(split)
    in_specs = (P(None, split), wide, narrow, narrow, wide, wide, narrow, narrow, wide)
    return jax.shard_map(
        on_device, mesh=mesh, in_specs=in_specs, out_specs=P(None, None, split), check_vma=False
    )
```

```python
import functools

import jax
import jax.numpy as jnp
from jax import lax
from jax.experimental import pallas as pl
from jax.experimental.pallas import tpu as pltpu
from jax.sharding import PartitionSpec as P

PRODUCTS = 4
REACH = 4
LEVELS = 3
SPAN = 2 * REACH + 1

F32 = jnp.float32
BF16 = jnp.bfloat16
IN_VMEM = pl.BlockSpec(memory_space=pltpu.VMEM)
IN_SMEM = pl.BlockSpec(memory_space=pltpu.SMEM)
IN_HBM = pl.BlockSpec(memory_space=pltpu.HBM)
ANYWHERE = pl.BlockSpec(memory_space=pl.ANY)


def dot_nt(a, b):
    return lax.dot_general(a, b, (((1,), (1,)), ((), ())), preferred_element_type=F32)


def dot_nn(a, b):
    return lax.dot_general(a, b, (((1,), (0,)), ((), ())), preferred_element_type=F32)


def halves(value):
    upper = value.astype(BF16)
    return upper, (value - upper.astype(F32)).astype(BF16)


class Plan:
    def __init__(self, block_shape, tile_shape, coupling_shape, members, loop_size):
        self.rhs, self.shard_len = block_shape
        self.tiles, self.size, _ = tile_shape
        self.slots, self.rank, _ = coupling_shape
        self.members, self.loop_size = members, loop_size
        self.per_device = self.shard_len // self.size
        self.width = self.per_device * self.rank
        self.cells = self.per_device * SPAN
        self.block_clusters = self.per_device * members
        distances = [d % loop_size for d in (2, loop_size - 2, loop_size // 2)]
        self.hops = sorted(set(distances))
        self.sets = [[i for i, d in enumerate(distances) if d == hop] for hop in self.hops]
        self.paired = len(self.hops) == 1 and 2 * self.hops[0] == loop_size and members == 4
        devices = members * loop_size
        self.near = [(i, i ^ 1) for i in range(devices)]
        self.over = [(i, (i + 1 if i % 2 else i - 1) % devices) for i in range(devices)]
        places = [(l, m) for l in range(loop_size) for m in range(members)]
        self.across = [
            [
                (l * members + m, (l + self.hops[0]) % loop_size * members + (m ^ (m % 2 * 2) ^ other))
                for l, m in places
            ]
            for other in range(2)
        ]
        self.routes = [
            [(l * members + m, (l + hop) % loop_size * members + (m + step) % members) for l, m in places]
            for hop in self.hops
            for step in range(members)
        ]

    def panel(self, ref, c):
        return ref[:, c * self.size : (c + 1) * self.size]

    def member(self, index_ref):
        return lax.rem(index_ref[0], self.members)

    def send_far(self, index_ref, x, cb_ref, g_ref, out_refs):
        coeffs = dot_nt(x, cb_ref[...]).astype(BF16)
        totals = [sum(dot_nt(coeffs, g_ref[level]) for level in levels) for levels in self.sets]
        if not self.paired:
            for i, out_ref in enumerate(out_refs):
                step = i % self.members * self.width
                out_ref[...] = totals[i // self.members][:, step : step + self.width].astype(BF16)
            return
        message_ref, keep_ref = out_refs
        (total,) = totals
        member = self.member(index_ref)
        second = lax.rem(member, 2) != lax.div(member, 2)
        first, last = total[:, : 2 * self.width], total[:, 2 * self.width :]
        keep_ref[...] = jnp.where(second, last, first)
        upper, lower = halves(jnp.where(second, first, last))
        message_ref[:, : self.shard_len] = x
        message_ref[:, self.shard_len : self.shard_len + 2 * self.width] = upper
        message_ref[:, self.shard_len + 2 * self.width :] = lower

    def relay_far(self, index_ref, keep_ref, message_ref, out_refs):
        upper = message_ref[:, self.shard_len : self.shard_len + 2 * self.width].astype(F32)
        lower = message_ref[:, self.shard_len + 2 * self.width :].astype(F32)
        total = (keep_ref[...] + (upper + lower)).astype(BF16)
        second = lax.rem(index_ref[0], 2) == 1
        first, last = total[:, : self.width], total[:, self.width :]
        out_refs[0][...] = jnp.where(second, last, first)
        out_refs[1][...] = jnp.where(second, first, last)

    def far_sum(self, far_refs):
        return sum(ref[...].astype(F32) for ref in far_refs)

    def near_sums(self, x_ref, d_ref, acc_ref, first, start_ref=None):
        panels = [self.panel(x_ref, c) for c in range(self.per_device)]
        for r in range(self.per_device):
            value = None if start_ref is None else self.panel(start_ref, r)
            for c in range(self.per_device):
                offset = first + c - r
                if -REACH <= offset <= REACH:
                    term = dot_nt(panels[c], d_ref[r * SPAN + offset + REACH])
                    value = term if value is None else value + term
            acc_ref[:, r * self.size : (r + 1) * self.size] = value

    def halo_sums(self, below, x_ref, d_ref, acc_ref, start_ref):
        @pl.when(below)
        def _():
            self.near_sums(x_ref, d_ref, acc_ref, -self.per_device, start_ref)

        @pl.when(jnp.logical_not(below))
        def _():
            self.near_sums(x_ref, d_ref, acc_ref, self.per_device, start_ref)

    def next_block(self, acc_ref, rb_ref, far_refs):
        both = jnp.concatenate(halves(self.far_sum(far_refs)), axis=1)
        return (acc_ref[...] + dot_nn(both, rb_ref[...])).astype(BF16)


def prepare_kernel(plan, index_ref, *refs):
    sources, refs = refs[:5], refs[5:]
    x_ref, g_ref, cb_ref = refs[:3]
    sends, (rows_ref, cols_ref, col_ref, coup_ref, sems) = refs[3:-5], refs[-5:]
    targets = (rows_ref, cols_ref, x_ref, col_ref, coup_ref)
    copies = [
        pltpu.make_async_copy(source, target, sems.at[i])
        for i, (source, target) in enumerate(zip(sources, targets))
    ]
    for copy in copies:
        copy.start()
    rank, size = plan.rank, plan.size
    cb_ref[...] = jnp.zeros_like(cb_ref)
    g_ref[...] = jnp.zeros_like(g_ref)
    for copy in copies:
        copy.wait()
    for c in range(plan.per_device):
        cb_ref[c * rank : (c + 1) * rank, c * size : (c + 1) * size] = col_ref[c]
    column = lax.broadcasted_iota(jnp.int32, (rank, plan.width), 1) // rank
    shift = 0 if plan.paired else plan.member(index_ref)
    for s in range(plan.slots):
        level = lax.div(rows_ref[s], plan.block_clusters)
        row = lax.rem(rows_ref[s], plan.block_clusters)
        step = lax.rem(lax.div(row, plan.per_device) - shift + plan.members, plan.members)
        place = step * plan.per_device + lax.rem(row, plan.per_device)
        where = (level, pl.ds(pl.multiple_of(place * rank, rank), rank), slice(None))
        tile = coup_ref[s].astype(F32)
        wide = jnp.where(column == cols_ref[s], jnp.concatenate([tile] * plan.per_device, axis=1), 0.0)
        g_ref[where] = g_ref[where] + wide.astype(BF16)
    plan.send_far(index_ref, x_ref[...], cb_ref, g_ref, sends)


def relay_kernel(plan, index_ref, keep_ref, message_ref, *out_refs):
    plan.relay_far(index_ref, keep_ref, message_ref, out_refs)


def first_own_kernel(plan, *refs):
    index_ref, x_ref, near_ref, rows_hbm, offsets_hbm, row_hbm, tiles_hbm = refs[:7]
    acc_ref, d_ref, rb_ref, rows_ref, offsets_ref, row_ref, present, sems, tile_sems = refs[-9:]
    pairs = ((rows_hbm, rows_ref), (offsets_hbm, offsets_ref), (row_hbm, row_ref))
    copies = [pltpu.make_async_copy(*pair, sems.at[i]) for i, pair in enumerate(pairs)]
    for copy in copies:
        copy.start()
    rb_ref[...] = jnp.zeros_like(rb_ref)
    for cell in range(plan.cells):
        present[cell] = 0
    copies[0].wait()
    copies[1].wait()
    tiles = []
    for s in range(plan.tiles):
        cell = rows_ref[s] * SPAN + offsets_ref[s] + REACH
        present[cell] = 1
        tiles.append(pltpu.make_async_copy(tiles_hbm.at[s], d_ref.at[cell], tile_sems.at[s]))
        tiles[-1].start()
    copies[2].wait()
    rank, size = plan.rank, plan.size
    for c in range(plan.per_device):
        for start in (c * rank, plan.width + c * rank):
            rb_ref[start : start + rank, c * size : (c + 1) * size] = row_ref[c]
    for copy in tiles:
        copy.wait()

    @pl.loop(0, plan.cells)
    def _(cell):
        @pl.when(present[cell] == 0)
        def _():
            d_ref[cell] = jnp.zeros(d_ref.shape[1:], d_ref.dtype)

    plan.near_sums(x_ref, d_ref, acc_ref, 0)
    plan.halo_sums(lax.rem(index_ref[0], 2) == 1, near_ref, d_ref, acc_ref, acc_ref)


def own_kernel(plan, slot, *refs):
    index_ref, x_ref, near_ref, d_ref = refs[:4]
    acc_ref, krylov_ref, sem = refs[-3:]
    copy = pltpu.make_async_copy(x_ref, krylov_ref.at[slot], sem)
    copy.start()
    plan.near_sums(x_ref, d_ref, acc_ref, 0)
    plan.halo_sums(lax.rem(index_ref[0], 2) == 1, near_ref, d_ref, acc_ref, acc_ref)
    copy.wait()


def halo_kernel(plan, index_ref, acc_ref, over_ref, d_ref, *refs):
    plan.halo_sums(lax.rem(index_ref[0], 2) == 0, over_ref, d_ref, refs[-1], acc_ref)


def finish_kernel(plan, fars, *refs):
    index_ref, acc_ref, rb_ref, cb_ref, g_ref = refs[:5]
    far_refs, (x_ref, *sends) = refs[5 : 5 + fars], refs[5 + fars :]
    x = plan.next_block(acc_ref, rb_ref, far_refs)
    x_ref[...] = x
    plan.send_far(index_ref, x, cb_ref, g_ref, sends)


def last_kernel(plan, fars, slot, *refs):
    acc_ref, rb_ref = refs[:2]
    far_refs, (_, krylov_ref, x_ref, sem) = refs[2 : 2 + fars], refs[2 + fars :]
    x_ref[...] = plan.next_block(acc_ref, rb_ref, far_refs)
    copy = pltpu.make_async_copy(x_ref, krylov_ref.at[slot], sem)
    copy.start()
    copy.wait()


def call(kernel, name, ins, specs, outs, out_specs=None, scratch=(), aliases=None):
    spaces = {id(IN_VMEM): pltpu.VMEM, id(IN_HBM): pltpu.HBM}
    ins = [
        pltpu.with_memory_space_constraint(v, spaces[id(spec)]) if id(spec) in spaces else v
        for v, spec in zip(ins, specs)
    ]
    return pl.pallas_call(
        kernel,
        in_specs=list(specs),
        out_specs=out_specs or [IN_VMEM] * len(outs),
        out_shape=list(outs),
        scratch_shapes=list(scratch),
        input_output_aliases=aliases or {},
        compiler_params=pltpu.CompilerParams(vmem_limit_bytes=16 * 2**20),
        cost_estimate=pl.CostEstimate(flops=10**9, bytes_accessed=2**22, transcendentals=0),
        name=name,
    )(*ins)


def on_device(
    block, near_tiles, near_rows, near_offsets, col_basis, couplings, far_rows, far_cols, row_basis
):
    axes = ("loop", "far")
    plan = Plan(
        block.shape, near_tiles.shape, couplings.shape, lax.axis_size("far"), lax.axis_size("loop")
    )
    rhs, shard_len, width = plan.rhs, plan.shard_len, plan.width
    block_out = pltpu.VMEM((rhs, shard_len), BF16)
    acc_out = pltpu.VMEM((rhs, shard_len), F32)
    relay_out = pltpu.VMEM((rhs, width), BF16)
    krylov_out = jax.ShapeDtypeStruct((PRODUCTS, rhs, shard_len), BF16)
    if plan.paired:
        sends_out = [
            pltpu.VMEM((rhs, shard_len + 4 * width), BF16),
            pltpu.VMEM((rhs, 2 * width), F32),
        ]
    else:
        sends_out = [pltpu.VMEM((rhs, width), BF16)] * len(plan.routes)
    index = lax.axis_index(axes).astype(jnp.int32).reshape(1)

    def scratch_for(*arrays):
        return [
            pltpu.SMEM(v.shape, v.dtype) if v.dtype == jnp.int32 else pltpu.VMEM(v.shape, v.dtype)
            for v in arrays
        ]

    current, sends, krylov = block, None, None
    for product in range(PRODUCTS):
        if product == 0:
            ins = [far_rows, far_cols, block, col_basis, couplings]
            current, coupled, col_wide, *sends = call(
                functools.partial(prepare_kernel, plan),
                "prepare",
                [index, *ins],
                [IN_SMEM] + [IN_HBM] * 5,
                [
                    block_out,
                    pltpu.VMEM((LEVELS, plan.members * width, width), BF16),
                    pltpu.VMEM((width, shard_len), BF16),
                    *sends_out,
                ],
                scratch=scratch_for(far_rows, far_cols, col_basis, couplings)
                + [pltpu.SemaphoreType.DMA((5,))],
            )
        near = lax.ppermute(sends[0] if plan.paired else current, axes, plan.near)
        over = lax.ppermute(block if product == 0 else current, axes, plan.over)
        if plan.paired:
            sends = call(
                functools.partial(relay_kernel, plan),
                "relay",
                [index, sends[1], near],
                [IN_SMEM] + [IN_VMEM] * 2,
                [relay_out] * 2,
            )
            routes = plan.across
        else:
            routes = plan.routes
        fars = [lax.ppermute(s, axes, route) for s, route in zip(sends, routes)]
        after = sends if plan.paired else []
        if product == 0:
            acc, dense, row_wide = call(
                functools.partial(first_own_kernel, plan),
                "first_own",
                [index, current, near, near_rows, near_offsets, row_basis, near_tiles, *after],
                [IN_SMEM] + [IN_VMEM] * 2 + [IN_HBM] * 4 + [ANYWHERE] * len(after),
                [
                    acc_out,
                    pltpu.VMEM((plan.cells, plan.size, plan.size), BF16),
                    pltpu.VMEM((2 * width, shard_len), BF16),
                ],
                scratch=scratch_for(near_rows, near_offsets, row_basis)
                + [
                    pltpu.SMEM((plan.cells,), jnp.int32),
                    pltpu.SemaphoreType.DMA((3,)),
                    pltpu.SemaphoreType.DMA((plan.tiles,)),
                ],
            )
        else:
            ins = [index, current, near, dense, *after] + ([krylov] if product > 1 else [])
            acc, krylov = call(
                functools.partial(own_kernel, plan, product - 1),
                "own",
                ins,
                [IN_SMEM] + [IN_VMEM] * 3 + [ANYWHERE] * (len(ins) - 4),
                [acc_out, krylov_out],
                [IN_VMEM, ANYWHERE],
                [pltpu.SemaphoreType.DMA],
                {len(ins) - 1: 1} if product > 1 else None,
            )
        (acc,) = call(
            functools.partial(halo_kernel, plan),
            "halo",
            [index, acc, over, dense],
            [IN_SMEM] + [IN_VMEM] * 3,
            [acc_out],
        )
        if product < PRODUCTS - 1:
            ins = [index, acc, row_wide, col_wide, coupled, *fars]
            current, *sends = call(
                functools.partial(finish_kernel, plan, len(fars)),
                "finish",
                ins,
                [IN_SMEM] + [IN_VMEM] * (len(ins) - 1),
                [block_out, *sends_out],
            )
        else:
            ins = [acc, row_wide, *fars, krylov]
            (krylov,) = call(
                functools.partial(last_kernel, plan, len(fars), product),
                "last",
                ins,
                [IN_VMEM] * (len(ins) - 1) + [ANYWHERE],
                [krylov_out],
                [ANYWHERE],
                [pltpu.VMEM((rhs, shard_len), BF16), pltpu.SemaphoreType.DMA],
                {len(ins) - 1: 0},
            )
    return krylov


def solution(mesh):
    split = ("groups", "loop", "far")
    wide, narrow = P(split, None, None), P(split)
    in_specs = (P(None, split), wide, narrow, narrow, wide, wide, narrow, narrow, wide)
    return jax.shard_map(
        on_device, mesh=mesh, in_specs=in_specs, out_specs=P(None, None, split), check_vma=False
    )
```

```python
import functools

import jax
import jax.numpy as jnp
from jax import lax
from jax.experimental import pallas as pl
from jax.experimental.pallas import tpu as pltpu
from jax.sharding import PartitionSpec as P

PRODUCTS = 4
REACH = 4
LEVELS = 3
SPAN = 2 * REACH + 1

F32 = jnp.float32
BF16 = jnp.bfloat16
IN_VMEM = pl.BlockSpec(memory_space=pltpu.VMEM)
IN_SMEM = pl.BlockSpec(memory_space=pltpu.SMEM)
IN_HBM = pl.BlockSpec(memory_space=pltpu.HBM)
ANYWHERE = pl.BlockSpec(memory_space=pl.ANY)


def dot_nt(a, b):
    return lax.dot_general(a, b, (((1,), (1,)), ((), ())), preferred_element_type=F32)


def dot_nn(a, b):
    return lax.dot_general(a, b, (((1,), (0,)), ((), ())), preferred_element_type=F32)


def halves(value):
    upper = value.astype(BF16)
    return upper, (value - upper.astype(F32)).astype(BF16)


class Plan:
    def __init__(self, block_shape, tile_shape, coupling_shape, members, loop_size):
        self.rhs, self.shard_len = block_shape
        self.tiles, self.size, _ = tile_shape
        self.slots, self.rank, _ = coupling_shape
        self.members, self.loop_size = members, loop_size
        self.per_device = self.shard_len // self.size
        self.width = self.per_device * self.rank
        self.cells = self.per_device * SPAN
        self.block_clusters = self.per_device * members
        distances = [d % loop_size for d in (2, loop_size - 2, loop_size // 2)]
        self.hops = sorted(set(distances))
        self.sets = [[i for i, d in enumerate(distances) if d == hop] for hop in self.hops]
        self.paired = len(self.hops) == 1 and 2 * self.hops[0] == loop_size and members == 4
        devices = members * loop_size
        self.near = [(i, i ^ 1) for i in range(devices)]
        self.over = [(i, (i + 1 if i % 2 else i - 1) % devices) for i in range(devices)]
        places = [(l, m) for l in range(loop_size) for m in range(members)]
        self.across = [
            [
                (l * members + m, (l + self.hops[0]) % loop_size * members + (m ^ other))
                for l, m in places
            ]
            for other in (2, 0)
        ]
        self.routes = [
            [(l * members + m, (l + hop) % loop_size * members + (m + step) % members) for l, m in places]
            for hop in self.hops
            for step in range(members)
        ]

    def panel(self, ref, c):
        return ref[:, c * self.size : (c + 1) * self.size]

    def member(self, index_ref):
        return lax.rem(index_ref[0], self.members)

    def send_far(self, index_ref, x, cb_ref, g_ref, out_refs):
        coeffs = dot_nt(x, cb_ref[...]).astype(BF16)
        totals = [sum(dot_nt(coeffs, g_ref[level]) for level in levels) for levels in self.sets]
        if not self.paired:
            for i, out_ref in enumerate(out_refs):
                step = i % self.members * self.width
                out_ref[...] = totals[i // self.members][:, step : step + self.width].astype(BF16)
            return
        message_ref, keep_ref = out_refs
        (total,) = totals
        pieces = [total[:, i * self.width : (i + 1) * self.width] for i in range(self.members)]
        even = jnp.concatenate(pieces[0::2], axis=1)
        odd = jnp.concatenate(pieces[1::2], axis=1)
        second = lax.rem(index_ref[0], 2) == 1
        keep_ref[...] = jnp.where(second, odd, even)
        upper, lower = halves(jnp.where(second, even, odd))
        message_ref[:, : self.shard_len] = x
        message_ref[:, self.shard_len : self.shard_len + 2 * self.width] = upper
        message_ref[:, self.shard_len + 2 * self.width :] = lower

    def relay_far(self, index_ref, keep_ref, message_ref, out_refs):
        upper = message_ref[:, self.shard_len : self.shard_len + 2 * self.width].astype(F32)
        lower = message_ref[:, self.shard_len + 2 * self.width :].astype(F32)
        total = (keep_ref[...] + (upper + lower)).astype(BF16)
        second = self.member(index_ref) >= 2
        first, last = total[:, : self.width], total[:, self.width :]
        out_refs[0][...] = jnp.where(second, first, last)
        out_refs[1][...] = jnp.where(second, last, first)

    def far_sum(self, far_refs):
        return sum(ref[...].astype(F32) for ref in far_refs)

    def near_sums(self, x_ref, d_ref, acc_ref, first, start_ref=None):
        panels = [self.panel(x_ref, c) for c in range(self.per_device)]
        for r in range(self.per_device):
            value = None if start_ref is None else self.panel(start_ref, r)
            for c in range(self.per_device):
                offset = first + c - r
                if -REACH <= offset <= REACH:
                    term = dot_nt(panels[c], d_ref[r * SPAN + offset + REACH])
                    value = term if value is None else value + term
            acc_ref[:, r * self.size : (r + 1) * self.size] = value

    def halo_sums(self, below, x_ref, d_ref, acc_ref, start_ref):
        @pl.when(below)
        def _():
            self.near_sums(x_ref, d_ref, acc_ref, -self.per_device, start_ref)

        @pl.when(jnp.logical_not(below))
        def _():
            self.near_sums(x_ref, d_ref, acc_ref, self.per_device, start_ref)

    def next_block(self, acc_ref, rb_ref, far_refs):
        both = jnp.concatenate(halves(self.far_sum(far_refs)), axis=1)
        return (acc_ref[...] + dot_nn(both, rb_ref[...])).astype(BF16)


def prepare_kernel(plan, index_ref, *refs):
    sources, refs = refs[:5], refs[5:]
    x_ref, g_ref, cb_ref = refs[:3]
    sends, (rows_ref, cols_ref, col_ref, coup_ref, sems) = refs[3:-5], refs[-5:]
    targets = (rows_ref, cols_ref, x_ref, col_ref, coup_ref)
    copies = [
        pltpu.make_async_copy(source, target, sems.at[i])
        for i, (source, target) in enumerate(zip(sources, targets))
    ]
    for copy in copies:
        copy.start()
    rank, size = plan.rank, plan.size
    cb_ref[...] = jnp.zeros_like(cb_ref)
    g_ref[...] = jnp.zeros_like(g_ref)
    for copy in copies:
        copy.wait()
    for c in range(plan.per_device):
        cb_ref[c * rank : (c + 1) * rank, c * size : (c + 1) * size] = col_ref[c]
    column = lax.broadcasted_iota(jnp.int32, (rank, plan.width), 1) // rank
    shift = 0 if plan.paired else plan.member(index_ref)
    for s in range(plan.slots):
        level = lax.div(rows_ref[s], plan.block_clusters)
        row = lax.rem(rows_ref[s], plan.block_clusters)
        step = lax.rem(lax.div(row, plan.per_device) - shift + plan.members, plan.members)
        place = step * plan.per_device + lax.rem(row, plan.per_device)
        where = (level, pl.ds(pl.multiple_of(place * rank, rank), rank), slice(None))
        tile = coup_ref[s].astype(F32)
        wide = jnp.where(column == cols_ref[s], jnp.concatenate([tile] * plan.per_device, axis=1), 0.0)
        g_ref[where] = g_ref[where] + wide.astype(BF16)
    plan.send_far(index_ref, x_ref[...], cb_ref, g_ref, sends)


def relay_kernel(plan, index_ref, keep_ref, message_ref, *out_refs):
    plan.relay_far(index_ref, keep_ref, message_ref, out_refs)


def first_own_kernel(plan, *refs):
    index_ref, x_ref, near_ref, rows_hbm, offsets_hbm, row_hbm, tiles_hbm = refs[:7]
    acc_ref, d_ref, rb_ref, rows_ref, offsets_ref, row_ref, present, sems, tile_sems = refs[-9:]
    pairs = ((rows_hbm, rows_ref), (offsets_hbm, offsets_ref), (row_hbm, row_ref))
    copies = [pltpu.make_async_copy(*pair, sems.at[i]) for i, pair in enumerate(pairs)]
    for copy in copies:
        copy.start()
    rb_ref[...] = jnp.zeros_like(rb_ref)
    for cell in range(plan.cells):
        present[cell] = 0
    copies[0].wait()
    copies[1].wait()
    tiles = []
    for s in range(plan.tiles):
        cell = rows_ref[s] * SPAN + offsets_ref[s] + REACH
        present[cell] = 1
        tiles.append(pltpu.make_async_copy(tiles_hbm.at[s], d_ref.at[cell], tile_sems.at[s]))
        tiles[-1].start()
    copies[2].wait()
    rank, size = plan.rank, plan.size
    for c in range(plan.per_device):
        for start in (c * rank, plan.width + c * rank):
            rb_ref[start : start + rank, c * size : (c + 1) * size] = row_ref[c]
    for copy in tiles:
        copy.wait()

    @pl.loop(0, plan.cells)
    def _(cell):
        @pl.when(present[cell] == 0)
        def _():
            d_ref[cell] = jnp.zeros(d_ref.shape[1:], d_ref.dtype)

    plan.near_sums(x_ref, d_ref, acc_ref, 0)
    plan.halo_sums(lax.rem(index_ref[0], 2) == 1, near_ref, d_ref, acc_ref, acc_ref)


def own_kernel(plan, slot, *refs):
    index_ref, x_ref, near_ref, d_ref = refs[:4]
    acc_ref, krylov_ref, sem = refs[-3:]
    copy = pltpu.make_async_copy(x_ref, krylov_ref.at[slot], sem)
    copy.start()
    plan.near_sums(x_ref, d_ref, acc_ref, 0)
    plan.halo_sums(lax.rem(index_ref[0], 2) == 1, near_ref, d_ref, acc_ref, acc_ref)
    copy.wait()


def halo_kernel(plan, index_ref, acc_ref, over_ref, d_ref, *refs):
    plan.halo_sums(lax.rem(index_ref[0], 2) == 0, over_ref, d_ref, refs[-1], acc_ref)


def finish_kernel(plan, fars, *refs):
    index_ref, acc_ref, rb_ref, cb_ref, g_ref = refs[:5]
    far_refs, (x_ref, *sends) = refs[5 : 5 + fars], refs[5 + fars :]
    x = plan.next_block(acc_ref, rb_ref, far_refs)
    x_ref[...] = x
    plan.send_far(index_ref, x, cb_ref, g_ref, sends)


def last_kernel(plan, fars, slot, *refs):
    acc_ref, rb_ref = refs[:2]
    far_refs, (_, krylov_ref, x_ref, sem) = refs[2 : 2 + fars], refs[2 + fars :]
    x_ref[...] = plan.next_block(acc_ref, rb_ref, far_refs)
    copy = pltpu.make_async_copy(x_ref, krylov_ref.at[slot], sem)
    copy.start()
    copy.wait()


def call(kernel, name, ins, specs, outs, out_specs=None, scratch=(), aliases=None):
    spaces = {id(IN_VMEM): pltpu.VMEM, id(IN_HBM): pltpu.HBM}
    ins = [
        pltpu.with_memory_space_constraint(v, spaces[id(spec)]) if id(spec) in spaces else v
        for v, spec in zip(ins, specs)
    ]
    return pl.pallas_call(
        kernel,
        in_specs=list(specs),
        out_specs=out_specs or [IN_VMEM] * len(outs),
        out_shape=list(outs),
        scratch_shapes=list(scratch),
        input_output_aliases=aliases or {},
        compiler_params=pltpu.CompilerParams(vmem_limit_bytes=16 * 2**20),
        cost_estimate=pl.CostEstimate(flops=10**9, bytes_accessed=2**22, transcendentals=0),
        name=name,
    )(*ins)


def on_device(
    block, near_tiles, near_rows, near_offsets, col_basis, couplings, far_rows, far_cols, row_basis
):
    axes = ("loop", "far")
    plan = Plan(
        block.shape, near_tiles.shape, couplings.shape, lax.axis_size("far"), lax.axis_size("loop")
    )
    rhs, shard_len, width = plan.rhs, plan.shard_len, plan.width
    block_out = pltpu.VMEM((rhs, shard_len), BF16)
    acc_out = pltpu.VMEM((rhs, shard_len), F32)
    relay_out = pltpu.VMEM((rhs, width), BF16)
    krylov_out = jax.ShapeDtypeStruct((PRODUCTS, rhs, shard_len), BF16)
    if plan.paired:
        sends_out = [
            pltpu.VMEM((rhs, shard_len + 4 * width), BF16),
            pltpu.VMEM((rhs, 2 * width), F32),
        ]
    else:
        sends_out = [pltpu.VMEM((rhs, width), BF16)] * len(plan.routes)
    index = lax.axis_index(axes).astype(jnp.int32).reshape(1)

    def scratch_for(*arrays):
        return [
            pltpu.SMEM(v.shape, v.dtype) if v.dtype == jnp.int32 else pltpu.VMEM(v.shape, v.dtype)
            for v in arrays
        ]

    current, sends, krylov = block, None, None
    for product in range(PRODUCTS):
        if product == 0:
            ins = [far_rows, far_cols, block, col_basis, couplings]
            current, coupled, col_wide, *sends = call(
                functools.partial(prepare_kernel, plan),
                "prepare",
                [index, *ins],
                [IN_SMEM] + [IN_HBM] * 5,
                [
                    block_out,
                    pltpu.VMEM((LEVELS, plan.members * width, width), BF16),
                    pltpu.VMEM((width, shard_len), BF16),
                    *sends_out,
                ],
                scratch=scratch_for(far_rows, far_cols, col_basis, couplings)
                + [pltpu.SemaphoreType.DMA((5,))],
            )
        near = lax.ppermute(sends[0] if plan.paired else current, axes, plan.near)
        over = lax.ppermute(block if product == 0 else current, axes, plan.over)
        if plan.paired:
            sends = call(
                functools.partial(relay_kernel, plan),
                "relay",
                [index, sends[1], near],
                [IN_SMEM] + [IN_VMEM] * 2,
                [relay_out] * 2,
            )
            routes = plan.across
        else:
            routes = plan.routes
        fars = [lax.ppermute(s, axes, route) for s, route in zip(sends, routes)]
        after = sends if plan.paired else []
        if product == 0:
            acc, dense, row_wide = call(
                functools.partial(first_own_kernel, plan),
                "first_own",
                [index, current, near, near_rows, near_offsets, row_basis, near_tiles, *after],
                [IN_SMEM] + [IN_VMEM] * 2 + [IN_HBM] * 4 + [ANYWHERE] * len(after),
                [
                    acc_out,
                    pltpu.VMEM((plan.cells, plan.size, plan.size), BF16),
                    pltpu.VMEM((2 * width, shard_len), BF16),
                ],
                scratch=scratch_for(near_rows, near_offsets, row_basis)
                + [
                    pltpu.SMEM((plan.cells,), jnp.int32),
                    pltpu.SemaphoreType.DMA((3,)),
                    pltpu.SemaphoreType.DMA((plan.tiles,)),
                ],
            )
        else:
            ins = [index, current, near, dense, *after] + ([krylov] if product > 1 else [])
            acc, krylov = call(
                functools.partial(own_kernel, plan, product - 1),
                "own",
                ins,
                [IN_SMEM] + [IN_VMEM] * 3 + [ANYWHERE] * (len(ins) - 4),
                [acc_out, krylov_out],
                [IN_VMEM, ANYWHERE],
                [pltpu.SemaphoreType.DMA],
                {len(ins) - 1: 1} if product > 1 else None,
            )
        (acc,) = call(
            functools.partial(halo_kernel, plan),
            "halo",
            [index, acc, over, dense],
            [IN_SMEM] + [IN_VMEM] * 3,
            [acc_out],
        )
        if product < PRODUCTS - 1:
            ins = [index, acc, row_wide, col_wide, coupled, *fars]
            current, *sends = call(
                functools.partial(finish_kernel, plan, len(fars)),
                "finish",
                ins,
                [IN_SMEM] + [IN_VMEM] * (len(ins) - 1),
                [block_out, *sends_out],
            )
        else:
            ins = [acc, row_wide, *fars, krylov]
            (krylov,) = call(
                functools.partial(last_kernel, plan, len(fars), product),
                "last",
                ins,
                [IN_VMEM] * (len(ins) - 1) + [ANYWHERE],
                [krylov_out],
                [ANYWHERE],
                [pltpu.VMEM((rhs, shard_len), BF16), pltpu.SemaphoreType.DMA],
                {len(ins) - 1: 0},
            )
    return krylov


def solution(mesh):
    split = ("groups", "loop", "far")
    wide, narrow = P(split, None, None), P(split)
    in_specs = (P(None, split), wide, narrow, narrow, wide, wide, narrow, narrow, wide)
    return jax.shard_map(
        on_device, mesh=mesh, in_specs=in_specs, out_specs=P(None, None, split), check_vma=False
    )
```

```python
import functools

import jax
import jax.numpy as jnp
from jax import lax
from jax.experimental import pallas as pl
from jax.experimental.pallas import tpu as pltpu
from jax.sharding import PartitionSpec as P

PRODUCTS = 4
REACH = 4
LEVELS = 3
SPAN = 2 * REACH + 1

F32 = jnp.float32
BF16 = jnp.bfloat16
IN_VMEM = pl.BlockSpec(memory_space=pltpu.VMEM)
IN_SMEM = pl.BlockSpec(memory_space=pltpu.SMEM)
IN_HBM = pl.BlockSpec(memory_space=pltpu.HBM)
ANYWHERE = pl.BlockSpec(memory_space=pl.ANY)


def dot_nt(a, b):
    return lax.dot_general(a, b, (((1,), (1,)), ((), ())), preferred_element_type=F32)


def dot_nn(a, b):
    return lax.dot_general(a, b, (((1,), (0,)), ((), ())), preferred_element_type=F32)


def halves(value):
    upper = value.astype(BF16)
    return upper, (value - upper.astype(F32)).astype(BF16)


class Plan:
    def __init__(self, block_shape, tile_shape, coupling_shape, members, loop_size):
        self.rhs, self.shard_len = block_shape
        self.tiles, self.size, _ = tile_shape
        self.slots, self.rank, _ = coupling_shape
        self.members, self.loop_size = members, loop_size
        self.per_device = self.shard_len // self.size
        self.width = self.per_device * self.rank
        self.cells = self.per_device * SPAN
        self.block_clusters = self.per_device * members
        distances = [d % loop_size for d in (2, loop_size - 2, loop_size // 2)]
        self.hops = sorted(set(distances))
        self.sets = [[i for i, d in enumerate(distances) if d == hop] for hop in self.hops]
        self.paired = len(self.hops) == 1 and 2 * self.hops[0] == loop_size and members == 4
        devices = members * loop_size
        self.near = [(i, i ^ 1) for i in range(devices)]
        self.over = [(i, (i + 1 if i % 2 else i - 1) % devices) for i in range(devices)]
        places = [(l, m) for l in range(loop_size) for m in range(members)]
        self.across = [
            [
                (l * members + m, (l + self.hops[0]) % loop_size * members + (m ^ (m % 2 * 2) ^ other))
                for l, m in places
            ]
            for other in range(2)
        ]
        self.routes = [
            [(l * members + m, (l + hop) % loop_size * members + (m + step) % members) for l, m in places]
            for hop in self.hops
            for step in range(members)
        ]

    def panel(self, ref, c):
        return ref[:, c * self.size : (c + 1) * self.size]

    def member(self, index_ref):
        return lax.rem(index_ref[0], self.members)

    def send_far(self, index_ref, x, cb_ref, g_ref, out_refs):
        coeffs = dot_nt(x, cb_ref[...]).astype(BF16)
        totals = [sum(dot_nt(coeffs, g_ref[level]) for level in levels) for levels in self.sets]
        if not self.paired:
            for i, out_ref in enumerate(out_refs):
                step = i % self.members * self.width
                out_ref[...] = totals[i // self.members][:, step : step + self.width].astype(BF16)
            return
        message_ref, keep_ref = out_refs
        (total,) = totals
        member = self.member(index_ref)
        second = lax.rem(member, 2) != lax.div(member, 2)
        first, last = total[:, : 2 * self.width], total[:, 2 * self.width :]
        keep_ref[...] = jnp.where(second, last, first)
        upper, lower = halves(jnp.where(second, first, last))
        message_ref[:, : self.shard_len] = x
        message_ref[:, self.shard_len : self.shard_len + 2 * self.width] = upper
        message_ref[:, self.shard_len + 2 * self.width :] = lower

    def relay_far(self, index_ref, keep_ref, message_ref, out_refs):
        upper = message_ref[:, self.shard_len : self.shard_len + 2 * self.width].astype(F32)
        lower = message_ref[:, self.shard_len + 2 * self.width :].astype(F32)
        total = (keep_ref[...] + (upper + lower)).astype(BF16)
        second = lax.rem(index_ref[0], 2) == 1
        first, last = total[:, : self.width], total[:, self.width :]
        out_refs[0][...] = jnp.where(second, last, first)
        out_refs[1][...] = jnp.where(second, first, last)

    def far_sum(self, far_refs):
        return sum(ref[...].astype(F32) for ref in far_refs)

    def near_sums(self, x_ref, d_ref, acc_ref, first, start_ref=None):
        panels = [self.panel(x_ref, c) for c in range(self.per_device)]
        for r in range(self.per_device):
            value = None if start_ref is None else self.panel(start_ref, r)
            for c in range(self.per_device):
                offset = first + c - r
                if -REACH <= offset <= REACH:
                    term = dot_nt(panels[c], d_ref[r * SPAN + offset + REACH])
                    value = term if value is None else value + term
            acc_ref[:, r * self.size : (r + 1) * self.size] = value

    def halo_sums(self, below, x_ref, d_ref, acc_ref, start_ref):
        @pl.when(below)
        def _():
            self.near_sums(x_ref, d_ref, acc_ref, -self.per_device, start_ref)

        @pl.when(jnp.logical_not(below))
        def _():
            self.near_sums(x_ref, d_ref, acc_ref, self.per_device, start_ref)

    def far_halves(self, far_refs):
        return jnp.concatenate(halves(self.far_sum(far_refs)), axis=1)

    def next_panel(self, acc_ref, rb_ref, both, c):
        return (self.panel(acc_ref, c) + dot_nn(both, self.panel(rb_ref, c))).astype(BF16)

    def next_block(self, acc_ref, rb_ref, far_refs):
        both = self.far_halves(far_refs)
        panels = [self.next_panel(acc_ref, rb_ref, both, c) for c in range(self.per_device)]
        return jnp.concatenate(panels, axis=1)


def prepare_kernel(plan, index_ref, *refs):
    sources, refs = refs[:7], refs[7:]
    x_ref, g_ref, cb_ref, order_ref = refs[:4]
    sends, (near_ref, offsets_ref, rows_ref, cols_ref, col_ref, coup_ref, sems) = refs[4:-7], refs[-7:]
    targets = (near_ref, offsets_ref, rows_ref, cols_ref, x_ref, col_ref, coup_ref)
    copies = [
        pltpu.make_async_copy(source, target, sems.at[i])
        for i, (source, target) in enumerate(zip(sources, targets))
    ]
    for copy in copies:
        copy.start()
    rank, size = plan.rank, plan.size
    cb_ref[...] = jnp.zeros_like(cb_ref)
    g_ref[...] = jnp.zeros_like(g_ref)
    for copy in copies:
        copy.wait()
    first, last = jnp.int32(0), jnp.int32(plan.tiles - 1)
    for s in range(plan.tiles):
        place = near_ref[s] + offsets_ref[s]
        own = jnp.logical_and(place >= 0, place < plan.per_device).astype(jnp.int32)
        where = jnp.where(own == 1, first, last)
        order_ref[where] = s
        order_ref[plan.tiles + where] = near_ref[s] * SPAN + offsets_ref[s] + REACH
        first, last = first + own, last - (1 - own)
    order_ref[2 * plan.tiles] = first
    for c in range(plan.per_device):
        cb_ref[c * rank : (c + 1) * rank, c * size : (c + 1) * size] = col_ref[c]
    column = lax.broadcasted_iota(jnp.int32, (rank, plan.width), 1) // rank
    shift = 0 if plan.paired else plan.member(index_ref)
    for s in range(plan.slots):
        level = lax.div(rows_ref[s], plan.block_clusters)
        row = lax.rem(rows_ref[s], plan.block_clusters)
        step = lax.rem(lax.div(row, plan.per_device) - shift + plan.members, plan.members)
        place = step * plan.per_device + lax.rem(row, plan.per_device)
        where = (level, pl.ds(pl.multiple_of(place * rank, rank), rank), slice(None))
        tile = coup_ref[s].astype(F32)
        wide = jnp.where(column == cols_ref[s], jnp.concatenate([tile] * plan.per_device, axis=1), 0.0)
        g_ref[where] = g_ref[where] + wide.astype(BF16)
    plan.send_far(index_ref, x_ref[...], cb_ref, g_ref, sends)


def relay_kernel(plan, index_ref, keep_ref, message_ref, *out_refs):
    plan.relay_far(index_ref, keep_ref, message_ref, out_refs)


def first_own_kernel(plan, *refs):
    index_ref, order_ref, x_ref, near_ref, row_hbm, tiles_hbm = refs[:6]
    acc_ref, d_ref, rb_ref, row_ref, empty, sem, tile_sems = refs[-7:]
    rank, size = plan.rank, plan.size

    def tile_copy(place):
        source, cell = order_ref[place], order_ref[plan.tiles + place]
        return pltpu.make_async_copy(tiles_hbm.at[source], d_ref.at[cell], tile_sems.at[place])

    def wait_for(first, last):
        @pl.loop(first, last)
        def _(place):
            tile_copy(place).wait()

    for place in range(plan.tiles):
        tile_copy(place).start()
    copy = pltpu.make_async_copy(row_hbm, row_ref, sem)
    copy.start()
    for cell in range(plan.cells):
        empty[cell] = 1
    for place in range(plan.tiles):
        empty[order_ref[plan.tiles + place]] = 0
    count = jnp.int32(0)
    for cell in range(plan.cells):
        missing = empty[cell]
        empty[plan.cells + count] = cell
        count = count + missing

    @pl.loop(0, count)
    def _(place):
        d_ref[empty[plan.cells + place]] = jnp.zeros(d_ref.shape[1:], d_ref.dtype)

    rb_ref[...] = jnp.zeros_like(rb_ref)
    copy.wait()
    for c in range(plan.per_device):
        for start in (c * rank, plan.width + c * rank):
            rb_ref[start : start + rank, c * size : (c + 1) * size] = row_ref[c]
    own = order_ref[2 * plan.tiles]
    wait_for(0, own)
    plan.near_sums(x_ref, d_ref, acc_ref, 0)
    wait_for(own, plan.tiles)
    plan.halo_sums(lax.rem(index_ref[0], 2) == 1, near_ref, d_ref, acc_ref, acc_ref)


def own_kernel(plan, slot, *refs):
    index_ref, x_ref, near_ref, d_ref = refs[:4]
    acc_ref, krylov_ref, sem = refs[-3:]
    copy = pltpu.make_async_copy(x_ref, krylov_ref.at[slot], sem)
    copy.start()
    plan.near_sums(x_ref, d_ref, acc_ref, 0)
    plan.halo_sums(lax.rem(index_ref[0], 2) == 1, near_ref, d_ref, acc_ref, acc_ref)
    copy.wait()


def halo_kernel(plan, index_ref, acc_ref, over_ref, d_ref, *refs):
    plan.halo_sums(lax.rem(index_ref[0], 2) == 0, over_ref, d_ref, refs[-1], acc_ref)


def finish_kernel(plan, fars, *refs):
    index_ref, acc_ref, rb_ref, cb_ref, g_ref = refs[:5]
    far_refs, (x_ref, *sends) = refs[5 : 5 + fars], refs[5 + fars :]
    x = plan.next_block(acc_ref, rb_ref, far_refs)
    x_ref[...] = x
    plan.send_far(index_ref, x, cb_ref, g_ref, sends)


def last_kernel(plan, fars, slot, *refs):
    acc_ref, rb_ref = refs[:2]
    far_refs, (_, krylov_ref, x_ref, sem) = refs[2 : 2 + fars], refs[2 + fars :]
    both = plan.far_halves(far_refs)
    copies = []
    for c in range(plan.per_device):
        columns = pl.ds(c * plan.size, plan.size)
        x_ref[:, columns] = plan.next_panel(acc_ref, rb_ref, both, c)
        copies.append(
            pltpu.make_async_copy(x_ref.at[:, columns], krylov_ref.at[slot, :, columns], sem.at[c])
        )
        copies[-1].start()
    for copy in copies:
        copy.wait()


def call(kernel, name, ins, specs, outs, out_specs=None, scratch=(), aliases=None):
    spaces = {id(IN_VMEM): pltpu.VMEM, id(IN_HBM): pltpu.HBM}
    ins = [
        pltpu.with_memory_space_constraint(v, spaces[id(spec)]) if id(spec) in spaces else v
        for v, spec in zip(ins, specs)
    ]
    return pl.pallas_call(
        kernel,
        in_specs=list(specs),
        out_specs=out_specs or [IN_VMEM] * len(outs),
        out_shape=list(outs),
        scratch_shapes=list(scratch),
        input_output_aliases=aliases or {},
        compiler_params=pltpu.CompilerParams(vmem_limit_bytes=16 * 2**20),
        cost_estimate=pl.CostEstimate(flops=10**9, bytes_accessed=2**22, transcendentals=0),
        name=name,
    )(*ins)


def on_device(
    block, near_tiles, near_rows, near_offsets, col_basis, couplings, far_rows, far_cols, row_basis
):
    axes = ("loop", "far")
    plan = Plan(
        block.shape, near_tiles.shape, couplings.shape, lax.axis_size("far"), lax.axis_size("loop")
    )
    rhs, shard_len, width = plan.rhs, plan.shard_len, plan.width
    block_out = pltpu.VMEM((rhs, shard_len), BF16)
    acc_out = pltpu.VMEM((rhs, shard_len), F32)
    relay_out = pltpu.VMEM((rhs, width), BF16)
    krylov_out = jax.ShapeDtypeStruct((PRODUCTS, rhs, shard_len), BF16)
    if plan.paired:
        sends_out = [
            pltpu.VMEM((rhs, shard_len + 4 * width), BF16),
            pltpu.VMEM((rhs, 2 * width), F32),
        ]
    else:
        sends_out = [pltpu.VMEM((rhs, width), BF16)] * len(plan.routes)
    index = lax.axis_index(axes).astype(jnp.int32).reshape(1)

    def scratch_for(*arrays):
        return [
            pltpu.SMEM(v.shape, v.dtype) if v.dtype == jnp.int32 else pltpu.VMEM(v.shape, v.dtype)
            for v in arrays
        ]

    current, sends, krylov = block, None, None
    for product in range(PRODUCTS):
        if product == 0:
            ins = [near_rows, near_offsets, far_rows, far_cols, block, col_basis, couplings]
            current, coupled, col_wide, order, *sends = call(
                functools.partial(prepare_kernel, plan),
                "prepare",
                [index, *ins],
                [IN_SMEM] + [IN_HBM] * 7,
                [
                    block_out,
                    pltpu.VMEM((LEVELS, plan.members * width, width), BF16),
                    pltpu.VMEM((width, shard_len), BF16),
                    pltpu.SMEM((2 * plan.tiles + 1,), jnp.int32),
                    *sends_out,
                ],
                [IN_VMEM] * 3 + [IN_SMEM] + [IN_VMEM] * len(sends_out),
                scratch=scratch_for(near_rows, near_offsets, far_rows, far_cols, col_basis, couplings)
                + [pltpu.SemaphoreType.DMA((7,))],
            )
        near = lax.ppermute(sends[0] if plan.paired else current, axes, plan.near)
        over = lax.ppermute(block if product == 0 else current, axes, plan.over)
        if plan.paired:
            sends = call(
                functools.partial(relay_kernel, plan),
                "relay",
                [index, sends[1], near],
                [IN_SMEM] + [IN_VMEM] * 2,
                [relay_out] * 2,
            )
            routes = plan.across
        else:
            routes = plan.routes
        fars = [lax.ppermute(s, axes, route) for s, route in zip(sends, routes)]
        after = sends if plan.paired else []
        if product == 0:
            acc, dense, row_wide = call(
                functools.partial(first_own_kernel, plan),
                "first_own",
                [index, order, current, near, row_basis, near_tiles, *after],
                [IN_SMEM] * 2 + [IN_VMEM] * 2 + [IN_HBM] * 2 + [ANYWHERE] * len(after),
                [
                    acc_out,
                    pltpu.VMEM((plan.cells, plan.size, plan.size), BF16),
                    pltpu.VMEM((2 * width, shard_len), BF16),
                ],
                scratch=scratch_for(row_basis)
                + [
                    pltpu.SMEM((2 * plan.cells + 1,), jnp.int32),
                    pltpu.SemaphoreType.DMA,
                    pltpu.SemaphoreType.DMA((plan.tiles,)),
                ],
            )
        else:
            ins = [index, current, near, dense, *after] + ([krylov] if product > 1 else [])
            acc, krylov = call(
                functools.partial(own_kernel, plan, product - 1),
                "own",
                ins,
                [IN_SMEM] + [IN_VMEM] * 3 + [ANYWHERE] * (len(ins) - 4),
                [acc_out, krylov_out],
                [IN_VMEM, ANYWHERE],
                [pltpu.SemaphoreType.DMA],
                {len(ins) - 1: 1} if product > 1 else None,
            )
        (acc,) = call(
            functools.partial(halo_kernel, plan),
            "halo",
            [index, acc, over, dense],
            [IN_SMEM] + [IN_VMEM] * 3,
            [acc_out],
        )
        if product < PRODUCTS - 1:
            ins = [index, acc, row_wide, col_wide, coupled, *fars]
            current, *sends = call(
                functools.partial(finish_kernel, plan, len(fars)),
                "finish",
                ins,
                [IN_SMEM] + [IN_VMEM] * (len(ins) - 1),
                [block_out, *sends_out],
            )
        else:
            ins = [acc, row_wide, *fars, krylov]
            (krylov,) = call(
                functools.partial(last_kernel, plan, len(fars), product),
                "last",
                ins,
                [IN_VMEM] * (len(ins) - 1) + [ANYWHERE],
                [krylov_out],
                [ANYWHERE],
                [
                    pltpu.VMEM((rhs, shard_len), BF16),
                    pltpu.SemaphoreType.DMA((plan.per_device,)),
                ],
                {len(ins) - 1: 0},
            )
    return krylov


def solution(mesh):
    split = ("groups", "loop", "far")
    wide, narrow = P(split, None, None), P(split)
    in_specs = (P(None, split), wide, narrow, narrow, wide, wide, narrow, narrow, wide)
    return jax.shard_map(
        on_device, mesh=mesh, in_specs=in_specs, out_specs=P(None, None, split), check_vma=False
    )
```

```python
import functools

import jax
import jax.numpy as jnp
from jax import lax
from jax.experimental import pallas as pl
from jax.experimental.pallas import tpu as pltpu
from jax.sharding import PartitionSpec as P

PRODUCTS = 4
REACH = 4
LEVELS = 3
SPAN = 2 * REACH + 1

F32 = jnp.float32
BF16 = jnp.bfloat16
IN_VMEM = pl.BlockSpec(memory_space=pltpu.VMEM)
IN_SMEM = pl.BlockSpec(memory_space=pltpu.SMEM)
IN_HBM = pl.BlockSpec(memory_space=pltpu.HBM)
ANYWHERE = pl.BlockSpec(memory_space=pl.ANY)


def dot_nt(a, b):
    return lax.dot_general(a, b, (((1,), (1,)), ((), ())), preferred_element_type=F32)


def dot_nn(a, b):
    return lax.dot_general(a, b, (((1,), (0,)), ((), ())), preferred_element_type=F32)


def halves(value):
    upper = value.astype(BF16)
    return upper, (value - upper.astype(F32)).astype(BF16)


class Plan:
    def __init__(self, block_shape, tile_shape, coupling_shape, members, loop_size):
        self.rhs, self.shard_len = block_shape
        self.tiles, self.size, _ = tile_shape
        self.slots, self.rank, _ = coupling_shape
        self.members, self.loop_size = members, loop_size
        self.per_device = self.shard_len // self.size
        self.width = self.per_device * self.rank
        self.cells = self.per_device * SPAN
        self.block_clusters = self.per_device * members
        distances = [d % loop_size for d in (2, loop_size - 2, loop_size // 2)]
        self.hops = sorted(set(distances))
        self.sets = [[i for i, d in enumerate(distances) if d == hop] for hop in self.hops]
        self.paired = len(self.hops) == 1 and 2 * self.hops[0] == loop_size and members == 4
        devices = members * loop_size
        self.near = [(i, i ^ 1) for i in range(devices)]
        self.over = [(i, (i + 1 if i % 2 else i - 1) % devices) for i in range(devices)]
        places = [(l, m) for l in range(loop_size) for m in range(members)]
        self.across = [
            [
                (l * members + m, (l + self.hops[0]) % loop_size * members + (m ^ (m % 2 * 2) ^ other))
                for l, m in places
            ]
            for other in range(2)
        ]
        self.routes = [
            [(l * members + m, (l + hop) % loop_size * members + (m + step) % members) for l, m in places]
            for hop in self.hops
            for step in range(members)
        ]

    def panel(self, ref, c):
        return ref[:, c * self.size : (c + 1) * self.size]

    def member(self, index_ref):
        return lax.rem(index_ref[0], self.members)

    def send_far(self, index_ref, x, cb_ref, g_ref, out_refs):
        coeffs = dot_nt(x, cb_ref[...]).astype(BF16)
        totals = [sum(dot_nt(coeffs, g_ref[level]) for level in levels) for levels in self.sets]
        if not self.paired:
            for i, out_ref in enumerate(out_refs):
                step = i % self.members * self.width
                out_ref[...] = totals[i // self.members][:, step : step + self.width].astype(BF16)
            return
        message_ref, keep_ref = out_refs
        (total,) = totals
        member = self.member(index_ref)
        second = lax.rem(member, 2) != lax.div(member, 2)
        first, last = total[:, : 2 * self.width], total[:, 2 * self.width :]
        keep_ref[...] = jnp.where(second, last, first)
        upper, lower = halves(jnp.where(second, first, last))
        message_ref[:, : self.shard_len] = x
        message_ref[:, self.shard_len : self.shard_len + 2 * self.width] = upper
        message_ref[:, self.shard_len + 2 * self.width :] = lower

    def relay_far(self, index_ref, keep_ref, message_ref, out_refs):
        upper = message_ref[:, self.shard_len : self.shard_len + 2 * self.width].astype(F32)
        lower = message_ref[:, self.shard_len + 2 * self.width :].astype(F32)
        total = (keep_ref[...] + (upper + lower)).astype(BF16)
        second = lax.rem(index_ref[0], 2) == 1
        first, last = total[:, : self.width], total[:, self.width :]
        out_refs[0][...] = jnp.where(second, last, first)
        out_refs[1][...] = jnp.where(second, first, last)

    def far_sum(self, far_refs):
        return sum(ref[...].astype(F32) for ref in far_refs)

    def near_sums(self, x_ref, d_ref, acc_ref, first, start_ref=None):
        panels = [self.panel(x_ref, c) for c in range(self.per_device)]
        for r in range(self.per_device):
            value = None if start_ref is None else self.panel(start_ref, r)
            for c in range(self.per_device):
                offset = first + c - r
                if -REACH <= offset <= REACH:
                    term = dot_nt(panels[c], d_ref[r * SPAN + offset + REACH])
                    value = term if value is None else value + term
            acc_ref[:, r * self.size : (r + 1) * self.size] = value

    def halo_sums(self, below, x_ref, d_ref, acc_ref, start_ref):
        @pl.when(below)
        def _():
            self.near_sums(x_ref, d_ref, acc_ref, -self.per_device, start_ref)

        @pl.when(jnp.logical_not(below))
        def _():
            self.near_sums(x_ref, d_ref, acc_ref, self.per_device, start_ref)

    def far_halves(self, far_refs):
        return jnp.concatenate(halves(self.far_sum(far_refs)), axis=1)

    def next_panel(self, acc_ref, rb_ref, both, c):
        return (self.panel(acc_ref, c) + dot_nn(both, self.panel(rb_ref, c))).astype(BF16)

    def next_block(self, acc_ref, rb_ref, far_refs):
        both = self.far_halves(far_refs)
        panels = [self.next_panel(acc_ref, rb_ref, both, c) for c in range(self.per_device)]
        return jnp.concatenate(panels, axis=1)


def prepare_kernel(plan, index_ref, *refs):
    sources, tiles_hbm, refs = refs[:8], refs[8], refs[9:]
    x_ref, d_ref, g_ref, cb_ref, rb_ref = refs[:5]
    sends, held = refs[5:-11], refs[-11:]
    near_ref, offsets_ref, rows_ref, cols_ref, col_ref, coup_ref, row_ref, taken, empty, sems, tile_sems = held
    targets = (near_ref, offsets_ref, rows_ref, cols_ref, x_ref, col_ref, coup_ref, row_ref)
    copies = [
        pltpu.make_async_copy(source, target, sems.at[i])
        for i, (source, target) in enumerate(zip(sources, targets))
    ]
    for copy in copies:
        copy.start()
    rank, size = plan.rank, plan.size
    for cell in range(plan.cells):
        taken[cell] = 0
    cb_ref[...] = jnp.zeros_like(cb_ref)
    rb_ref[...] = jnp.zeros_like(rb_ref)
    g_ref[...] = jnp.zeros_like(g_ref)
    copies[0].wait()
    copies[1].wait()
    tiles = []
    for s in range(plan.tiles):
        cell = near_ref[s] * SPAN + offsets_ref[s] + REACH
        taken[cell] = 1
        tiles.append(pltpu.make_async_copy(tiles_hbm.at[s], d_ref.at[cell], tile_sems.at[s]))
        tiles[-1].start()
    for copy in copies[2:]:
        copy.wait()
    count = jnp.int32(0)
    for cell in range(plan.cells):
        empty[count] = cell
        count = count + 1 - taken[cell]
    for place in range(plan.cells - plan.tiles):
        d_ref[empty[place]] = jnp.zeros(d_ref.shape[1:], d_ref.dtype)
    for c in range(plan.per_device):
        columns = slice(c * size, (c + 1) * size)
        cb_ref[c * rank : (c + 1) * rank, columns] = col_ref[c]
        for start in (c * rank, plan.width + c * rank):
            rb_ref[start : start + rank, columns] = row_ref[c]
    column = lax.broadcasted_iota(jnp.int32, (rank, plan.width), 1) // rank
    shift = 0 if plan.paired else plan.member(index_ref)
    for s in range(plan.slots):
        level = lax.div(rows_ref[s], plan.block_clusters)
        row = lax.rem(rows_ref[s], plan.block_clusters)
        step = lax.rem(lax.div(row, plan.per_device) - shift + plan.members, plan.members)
        place = step * plan.per_device + lax.rem(row, plan.per_device)
        where = (level, pl.ds(pl.multiple_of(place * rank, rank), rank), slice(None))
        tile = coup_ref[s].astype(F32)
        wide = jnp.where(column == cols_ref[s], jnp.concatenate([tile] * plan.per_device, axis=1), 0.0)
        g_ref[where] = g_ref[where] + wide.astype(BF16)
    plan.send_far(index_ref, x_ref[...], cb_ref, g_ref, sends)
    for copy in tiles:
        copy.wait()


def relay_kernel(plan, index_ref, keep_ref, message_ref, *out_refs):
    plan.relay_far(index_ref, keep_ref, message_ref, out_refs)


def own_kernel(plan, slot, *refs):
    index_ref, x_ref, near_ref, d_ref = refs[:4]
    acc_ref = refs[-1] if slot is None else refs[-3]
    if slot is not None:
        copy = pltpu.make_async_copy(x_ref, refs[-2].at[slot], refs[-1])
        copy.start()
    plan.near_sums(x_ref, d_ref, acc_ref, 0)
    plan.halo_sums(lax.rem(index_ref[0], 2) == 1, near_ref, d_ref, acc_ref, acc_ref)
    if slot is not None:
        copy.wait()


def halo_kernel(plan, index_ref, acc_ref, over_ref, d_ref, *refs):
    plan.halo_sums(lax.rem(index_ref[0], 2) == 0, over_ref, d_ref, refs[-1], acc_ref)


def finish_kernel(plan, fars, *refs):
    index_ref, acc_ref, rb_ref, cb_ref, g_ref = refs[:5]
    far_refs, (x_ref, *sends) = refs[5 : 5 + fars], refs[5 + fars :]
    x = plan.next_block(acc_ref, rb_ref, far_refs)
    x_ref[...] = x
    plan.send_far(index_ref, x, cb_ref, g_ref, sends)


def last_kernel(plan, fars, slot, *refs):
    acc_ref, rb_ref = refs[:2]
    far_refs, (_, krylov_ref, x_ref, sem) = refs[2 : 2 + fars], refs[2 + fars :]
    both = plan.far_halves(far_refs)
    copies = []
    for c in range(plan.per_device):
        columns = pl.ds(c * plan.size, plan.size)
        x_ref[:, columns] = plan.next_panel(acc_ref, rb_ref, both, c)
        copies.append(
            pltpu.make_async_copy(x_ref.at[:, columns], krylov_ref.at[slot, :, columns], sem.at[c])
        )
        copies[-1].start()
    for copy in copies:
        copy.wait()


def call(kernel, name, ins, specs, outs, out_specs=None, scratch=(), aliases=None):
    spaces = {id(IN_VMEM): pltpu.VMEM, id(IN_HBM): pltpu.HBM}
    ins = [
        pltpu.with_memory_space_constraint(v, spaces[id(spec)]) if id(spec) in spaces else v
        for v, spec in zip(ins, specs)
    ]
    return pl.pallas_call(
        kernel,
        in_specs=list(specs),
        out_specs=out_specs or [IN_VMEM] * len(outs),
        out_shape=list(outs),
        scratch_shapes=list(scratch),
        input_output_aliases=aliases or {},
        compiler_params=pltpu.CompilerParams(vmem_limit_bytes=16 * 2**20),
        cost_estimate=pl.CostEstimate(flops=10**9, bytes_accessed=2**22, transcendentals=0),
        name=name,
    )(*ins)


def on_device(
    block, near_tiles, near_rows, near_offsets, col_basis, couplings, far_rows, far_cols, row_basis
):
    axes = ("loop", "far")
    plan = Plan(
        block.shape, near_tiles.shape, couplings.shape, lax.axis_size("far"), lax.axis_size("loop")
    )
    rhs, shard_len, width = plan.rhs, plan.shard_len, plan.width
    block_out = pltpu.VMEM((rhs, shard_len), BF16)
    acc_out = pltpu.VMEM((rhs, shard_len), F32)
    relay_out = pltpu.VMEM((rhs, width), BF16)
    krylov_out = jax.ShapeDtypeStruct((PRODUCTS, rhs, shard_len), BF16)
    if plan.paired:
        sends_out = [
            pltpu.VMEM((rhs, shard_len + 4 * width), BF16),
            pltpu.VMEM((rhs, 2 * width), F32),
        ]
    else:
        sends_out = [pltpu.VMEM((rhs, width), BF16)] * len(plan.routes)
    index = lax.axis_index(axes).astype(jnp.int32).reshape(1)

    def scratch_for(*arrays):
        return [
            pltpu.SMEM(v.shape, v.dtype) if v.dtype == jnp.int32 else pltpu.VMEM(v.shape, v.dtype)
            for v in arrays
        ]

    current, sends, krylov = block, None, None
    for product in range(PRODUCTS):
        if product == 0:
            small = [near_rows, near_offsets, far_rows, far_cols]
            bases = [col_basis, couplings, row_basis]
            current, dense, coupled, col_wide, row_wide, *sends = call(
                functools.partial(prepare_kernel, plan),
                "prepare",
                [index, *small, block, *bases, near_tiles],
                [IN_SMEM] + [IN_HBM] * 9,
                [
                    block_out,
                    pltpu.VMEM((plan.cells, plan.size, plan.size), BF16),
                    pltpu.VMEM((LEVELS, plan.members * width, width), BF16),
                    pltpu.VMEM((width, shard_len), BF16),
                    pltpu.VMEM((2 * width, shard_len), BF16),
                    *sends_out,
                ],
                scratch=scratch_for(*small, *bases)
                + [
                    pltpu.SMEM((plan.cells,), jnp.int32),
                    pltpu.SMEM((plan.cells,), jnp.int32),
                    pltpu.SemaphoreType.DMA((8,)),
                    pltpu.SemaphoreType.DMA((plan.tiles,)),
                ],
            )
        near = lax.ppermute(sends[0] if plan.paired else current, axes, plan.near)
        over = lax.ppermute(block if product == 0 else current, axes, plan.over)
        if plan.paired:
            sends = call(
                functools.partial(relay_kernel, plan),
                "relay",
                [index, sends[1], near],
                [IN_SMEM] + [IN_VMEM] * 2,
                [relay_out] * 2,
            )
            routes = plan.across
        else:
            routes = plan.routes
        fars = [lax.ppermute(s, axes, route) for s, route in zip(sends, routes)]
        after = sends if plan.paired else []
        ins, outs = [index, current, near, dense, *after], [acc_out]
        specs = [IN_SMEM] + [IN_VMEM] * 3 + [ANYWHERE] * len(after)
        out_specs, scratch, aliases = [IN_VMEM], [], None
        if product > 0:
            outs, out_specs, scratch = outs + [krylov_out], out_specs + [ANYWHERE], [pltpu.SemaphoreType.DMA]
        if product > 1:
            aliases = {len(ins): 1}
            ins, specs = ins + [krylov], specs + [ANYWHERE]
        slot = product - 1 if product else None
        acc, *rest = call(
            functools.partial(own_kernel, plan, slot), "own", ins, specs, outs, out_specs, scratch, aliases
        )
        krylov = rest[0] if rest else None
        (acc,) = call(
            functools.partial(halo_kernel, plan),
            "halo",
            [index, acc, over, dense],
            [IN_SMEM] + [IN_VMEM] * 3,
            [acc_out],
        )
        if product < PRODUCTS - 1:
            ins = [index, acc, row_wide, col_wide, coupled, *fars]
            current, *sends = call(
                functools.partial(finish_kernel, plan, len(fars)),
                "finish",
                ins,
                [IN_SMEM] + [IN_VMEM] * (len(ins) - 1),
                [block_out, *sends_out],
            )
        else:
            ins = [acc, row_wide, *fars, krylov]
            (krylov,) = call(
                functools.partial(last_kernel, plan, len(fars), product),
                "last",
                ins,
                [IN_VMEM] * (len(ins) - 1) + [ANYWHERE],
                [krylov_out],
                [ANYWHERE],
                [
                    pltpu.VMEM((rhs, shard_len), BF16),
                    pltpu.SemaphoreType.DMA((plan.per_device,)),
                ],
                {len(ins) - 1: 0},
            )
    return krylov


def solution(mesh):
    split = ("groups", "loop", "far")
    wide, narrow = P(split, None, None), P(split)
    in_specs = (P(None, split), wide, narrow, narrow, wide, wide, narrow, narrow, wide)
    return jax.shard_map(
        on_device, mesh=mesh, in_specs=in_specs, out_specs=P(None, None, split), check_vma=False
    )
```

```python
import functools

import jax
import jax.numpy as jnp
from jax import lax
from jax.experimental import pallas as pl
from jax.experimental.pallas import tpu as pltpu
from jax.sharding import PartitionSpec as P

PRODUCTS = 4
REACH = 4
LEVELS = 3
SPAN = 2 * REACH + 1

F32 = jnp.float32
BF16 = jnp.bfloat16
IN_VMEM = pl.BlockSpec(memory_space=pltpu.VMEM)
IN_SMEM = pl.BlockSpec(memory_space=pltpu.SMEM)
IN_HBM = pl.BlockSpec(memory_space=pltpu.HBM)
ANYWHERE = pl.BlockSpec(memory_space=pl.ANY)


def dot_nt(a, b):
    return lax.dot_general(a, b, (((1,), (1,)), ((), ())), preferred_element_type=F32)


def dot_nn(a, b):
    return lax.dot_general(a, b, (((1,), (0,)), ((), ())), preferred_element_type=F32)


def halves(value):
    upper = value.astype(BF16)
    return upper, (value - upper.astype(F32)).astype(BF16)


class Plan:
    def __init__(self, block_shape, tile_shape, coupling_shape, members, loop_size):
        self.rhs, self.shard_len = block_shape
        self.tiles, self.size, _ = tile_shape
        self.slots, self.rank, _ = coupling_shape
        self.members, self.loop_size = members, loop_size
        self.per_device = self.shard_len // self.size
        self.width = self.per_device * self.rank
        self.cells = self.per_device * SPAN
        self.block_clusters = self.per_device * members
        distances = [d % loop_size for d in (2, loop_size - 2, loop_size // 2)]
        self.hops = sorted(set(distances))
        self.sets = [[i for i, d in enumerate(distances) if d == hop] for hop in self.hops]
        self.paired = len(self.hops) == 1 and 2 * self.hops[0] == loop_size and members == 4
        devices = members * loop_size
        self.near = [(i, i ^ 1) for i in range(devices)]
        self.over = [(i, (i + 1 if i % 2 else i - 1) % devices) for i in range(devices)]
        places = [(l, m) for l in range(loop_size) for m in range(members)]
        self.across = [
            [
                (l * members + m, (l + self.hops[0]) % loop_size * members + (m ^ (m % 2 * 2) ^ other))
                for l, m in places
            ]
            for other in range(2)
        ]
        self.routes = [
            [(l * members + m, (l + hop) % loop_size * members + (m + step) % members) for l, m in places]
            for hop in self.hops
            for step in range(members)
        ]

    def panel(self, ref, c):
        return ref[:, c * self.size : (c + 1) * self.size]

    def member(self, index_ref):
        return lax.rem(index_ref[0], self.members)

    def send_far(self, index_ref, x, cb_ref, g_ref, out_refs):
        coeffs = dot_nt(x, cb_ref[...]).astype(BF16)
        totals = [sum(dot_nt(coeffs, g_ref[level]) for level in levels) for levels in self.sets]
        if not self.paired:
            for i, out_ref in enumerate(out_refs):
                step = i % self.members * self.width
                out_ref[...] = totals[i // self.members][:, step : step + self.width].astype(BF16)
            return
        message_ref, keep_ref = out_refs
        (total,) = totals
        member = self.member(index_ref)
        second = lax.rem(member, 2) != lax.div(member, 2)
        first, last = total[:, : 2 * self.width], total[:, 2 * self.width :]
        keep_ref[...] = jnp.where(second, last, first)
        upper, lower = halves(jnp.where(second, first, last))
        message_ref[:, : self.shard_len] = x
        message_ref[:, self.shard_len : self.shard_len + 2 * self.width] = upper
        message_ref[:, self.shard_len + 2 * self.width :] = lower

    def relay_far(self, index_ref, keep_ref, message_ref, out_refs):
        upper = message_ref[:, self.shard_len : self.shard_len + 2 * self.width].astype(F32)
        lower = message_ref[:, self.shard_len + 2 * self.width :].astype(F32)
        total = (keep_ref[...] + (upper + lower)).astype(BF16)
        second = lax.rem(index_ref[0], 2) == 1
        first, last = total[:, : self.width], total[:, self.width :]
        out_refs[0][...] = jnp.where(second, last, first)
        out_refs[1][...] = jnp.where(second, first, last)

    def far_sum(self, far_refs):
        return sum(ref[...].astype(F32) for ref in far_refs)

    def near_sums(self, x_ref, d_ref, acc_ref, first, start_ref=None):
        panels = [self.panel(x_ref, c) for c in range(self.per_device)]
        for r in range(self.per_device):
            value = None if start_ref is None else self.panel(start_ref, r)
            for c in range(self.per_device):
                offset = first + c - r
                if -REACH <= offset <= REACH:
                    term = dot_nt(panels[c], d_ref[r * SPAN + offset + REACH])
                    value = term if value is None else value + term
            acc_ref[:, r * self.size : (r + 1) * self.size] = value

    def halo_sums(self, below, x_ref, d_ref, acc_ref, start_ref):
        @pl.when(below)
        def _():
            self.near_sums(x_ref, d_ref, acc_ref, -self.per_device, start_ref)

        @pl.when(jnp.logical_not(below))
        def _():
            self.near_sums(x_ref, d_ref, acc_ref, self.per_device, start_ref)

    def far_halves(self, far_refs):
        return jnp.concatenate(halves(self.far_sum(far_refs)), axis=1)

    def next_panel(self, acc_ref, rb_ref, both, c):
        return (self.panel(acc_ref, c) + dot_nn(both, self.panel(rb_ref, c))).astype(BF16)

    def next_block(self, acc_ref, rb_ref, far_refs):
        both = self.far_halves(far_refs)
        panels = [self.next_panel(acc_ref, rb_ref, both, c) for c in range(self.per_device)]
        return jnp.concatenate(panels, axis=1)


def prepare_kernel(plan, index_ref, *refs):
    sources, refs = refs[:7], refs[7:]
    x_ref, d_ref, g_ref, cb_ref, near_ref, offsets_ref = refs[:6]
    sends, (rows_ref, cols_ref, col_ref, coup_ref, sems) = refs[6:-5], refs[-5:]
    targets = (near_ref, offsets_ref, rows_ref, cols_ref, x_ref, col_ref, coup_ref)
    copies = [
        pltpu.make_async_copy(source, target, sems.at[i])
        for i, (source, target) in enumerate(zip(sources, targets))
    ]
    for copy in copies:
        copy.start()
    rank, size = plan.rank, plan.size
    cb_ref[...] = jnp.zeros_like(cb_ref)
    g_ref[...] = jnp.zeros_like(g_ref)
    for cell in range(plan.cells):
        d_ref[cell] = jnp.zeros(d_ref.shape[1:], d_ref.dtype)
    for copy in copies:
        copy.wait()
    for c in range(plan.per_device):
        cb_ref[c * rank : (c + 1) * rank, c * size : (c + 1) * size] = col_ref[c]
    column = lax.broadcasted_iota(jnp.int32, (rank, plan.width), 1) // rank
    shift = 0 if plan.paired else plan.member(index_ref)
    for s in range(plan.slots):
        level = lax.div(rows_ref[s], plan.block_clusters)
        row = lax.rem(rows_ref[s], plan.block_clusters)
        step = lax.rem(lax.div(row, plan.per_device) - shift + plan.members, plan.members)
        place = step * plan.per_device + lax.rem(row, plan.per_device)
        where = (level, pl.ds(pl.multiple_of(place * rank, rank), rank), slice(None))
        tile = coup_ref[s].astype(F32)
        wide = jnp.where(column == cols_ref[s], jnp.concatenate([tile] * plan.per_device, axis=1), 0.0)
        g_ref[where] = g_ref[where] + wide.astype(BF16)
    plan.send_far(index_ref, x_ref[...], cb_ref, g_ref, sends)


def relay_kernel(plan, index_ref, keep_ref, message_ref, *out_refs):
    plan.relay_far(index_ref, keep_ref, message_ref, out_refs)


def first_own_kernel(plan, *refs):
    index_ref, rows_ref, offsets_ref, x_ref, near_ref, row_hbm, tiles_hbm = refs[:7]
    acc_ref, d_ref, rb_ref, row_ref, sem, tile_sems = refs[-6:]
    rank, size = plan.rank, plan.size
    copies = []
    for s in range(plan.tiles):
        cell = rows_ref[s] * SPAN + offsets_ref[s] + REACH
        copies.append(pltpu.make_async_copy(tiles_hbm.at[s], d_ref.at[cell], tile_sems.at[s]))
        copies[-1].start()
    copy = pltpu.make_async_copy(row_hbm, row_ref, sem)
    copy.start()
    rb_ref[...] = jnp.zeros_like(rb_ref)
    copy.wait()
    for c in range(plan.per_device):
        for start in (c * rank, plan.width + c * rank):
            rb_ref[start : start + rank, c * size : (c + 1) * size] = row_ref[c]
    for copy in copies:
        copy.wait()
    plan.near_sums(x_ref, d_ref, acc_ref, 0)
    plan.halo_sums(lax.rem(index_ref[0], 2) == 1, near_ref, d_ref, acc_ref, acc_ref)


def own_kernel(plan, slot, *refs):
    index_ref, x_ref, near_ref, d_ref = refs[:4]
    acc_ref, krylov_ref, sem = refs[-3:]
    copy = pltpu.make_async_copy(x_ref, krylov_ref.at[slot], sem)
    copy.start()
    plan.near_sums(x_ref, d_ref, acc_ref, 0)
    plan.halo_sums(lax.rem(index_ref[0], 2) == 1, near_ref, d_ref, acc_ref, acc_ref)
    copy.wait()


def halo_kernel(plan, index_ref, acc_ref, over_ref, d_ref, *refs):
    plan.halo_sums(lax.rem(index_ref[0], 2) == 0, over_ref, d_ref, refs[-1], acc_ref)


def finish_kernel(plan, fars, *refs):
    index_ref, acc_ref, rb_ref, cb_ref, g_ref = refs[:5]
    far_refs, (x_ref, *sends) = refs[5 : 5 + fars], refs[5 + fars :]
    x = plan.next_block(acc_ref, rb_ref, far_refs)
    x_ref[...] = x
    plan.send_far(index_ref, x, cb_ref, g_ref, sends)


def last_kernel(plan, fars, slot, *refs):
    acc_ref, rb_ref = refs[:2]
    far_refs, (_, krylov_ref, x_ref, sem) = refs[2 : 2 + fars], refs[2 + fars :]
    both = plan.far_halves(far_refs)
    copies = []
    for c in range(plan.per_device):
        columns = pl.ds(c * plan.size, plan.size)
        x_ref[:, columns] = plan.next_panel(acc_ref, rb_ref, both, c)
        copies.append(
            pltpu.make_async_copy(x_ref.at[:, columns], krylov_ref.at[slot, :, columns], sem.at[c])
        )
        copies[-1].start()
    for copy in copies:
        copy.wait()


def call(kernel, name, ins, specs, outs, out_specs=None, scratch=(), aliases=None):
    spaces = {id(IN_VMEM): pltpu.VMEM, id(IN_HBM): pltpu.HBM}
    ins = [
        pltpu.with_memory_space_constraint(v, spaces[id(spec)]) if id(spec) in spaces else v
        for v, spec in zip(ins, specs)
    ]
    return pl.pallas_call(
        kernel,
        in_specs=list(specs),
        out_specs=out_specs or [IN_VMEM] * len(outs),
        out_shape=list(outs),
        scratch_shapes=list(scratch),
        input_output_aliases=aliases or {},
        compiler_params=pltpu.CompilerParams(vmem_limit_bytes=16 * 2**20),
        cost_estimate=pl.CostEstimate(flops=10**9, bytes_accessed=2**22, transcendentals=0),
        name=name,
    )(*ins)


def on_device(
    block, near_tiles, near_rows, near_offsets, col_basis, couplings, far_rows, far_cols, row_basis
):
    axes = ("loop", "far")
    plan = Plan(
        block.shape, near_tiles.shape, couplings.shape, lax.axis_size("far"), lax.axis_size("loop")
    )
    rhs, shard_len, width = plan.rhs, plan.shard_len, plan.width
    block_out = pltpu.VMEM((rhs, shard_len), BF16)
    acc_out = pltpu.VMEM((rhs, shard_len), F32)
    relay_out = pltpu.VMEM((rhs, width), BF16)
    krylov_out = jax.ShapeDtypeStruct((PRODUCTS, rhs, shard_len), BF16)
    if plan.paired:
        sends_out = [
            pltpu.VMEM((rhs, shard_len + 4 * width), BF16),
            pltpu.VMEM((rhs, 2 * width), F32),
        ]
    else:
        sends_out = [pltpu.VMEM((rhs, width), BF16)] * len(plan.routes)
    index = lax.axis_index(axes).astype(jnp.int32).reshape(1)

    def scratch_for(*arrays):
        return [
            pltpu.SMEM(v.shape, v.dtype) if v.dtype == jnp.int32 else pltpu.VMEM(v.shape, v.dtype)
            for v in arrays
        ]

    current, sends, krylov = block, None, None
    for product in range(PRODUCTS):
        if product == 0:
            ins = [near_rows, near_offsets, far_rows, far_cols, block, col_basis, couplings]
            current, dense, coupled, col_wide, row_slots, offset_slots, *sends = call(
                functools.partial(prepare_kernel, plan),
                "prepare",
                [index, *ins],
                [IN_SMEM] + [IN_HBM] * 7,
                [
                    block_out,
                    pltpu.VMEM((plan.cells, plan.size, plan.size), BF16),
                    pltpu.VMEM((LEVELS, plan.members * width, width), BF16),
                    pltpu.VMEM((width, shard_len), BF16),
                    *scratch_for(near_rows, near_offsets),
                    *sends_out,
                ],
                [IN_VMEM] * 4 + [IN_SMEM] * 2 + [IN_VMEM] * len(sends_out),
                scratch=scratch_for(far_rows, far_cols, col_basis, couplings)
                + [pltpu.SemaphoreType.DMA((7,))],
            )
        near = lax.ppermute(sends[0] if plan.paired else current, axes, plan.near)
        over = lax.ppermute(block if product == 0 else current, axes, plan.over)
        if plan.paired:
            sends = call(
                functools.partial(relay_kernel, plan),
                "relay",
                [index, sends[1], near],
                [IN_SMEM] + [IN_VMEM] * 2,
                [relay_out] * 2,
            )
            routes = plan.across
        else:
            routes = plan.routes
        fars = [lax.ppermute(s, axes, route) for s, route in zip(sends, routes)]
        after = sends if plan.paired else []
        if product == 0:
            ins = [index, row_slots, offset_slots, current, near, row_basis, near_tiles, dense, *after]
            acc, dense, row_wide = call(
                functools.partial(first_own_kernel, plan),
                "first_own",
                ins,
                [IN_SMEM] * 3 + [IN_VMEM] * 2 + [IN_HBM] * 2 + [IN_VMEM] + [ANYWHERE] * len(after),
                [
                    acc_out,
                    pltpu.VMEM((plan.cells, plan.size, plan.size), BF16),
                    pltpu.VMEM((2 * width, shard_len), BF16),
                ],
                scratch=scratch_for(row_basis)
                + [pltpu.SemaphoreType.DMA, pltpu.SemaphoreType.DMA((plan.tiles,))],
                aliases={7: 1},
            )
        else:
            ins = [index, current, near, dense, *after] + ([krylov] if product > 1 else [])
            acc, krylov = call(
                functools.partial(own_kernel, plan, product - 1),
                "own",
                ins,
                [IN_SMEM] + [IN_VMEM] * 3 + [ANYWHERE] * (len(ins) - 4),
                [acc_out, krylov_out],
                [IN_VMEM, ANYWHERE],
                [pltpu.SemaphoreType.DMA],
                {len(ins) - 1: 1} if product > 1 else None,
            )
        (acc,) = call(
            functools.partial(halo_kernel, plan),
            "halo",
            [index, acc, over, dense],
            [IN_SMEM] + [IN_VMEM] * 3,
            [acc_out],
        )
        if product < PRODUCTS - 1:
            ins = [index, acc, row_wide, col_wide, coupled, *fars]
            current, *sends = call(
                functools.partial(finish_kernel, plan, len(fars)),
                "finish",
                ins,
                [IN_SMEM] + [IN_VMEM] * (len(ins) - 1),
                [block_out, *sends_out],
            )
        else:
            ins = [acc, row_wide, *fars, krylov]
            (krylov,) = call(
                functools.partial(last_kernel, plan, len(fars), product),
                "last",
                ins,
                [IN_VMEM] * (len(ins) - 1) + [ANYWHERE],
                [krylov_out],
                [ANYWHERE],
                [
                    pltpu.VMEM((rhs, shard_len), BF16),
                    pltpu.SemaphoreType.DMA((plan.per_device,)),
                ],
                {len(ins) - 1: 0},
            )
    return krylov


def solution(mesh):
    split = ("groups", "loop", "far")
    wide, narrow = P(split, None, None), P(split)
    in_specs = (P(None, split), wide, narrow, narrow, wide, wide, narrow, narrow, wide)
    return jax.shard_map(
        on_device, mesh=mesh, in_specs=in_specs, out_specs=P(None, None, split), check_vma=False
    )
```

```python
import functools

import jax
import jax.numpy as jnp
from jax import lax
from jax.experimental import pallas as pl
from jax.experimental.pallas import tpu as pltpu
from jax.sharding import PartitionSpec as P

PRODUCTS = 4
REACH = 4
LEVELS = 3
SPAN = 2 * REACH + 1

F32 = jnp.float32
BF16 = jnp.bfloat16
IN_VMEM = pl.BlockSpec(memory_space=pltpu.VMEM)
PREFETCHED = pl.BlockSpec(memory_space=pltpu.VMEM)
IN_SMEM = pl.BlockSpec(memory_space=pltpu.SMEM)
IN_HBM = pl.BlockSpec(memory_space=pltpu.HBM)
ANYWHERE = pl.BlockSpec(memory_space=pl.ANY)


def dot_nt(a, b):
    return lax.dot_general(a, b, (((1,), (1,)), ((), ())), preferred_element_type=F32)


def dot_nn(a, b):
    return lax.dot_general(a, b, (((1,), (0,)), ((), ())), preferred_element_type=F32)


def halves(value):
    upper = value.astype(BF16)
    return upper, (value - upper.astype(F32)).astype(BF16)


class Plan:
    def __init__(self, block_shape, tile_shape, coupling_shape, members, loop_size):
        self.rhs, self.shard_len = block_shape
        self.tiles, self.size, _ = tile_shape
        self.slots, self.rank, _ = coupling_shape
        self.members, self.loop_size = members, loop_size
        self.per_device = self.shard_len // self.size
        self.width = self.per_device * self.rank
        self.cells = self.per_device * SPAN
        self.block_clusters = self.per_device * members
        distances = [d % loop_size for d in (2, loop_size - 2, loop_size // 2)]
        self.hops = sorted(set(distances))
        self.sets = [[i for i, d in enumerate(distances) if d == hop] for hop in self.hops]
        self.paired = len(self.hops) == 1 and 2 * self.hops[0] == loop_size and members == 4
        devices = members * loop_size
        self.near = [(i, i ^ 1) for i in range(devices)]
        self.over = [(i, (i + 1 if i % 2 else i - 1) % devices) for i in range(devices)]
        places = [(l, m) for l in range(loop_size) for m in range(members)]
        self.across = [
            [
                (l * members + m, (l + self.hops[0]) % loop_size * members + (m ^ (m % 2 * 2) ^ other))
                for l, m in places
            ]
            for other in range(2)
        ]
        self.routes = [
            [(l * members + m, (l + hop) % loop_size * members + (m + step) % members) for l, m in places]
            for hop in self.hops
            for step in range(members)
        ]

    def panel(self, ref, c):
        return ref[:, c * self.size : (c + 1) * self.size]

    def member(self, index_ref):
        return lax.rem(index_ref[0], self.members)

    def send_far(self, index_ref, x, cb_ref, g_ref, out_refs):
        coeffs = dot_nt(x, cb_ref[...]).astype(BF16)
        totals = [sum(dot_nt(coeffs, g_ref[level]) for level in levels) for levels in self.sets]
        if not self.paired:
            for i, out_ref in enumerate(out_refs):
                step = i % self.members * self.width
                out_ref[...] = totals[i // self.members][:, step : step + self.width].astype(BF16)
            return
        message_ref, keep_ref = out_refs
        (total,) = totals
        member = self.member(index_ref)
        second = lax.rem(member, 2) != lax.div(member, 2)
        first, last = total[:, : 2 * self.width], total[:, 2 * self.width :]
        keep_ref[...] = jnp.where(second, last, first)
        upper, lower = halves(jnp.where(second, first, last))
        message_ref[:, : self.shard_len] = x
        message_ref[:, self.shard_len : self.shard_len + 2 * self.width] = upper
        message_ref[:, self.shard_len + 2 * self.width :] = lower

    def relay_far(self, index_ref, keep_ref, message_ref, out_refs):
        upper = message_ref[:, self.shard_len : self.shard_len + 2 * self.width].astype(F32)
        lower = message_ref[:, self.shard_len + 2 * self.width :].astype(F32)
        total = (keep_ref[...] + (upper + lower)).astype(BF16)
        second = lax.rem(index_ref[0], 2) == 1
        first, last = total[:, : self.width], total[:, self.width :]
        out_refs[0][...] = jnp.where(second, last, first)
        out_refs[1][...] = jnp.where(second, first, last)

    def far_sum(self, far_refs):
        return sum(ref[...].astype(F32) for ref in far_refs)

    def near_sums(self, x_ref, d_ref, acc_ref, first, start_ref=None):
        panels = [self.panel(x_ref, c) for c in range(self.per_device)]
        for r in range(self.per_device):
            value = None if start_ref is None else self.panel(start_ref, r)
            for c in range(self.per_device):
                offset = first + c - r
                if -REACH <= offset <= REACH:
                    term = dot_nt(panels[c], d_ref[r * SPAN + offset + REACH])
                    value = term if value is None else value + term
            acc_ref[:, r * self.size : (r + 1) * self.size] = value

    def halo_sums(self, below, x_ref, d_ref, acc_ref, start_ref):
        @pl.when(below)
        def _():
            self.near_sums(x_ref, d_ref, acc_ref, -self.per_device, start_ref)

        @pl.when(jnp.logical_not(below))
        def _():
            self.near_sums(x_ref, d_ref, acc_ref, self.per_device, start_ref)

    def far_halves(self, far_refs):
        return jnp.concatenate(halves(self.far_sum(far_refs)), axis=1)

    def next_panel(self, acc_ref, rb_ref, both, c):
        return (self.panel(acc_ref, c) + dot_nn(both, self.panel(rb_ref, c))).astype(BF16)

    def next_block(self, acc_ref, rb_ref, far_refs):
        both = self.far_halves(far_refs)
        panels = [self.next_panel(acc_ref, rb_ref, both, c) for c in range(self.per_device)]
        return jnp.concatenate(panels, axis=1)


def prepare_kernel(plan, index_ref, *refs):
    sources, refs = refs[:7], refs[7:]
    x_ref, d_ref, g_ref, cb_ref, near_ref, offsets_ref = refs[:6]
    sends, (rows_ref, cols_ref, col_ref, coup_ref, sems) = refs[6:-5], refs[-5:]
    targets = (near_ref, offsets_ref, rows_ref, cols_ref, x_ref, col_ref, coup_ref)
    copies = [
        pltpu.make_async_copy(source, target, sems.at[i])
        for i, (source, target) in enumerate(zip(sources, targets))
    ]
    for copy in copies:
        copy.start()
    rank, size = plan.rank, plan.size
    cb_ref[...] = jnp.zeros_like(cb_ref)
    g_ref[...] = jnp.zeros_like(g_ref)
    for cell in range(plan.cells):
        d_ref[cell] = jnp.zeros(d_ref.shape[1:], d_ref.dtype)
    for copy in copies:
        copy.wait()
    for c in range(plan.per_device):
        cb_ref[c * rank : (c + 1) * rank, c * size : (c + 1) * size] = col_ref[c]
    column = lax.broadcasted_iota(jnp.int32, (rank, plan.width), 1) // rank
    shift = 0 if plan.paired else plan.member(index_ref)
    for s in range(plan.slots):
        level = lax.div(rows_ref[s], plan.block_clusters)
        row = lax.rem(rows_ref[s], plan.block_clusters)
        step = lax.rem(lax.div(row, plan.per_device) - shift + plan.members, plan.members)
        place = step * plan.per_device + lax.rem(row, plan.per_device)
        where = (level, pl.ds(pl.multiple_of(place * rank, rank), rank), slice(None))
        tile = coup_ref[s].astype(F32)
        wide = jnp.where(column == cols_ref[s], jnp.concatenate([tile] * plan.per_device, axis=1), 0.0)
        g_ref[where] = g_ref[where] + wide.astype(BF16)
    plan.send_far(index_ref, x_ref[...], cb_ref, g_ref, sends)


def relay_kernel(plan, index_ref, keep_ref, message_ref, *out_refs):
    plan.relay_far(index_ref, keep_ref, message_ref, out_refs)


def first_own_kernel(plan, *refs):
    index_ref, rows_ref, offsets_ref, x_ref, near_ref, row_ref, tiles_ref = refs[:7]
    acc_ref, d_ref, rb_ref = refs[-3:]
    rank, size = plan.rank, plan.size
    for s in range(plan.tiles):
        d_ref[rows_ref[s] * SPAN + offsets_ref[s] + REACH] = tiles_ref[s]
    rb_ref[...] = jnp.zeros_like(rb_ref)
    for c in range(plan.per_device):
        for start in (c * rank, plan.width + c * rank):
            rb_ref[start : start + rank, c * size : (c + 1) * size] = row_ref[c]
    plan.near_sums(x_ref, d_ref, acc_ref, 0)
    plan.halo_sums(lax.rem(index_ref[0], 2) == 1, near_ref, d_ref, acc_ref, acc_ref)


def own_kernel(plan, slot, *refs):
    index_ref, x_ref, near_ref, d_ref = refs[:4]
    acc_ref, krylov_ref, sem = refs[-3:]
    copy = pltpu.make_async_copy(x_ref, krylov_ref.at[slot], sem)
    copy.start()
    plan.near_sums(x_ref, d_ref, acc_ref, 0)
    plan.halo_sums(lax.rem(index_ref[0], 2) == 1, near_ref, d_ref, acc_ref, acc_ref)
    copy.wait()


def halo_kernel(plan, index_ref, acc_ref, over_ref, d_ref, *refs):
    plan.halo_sums(lax.rem(index_ref[0], 2) == 0, over_ref, d_ref, refs[-1], acc_ref)


def finish_kernel(plan, fars, *refs):
    index_ref, acc_ref, rb_ref, cb_ref, g_ref = refs[:5]
    far_refs, (x_ref, *sends) = refs[5 : 5 + fars], refs[5 + fars :]
    x = plan.next_block(acc_ref, rb_ref, far_refs)
    x_ref[...] = x
    plan.send_far(index_ref, x, cb_ref, g_ref, sends)


def last_kernel(plan, fars, slot, *refs):
    acc_ref, rb_ref = refs[:2]
    far_refs, (_, krylov_ref, x_ref, sem) = refs[2 : 2 + fars], refs[2 + fars :]
    both = plan.far_halves(far_refs)
    copies = []
    for c in range(plan.per_device):
        columns = pl.ds(c * plan.size, plan.size)
        x_ref[:, columns] = plan.next_panel(acc_ref, rb_ref, both, c)
        copies.append(
            pltpu.make_async_copy(x_ref.at[:, columns], krylov_ref.at[slot, :, columns], sem.at[c])
        )
        copies[-1].start()
    for copy in copies:
        copy.wait()


def call(kernel, name, ins, specs, outs, out_specs=None, scratch=(), aliases=None):
    spaces = {id(IN_VMEM): pltpu.VMEM, id(IN_HBM): pltpu.HBM}
    ins = [
        pltpu.with_memory_space_constraint(v, spaces[id(spec)]) if id(spec) in spaces else v
        for v, spec in zip(ins, specs)
    ]
    return pl.pallas_call(
        kernel,
        in_specs=list(specs),
        out_specs=out_specs or [IN_VMEM] * len(outs),
        out_shape=list(outs),
        scratch_shapes=list(scratch),
        input_output_aliases=aliases or {},
        compiler_params=pltpu.CompilerParams(vmem_limit_bytes=16 * 2**20),
        cost_estimate=pl.CostEstimate(flops=10**9, bytes_accessed=2**22, transcendentals=0),
        name=name,
    )(*ins)


def on_device(
    block, near_tiles, near_rows, near_offsets, col_basis, couplings, far_rows, far_cols, row_basis
):
    axes = ("loop", "far")
    plan = Plan(
        block.shape, near_tiles.shape, couplings.shape, lax.axis_size("far"), lax.axis_size("loop")
    )
    rhs, shard_len, width = plan.rhs, plan.shard_len, plan.width
    block_out = pltpu.VMEM((rhs, shard_len), BF16)
    acc_out = pltpu.VMEM((rhs, shard_len), F32)
    relay_out = pltpu.VMEM((rhs, width), BF16)
    krylov_out = jax.ShapeDtypeStruct((PRODUCTS, rhs, shard_len), BF16)
    if plan.paired:
        sends_out = [
            pltpu.VMEM((rhs, shard_len + 4 * width), BF16),
            pltpu.VMEM((rhs, 2 * width), F32),
        ]
    else:
        sends_out = [pltpu.VMEM((rhs, width), BF16)] * len(plan.routes)
    index = lax.axis_index(axes).astype(jnp.int32).reshape(1)

    def scratch_for(*arrays):
        return [
            pltpu.SMEM(v.shape, v.dtype) if v.dtype == jnp.int32 else pltpu.VMEM(v.shape, v.dtype)
            for v in arrays
        ]

    current, sends, krylov = block, None, None
    for product in range(PRODUCTS):
        if product == 0:
            ins = [near_rows, near_offsets, far_rows, far_cols, block, col_basis, couplings]
            current, dense, coupled, col_wide, row_slots, offset_slots, *sends = call(
                functools.partial(prepare_kernel, plan),
                "prepare",
                [index, *ins],
                [IN_SMEM] + [IN_HBM] * 7,
                [
                    block_out,
                    pltpu.VMEM((plan.cells, plan.size, plan.size), BF16),
                    pltpu.VMEM((LEVELS, plan.members * width, width), BF16),
                    pltpu.VMEM((width, shard_len), BF16),
                    *scratch_for(near_rows, near_offsets),
                    *sends_out,
                ],
                [IN_VMEM] * 4 + [IN_SMEM] * 2 + [IN_VMEM] * len(sends_out),
                scratch=scratch_for(far_rows, far_cols, col_basis, couplings)
                + [pltpu.SemaphoreType.DMA((7,))],
            )
        near = lax.ppermute(sends[0] if plan.paired else current, axes, plan.near)
        over = lax.ppermute(block if product == 0 else current, axes, plan.over)
        if plan.paired:
            sends = call(
                functools.partial(relay_kernel, plan),
                "relay",
                [index, sends[1], near],
                [IN_SMEM] + [IN_VMEM] * 2,
                [relay_out] * 2,
            )
            routes = plan.across
        else:
            routes = plan.routes
        fars = [lax.ppermute(s, axes, route) for s, route in zip(sends, routes)]
        after = sends if plan.paired else []
        if product == 0:
            ins = [index, row_slots, offset_slots, current, near, row_basis, near_tiles, dense, *after]
            acc, dense, row_wide = call(
                functools.partial(first_own_kernel, plan),
                "first_own",
                ins,
                [IN_SMEM] * 3 + [IN_VMEM] * 2 + [PREFETCHED] * 2 + [IN_VMEM] + [ANYWHERE] * len(after),
                [
                    acc_out,
                    pltpu.VMEM((plan.cells, plan.size, plan.size), BF16),
                    pltpu.VMEM((2 * width, shard_len), BF16),
                ],
                aliases={7: 1},
            )
        else:
            ins = [index, current, near, dense, *after] + ([krylov] if product > 1 else [])
            acc, krylov = call(
                functools.partial(own_kernel, plan, product - 1),
                "own",
                ins,
                [IN_SMEM] + [IN_VMEM] * 3 + [ANYWHERE] * (len(ins) - 4),
                [acc_out, krylov_out],
                [IN_VMEM, ANYWHERE],
                [pltpu.SemaphoreType.DMA],
                {len(ins) - 1: 1} if product > 1 else None,
            )
        (acc,) = call(
            functools.partial(halo_kernel, plan),
            "halo",
            [index, acc, over, dense],
            [IN_SMEM] + [IN_VMEM] * 3,
            [acc_out],
        )
        if product < PRODUCTS - 1:
            ins = [index, acc, row_wide, col_wide, coupled, *fars]
            current, *sends = call(
                functools.partial(finish_kernel, plan, len(fars)),
                "finish",
                ins,
                [IN_SMEM] + [IN_VMEM] * (len(ins) - 1),
                [block_out, *sends_out],
            )
        else:
            ins = [acc, row_wide, *fars, krylov]
            (krylov,) = call(
                functools.partial(last_kernel, plan, len(fars), product),
                "last",
                ins,
                [IN_VMEM] * (len(ins) - 1) + [ANYWHERE],
                [krylov_out],
                [ANYWHERE],
                [
                    pltpu.VMEM((rhs, shard_len), BF16),
                    pltpu.SemaphoreType.DMA((plan.per_device,)),
                ],
                {len(ins) - 1: 0},
            )
    return krylov


def solution(mesh):
    split = ("groups", "loop", "far")
    wide, narrow = P(split, None, None), P(split)
    in_specs = (P(None, split), wide, narrow, narrow, wide, wide, narrow, narrow, wide)
    return jax.shard_map(
        on_device, mesh=mesh, in_specs=in_specs, out_specs=P(None, None, split), check_vma=False
    )
```

```python
import functools

import jax
import jax.numpy as jnp
from jax import lax
from jax.experimental import pallas as pl
from jax.experimental.pallas import tpu as pltpu
from jax.sharding import PartitionSpec as P

PRODUCTS = 4
REACH = 4
LEVELS = 3
SPAN = 2 * REACH + 1

BRIEF, USUAL, LONG, LOADING = (10**6, 2**16), (10**9, 2**22), (4 * 10**9, 2**22), (10**6, 2**23)

F32 = jnp.float32
BF16 = jnp.bfloat16
IN_VMEM = pl.BlockSpec(memory_space=pltpu.VMEM)
PREFETCHED = pl.BlockSpec(memory_space=pltpu.VMEM)
IN_SMEM = pl.BlockSpec(memory_space=pltpu.SMEM)
IN_HBM = pl.BlockSpec(memory_space=pltpu.HBM)
ANYWHERE = pl.BlockSpec(memory_space=pl.ANY)


def dot_nt(a, b):
    return lax.dot_general(a, b, (((1,), (1,)), ((), ())), preferred_element_type=F32)


def dot_nn(a, b):
    return lax.dot_general(a, b, (((1,), (0,)), ((), ())), preferred_element_type=F32)


def halves(value):
    upper = value.astype(BF16)
    return upper, (value - upper.astype(F32)).astype(BF16)


class Plan:
    def __init__(self, block_shape, tile_shape, coupling_shape, members, loop_size):
        self.rhs, self.shard_len = block_shape
        self.tiles, self.size, _ = tile_shape
        self.slots, self.rank, _ = coupling_shape
        self.members, self.loop_size = members, loop_size
        self.per_device = self.shard_len // self.size
        self.width = self.per_device * self.rank
        self.cells = self.per_device * SPAN
        self.block_clusters = self.per_device * members
        distances = [d % loop_size for d in (2, loop_size - 2, loop_size // 2)]
        self.hops = sorted(set(distances))
        self.sets = [[i for i, d in enumerate(distances) if d == hop] for hop in self.hops]
        self.paired = len(self.hops) == 1 and 2 * self.hops[0] == loop_size and members == 4
        devices = members * loop_size
        self.near = [(i, i ^ 1) for i in range(devices)]
        self.over = [(i, (i + 1 if i % 2 else i - 1) % devices) for i in range(devices)]
        places = [(l, m) for l in range(loop_size) for m in range(members)]
        self.across = [
            [
                (l * members + m, (l + self.hops[0]) % loop_size * members + (m ^ (m % 2 * 2) ^ other))
                for l, m in places
            ]
            for other in range(2)
        ]
        self.routes = [
            [(l * members + m, (l + hop) % loop_size * members + (m + step) % members) for l, m in places]
            for hop in self.hops
            for step in range(members)
        ]

    def panel(self, ref, c):
        return ref[:, c * self.size : (c + 1) * self.size]

    def member(self, index_ref):
        return lax.rem(index_ref[0], self.members)

    def send_far(self, index_ref, x, cb_ref, g_ref, out_refs):
        coeffs = dot_nt(x, cb_ref[...]).astype(BF16)
        totals = [sum(dot_nt(coeffs, g_ref[level]) for level in levels) for levels in self.sets]
        if not self.paired:
            for i, out_ref in enumerate(out_refs):
                step = i % self.members * self.width
                out_ref[...] = totals[i // self.members][:, step : step + self.width].astype(BF16)
            return
        message_ref, keep_ref = out_refs
        (total,) = totals
        member = self.member(index_ref)
        second = lax.rem(member, 2) != lax.div(member, 2)
        first, last = total[:, : 2 * self.width], total[:, 2 * self.width :]
        keep_ref[...] = jnp.where(second, last, first)
        upper, lower = halves(jnp.where(second, first, last))
        start = message_ref.shape[1] - 4 * self.width
        if start:
            message_ref[:, :start] = x
        message_ref[:, start : start + 2 * self.width] = upper
        message_ref[:, start + 2 * self.width :] = lower

    def relay_far(self, index_ref, keep_ref, message_ref, out_refs):
        start = message_ref.shape[1] - 4 * self.width
        upper = message_ref[:, start : start + 2 * self.width].astype(F32)
        lower = message_ref[:, start + 2 * self.width :].astype(F32)
        total = (keep_ref[...] + (upper + lower)).astype(BF16)
        second = lax.rem(index_ref[0], 2) == 1
        first, last = total[:, : self.width], total[:, self.width :]
        out_refs[0][...] = jnp.where(second, last, first)
        out_refs[1][...] = jnp.where(second, first, last)

    def far_sum(self, far_refs):
        return sum(ref[...].astype(F32) for ref in far_refs)

    def near_sums(self, x_ref, d_ref, acc_ref, first, start_ref=None):
        panels = [self.panel(x_ref, c) for c in range(self.per_device)]
        for r in range(self.per_device):
            value = None if start_ref is None else self.panel(start_ref, r)
            for c in range(self.per_device):
                offset = first + c - r
                if -REACH <= offset <= REACH:
                    term = dot_nt(panels[c], d_ref[r * SPAN + offset + REACH])
                    value = term if value is None else value + term
            acc_ref[:, r * self.size : (r + 1) * self.size] = value

    def halo_sums(self, below, x_ref, d_ref, acc_ref, start_ref):
        @pl.when(below)
        def _():
            self.near_sums(x_ref, d_ref, acc_ref, -self.per_device, start_ref)

        @pl.when(jnp.logical_not(below))
        def _():
            self.near_sums(x_ref, d_ref, acc_ref, self.per_device, start_ref)

    def far_halves(self, far_refs):
        return jnp.concatenate(halves(self.far_sum(far_refs)), axis=1)

    def next_panel(self, acc_ref, rb_ref, both, c):
        return (self.panel(acc_ref, c) + dot_nn(both, self.panel(rb_ref, c))).astype(BF16)

    def next_block(self, acc_ref, rb_ref, far_refs):
        both = self.far_halves(far_refs)
        panels = [self.next_panel(acc_ref, rb_ref, both, c) for c in range(self.per_device)]
        return jnp.concatenate(panels, axis=1)


def prepare_kernel(plan, index_ref, *refs):
    sources, refs = refs[:7], refs[7:]
    x_ref, g_ref, cb_ref, near_ref, offsets_ref = refs[:5]
    sends, (rows_ref, cols_ref, col_ref, coup_ref, sems) = refs[5:-5], refs[-5:]
    targets = (near_ref, offsets_ref, rows_ref, cols_ref, x_ref, col_ref, coup_ref)
    copies = [
        pltpu.make_async_copy(source, target, sems.at[i])
        for i, (source, target) in enumerate(zip(sources, targets))
    ]
    for copy in copies:
        copy.start()
    rank, size = plan.rank, plan.size
    cb_ref[...] = jnp.zeros_like(cb_ref)
    g_ref[...] = jnp.zeros_like(g_ref)
    for copy in copies:
        copy.wait()
    for c in range(plan.per_device):
        cb_ref[c * rank : (c + 1) * rank, c * size : (c + 1) * size] = col_ref[c]
    column = lax.broadcasted_iota(jnp.int32, (rank, plan.width), 1) // rank
    shift = 0 if plan.paired else plan.member(index_ref)
    for s in range(plan.slots):
        level = lax.div(rows_ref[s], plan.block_clusters)
        row = lax.rem(rows_ref[s], plan.block_clusters)
        step = lax.rem(lax.div(row, plan.per_device) - shift + plan.members, plan.members)
        place = step * plan.per_device + lax.rem(row, plan.per_device)
        where = (level, pl.ds(pl.multiple_of(place * rank, rank), rank), slice(None))
        tile = coup_ref[s].astype(F32)
        wide = jnp.where(column == cols_ref[s], jnp.concatenate([tile] * plan.per_device, axis=1), 0.0)
        g_ref[where] = g_ref[where] + wide.astype(BF16)
    plan.send_far(index_ref, x_ref[...], cb_ref, g_ref, sends)


def relay_kernel(plan, index_ref, keep_ref, message_ref, *out_refs):
    plan.relay_far(index_ref, keep_ref, message_ref, out_refs)


def first_own_kernel(plan, *refs):
    index_ref, rows_ref, offsets_ref, x_ref, near_ref, row_ref, tiles_ref = refs[:7]
    acc_ref, d_ref, rb_ref = refs[-3:]
    rank, size = plan.rank, plan.size
    for cell in range(plan.cells):
        d_ref[cell] = jnp.zeros(d_ref.shape[1:], d_ref.dtype)
    for s in range(plan.tiles):
        d_ref[rows_ref[s] * SPAN + offsets_ref[s] + REACH] = tiles_ref[s]
    rb_ref[...] = jnp.zeros_like(rb_ref)
    for c in range(plan.per_device):
        for start in (c * rank, plan.width + c * rank):
            rb_ref[start : start + rank, c * size : (c + 1) * size] = row_ref[c]
    plan.near_sums(x_ref, d_ref, acc_ref, 0)
    plan.halo_sums(lax.rem(index_ref[0], 2) == 1, near_ref, d_ref, acc_ref, acc_ref)


def own_kernel(plan, slot, *refs):
    index_ref, x_ref, near_ref, d_ref = refs[:4]
    acc_ref, krylov_ref, sem = refs[-3:]
    copy = pltpu.make_async_copy(x_ref, krylov_ref.at[slot], sem)
    copy.start()
    plan.near_sums(x_ref, d_ref, acc_ref, 0)
    plan.halo_sums(lax.rem(index_ref[0], 2) == 1, near_ref, d_ref, acc_ref, acc_ref)
    copy.wait()


def halo_kernel(plan, index_ref, acc_ref, over_ref, d_ref, *refs):
    plan.halo_sums(lax.rem(index_ref[0], 2) == 0, over_ref, d_ref, refs[-1], acc_ref)


def finish_kernel(plan, fars, *refs):
    index_ref, acc_ref, rb_ref, cb_ref, g_ref = refs[:5]
    far_refs, (x_ref, *sends) = refs[5 : 5 + fars], refs[5 + fars :]
    x = plan.next_block(acc_ref, rb_ref, far_refs)
    x_ref[...] = x
    plan.send_far(index_ref, x, cb_ref, g_ref, sends)


def last_kernel(plan, fars, slot, *refs):
    acc_ref, rb_ref = refs[:2]
    far_refs, (_, krylov_ref, x_ref, sem) = refs[2 : 2 + fars], refs[2 + fars :]
    both = plan.far_halves(far_refs)
    copies = []
    for c in range(plan.per_device):
        columns = pl.ds(c * plan.size, plan.size)
        x_ref[:, columns] = plan.next_panel(acc_ref, rb_ref, both, c)
        copies.append(
            pltpu.make_async_copy(x_ref.at[:, columns], krylov_ref.at[slot, :, columns], sem.at[c])
        )
        copies[-1].start()
    for copy in copies:
        copy.wait()


def call(kernel, name, ins, specs, outs, out_specs=None, scratch=(), aliases=None, cost=USUAL):
    spaces = {id(IN_VMEM): pltpu.VMEM, id(IN_HBM): pltpu.HBM}
    ins = [
        pltpu.with_memory_space_constraint(v, spaces[id(spec)]) if id(spec) in spaces else v
        for v, spec in zip(ins, specs)
    ]
    return pl.pallas_call(
        kernel,
        in_specs=list(specs),
        out_specs=out_specs or [IN_VMEM] * len(outs),
        out_shape=list(outs),
        scratch_shapes=list(scratch),
        input_output_aliases=aliases or {},
        compiler_params=pltpu.CompilerParams(vmem_limit_bytes=16 * 2**20),
        cost_estimate=pl.CostEstimate(flops=cost[0], bytes_accessed=cost[1], transcendentals=0),
        name=name,
    )(*ins)


def on_device(
    block, near_tiles, near_rows, near_offsets, col_basis, couplings, far_rows, far_cols, row_basis
):
    axes = ("loop", "far")
    plan = Plan(
        block.shape, near_tiles.shape, couplings.shape, lax.axis_size("far"), lax.axis_size("loop")
    )
    rhs, shard_len, width = plan.rhs, plan.shard_len, plan.width
    block_out = pltpu.VMEM((rhs, shard_len), BF16)
    acc_out = pltpu.VMEM((rhs, shard_len), F32)
    relay_out = pltpu.VMEM((rhs, width), BF16)
    krylov_out = jax.ShapeDtypeStruct((PRODUCTS, rhs, shard_len), BF16)
    if plan.paired:
        kept = pltpu.VMEM((rhs, 2 * width), F32)
        first_out = [pltpu.VMEM((rhs, 4 * width), BF16), kept]
        sends_out = [pltpu.VMEM((rhs, shard_len + 4 * width), BF16), kept]
    else:
        first_out = sends_out = [pltpu.VMEM((rhs, width), BF16)] * len(plan.routes)
    index = lax.axis_index(axes).astype(jnp.int32).reshape(1)

    def scratch_for(*arrays):
        return [
            pltpu.SMEM(v.shape, v.dtype) if v.dtype == jnp.int32 else pltpu.VMEM(v.shape, v.dtype)
            for v in arrays
        ]

    current, sends, krylov = block, None, None
    for product in range(PRODUCTS):
        if product == 0:
            near = lax.ppermute(block, axes, plan.near)
            over = lax.ppermute(block, axes, plan.over)
            ins = [near_rows, near_offsets, far_rows, far_cols, block, col_basis, couplings]
            current, coupled, col_wide, row_slots, offset_slots, *sends = call(
                functools.partial(prepare_kernel, plan),
                "prepare",
                [index, *ins],
                [IN_SMEM] + [IN_HBM] * 7,
                [
                    block_out,
                    pltpu.VMEM((LEVELS, plan.members * width, width), BF16),
                    pltpu.VMEM((width, shard_len), BF16),
                    *scratch_for(near_rows, near_offsets),
                    *first_out,
                ],
                [IN_VMEM] * 3 + [IN_SMEM] * 2 + [IN_VMEM] * len(sends_out),
                scratch=scratch_for(far_rows, far_cols, col_basis, couplings)
                + [pltpu.SemaphoreType.DMA((7,))],
                cost=LONG,
            )
        if product > 0:
            over = lax.ppermute(current, axes, plan.over)
            near = message = lax.ppermute(sends[0] if plan.paired else current, axes, plan.near)
        elif plan.paired:
            message = lax.ppermute(sends[0], axes, plan.near)
        if plan.paired:
            sends = call(
                functools.partial(relay_kernel, plan),
                "relay",
                [index, sends[1], message],
                [IN_SMEM] + [IN_VMEM] * 2,
                [relay_out] * 2,
                cost=BRIEF if product == 0 else USUAL,
            )
            routes = plan.across
        else:
            routes = plan.routes
        fars = [lax.ppermute(s, axes, route) for s, route in zip(sends, routes)]
        after = sends if plan.paired else []
        if product == 0:
            ins = [index, row_slots, offset_slots, current, near, row_basis, near_tiles, *after]
            acc, dense, row_wide = call(
                functools.partial(first_own_kernel, plan),
                "first_own",
                ins,
                [IN_SMEM] * 3 + [IN_VMEM] * 2 + [PREFETCHED] * 2 + [ANYWHERE] * len(after),
                [
                    acc_out,
                    pltpu.VMEM((plan.cells, plan.size, plan.size), BF16),
                    pltpu.VMEM((2 * width, shard_len), BF16),
                ],
                cost=LOADING,
            )
        else:
            ins = [index, current, near, dense, *after] + ([krylov] if product > 1 else [])
            acc, krylov = call(
                functools.partial(own_kernel, plan, product - 1),
                "own",
                ins,
                [IN_SMEM] + [IN_VMEM] * 3 + [ANYWHERE] * (len(ins) - 4),
                [acc_out, krylov_out],
                [IN_VMEM, ANYWHERE],
                [pltpu.SemaphoreType.DMA],
                {len(ins) - 1: 1} if product > 1 else None,
            )
        (acc,) = call(
            functools.partial(halo_kernel, plan),
            "halo",
            [index, acc, over, dense],
            [IN_SMEM] + [IN_VMEM] * 3,
            [acc_out],
            cost=BRIEF if product == 0 else USUAL,
        )
        if product < PRODUCTS - 1:
            ins = [index, acc, row_wide, col_wide, coupled, *fars]
            current, *sends = call(
                functools.partial(finish_kernel, plan, len(fars)),
                "finish",
                ins,
                [IN_SMEM] + [IN_VMEM] * (len(ins) - 1),
                [block_out, *sends_out],
            )
        else:
            ins = [acc, row_wide, *fars, krylov]
            (krylov,) = call(
                functools.partial(last_kernel, plan, len(fars), product),
                "last",
                ins,
                [IN_VMEM] * (len(ins) - 1) + [ANYWHERE],
                [krylov_out],
                [ANYWHERE],
                [
                    pltpu.VMEM((rhs, shard_len), BF16),
                    pltpu.SemaphoreType.DMA((plan.per_device,)),
                ],
                {len(ins) - 1: 0},
            )
    return krylov


def solution(mesh):
    split = ("groups", "loop", "far")
    wide, narrow = P(split, None, None), P(split)
    in_specs = (P(None, split), wide, narrow, narrow, wide, wide, narrow, narrow, wide)
    return jax.shard_map(
        on_device, mesh=mesh, in_specs=in_specs, out_specs=P(None, None, split), check_vma=False
    )
```

```python
import functools

import jax
import jax.numpy as jnp
from jax import lax
from jax.experimental import pallas as pl
from jax.experimental.pallas import tpu as pltpu
from jax.sharding import PartitionSpec as P

PRODUCTS = 4
REACH = 4
LEVELS = 3
SPAN = 2 * REACH + 1

BRIEF, USUAL, LONG, LOADING = (10**6, 2**16), (10**9, 2**22), (4 * 10**9, 2**22), (10**6, 2**23)

F32 = jnp.float32
BF16 = jnp.bfloat16
IN_VMEM = pl.BlockSpec(memory_space=pltpu.VMEM)
PREFETCHED = pl.BlockSpec(memory_space=pltpu.VMEM)
IN_SMEM = pl.BlockSpec(memory_space=pltpu.SMEM)
IN_HBM = pl.BlockSpec(memory_space=pltpu.HBM)
ANYWHERE = pl.BlockSpec(memory_space=pl.ANY)


def dot_nt(a, b):
    return lax.dot_general(a, b, (((1,), (1,)), ((), ())), preferred_element_type=F32)


def dot_nn(a, b):
    return lax.dot_general(a, b, (((1,), (0,)), ((), ())), preferred_element_type=F32)


def halves(value):
    upper = value.astype(BF16)
    return upper, (value - upper.astype(F32)).astype(BF16)


class Plan:
    def __init__(self, block_shape, tile_shape, coupling_shape, members, loop_size):
        self.rhs, self.shard_len = block_shape
        self.tiles, self.size, _ = tile_shape
        self.slots, self.rank, _ = coupling_shape
        self.members, self.loop_size = members, loop_size
        self.per_device = self.shard_len // self.size
        self.width = self.per_device * self.rank
        self.cells = self.per_device * SPAN
        self.block_clusters = self.per_device * members
        distances = [d % loop_size for d in (2, loop_size - 2, loop_size // 2)]
        self.hops = sorted(set(distances))
        self.set_of = [self.hops.index(d) for d in distances]
        self.paired = len(self.hops) == 1 and 2 * self.hops[0] == loop_size and members == 4
        devices = members * loop_size
        self.near = [(i, i ^ 1) for i in range(devices)]
        self.over = [(i, (i + 1 if i % 2 else i - 1) % devices) for i in range(devices)]
        places = [(l, m) for l in range(loop_size) for m in range(members)]
        self.across = [
            [
                (l * members + m, (l + self.hops[0]) % loop_size * members + (m ^ (m % 2 * 2) ^ other))
                for l, m in places
            ]
            for other in range(2)
        ]
        self.routes = [
            [(l * members + m, (l + hop) % loop_size * members + (m + step) % members) for l, m in places]
            for hop in self.hops
            for step in range(members)
        ]

    def panel(self, ref, c):
        return ref[:, c * self.size : (c + 1) * self.size]

    def member(self, index_ref):
        return lax.rem(index_ref[0], self.members)

    def send_far(self, index_ref, x, cb_ref, g_ref, out_refs):
        coeffs = dot_nt(x, cb_ref[...]).astype(BF16)
        twice = jnp.concatenate([coeffs, coeffs], axis=1)
        totals = [dot_nt(twice, g_ref[index]) for index in range(len(self.hops))]
        if not self.paired:
            for i, out_ref in enumerate(out_refs):
                step = i % self.members * self.width
                out_ref[...] = totals[i // self.members][:, step : step + self.width].astype(BF16)
            return
        message_ref, keep_ref = out_refs
        (total,) = totals
        member = self.member(index_ref)
        second = lax.rem(member, 2) != lax.div(member, 2)
        first, last = total[:, : 2 * self.width], total[:, 2 * self.width :]
        keep_ref[...] = jnp.where(second, last, first)
        upper, lower = halves(jnp.where(second, first, last))
        start = message_ref.shape[1] - 4 * self.width
        if start:
            message_ref[:, :start] = x
        message_ref[:, start : start + 2 * self.width] = upper
        message_ref[:, start + 2 * self.width :] = lower

    def relay_far(self, index_ref, keep_ref, message_ref, out_refs):
        start = message_ref.shape[1] - 4 * self.width
        upper = message_ref[:, start : start + 2 * self.width].astype(F32)
        lower = message_ref[:, start + 2 * self.width :].astype(F32)
        total = (keep_ref[...] + (upper + lower)).astype(BF16)
        second = lax.rem(index_ref[0], 2) == 1
        first, last = total[:, : self.width], total[:, self.width :]
        out_refs[0][...] = jnp.where(second, last, first)
        out_refs[1][...] = jnp.where(second, first, last)

    def far_sum(self, far_refs):
        return sum(ref[...].astype(F32) for ref in far_refs)

    def near_sums(self, x_ref, d_ref, acc_ref, first, start_ref=None):
        panels = [self.panel(x_ref, c) for c in range(self.per_device)]
        for r in range(self.per_device):
            value = None if start_ref is None else self.panel(start_ref, r)
            for c in range(self.per_device):
                offset = first + c - r
                if -REACH <= offset <= REACH:
                    term = dot_nt(panels[c], d_ref[r * SPAN + offset + REACH])
                    value = term if value is None else value + term
            acc_ref[:, r * self.size : (r + 1) * self.size] = value

    def halo_sums(self, below, x_ref, d_ref, acc_ref, start_ref):
        @pl.when(below)
        def _():
            self.near_sums(x_ref, d_ref, acc_ref, -self.per_device, start_ref)

        @pl.when(jnp.logical_not(below))
        def _():
            self.near_sums(x_ref, d_ref, acc_ref, self.per_device, start_ref)

    def far_halves(self, far_refs):
        return jnp.concatenate(halves(self.far_sum(far_refs)), axis=1)

    def next_panel(self, acc_ref, rb_ref, both, c):
        return (self.panel(acc_ref, c) + dot_nn(both, self.panel(rb_ref, c))).astype(BF16)

    def next_block(self, acc_ref, rb_ref, far_refs):
        both = self.far_halves(far_refs)
        panels = [self.next_panel(acc_ref, rb_ref, both, c) for c in range(self.per_device)]
        return jnp.concatenate(panels, axis=1)


def prepare_kernel(plan, index_ref, *refs):
    sources, refs = refs[:7], refs[7:]
    x_ref, g_ref, cb_ref, near_ref, offsets_ref, rows_ref, cols_ref, col_ref, coup_ref, sum_ref, sems = refs
    targets = (near_ref, offsets_ref, rows_ref, cols_ref, x_ref, col_ref, coup_ref)
    copies = [
        pltpu.make_async_copy(source, target, sems.at[i])
        for i, (source, target) in enumerate(zip(sources, targets))
    ]
    for copy in copies:
        copy.start()
    rank, size = plan.rank, plan.size
    cb_ref[...] = jnp.zeros_like(cb_ref)
    sum_ref[...] = jnp.zeros_like(sum_ref)
    for copy in copies:
        copy.wait()
    for c in range(plan.per_device):
        cb_ref[c * rank : (c + 1) * rank, c * size : (c + 1) * size] = col_ref[c]
    column = lax.broadcasted_iota(jnp.int32, (rank, plan.width), 1) // rank
    shift = 0 if plan.paired else plan.member(index_ref)
    for s in range(plan.slots):
        row = lax.rem(rows_ref[s], plan.block_clusters)
        step = lax.rem(lax.div(row, plan.per_device) - shift + plan.members, plan.members)
        place = step * plan.per_device + lax.rem(row, plan.per_device)
        if len(plan.hops) > 1:
            level = lax.div(rows_ref[s], plan.block_clusters)
            index = sum(jnp.where(level == i, index, 0) for i, index in enumerate(plan.set_of))
        else:
            index = 0
        where = (index, pl.ds(pl.multiple_of(place * rank, rank), rank), slice(None))
        tile = coup_ref[s].astype(F32)
        wide = jnp.where(column == cols_ref[s], jnp.concatenate([tile] * plan.per_device, axis=1), 0.0)
        sum_ref[where] = sum_ref[where] + wide
    for index in range(len(plan.hops)):
        g_ref[index] = jnp.concatenate(halves(sum_ref[index]), axis=1)


def first_far_kernel(plan, index_ref, x_ref, cb_ref, g_ref, copy_ref, *out_refs):
    x = x_ref[...]
    plan.send_far(index_ref, x, cb_ref, g_ref, out_refs)
    copy_ref[...] = x


def relay_kernel(plan, index_ref, keep_ref, message_ref, *out_refs):
    plan.relay_far(index_ref, keep_ref, message_ref, out_refs)


def first_own_kernel(plan, *refs):
    index_ref, rows_ref, offsets_ref, x_ref, near_ref, row_ref, tiles_ref = refs[:7]
    acc_ref, d_ref, rb_ref = refs[-3:]
    rank, size = plan.rank, plan.size
    for cell in range(plan.cells):
        d_ref[cell] = jnp.zeros(d_ref.shape[1:], d_ref.dtype)
    for s in range(plan.tiles):
        d_ref[rows_ref[s] * SPAN + offsets_ref[s] + REACH] = tiles_ref[s]
    rb_ref[...] = jnp.zeros_like(rb_ref)
    for c in range(plan.per_device):
        for start in (c * rank, plan.width + c * rank):
            rb_ref[start : start + rank, c * size : (c + 1) * size] = row_ref[c]
    plan.near_sums(x_ref, d_ref, acc_ref, 0)
    plan.halo_sums(lax.rem(index_ref[0], 2) == 1, near_ref, d_ref, acc_ref, acc_ref)


def own_kernel(plan, slot, *refs):
    index_ref, x_ref, near_ref, d_ref = refs[:4]
    acc_ref, krylov_ref, sem = refs[-3:]
    copy = pltpu.make_async_copy(x_ref, krylov_ref.at[slot], sem)
    copy.start()
    plan.near_sums(x_ref, d_ref, acc_ref, 0)
    plan.halo_sums(lax.rem(index_ref[0], 2) == 1, near_ref, d_ref, acc_ref, acc_ref)
    copy.wait()


def halo_kernel(plan, index_ref, acc_ref, over_ref, d_ref, *refs):
    plan.halo_sums(lax.rem(index_ref[0], 2) == 0, over_ref, d_ref, refs[-1], acc_ref)


def finish_kernel(plan, fars, *refs):
    index_ref, acc_ref, rb_ref, cb_ref, g_ref = refs[:5]
    far_refs, (x_ref, *sends) = refs[5 : 5 + fars], refs[5 + fars :]
    x = plan.next_block(acc_ref, rb_ref, far_refs)
    x_ref[...] = x
    plan.send_far(index_ref, x, cb_ref, g_ref, sends)


def last_kernel(plan, fars, slot, *refs):
    acc_ref, rb_ref = refs[:2]
    far_refs, (_, krylov_ref, x_ref, sem) = refs[2 : 2 + fars], refs[2 + fars :]
    both = plan.far_halves(far_refs)
    copies = []
    for c in range(plan.per_device):
        columns = pl.ds(c * plan.size, plan.size)
        x_ref[:, columns] = plan.next_panel(acc_ref, rb_ref, both, c)
        copies.append(
            pltpu.make_async_copy(x_ref.at[:, columns], krylov_ref.at[slot, :, columns], sem.at[c])
        )
        copies[-1].start()
    for copy in copies:
        copy.wait()


def call(kernel, name, ins, specs, outs, out_specs=None, scratch=(), aliases=None, cost=USUAL):
    spaces = {id(IN_VMEM): pltpu.VMEM, id(IN_HBM): pltpu.HBM}
    ins = [
        pltpu.with_memory_space_constraint(v, spaces[id(spec)]) if id(spec) in spaces else v
        for v, spec in zip(ins, specs)
    ]
    return pl.pallas_call(
        kernel,
        in_specs=list(specs),
        out_specs=out_specs or [IN_VMEM] * len(outs),
        out_shape=list(outs),
        scratch_shapes=list(scratch),
        input_output_aliases=aliases or {},
        compiler_params=pltpu.CompilerParams(vmem_limit_bytes=16 * 2**20),
        cost_estimate=pl.CostEstimate(flops=cost[0], bytes_accessed=cost[1], transcendentals=0),
        name=name,
    )(*ins)


def on_device(
    block, near_tiles, near_rows, near_offsets, col_basis, couplings, far_rows, far_cols, row_basis
):
    axes = ("loop", "far")
    plan = Plan(
        block.shape, near_tiles.shape, couplings.shape, lax.axis_size("far"), lax.axis_size("loop")
    )
    rhs, shard_len, width = plan.rhs, plan.shard_len, plan.width
    block_out = pltpu.VMEM((rhs, shard_len), BF16)
    acc_out = pltpu.VMEM((rhs, shard_len), F32)
    relay_out = pltpu.VMEM((rhs, width), BF16)
    krylov_out = jax.ShapeDtypeStruct((PRODUCTS, rhs, shard_len), BF16)
    if plan.paired:
        kept = pltpu.VMEM((rhs, 2 * width), F32)
        first_out = [pltpu.VMEM((rhs, 4 * width), BF16), kept]
        sends_out = [pltpu.VMEM((rhs, shard_len + 4 * width), BF16), kept]
    else:
        first_out = sends_out = [pltpu.VMEM((rhs, width), BF16)] * len(plan.routes)
    index = lax.axis_index(axes).astype(jnp.int32).reshape(1)

    def scratch_for(*arrays):
        return [
            pltpu.SMEM(v.shape, v.dtype) if v.dtype == jnp.int32 else pltpu.VMEM(v.shape, v.dtype)
            for v in arrays
        ]

    current, sends, krylov = block, None, None
    for product in range(PRODUCTS):
        if product == 0:
            ins = [near_rows, near_offsets, far_rows, far_cols, block, col_basis, couplings]
            matrix = (len(plan.hops), plan.members * width, 2 * width)
            current, coupled, col_wide, row_slots, offset_slots = call(
                functools.partial(prepare_kernel, plan),
                "prepare",
                [index, *ins],
                [IN_SMEM] + [IN_HBM] * 7,
                [
                    block_out,
                    pltpu.VMEM(matrix, BF16),
                    pltpu.VMEM((width, shard_len), BF16),
                    *scratch_for(near_rows, near_offsets),
                ],
                [IN_VMEM] * 3 + [IN_SMEM] * 2,
                scratch=scratch_for(far_rows, far_cols, col_basis, couplings)
                + [pltpu.VMEM(matrix[:2] + (width,), F32), pltpu.SemaphoreType.DMA((7,))],
            )
            over = lax.ppermute(current, axes, plan.over)
            current, *sends = call(
                functools.partial(first_far_kernel, plan),
                "first_far",
                [index, current, col_wide, coupled],
                [IN_SMEM] + [IN_VMEM] * 3,
                [block_out, *first_out],
                cost=LONG,
            )
        if product > 0:
            over = lax.ppermute(current, axes, plan.over)
            near = message = lax.ppermute(sends[0] if plan.paired else current, axes, plan.near)
        else:
            message = lax.ppermute(sends[0], axes, plan.near) if plan.paired else None
            near = lax.ppermute(current, axes, plan.near)
        if plan.paired:
            sends = call(
                functools.partial(relay_kernel, plan),
                "relay",
                [index, sends[1], message],
                [IN_SMEM] + [IN_VMEM] * 2,
                [relay_out] * 2,
                cost=BRIEF if product == 0 else USUAL,
            )
            routes = plan.across
        else:
            routes = plan.routes
        fars = [lax.ppermute(s, axes, route) for s, route in zip(sends, routes)]
        after = sends if plan.paired else []
        if product == 0:
            ins = [index, row_slots, offset_slots, current, near, row_basis, near_tiles, *after]
            acc, dense, row_wide = call(
                functools.partial(first_own_kernel, plan),
                "first_own",
                ins,
                [IN_SMEM] * 3 + [IN_VMEM] * 2 + [PREFETCHED] * 2 + [ANYWHERE] * len(after),
                [
                    acc_out,
                    pltpu.VMEM((plan.cells, plan.size, plan.size), BF16),
                    pltpu.VMEM((2 * width, shard_len), BF16),
                ],
                cost=LOADING,
            )
        else:
            ins = [index, current, near, dense, *after] + ([krylov] if product > 1 else [])
            acc, krylov = call(
                functools.partial(own_kernel, plan, product - 1),
                "own",
                ins,
                [IN_SMEM] + [IN_VMEM] * 3 + [ANYWHERE] * (len(ins) - 4),
                [acc_out, krylov_out],
                [IN_VMEM, ANYWHERE],
                [pltpu.SemaphoreType.DMA],
                {len(ins) - 1: 1} if product > 1 else None,
            )
        (acc,) = call(
            functools.partial(halo_kernel, plan),
            "halo",
            [index, acc, over, dense],
            [IN_SMEM] + [IN_VMEM] * 3,
            [acc_out],
            cost=BRIEF if product == 0 else USUAL,
        )
        if product < PRODUCTS - 1:
            ins = [index, acc, row_wide, col_wide, coupled, *fars]
            current, *sends = call(
                functools.partial(finish_kernel, plan, len(fars)),
                "finish",
                ins,
                [IN_SMEM] + [IN_VMEM] * (len(ins) - 1),
                [block_out, *sends_out],
            )
        else:
            ins = [acc, row_wide, *fars, krylov]
            (krylov,) = call(
                functools.partial(last_kernel, plan, len(fars), product),
                "last",
                ins,
                [IN_VMEM] * (len(ins) - 1) + [ANYWHERE],
                [krylov_out],
                [ANYWHERE],
                [
                    pltpu.VMEM((rhs, shard_len), BF16),
                    pltpu.SemaphoreType.DMA((plan.per_device,)),
                ],
                {len(ins) - 1: 0},
            )
    return krylov


def solution(mesh):
    split = ("groups", "loop", "far")
    wide, narrow = P(split, None, None), P(split)
    in_specs = (P(None, split), wide, narrow, narrow, wide, wide, narrow, narrow, wide)
    return jax.shard_map(
        on_device, mesh=mesh, in_specs=in_specs, out_specs=P(None, None, split), check_vma=False
    )
```

```python
import functools

import jax
import jax.numpy as jnp
from jax import lax
from jax.experimental import pallas as pl
from jax.experimental.pallas import tpu as pltpu
from jax.sharding import PartitionSpec as P

PRODUCTS = 4
REACH = 4
LEVELS = 3
SPAN = 2 * REACH + 1

F32 = jnp.float32
BF16 = jnp.bfloat16
IN_VMEM = pl.BlockSpec(memory_space=pltpu.VMEM)
PREFETCHED = pl.BlockSpec(memory_space=pltpu.VMEM)
IN_SMEM = pl.BlockSpec(memory_space=pltpu.SMEM)
IN_HBM = pl.BlockSpec(memory_space=pltpu.HBM)
ANYWHERE = pl.BlockSpec(memory_space=pl.ANY)


def dot_nt(a, b):
    return lax.dot_general(a, b, (((1,), (1,)), ((), ())), preferred_element_type=F32)


def dot_nn(a, b):
    return lax.dot_general(a, b, (((1,), (0,)), ((), ())), preferred_element_type=F32)


def halves(value):
    upper = value.astype(BF16)
    return upper, (value - upper.astype(F32)).astype(BF16)


class Plan:
    def __init__(self, block_shape, tile_shape, coupling_shape, members, loop_size):
        self.rhs, self.shard_len = block_shape
        self.tiles, self.size, _ = tile_shape
        self.slots, self.rank, _ = coupling_shape
        self.members, self.loop_size = members, loop_size
        self.per_device = self.shard_len // self.size
        self.width = self.per_device * self.rank
        self.cells = self.per_device * SPAN
        self.block_clusters = self.per_device * members
        distances = [d % loop_size for d in (2, loop_size - 2, loop_size // 2)]
        self.hops = sorted(set(distances))
        self.set_of = [self.hops.index(d) for d in distances]
        self.paired = len(self.hops) == 1 and 2 * self.hops[0] == loop_size and members == 4
        devices = members * loop_size
        self.near = [(i, i ^ 1) for i in range(devices)]
        self.over = [(i, (i + 1 if i % 2 else i - 1) % devices) for i in range(devices)]
        places = [(l, m) for l in range(loop_size) for m in range(members)]
        self.across = [
            [
                (l * members + m, (l + self.hops[0]) % loop_size * members + (m ^ (m % 2 * 2) ^ other))
                for l, m in places
            ]
            for other in range(2)
        ]
        self.routes = [
            [(l * members + m, (l + hop) % loop_size * members + (m + step) % members) for l, m in places]
            for hop in self.hops
            for step in range(members)
        ]

    def panel(self, ref, c):
        return ref[:, c * self.size : (c + 1) * self.size]

    def member(self, index_ref):
        return lax.rem(index_ref[0], self.members)

    def send_far(self, index_ref, x, cb_ref, g_ref, out_refs):
        coeffs = dot_nt(x, cb_ref[...]).astype(BF16)
        twice = jnp.concatenate([coeffs, coeffs], axis=1)
        totals = [dot_nt(twice, g_ref[index]) for index in range(len(self.hops))]
        if not self.paired:
            for i, out_ref in enumerate(out_refs):
                step = i % self.members * self.width
                out_ref[...] = totals[i // self.members][:, step : step + self.width].astype(BF16)
            return
        message_ref, keep_ref = out_refs
        (total,) = totals
        member = self.member(index_ref)
        second = lax.rem(member, 2) != lax.div(member, 2)
        first, last = total[:, : 2 * self.width], total[:, 2 * self.width :]
        keep_ref[...] = jnp.where(second, last, first)
        upper, lower = halves(jnp.where(second, first, last))
        message_ref[:, : self.shard_len] = x
        message_ref[:, self.shard_len : self.shard_len + 2 * self.width] = upper
        message_ref[:, self.shard_len + 2 * self.width :] = lower

    def relay_far(self, index_ref, keep_ref, message_ref, out_refs):
        upper = message_ref[:, self.shard_len : self.shard_len + 2 * self.width].astype(F32)
        lower = message_ref[:, self.shard_len + 2 * self.width :].astype(F32)
        total = (keep_ref[...] + (upper + lower)).astype(BF16)
        second = lax.rem(index_ref[0], 2) == 1
        first, last = total[:, : self.width], total[:, self.width :]
        out_refs[0][...] = jnp.where(second, last, first)
        out_refs[1][...] = jnp.where(second, first, last)

    def far_sum(self, far_refs):
        return sum(ref[...].astype(F32) for ref in far_refs)

    def near_sums(self, x_ref, d_ref, acc_ref, first, start_ref=None):
        panels = [self.panel(x_ref, c) for c in range(self.per_device)]
        for r in range(self.per_device):
            value = None if start_ref is None else self.panel(start_ref, r)
            for c in range(self.per_device):
                offset = first + c - r
                if -REACH <= offset <= REACH:
                    term = dot_nt(panels[c], d_ref[r * SPAN + offset + REACH])
                    value = term if value is None else value + term
            acc_ref[:, r * self.size : (r + 1) * self.size] = value

    def halo_sums(self, below, x_ref, d_ref, acc_ref, start_ref):
        @pl.when(below)
        def _():
            self.near_sums(x_ref, d_ref, acc_ref, -self.per_device, start_ref)

        @pl.when(jnp.logical_not(below))
        def _():
            self.near_sums(x_ref, d_ref, acc_ref, self.per_device, start_ref)

    def far_halves(self, far_refs):
        return jnp.concatenate(halves(self.far_sum(far_refs)), axis=1)

    def next_panel(self, acc_ref, rb_ref, both, c):
        return (self.panel(acc_ref, c) + dot_nn(both, self.panel(rb_ref, c))).astype(BF16)

    def next_block(self, acc_ref, rb_ref, far_refs):
        both = self.far_halves(far_refs)
        panels = [self.next_panel(acc_ref, rb_ref, both, c) for c in range(self.per_device)]
        return jnp.concatenate(panels, axis=1)


def prepare_kernel(plan, index_ref, *refs):
    sources, refs = refs[:7], refs[7:]
    x_ref, g_ref, cb_ref, near_ref, offsets_ref = refs[:5]
    sends, (rows_ref, cols_ref, col_ref, coup_ref, sum_ref, sems) = refs[5:-6], refs[-6:]
    targets = (near_ref, offsets_ref, rows_ref, cols_ref, x_ref, col_ref, coup_ref)
    copies = [
        pltpu.make_async_copy(source, target, sems.at[i])
        for i, (source, target) in enumerate(zip(sources, targets))
    ]
    for copy in copies:
        copy.start()
    rank, size = plan.rank, plan.size
    cb_ref[...] = jnp.zeros_like(cb_ref)
    sum_ref[...] = jnp.zeros_like(sum_ref)
    for copy in copies:
        copy.wait()
    for c in range(plan.per_device):
        cb_ref[c * rank : (c + 1) * rank, c * size : (c + 1) * size] = col_ref[c]
    column = lax.broadcasted_iota(jnp.int32, (rank, plan.width), 1) // rank
    shift = 0 if plan.paired else plan.member(index_ref)
    for s in range(plan.slots):
        row = lax.rem(rows_ref[s], plan.block_clusters)
        step = lax.rem(lax.div(row, plan.per_device) - shift + plan.members, plan.members)
        place = step * plan.per_device + lax.rem(row, plan.per_device)
        if len(plan.hops) > 1:
            level = lax.div(rows_ref[s], plan.block_clusters)
            index = sum(jnp.where(level == i, index, 0) for i, index in enumerate(plan.set_of))
        else:
            index = 0
        where = (index, pl.ds(pl.multiple_of(place * rank, rank), rank), slice(None))
        tile = coup_ref[s].astype(F32)
        wide = jnp.where(column == cols_ref[s], jnp.concatenate([tile] * plan.per_device, axis=1), 0.0)
        sum_ref[where] = sum_ref[where] + wide
    for index in range(len(plan.hops)):
        g_ref[index] = jnp.concatenate(halves(sum_ref[index]), axis=1)
    plan.send_far(index_ref, x_ref[...], cb_ref, g_ref, sends)


def relay_kernel(plan, index_ref, keep_ref, message_ref, *out_refs):
    plan.relay_far(index_ref, keep_ref, message_ref, out_refs)


def first_own_kernel(plan, *refs):
    index_ref, rows_ref, offsets_ref, x_ref, near_ref, row_ref, tiles_ref = refs[:7]
    acc_ref, d_ref, rb_ref = refs[-3:]
    rank, size = plan.rank, plan.size
    for cell in range(plan.cells):
        d_ref[cell] = jnp.zeros(d_ref.shape[1:], d_ref.dtype)
    for s in range(plan.tiles):
        d_ref[rows_ref[s] * SPAN + offsets_ref[s] + REACH] = tiles_ref[s]
    rb_ref[...] = jnp.zeros_like(rb_ref)
    for c in range(plan.per_device):
        for start in (c * rank, plan.width + c * rank):
            rb_ref[start : start + rank, c * size : (c + 1) * size] = row_ref[c]
    plan.near_sums(x_ref, d_ref, acc_ref, 0)
    plan.halo_sums(lax.rem(index_ref[0], 2) == 1, near_ref, d_ref, acc_ref, acc_ref)


def own_kernel(plan, slot, *refs):
    index_ref, x_ref, near_ref, d_ref = refs[:4]
    acc_ref, krylov_ref, sem = refs[-3:]
    copy = pltpu.make_async_copy(x_ref, krylov_ref.at[slot], sem)
    copy.start()
    plan.near_sums(x_ref, d_ref, acc_ref, 0)
    plan.halo_sums(lax.rem(index_ref[0], 2) == 1, near_ref, d_ref, acc_ref, acc_ref)
    copy.wait()


def halo_kernel(plan, index_ref, acc_ref, over_ref, d_ref, *refs):
    plan.halo_sums(lax.rem(index_ref[0], 2) == 0, over_ref, d_ref, refs[-1], acc_ref)


def finish_kernel(plan, fars, *refs):
    index_ref, acc_ref, rb_ref, cb_ref, g_ref = refs[:5]
    far_refs, (x_ref, *sends) = refs[5 : 5 + fars], refs[5 + fars :]
    x = plan.next_block(acc_ref, rb_ref, far_refs)
    x_ref[...] = x
    plan.send_far(index_ref, x, cb_ref, g_ref, sends)


def last_kernel(plan, fars, slot, *refs):
    acc_ref, rb_ref = refs[:2]
    far_refs, (_, krylov_ref, x_ref, sem) = refs[2 : 2 + fars], refs[2 + fars :]
    both = plan.far_halves(far_refs)
    copies = []
    for c in range(plan.per_device):
        columns = pl.ds(c * plan.size, plan.size)
        x_ref[:, columns] = plan.next_panel(acc_ref, rb_ref, both, c)
        copies.append(
            pltpu.make_async_copy(x_ref.at[:, columns], krylov_ref.at[slot, :, columns], sem.at[c])
        )
        copies[-1].start()
    for copy in copies:
        copy.wait()


def call(kernel, name, ins, specs, outs, out_specs=None, scratch=(), aliases=None):
    spaces = {id(IN_VMEM): pltpu.VMEM, id(IN_HBM): pltpu.HBM}
    ins = [
        pltpu.with_memory_space_constraint(v, spaces[id(spec)]) if id(spec) in spaces else v
        for v, spec in zip(ins, specs)
    ]
    return pl.pallas_call(
        kernel,
        in_specs=list(specs),
        out_specs=out_specs or [IN_VMEM] * len(outs),
        out_shape=list(outs),
        scratch_shapes=list(scratch),
        input_output_aliases=aliases or {},
        compiler_params=pltpu.CompilerParams(vmem_limit_bytes=16 * 2**20),
        cost_estimate=pl.CostEstimate(flops=10**9, bytes_accessed=2**22, transcendentals=0),
        name=name,
    )(*ins)


def on_device(
    block, near_tiles, near_rows, near_offsets, col_basis, couplings, far_rows, far_cols, row_basis
):
    axes = ("loop", "far")
    plan = Plan(
        block.shape, near_tiles.shape, couplings.shape, lax.axis_size("far"), lax.axis_size("loop")
    )
    rhs, shard_len, width = plan.rhs, plan.shard_len, plan.width
    block_out = pltpu.VMEM((rhs, shard_len), BF16)
    acc_out = pltpu.VMEM((rhs, shard_len), F32)
    relay_out = pltpu.VMEM((rhs, width), BF16)
    krylov_out = jax.ShapeDtypeStruct((PRODUCTS, rhs, shard_len), BF16)
    if plan.paired:
        sends_out = [
            pltpu.VMEM((rhs, shard_len + 4 * width), BF16),
            pltpu.VMEM((rhs, 2 * width), F32),
        ]
    else:
        sends_out = [pltpu.VMEM((rhs, width), BF16)] * len(plan.routes)
    index = lax.axis_index(axes).astype(jnp.int32).reshape(1)

    def scratch_for(*arrays):
        return [
            pltpu.SMEM(v.shape, v.dtype) if v.dtype == jnp.int32 else pltpu.VMEM(v.shape, v.dtype)
            for v in arrays
        ]

    current, sends, krylov = block, None, None
    for product in range(PRODUCTS):
        if product == 0:
            ins = [near_rows, near_offsets, far_rows, far_cols, block, col_basis, couplings]
            matrix = (len(plan.hops), plan.members * width, 2 * width)
            current, coupled, col_wide, row_slots, offset_slots, *sends = call(
                functools.partial(prepare_kernel, plan),
                "prepare",
                [index, *ins],
                [IN_SMEM] + [IN_HBM] * 7,
                [
                    block_out,
                    pltpu.VMEM(matrix, BF16),
                    pltpu.VMEM((width, shard_len), BF16),
                    *scratch_for(near_rows, near_offsets),
                    *sends_out,
                ],
                [IN_VMEM] * 3 + [IN_SMEM] * 2 + [IN_VMEM] * len(sends_out),
                scratch=scratch_for(far_rows, far_cols, col_basis, couplings)
                + [pltpu.VMEM(matrix[:2] + (width,), F32), pltpu.SemaphoreType.DMA((7,))],
            )
        over = lax.ppermute(block if product == 0 else current, axes, plan.over)
        near = lax.ppermute(sends[0] if plan.paired else current, axes, plan.near)
        if plan.paired:
            sends = call(
                functools.partial(relay_kernel, plan),
                "relay",
                [index, sends[1], near],
                [IN_SMEM] + [IN_VMEM] * 2,
                [relay_out] * 2,
            )
            routes = plan.across
        else:
            routes = plan.routes
        fars = [lax.ppermute(s, axes, route) for s, route in zip(sends, routes)]
        after = sends if plan.paired else []
        if product == 0:
            ins = [index, row_slots, offset_slots, current, near, row_basis, near_tiles, *after]
            acc, dense, row_wide = call(
                functools.partial(first_own_kernel, plan),
                "first_own",
                ins,
                [IN_SMEM] * 3 + [IN_VMEM] * 2 + [PREFETCHED] * 2 + [ANYWHERE] * len(after),
                [
                    acc_out,
                    pltpu.VMEM((plan.cells, plan.size, plan.size), BF16),
                    pltpu.VMEM((2 * width, shard_len), BF16),
                ],
            )
        else:
            ins = [index, current, near, dense, *after] + ([krylov] if product > 1 else [])
            acc, krylov = call(
                functools.partial(own_kernel, plan, product - 1),
                "own",
                ins,
                [IN_SMEM] + [IN_VMEM] * 3 + [ANYWHERE] * (len(ins) - 4),
                [acc_out, krylov_out],
                [IN_VMEM, ANYWHERE],
                [pltpu.SemaphoreType.DMA],
                {len(ins) - 1: 1} if product > 1 else None,
            )
        (acc,) = call(
            functools.partial(halo_kernel, plan),
            "halo",
            [index, acc, over, dense],
            [IN_SMEM] + [IN_VMEM] * 3,
            [acc_out],
        )
        if product < PRODUCTS - 1:
            ins = [index, acc, row_wide, col_wide, coupled, *fars]
            current, *sends = call(
                functools.partial(finish_kernel, plan, len(fars)),
                "finish",
                ins,
                [IN_SMEM] + [IN_VMEM] * (len(ins) - 1),
                [block_out, *sends_out],
            )
        else:
            ins = [acc, row_wide, *fars, krylov]
            (krylov,) = call(
                functools.partial(last_kernel, plan, len(fars), product),
                "last",
                ins,
                [IN_VMEM] * (len(ins) - 1) + [ANYWHERE],
                [krylov_out],
                [ANYWHERE],
                [
                    pltpu.VMEM((rhs, shard_len), BF16),
                    pltpu.SemaphoreType.DMA((plan.per_device,)),
                ],
                {len(ins) - 1: 0},
            )
    return krylov


def solution(mesh):
    split = ("groups", "loop", "far")
    wide, narrow = P(split, None, None), P(split)
    in_specs = (P(None, split), wide, narrow, narrow, wide, wide, narrow, narrow, wide)
    return jax.shard_map(
        on_device, mesh=mesh, in_specs=in_specs, out_specs=P(None, None, split), check_vma=False
    )
```

```python
import functools

import jax
import jax.numpy as jnp
from jax import lax
from jax.experimental import pallas as pl
from jax.experimental.pallas import tpu as pltpu
from jax.sharding import PartitionSpec as P

PRODUCTS = 4
REACH = 4
LEVELS = 3
SPAN = 2 * REACH + 1

F32 = jnp.float32
BF16 = jnp.bfloat16
IN_VMEM = pl.BlockSpec(memory_space=pltpu.VMEM)
PREFETCHED = pl.BlockSpec(memory_space=pltpu.VMEM)
IN_SMEM = pl.BlockSpec(memory_space=pltpu.SMEM)
IN_HBM = pl.BlockSpec(memory_space=pltpu.HBM)
ANYWHERE = pl.BlockSpec(memory_space=pl.ANY)


def dot_nt(a, b):
    return lax.dot_general(a, b, (((1,), (1,)), ((), ())), preferred_element_type=F32)


def dot_nn(a, b):
    return lax.dot_general(a, b, (((1,), (0,)), ((), ())), preferred_element_type=F32)


def halves(value):
    upper = value.astype(BF16)
    return upper, (value - upper.astype(F32)).astype(BF16)


class Plan:
    def __init__(self, block_shape, tile_shape, coupling_shape, members, loop_size):
        self.rhs, self.shard_len = block_shape
        self.tiles, self.size, _ = tile_shape
        self.slots, self.rank, _ = coupling_shape
        self.members, self.loop_size = members, loop_size
        self.per_device = self.shard_len // self.size
        self.width = self.per_device * self.rank
        self.cells = self.per_device * SPAN
        self.block_clusters = self.per_device * members
        distances = [d % loop_size for d in (2, loop_size - 2, loop_size // 2)]
        self.hops = sorted(set(distances))
        self.set_of = [self.hops.index(d) for d in distances]
        self.paired = len(self.hops) == 1 and 2 * self.hops[0] == loop_size and members == 4
        devices = members * loop_size
        self.near = [(i, i ^ 1) for i in range(devices)]
        self.over = [(i, (i + 1 if i % 2 else i - 1) % devices) for i in range(devices)]
        places = [(l, m) for l in range(loop_size) for m in range(members)]
        self.across = [
            [
                (l * members + m, (l + self.hops[0]) % loop_size * members + (m ^ (m % 2 * 2) ^ other))
                for l, m in places
            ]
            for other in (1, 0)
        ]
        self.routes = [
            [(l * members + m, (l + hop) % loop_size * members + (m + step) % members) for l, m in places]
            for hop in self.hops
            for step in range(members)
        ]

    def panel(self, ref, c):
        return ref[:, c * self.size : (c + 1) * self.size]

    def member(self, index_ref):
        return lax.rem(index_ref[0], self.members)

    def send_far(self, index_ref, x, cb_ref, g_ref, out_refs):
        coeffs = dot_nt(x, cb_ref[...]).astype(BF16)
        twice = jnp.concatenate([coeffs, coeffs], axis=1)
        totals = [dot_nt(twice, g_ref[index]) for index in range(len(self.hops))]
        if not self.paired:
            for i, out_ref in enumerate(out_refs):
                step = i % self.members * self.width
                out_ref[...] = totals[i // self.members][:, step : step + self.width].astype(BF16)
            return
        message_ref, keep_ref = out_refs
        (total,) = totals
        member = self.member(index_ref)
        second = lax.rem(member, 2) != lax.div(member, 2)
        first, last = total[:, : 2 * self.width], total[:, 2 * self.width :]
        keep_ref[...] = jnp.where(second, last, first)
        upper, lower = halves(jnp.where(second, first, last))
        message_ref[:, : self.shard_len] = x
        message_ref[:, self.shard_len : self.shard_len + 2 * self.width] = upper
        message_ref[:, self.shard_len + 2 * self.width :] = lower

    def relay_far(self, index_ref, keep_ref, message_ref, out_refs):
        upper = message_ref[:, self.shard_len : self.shard_len + 2 * self.width].astype(F32)
        lower = message_ref[:, self.shard_len + 2 * self.width :].astype(F32)
        total = (keep_ref[...] + (upper + lower)).astype(BF16)
        second = lax.rem(index_ref[0], 2) == 1
        first, last = total[:, : self.width], total[:, self.width :]
        out_refs[0][...] = jnp.where(second, first, last)
        out_refs[1][...] = jnp.where(second, last, first)

    def far_sum(self, far_refs):
        return sum(ref[...].astype(F32) for ref in far_refs)

    def near_sums(self, x_ref, d_ref, acc_ref, first, start_ref=None):
        panels = [self.panel(x_ref, c) for c in range(self.per_device)]
        for r in range(self.per_device):
            value = None if start_ref is None else self.panel(start_ref, r)
            for c in range(self.per_device):
                offset = first + c - r
                if -REACH <= offset <= REACH:
                    term = dot_nt(panels[c], d_ref[r * SPAN + offset + REACH])
                    value = term if value is None else value + term
            acc_ref[:, r * self.size : (r + 1) * self.size] = value

    def halo_sums(self, below, x_ref, d_ref, acc_ref, start_ref):
        @pl.when(below)
        def _():
            self.near_sums(x_ref, d_ref, acc_ref, -self.per_device, start_ref)

        @pl.when(jnp.logical_not(below))
        def _():
            self.near_sums(x_ref, d_ref, acc_ref, self.per_device, start_ref)

    def far_halves(self, far_refs):
        return jnp.concatenate(halves(self.far_sum(far_refs)), axis=1)

    def next_panel(self, acc_ref, rb_ref, both, c):
        return (self.panel(acc_ref, c) + dot_nn(both, self.panel(rb_ref, c))).astype(BF16)

    def next_block(self, acc_ref, rb_ref, far_refs):
        both = self.far_halves(far_refs)
        panels = [self.next_panel(acc_ref, rb_ref, both, c) for c in range(self.per_device)]
        return jnp.concatenate(panels, axis=1)


def prepare_kernel(plan, index_ref, *refs):
    sources, refs = refs[:7], refs[7:]
    x_ref, g_ref, cb_ref, near_ref, offsets_ref = refs[:5]
    sends, (rows_ref, cols_ref, col_ref, coup_ref, sum_ref, sems) = refs[5:-6], refs[-6:]
    targets = (near_ref, offsets_ref, rows_ref, cols_ref, x_ref, col_ref, coup_ref)
    copies = [
        pltpu.make_async_copy(source, target, sems.at[i])
        for i, (source, target) in enumerate(zip(sources, targets))
    ]
    for copy in copies:
        copy.start()
    rank, size = plan.rank, plan.size
    cb_ref[...] = jnp.zeros_like(cb_ref)
    sum_ref[...] = jnp.zeros_like(sum_ref)
    for copy in copies:
        copy.wait()
    for c in range(plan.per_device):
        cb_ref[c * rank : (c + 1) * rank, c * size : (c + 1) * size] = col_ref[c]
    column = lax.broadcasted_iota(jnp.int32, (rank, plan.width), 1) // rank
    shift = 0 if plan.paired else plan.member(index_ref)
    for s in range(plan.slots):
        row = lax.rem(rows_ref[s], plan.block_clusters)
        step = lax.rem(lax.div(row, plan.per_device) - shift + plan.members, plan.members)
        place = step * plan.per_device + lax.rem(row, plan.per_device)
        if len(plan.hops) > 1:
            level = lax.div(rows_ref[s], plan.block_clusters)
            index = sum(jnp.where(level == i, index, 0) for i, index in enumerate(plan.set_of))
        else:
            index = 0
        where = (index, pl.ds(pl.multiple_of(place * rank, rank), rank), slice(None))
        tile = coup_ref[s].astype(F32)
        wide = jnp.where(column == cols_ref[s], jnp.concatenate([tile] * plan.per_device, axis=1), 0.0)
        sum_ref[where] = sum_ref[where] + wide
    for index in range(len(plan.hops)):
        g_ref[index] = jnp.concatenate(halves(sum_ref[index]), axis=1)
    plan.send_far(index_ref, x_ref[...], cb_ref, g_ref, sends)


def relay_kernel(plan, index_ref, keep_ref, message_ref, *out_refs):
    plan.relay_far(index_ref, keep_ref, message_ref, out_refs)


def first_own_kernel(plan, *refs):
    index_ref, rows_ref, offsets_ref, x_ref, near_ref, row_ref, tiles_ref = refs[:7]
    acc_ref, d_ref, rb_ref = refs[-3:]
    rank, size = plan.rank, plan.size
    for cell in range(plan.cells):
        d_ref[cell] = jnp.zeros(d_ref.shape[1:], d_ref.dtype)
    for s in range(plan.tiles):
        d_ref[rows_ref[s] * SPAN + offsets_ref[s] + REACH] = tiles_ref[s]
    rb_ref[...] = jnp.zeros_like(rb_ref)
    for c in range(plan.per_device):
        for start in (c * rank, plan.width + c * rank):
            rb_ref[start : start + rank, c * size : (c + 1) * size] = row_ref[c]
    plan.near_sums(x_ref, d_ref, acc_ref, 0)
    plan.halo_sums(lax.rem(index_ref[0], 2) == 1, near_ref, d_ref, acc_ref, acc_ref)


def own_kernel(plan, slot, *refs):
    index_ref, x_ref, near_ref, d_ref = refs[:4]
    acc_ref, krylov_ref, sem = refs[-3:]
    copy = pltpu.make_async_copy(x_ref, krylov_ref.at[slot], sem)
    copy.start()
    plan.near_sums(x_ref, d_ref, acc_ref, 0)
    plan.halo_sums(lax.rem(index_ref[0], 2) == 1, near_ref, d_ref, acc_ref, acc_ref)
    copy.wait()


def halo_kernel(plan, index_ref, acc_ref, over_ref, d_ref, *refs):
    plan.halo_sums(lax.rem(index_ref[0], 2) == 0, over_ref, d_ref, refs[-1], acc_ref)


def finish_kernel(plan, fars, *refs):
    index_ref, acc_ref, rb_ref, cb_ref, g_ref = refs[:5]
    far_refs, (x_ref, *sends) = refs[5 : 5 + fars], refs[5 + fars :]
    x = plan.next_block(acc_ref, rb_ref, far_refs)
    x_ref[...] = x
    plan.send_far(index_ref, x, cb_ref, g_ref, sends)


def last_kernel(plan, fars, slot, *refs):
    acc_ref, rb_ref = refs[:2]
    far_refs, (_, krylov_ref, x_ref, sem) = refs[2 : 2 + fars], refs[2 + fars :]
    both = plan.far_halves(far_refs)
    copies = []
    for c in range(plan.per_device):
        columns = pl.ds(c * plan.size, plan.size)
        x_ref[:, columns] = plan.next_panel(acc_ref, rb_ref, both, c)
        copies.append(
            pltpu.make_async_copy(x_ref.at[:, columns], krylov_ref.at[slot, :, columns], sem.at[c])
        )
        copies[-1].start()
    for copy in copies:
        copy.wait()


def call(kernel, name, ins, specs, outs, out_specs=None, scratch=(), aliases=None):
    spaces = {id(IN_VMEM): pltpu.VMEM, id(IN_HBM): pltpu.HBM}
    ins = [
        pltpu.with_memory_space_constraint(v, spaces[id(spec)]) if id(spec) in spaces else v
        for v, spec in zip(ins, specs)
    ]
    return pl.pallas_call(
        kernel,
        in_specs=list(specs),
        out_specs=out_specs or [IN_VMEM] * len(outs),
        out_shape=list(outs),
        scratch_shapes=list(scratch),
        input_output_aliases=aliases or {},
        compiler_params=pltpu.CompilerParams(vmem_limit_bytes=16 * 2**20),
        cost_estimate=pl.CostEstimate(flops=10**9, bytes_accessed=2**22, transcendentals=0),
        name=name,
    )(*ins)


def on_device(
    block, near_tiles, near_rows, near_offsets, col_basis, couplings, far_rows, far_cols, row_basis
):
    axes = ("loop", "far")
    plan = Plan(
        block.shape, near_tiles.shape, couplings.shape, lax.axis_size("far"), lax.axis_size("loop")
    )
    rhs, shard_len, width = plan.rhs, plan.shard_len, plan.width
    block_out = pltpu.VMEM((rhs, shard_len), BF16)
    acc_out = pltpu.VMEM((rhs, shard_len), F32)
    relay_out = pltpu.VMEM((rhs, width), BF16)
    krylov_out = jax.ShapeDtypeStruct((PRODUCTS, rhs, shard_len), BF16)
    if plan.paired:
        sends_out = [
            pltpu.VMEM((rhs, shard_len + 4 * width), BF16),
            pltpu.VMEM((rhs, 2 * width), F32),
        ]
    else:
        sends_out = [pltpu.VMEM((rhs, width), BF16)] * len(plan.routes)
    index = lax.axis_index(axes).astype(jnp.int32).reshape(1)

    def scratch_for(*arrays):
        return [
            pltpu.SMEM(v.shape, v.dtype) if v.dtype == jnp.int32 else pltpu.VMEM(v.shape, v.dtype)
            for v in arrays
        ]

    current, sends, krylov = block, None, None
    for product in range(PRODUCTS):
        if product == 0:
            ins = [near_rows, near_offsets, far_rows, far_cols, block, col_basis, couplings]
            matrix = (len(plan.hops), plan.members * width, 2 * width)
            current, coupled, col_wide, row_slots, offset_slots, *sends = call(
                functools.partial(prepare_kernel, plan),
                "prepare",
                [index, *ins],
                [IN_SMEM] + [IN_HBM] * 7,
                [
                    block_out,
                    pltpu.VMEM(matrix, BF16),
                    pltpu.VMEM((width, shard_len), BF16),
                    *scratch_for(near_rows, near_offsets),
                    *sends_out,
                ],
                [IN_VMEM] * 3 + [IN_SMEM] * 2 + [IN_VMEM] * len(sends_out),
                scratch=scratch_for(far_rows, far_cols, col_basis, couplings)
                + [pltpu.VMEM(matrix[:2] + (width,), F32), pltpu.SemaphoreType.DMA((7,))],
            )
        over = lax.ppermute(block if product == 0 else current, axes, plan.over)
        near = lax.ppermute(sends[0] if plan.paired else current, axes, plan.near)
        if plan.paired:
            sends = call(
                functools.partial(relay_kernel, plan),
                "relay",
                [index, sends[1], near],
                [IN_SMEM] + [IN_VMEM] * 2,
                [relay_out] * 2,
            )
            routes = plan.across
        else:
            routes = plan.routes
        fars = [lax.ppermute(s, axes, route) for s, route in zip(sends, routes)]
        after = sends if plan.paired else []
        if product == 0:
            ins = [index, row_slots, offset_slots, current, near, row_basis, near_tiles, *after]
            acc, dense, row_wide = call(
                functools.partial(first_own_kernel, plan),
                "first_own",
                ins,
                [IN_SMEM] * 3 + [IN_VMEM] * 2 + [PREFETCHED] * 2 + [ANYWHERE] * len(after),
                [
                    acc_out,
                    pltpu.VMEM((plan.cells, plan.size, plan.size), BF16),
                    pltpu.VMEM((2 * width, shard_len), BF16),
                ],
            )
        else:
            ins = [index, current, near, dense, *after] + ([krylov] if product > 1 else [])
            acc, krylov = call(
                functools.partial(own_kernel, plan, product - 1),
                "own",
                ins,
                [IN_SMEM] + [IN_VMEM] * 3 + [ANYWHERE] * (len(ins) - 4),
                [acc_out, krylov_out],
                [IN_VMEM, ANYWHERE],
                [pltpu.SemaphoreType.DMA],
                {len(ins) - 1: 1} if product > 1 else None,
            )
        (acc,) = call(
            functools.partial(halo_kernel, plan),
            "halo",
            [index, acc, over, dense],
            [IN_SMEM] + [IN_VMEM] * 3,
            [acc_out],
        )
        if product < PRODUCTS - 1:
            ins = [index, acc, row_wide, col_wide, coupled, *fars]
            current, *sends = call(
                functools.partial(finish_kernel, plan, len(fars)),
                "finish",
                ins,
                [IN_SMEM] + [IN_VMEM] * (len(ins) - 1),
                [block_out, *sends_out],
            )
        else:
            ins = [acc, row_wide, *fars, krylov]
            (krylov,) = call(
                functools.partial(last_kernel, plan, len(fars), product),
                "last",
                ins,
                [IN_VMEM] * (len(ins) - 1) + [ANYWHERE],
                [krylov_out],
                [ANYWHERE],
                [
                    pltpu.VMEM((rhs, shard_len), BF16),
                    pltpu.SemaphoreType.DMA((plan.per_device,)),
                ],
                {len(ins) - 1: 0},
            )
    return krylov


def solution(mesh):
    split = ("groups", "loop", "far")
    wide, narrow = P(split, None, None), P(split)
    in_specs = (P(None, split), wide, narrow, narrow, wide, wide, narrow, narrow, wide)
    return jax.shard_map(
        on_device, mesh=mesh, in_specs=in_specs, out_specs=P(None, None, split), check_vma=False
    )
```

```python
import functools

import jax
import jax.numpy as jnp
from jax import lax
from jax.experimental import pallas as pl
from jax.experimental.pallas import tpu as pltpu
from jax.sharding import PartitionSpec as P

PRODUCTS = 4
REACH = 4
LEVELS = 3
SPAN = 2 * REACH + 1

F32 = jnp.float32
BF16 = jnp.bfloat16
IN_VMEM = pl.BlockSpec(memory_space=pltpu.VMEM)
PREFETCHED = pl.BlockSpec(memory_space=pltpu.VMEM)
IN_SMEM = pl.BlockSpec(memory_space=pltpu.SMEM)
IN_HBM = pl.BlockSpec(memory_space=pltpu.HBM)
ANYWHERE = pl.BlockSpec(memory_space=pl.ANY)


def dot_nt(a, b):
    return lax.dot_general(a, b, (((1,), (1,)), ((), ())), preferred_element_type=F32)


def dot_nn(a, b):
    return lax.dot_general(a, b, (((1,), (0,)), ((), ())), preferred_element_type=F32)


def halves(value):
    upper = value.astype(BF16)
    return upper, (value - upper.astype(F32)).astype(BF16)


class Plan:
    def __init__(self, block_shape, tile_shape, coupling_shape, members, loop_size):
        self.rhs, self.shard_len = block_shape
        self.tiles, self.size, _ = tile_shape
        self.slots, self.rank, _ = coupling_shape
        self.members, self.loop_size = members, loop_size
        self.per_device = self.shard_len // self.size
        self.width = self.per_device * self.rank
        self.cells = self.per_device * SPAN
        self.block_clusters = self.per_device * members
        distances = [d % loop_size for d in (2, loop_size - 2, loop_size // 2)]
        self.hops = sorted(set(distances))
        self.set_of = [self.hops.index(d) for d in distances]
        self.paired = len(self.hops) == 1 and 2 * self.hops[0] == loop_size and members == 4
        devices = members * loop_size
        self.near = [(i, i ^ 1) for i in range(devices)]
        self.over = [(i, (i + 1 if i % 2 else i - 1) % devices) for i in range(devices)]
        places = [(l, m) for l in range(loop_size) for m in range(members)]
        self.across = [
            [
                (l * members + m, (l + self.hops[0]) % loop_size * members + (m ^ other))
                for l, m in places
            ]
            for other in (0, 2)
        ]
        self.routes = [
            [(l * members + m, (l + hop) % loop_size * members + (m + step) % members) for l, m in places]
            for hop in self.hops
            for step in range(members)
        ]

    def panel(self, ref, c):
        return ref[:, c * self.size : (c + 1) * self.size]

    def member(self, index_ref):
        return lax.rem(index_ref[0], self.members)

    def send_far(self, index_ref, x, cb_ref, g_ref, out_refs):
        coeffs = dot_nt(x, cb_ref[...]).astype(BF16)
        twice = jnp.concatenate([coeffs, coeffs], axis=1)
        totals = [dot_nt(twice, g_ref[index]) for index in range(len(self.hops))]
        if not self.paired:
            for i, out_ref in enumerate(out_refs):
                step = i % self.members * self.width
                out_ref[...] = totals[i // self.members][:, step : step + self.width].astype(BF16)
            return
        message_ref, keep_ref = out_refs
        (total,) = totals
        pieces = [total[:, i * self.width : (i + 1) * self.width] for i in range(self.members)]
        even = jnp.concatenate(pieces[0::2], axis=1)
        odd = jnp.concatenate(pieces[1::2], axis=1)
        second = lax.rem(index_ref[0], 2) == 1
        keep_ref[...] = jnp.where(second, odd, even)
        upper, lower = halves(jnp.where(second, even, odd))
        message_ref[:, : self.shard_len] = x
        message_ref[:, self.shard_len : self.shard_len + 2 * self.width] = upper
        message_ref[:, self.shard_len + 2 * self.width :] = lower

    def relay_far(self, index_ref, keep_ref, message_ref, out_refs):
        upper = message_ref[:, self.shard_len : self.shard_len + 2 * self.width].astype(F32)
        lower = message_ref[:, self.shard_len + 2 * self.width :].astype(F32)
        total = (keep_ref[...] + (upper + lower)).astype(BF16)
        second = self.member(index_ref) >= 2
        first, last = total[:, : self.width], total[:, self.width :]
        out_refs[0][...] = jnp.where(second, last, first)
        out_refs[1][...] = jnp.where(second, first, last)

    def far_sum(self, far_refs):
        return sum(ref[...].astype(F32) for ref in far_refs)

    def near_sums(self, x_ref, d_ref, acc_ref, first, start_ref=None):
        panels = [self.panel(x_ref, c) for c in range(self.per_device)]
        for r in range(self.per_device):
            value = None if start_ref is None else self.panel(start_ref, r)
            for c in range(self.per_device):
                offset = first + c - r
                if -REACH <= offset <= REACH:
                    term = dot_nt(panels[c], d_ref[r * SPAN + offset + REACH])
                    value = term if value is None else value + term
            acc_ref[:, r * self.size : (r + 1) * self.size] = value

    def halo_sums(self, below, x_ref, d_ref, acc_ref, start_ref):
        @pl.when(below)
        def _():
            self.near_sums(x_ref, d_ref, acc_ref, -self.per_device, start_ref)

        @pl.when(jnp.logical_not(below))
        def _():
            self.near_sums(x_ref, d_ref, acc_ref, self.per_device, start_ref)

    def far_halves(self, far_refs):
        return jnp.concatenate(halves(self.far_sum(far_refs)), axis=1)

    def next_panel(self, acc_ref, rb_ref, both, c):
        return (self.panel(acc_ref, c) + dot_nn(both, self.panel(rb_ref, c))).astype(BF16)

    def next_block(self, acc_ref, rb_ref, far_refs):
        both = self.far_halves(far_refs)
        panels = [self.next_panel(acc_ref, rb_ref, both, c) for c in range(self.per_device)]
        return jnp.concatenate(panels, axis=1)


def prepare_kernel(plan, index_ref, *refs):
    sources, refs = refs[:7], refs[7:]
    x_ref, g_ref, cb_ref, near_ref, offsets_ref = refs[:5]
    sends, (rows_ref, cols_ref, col_ref, coup_ref, sum_ref, sems) = refs[5:-6], refs[-6:]
    targets = (near_ref, offsets_ref, rows_ref, cols_ref, x_ref, col_ref, coup_ref)
    copies = [
        pltpu.make_async_copy(source, target, sems.at[i])
        for i, (source, target) in enumerate(zip(sources, targets))
    ]
    for copy in copies:
        copy.start()
    rank, size = plan.rank, plan.size
    cb_ref[...] = jnp.zeros_like(cb_ref)
    sum_ref[...] = jnp.zeros_like(sum_ref)
    for copy in copies:
        copy.wait()
    for c in range(plan.per_device):
        cb_ref[c * rank : (c + 1) * rank, c * size : (c + 1) * size] = col_ref[c]
    column = lax.broadcasted_iota(jnp.int32, (rank, plan.width), 1) // rank
    shift = 0 if plan.paired else plan.member(index_ref)
    for s in range(plan.slots):
        row = lax.rem(rows_ref[s], plan.block_clusters)
        step = lax.rem(lax.div(row, plan.per_device) - shift + plan.members, plan.members)
        place = step * plan.per_device + lax.rem(row, plan.per_device)
        if len(plan.hops) > 1:
            level = lax.div(rows_ref[s], plan.block_clusters)
            index = sum(jnp.where(level == i, index, 0) for i, index in enumerate(plan.set_of))
        else:
            index = 0
        where = (index, pl.ds(pl.multiple_of(place * rank, rank), rank), slice(None))
        tile = coup_ref[s].astype(F32)
        wide = jnp.where(column == cols_ref[s], jnp.concatenate([tile] * plan.per_device, axis=1), 0.0)
        sum_ref[where] = sum_ref[where] + wide
    for index in range(len(plan.hops)):
        g_ref[index] = jnp.concatenate(halves(sum_ref[index]), axis=1)
    plan.send_far(index_ref, x_ref[...], cb_ref, g_ref, sends)


def relay_kernel(plan, index_ref, keep_ref, message_ref, *out_refs):
    plan.relay_far(index_ref, keep_ref, message_ref, out_refs)


def first_own_kernel(plan, *refs):
    index_ref, rows_ref, offsets_ref, x_ref, near_ref, row_ref, tiles_ref = refs[:7]
    acc_ref, d_ref, rb_ref = refs[-3:]
    rank, size = plan.rank, plan.size
    for cell in range(plan.cells):
        d_ref[cell] = jnp.zeros(d_ref.shape[1:], d_ref.dtype)
    for s in range(plan.tiles):
        d_ref[rows_ref[s] * SPAN + offsets_ref[s] + REACH] = tiles_ref[s]
    rb_ref[...] = jnp.zeros_like(rb_ref)
    for c in range(plan.per_device):
        for start in (c * rank, plan.width + c * rank):
            rb_ref[start : start + rank, c * size : (c + 1) * size] = row_ref[c]
    plan.near_sums(x_ref, d_ref, acc_ref, 0)
    plan.halo_sums(lax.rem(index_ref[0], 2) == 1, near_ref, d_ref, acc_ref, acc_ref)


def own_kernel(plan, slot, *refs):
    index_ref, x_ref, near_ref, d_ref = refs[:4]
    acc_ref, krylov_ref, sem = refs[-3:]
    copy = pltpu.make_async_copy(x_ref, krylov_ref.at[slot], sem)
    copy.start()
    plan.near_sums(x_ref, d_ref, acc_ref, 0)
    plan.halo_sums(lax.rem(index_ref[0], 2) == 1, near_ref, d_ref, acc_ref, acc_ref)
    copy.wait()


def halo_kernel(plan, index_ref, acc_ref, over_ref, d_ref, *refs):
    plan.halo_sums(lax.rem(index_ref[0], 2) == 0, over_ref, d_ref, refs[-1], acc_ref)


def finish_kernel(plan, fars, *refs):
    index_ref, acc_ref, rb_ref, cb_ref, g_ref = refs[:5]
    far_refs, (x_ref, *sends) = refs[5 : 5 + fars], refs[5 + fars :]
    x = plan.next_block(acc_ref, rb_ref, far_refs)
    x_ref[...] = x
    plan.send_far(index_ref, x, cb_ref, g_ref, sends)


def last_kernel(plan, fars, slot, *refs):
    acc_ref, rb_ref = refs[:2]
    far_refs, (_, krylov_ref, x_ref, sem) = refs[2 : 2 + fars], refs[2 + fars :]
    both = plan.far_halves(far_refs)
    copies = []
    for c in range(plan.per_device):
        columns = pl.ds(c * plan.size, plan.size)
        x_ref[:, columns] = plan.next_panel(acc_ref, rb_ref, both, c)
        copies.append(
            pltpu.make_async_copy(x_ref.at[:, columns], krylov_ref.at[slot, :, columns], sem.at[c])
        )
        copies[-1].start()
    for copy in copies:
        copy.wait()


def call(kernel, name, ins, specs, outs, out_specs=None, scratch=(), aliases=None):
    spaces = {id(IN_VMEM): pltpu.VMEM, id(IN_HBM): pltpu.HBM}
    ins = [
        pltpu.with_memory_space_constraint(v, spaces[id(spec)]) if id(spec) in spaces else v
        for v, spec in zip(ins, specs)
    ]
    return pl.pallas_call(
        kernel,
        in_specs=list(specs),
        out_specs=out_specs or [IN_VMEM] * len(outs),
        out_shape=list(outs),
        scratch_shapes=list(scratch),
        input_output_aliases=aliases or {},
        compiler_params=pltpu.CompilerParams(vmem_limit_bytes=16 * 2**20),
        cost_estimate=pl.CostEstimate(flops=10**9, bytes_accessed=2**22, transcendentals=0),
        name=name,
    )(*ins)


def on_device(
    block, near_tiles, near_rows, near_offsets, col_basis, couplings, far_rows, far_cols, row_basis
):
    axes = ("loop", "far")
    plan = Plan(
        block.shape, near_tiles.shape, couplings.shape, lax.axis_size("far"), lax.axis_size("loop")
    )
    rhs, shard_len, width = plan.rhs, plan.shard_len, plan.width
    block_out = pltpu.VMEM((rhs, shard_len), BF16)
    acc_out = pltpu.VMEM((rhs, shard_len), F32)
    relay_out = pltpu.VMEM((rhs, width), BF16)
    krylov_out = jax.ShapeDtypeStruct((PRODUCTS, rhs, shard_len), BF16)
    if plan.paired:
        sends_out = [
            pltpu.VMEM((rhs, shard_len + 4 * width), BF16),
            pltpu.VMEM((rhs, 2 * width), F32),
        ]
    else:
        sends_out = [pltpu.VMEM((rhs, width), BF16)] * len(plan.routes)
    index = lax.axis_index(axes).astype(jnp.int32).reshape(1)

    def scratch_for(*arrays):
        return [
            pltpu.SMEM(v.shape, v.dtype) if v.dtype == jnp.int32 else pltpu.VMEM(v.shape, v.dtype)
            for v in arrays
        ]

    current, sends, krylov = block, None, None
    for product in range(PRODUCTS):
        if product == 0:
            ins = [near_rows, near_offsets, far_rows, far_cols, block, col_basis, couplings]
            matrix = (len(plan.hops), plan.members * width, 2 * width)
            current, coupled, col_wide, row_slots, offset_slots, *sends = call(
                functools.partial(prepare_kernel, plan),
                "prepare",
                [index, *ins],
                [IN_SMEM] + [IN_HBM] * 7,
                [
                    block_out,
                    pltpu.VMEM(matrix, BF16),
                    pltpu.VMEM((width, shard_len), BF16),
                    *scratch_for(near_rows, near_offsets),
                    *sends_out,
                ],
                [IN_VMEM] * 3 + [IN_SMEM] * 2 + [IN_VMEM] * len(sends_out),
                scratch=scratch_for(far_rows, far_cols, col_basis, couplings)
                + [pltpu.VMEM(matrix[:2] + (width,), F32), pltpu.SemaphoreType.DMA((7,))],
            )
        over = lax.ppermute(block if product == 0 else current, axes, plan.over)
        near = lax.ppermute(sends[0] if plan.paired else current, axes, plan.near)
        if plan.paired:
            sends = call(
                functools.partial(relay_kernel, plan),
                "relay",
                [index, sends[1], near],
                [IN_SMEM] + [IN_VMEM] * 2,
                [relay_out] * 2,
            )
            routes = plan.across
        else:
            routes = plan.routes
        fars = [lax.ppermute(s, axes, route) for s, route in zip(sends, routes)]
        after = sends if plan.paired else []
        if product == 0:
            ins = [index, row_slots, offset_slots, current, near, row_basis, near_tiles, *after]
            acc, dense, row_wide = call(
                functools.partial(first_own_kernel, plan),
                "first_own",
                ins,
                [IN_SMEM] * 3 + [IN_VMEM] * 2 + [PREFETCHED] * 2 + [ANYWHERE] * len(after),
                [
                    acc_out,
                    pltpu.VMEM((plan.cells, plan.size, plan.size), BF16),
                    pltpu.VMEM((2 * width, shard_len), BF16),
                ],
            )
        else:
            ins = [index, current, near, dense, *after] + ([krylov] if product > 1 else [])
            acc, krylov = call(
                functools.partial(own_kernel, plan, product - 1),
                "own",
                ins,
                [IN_SMEM] + [IN_VMEM] * 3 + [ANYWHERE] * (len(ins) - 4),
                [acc_out, krylov_out],
                [IN_VMEM, ANYWHERE],
                [pltpu.SemaphoreType.DMA],
                {len(ins) - 1: 1} if product > 1 else None,
            )
        (acc,) = call(
            functools.partial(halo_kernel, plan),
            "halo",
            [index, acc, over, dense],
            [IN_SMEM] + [IN_VMEM] * 3,
            [acc_out],
        )
        if product < PRODUCTS - 1:
            ins = [index, acc, row_wide, col_wide, coupled, *fars]
            current, *sends = call(
                functools.partial(finish_kernel, plan, len(fars)),
                "finish",
                ins,
                [IN_SMEM] + [IN_VMEM] * (len(ins) - 1),
                [block_out, *sends_out],
            )
        else:
            ins = [acc, row_wide, *fars, krylov]
            (krylov,) = call(
                functools.partial(last_kernel, plan, len(fars), product),
                "last",
                ins,
                [IN_VMEM] * (len(ins) - 1) + [ANYWHERE],
                [krylov_out],
                [ANYWHERE],
                [
                    pltpu.VMEM((rhs, shard_len), BF16),
                    pltpu.SemaphoreType.DMA((plan.per_device,)),
                ],
                {len(ins) - 1: 0},
            )
    return krylov


def solution(mesh):
    split = ("groups", "loop", "far")
    wide, narrow = P(split, None, None), P(split)
    in_specs = (P(None, split), wide, narrow, narrow, wide, wide, narrow, narrow, wide)
    return jax.shard_map(
        on_device, mesh=mesh, in_specs=in_specs, out_specs=P(None, None, split), check_vma=False
    )
```

```python
import functools

import jax
import jax.numpy as jnp
from jax import lax
from jax.experimental import pallas as pl
from jax.experimental.pallas import tpu as pltpu
from jax.sharding import PartitionSpec as P

PRODUCTS = 4
REACH = 4
LEVELS = 3
SPAN = 2 * REACH + 1

F32 = jnp.float32
BF16 = jnp.bfloat16
IN_VMEM = pl.BlockSpec(memory_space=pltpu.VMEM)
PREFETCHED = pl.BlockSpec(memory_space=pltpu.VMEM)
IN_SMEM = pl.BlockSpec(memory_space=pltpu.SMEM)
IN_HBM = pl.BlockSpec(memory_space=pltpu.HBM)
ANYWHERE = pl.BlockSpec(memory_space=pl.ANY)


def dot_nt(a, b):
    return lax.dot_general(a, b, (((1,), (1,)), ((), ())), preferred_element_type=F32)


def dot_nn(a, b):
    return lax.dot_general(a, b, (((1,), (0,)), ((), ())), preferred_element_type=F32)


def halves(value):
    upper = value.astype(BF16)
    return upper, (value - upper.astype(F32)).astype(BF16)


class Plan:
    def __init__(self, block_shape, tile_shape, coupling_shape, members, loop_size):
        self.rhs, self.shard_len = block_shape
        self.tiles, self.size, _ = tile_shape
        self.slots, self.rank, _ = coupling_shape
        self.members, self.loop_size = members, loop_size
        self.per_device = self.shard_len // self.size
        self.width = self.per_device * self.rank
        self.cells = self.per_device * SPAN
        self.block_clusters = self.per_device * members
        distances = [d % loop_size for d in (2, loop_size - 2, loop_size // 2)]
        self.hops = sorted(set(distances))
        self.set_of = [self.hops.index(d) for d in distances]
        self.paired = len(self.hops) == 1 and 2 * self.hops[0] == loop_size and members == 4
        devices = members * loop_size
        self.near = [(i, i ^ 1) for i in range(devices)]
        self.over = [(i, (i + 1 if i % 2 else i - 1) % devices) for i in range(devices)]
        places = [(l, m) for l in range(loop_size) for m in range(members)]
        self.across = [
            [
                (l * members + m, (l + self.hops[0]) % loop_size * members + self.far_target(m, other))
                for l, m in places
            ]
            for other in (0, 1)
        ]
        self.routes = [
            [(l * members + m, (l + hop) % loop_size * members + (m + step) % members) for l, m in places]
            for hop in self.hops
            for step in range(members)
        ]

    def far_target(self, member, other):
        pair, core = divmod(member, 2)
        return 2 * (pair ^ core) + (pair ^ other)

    def panel(self, ref, c):
        return ref[:, c * self.size : (c + 1) * self.size]

    def member(self, index_ref):
        return lax.rem(index_ref[0], self.members)

    def send_far(self, index_ref, x, cb_ref, g_ref, out_refs):
        coeffs = dot_nt(x, cb_ref[...]).astype(BF16)
        twice = jnp.concatenate([coeffs, coeffs], axis=1)
        totals = [dot_nt(twice, g_ref[index]) for index in range(len(self.hops))]
        if not self.paired:
            for i, out_ref in enumerate(out_refs):
                step = i % self.members * self.width
                out_ref[...] = totals[i // self.members][:, step : step + self.width].astype(BF16)
            return
        message_ref, keep_ref = out_refs
        (total,) = totals
        member = self.member(index_ref)
        second = lax.rem(member, 2) != lax.div(member, 2)
        first, last = total[:, : 2 * self.width], total[:, 2 * self.width :]
        keep_ref[...] = jnp.where(second, last, first)
        upper, lower = halves(jnp.where(second, first, last))
        message_ref[:, : self.shard_len] = x
        message_ref[:, self.shard_len : self.shard_len + 2 * self.width] = upper
        message_ref[:, self.shard_len + 2 * self.width :] = lower

    def relay_far(self, index_ref, keep_ref, message_ref, out_refs):
        upper = message_ref[:, self.shard_len : self.shard_len + 2 * self.width].astype(F32)
        lower = message_ref[:, self.shard_len + 2 * self.width :].astype(F32)
        total = (keep_ref[...] + (upper + lower)).astype(BF16)
        second = self.member(index_ref) >= 2
        first, last = total[:, : self.width], total[:, self.width :]
        out_refs[0][...] = jnp.where(second, last, first)
        out_refs[1][...] = jnp.where(second, first, last)

    def far_sum(self, far_refs):
        return sum(ref[...].astype(F32) for ref in far_refs)

    def near_sums(self, x_ref, d_ref, acc_ref, first, start_ref=None):
        panels = [self.panel(x_ref, c) for c in range(self.per_device)]
        for r in range(self.per_device):
            value = None if start_ref is None else self.panel(start_ref, r)
            for c in range(self.per_device):
                offset = first + c - r
                if -REACH <= offset <= REACH:
                    term = dot_nt(panels[c], d_ref[r * SPAN + offset + REACH])
                    value = term if value is None else value + term
            acc_ref[:, r * self.size : (r + 1) * self.size] = value

    def halo_sums(self, below, x_ref, d_ref, acc_ref, start_ref):
        @pl.when(below)
        def _():
            self.near_sums(x_ref, d_ref, acc_ref, -self.per_device, start_ref)

        @pl.when(jnp.logical_not(below))
        def _():
            self.near_sums(x_ref, d_ref, acc_ref, self.per_device, start_ref)

    def far_halves(self, far_refs):
        return jnp.concatenate(halves(self.far_sum(far_refs)), axis=1)

    def next_panel(self, acc_ref, rb_ref, both, c):
        return (self.panel(acc_ref, c) + dot_nn(both, self.panel(rb_ref, c))).astype(BF16)

    def next_block(self, acc_ref, rb_ref, far_refs):
        both = self.far_halves(far_refs)
        panels = [self.next_panel(acc_ref, rb_ref, both, c) for c in range(self.per_device)]
        return jnp.concatenate(panels, axis=1)


def prepare_kernel(plan, index_ref, *refs):
    sources, refs = refs[:7], refs[7:]
    x_ref, g_ref, cb_ref, near_ref, offsets_ref = refs[:5]
    sends, (rows_ref, cols_ref, col_ref, coup_ref, sum_ref, sems) = refs[5:-6], refs[-6:]
    targets = (near_ref, offsets_ref, rows_ref, cols_ref, x_ref, col_ref, coup_ref)
    copies = [
        pltpu.make_async_copy(source, target, sems.at[i])
        for i, (source, target) in enumerate(zip(sources, targets))
    ]
    for copy in copies:
        copy.start()
    rank, size = plan.rank, plan.size
    cb_ref[...] = jnp.zeros_like(cb_ref)
    sum_ref[...] = jnp.zeros_like(sum_ref)
    for copy in copies:
        copy.wait()
    for c in range(plan.per_device):
        cb_ref[c * rank : (c + 1) * rank, c * size : (c + 1) * size] = col_ref[c]
    column = lax.broadcasted_iota(jnp.int32, (rank, plan.width), 1) // rank
    shift = 0 if plan.paired else plan.member(index_ref)
    for s in range(plan.slots):
        row = lax.rem(rows_ref[s], plan.block_clusters)
        step = lax.rem(lax.div(row, plan.per_device) - shift + plan.members, plan.members)
        place = step * plan.per_device + lax.rem(row, plan.per_device)
        if len(plan.hops) > 1:
            level = lax.div(rows_ref[s], plan.block_clusters)
            index = sum(jnp.where(level == i, index, 0) for i, index in enumerate(plan.set_of))
        else:
            index = 0
        where = (index, pl.ds(pl.multiple_of(place * rank, rank), rank), slice(None))
        tile = coup_ref[s].astype(F32)
        wide = jnp.where(column == cols_ref[s], jnp.concatenate([tile] * plan.per_device, axis=1), 0.0)
        sum_ref[where] = sum_ref[where] + wide
    for index in range(len(plan.hops)):
        g_ref[index] = jnp.concatenate(halves(sum_ref[index]), axis=1)
    plan.send_far(index_ref, x_ref[...], cb_ref, g_ref, sends)


def relay_kernel(plan, index_ref, keep_ref, message_ref, *out_refs):
    plan.relay_far(index_ref, keep_ref, message_ref, out_refs)


def first_own_kernel(plan, *refs):
    index_ref, rows_ref, offsets_ref, x_ref, near_ref, row_ref, tiles_ref = refs[:7]
    acc_ref, d_ref, rb_ref = refs[-3:]
    rank, size = plan.rank, plan.size
    for cell in range(plan.cells):
        d_ref[cell] = jnp.zeros(d_ref.shape[1:], d_ref.dtype)
    for s in range(plan.tiles):
        d_ref[rows_ref[s] * SPAN + offsets_ref[s] + REACH] = tiles_ref[s]
    rb_ref[...] = jnp.zeros_like(rb_ref)
    for c in range(plan.per_device):
        for start in (c * rank, plan.width + c * rank):
            rb_ref[start : start + rank, c * size : (c + 1) * size] = row_ref[c]
    plan.near_sums(x_ref, d_ref, acc_ref, 0)
    plan.halo_sums(lax.rem(index_ref[0], 2) == 1, near_ref, d_ref, acc_ref, acc_ref)


def own_kernel(plan, slot, *refs):
    index_ref, x_ref, near_ref, d_ref = refs[:4]
    acc_ref, krylov_ref, sem = refs[-3:]
    copy = pltpu.make_async_copy(x_ref, krylov_ref.at[slot], sem)
    copy.start()
    plan.near_sums(x_ref, d_ref, acc_ref, 0)
    plan.halo_sums(lax.rem(index_ref[0], 2) == 1, near_ref, d_ref, acc_ref, acc_ref)
    copy.wait()


def halo_kernel(plan, index_ref, acc_ref, over_ref, d_ref, *refs):
    plan.halo_sums(lax.rem(index_ref[0], 2) == 0, over_ref, d_ref, refs[-1], acc_ref)


def finish_kernel(plan, fars, *refs):
    index_ref, acc_ref, rb_ref, cb_ref, g_ref = refs[:5]
    far_refs, (x_ref, *sends) = refs[5 : 5 + fars], refs[5 + fars :]
    x = plan.next_block(acc_ref, rb_ref, far_refs)
    x_ref[...] = x
    plan.send_far(index_ref, x, cb_ref, g_ref, sends)


def last_kernel(plan, fars, slot, *refs):
    acc_ref, rb_ref = refs[:2]
    far_refs, (_, krylov_ref, x_ref, sem) = refs[2 : 2 + fars], refs[2 + fars :]
    both = plan.far_halves(far_refs)
    copies = []
    for c in range(plan.per_device):
        columns = pl.ds(c * plan.size, plan.size)
        x_ref[:, columns] = plan.next_panel(acc_ref, rb_ref, both, c)
        copies.append(
            pltpu.make_async_copy(x_ref.at[:, columns], krylov_ref.at[slot, :, columns], sem.at[c])
        )
        copies[-1].start()
    for copy in copies:
        copy.wait()


def call(kernel, name, ins, specs, outs, out_specs=None, scratch=(), aliases=None):
    spaces = {id(IN_VMEM): pltpu.VMEM, id(IN_HBM): pltpu.HBM}
    ins = [
        pltpu.with_memory_space_constraint(v, spaces[id(spec)]) if id(spec) in spaces else v
        for v, spec in zip(ins, specs)
    ]
    return pl.pallas_call(
        kernel,
        in_specs=list(specs),
        out_specs=out_specs or [IN_VMEM] * len(outs),
        out_shape=list(outs),
        scratch_shapes=list(scratch),
        input_output_aliases=aliases or {},
        compiler_params=pltpu.CompilerParams(vmem_limit_bytes=16 * 2**20),
        cost_estimate=pl.CostEstimate(flops=10**9, bytes_accessed=2**22, transcendentals=0),
        name=name,
    )(*ins)


def on_device(
    block, near_tiles, near_rows, near_offsets, col_basis, couplings, far_rows, far_cols, row_basis
):
    axes = ("loop", "far")
    plan = Plan(
        block.shape, near_tiles.shape, couplings.shape, lax.axis_size("far"), lax.axis_size("loop")
    )
    rhs, shard_len, width = plan.rhs, plan.shard_len, plan.width
    block_out = pltpu.VMEM((rhs, shard_len), BF16)
    acc_out = pltpu.VMEM((rhs, shard_len), F32)
    relay_out = pltpu.VMEM((rhs, width), BF16)
    krylov_out = jax.ShapeDtypeStruct((PRODUCTS, rhs, shard_len), BF16)
    if plan.paired:
        sends_out = [
            pltpu.VMEM((rhs, shard_len + 4 * width), BF16),
            pltpu.VMEM((rhs, 2 * width), F32),
        ]
    else:
        sends_out = [pltpu.VMEM((rhs, width), BF16)] * len(plan.routes)
    index = lax.axis_index(axes).astype(jnp.int32).reshape(1)

    def scratch_for(*arrays):
        return [
            pltpu.SMEM(v.shape, v.dtype) if v.dtype == jnp.int32 else pltpu.VMEM(v.shape, v.dtype)
            for v in arrays
        ]

    current, sends, krylov = block, None, None
    for product in range(PRODUCTS):
        if product == 0:
            ins = [near_rows, near_offsets, far_rows, far_cols, block, col_basis, couplings]
            matrix = (len(plan.hops), plan.members * width, 2 * width)
            current, coupled, col_wide, row_slots, offset_slots, *sends = call(
                functools.partial(prepare_kernel, plan),
                "prepare",
                [index, *ins],
                [IN_SMEM] + [IN_HBM] * 7,
                [
                    block_out,
                    pltpu.VMEM(matrix, BF16),
                    pltpu.VMEM((width, shard_len), BF16),
                    *scratch_for(near_rows, near_offsets),
                    *sends_out,
                ],
                [IN_VMEM] * 3 + [IN_SMEM] * 2 + [IN_VMEM] * len(sends_out),
                scratch=scratch_for(far_rows, far_cols, col_basis, couplings)
                + [pltpu.VMEM(matrix[:2] + (width,), F32), pltpu.SemaphoreType.DMA((7,))],
            )
        over = lax.ppermute(block if product == 0 else current, axes, plan.over)
        near = lax.ppermute(sends[0] if plan.paired else current, axes, plan.near)
        if plan.paired:
            sends = call(
                functools.partial(relay_kernel, plan),
                "relay",
                [index, sends[1], near],
                [IN_SMEM] + [IN_VMEM] * 2,
                [relay_out] * 2,
            )
            routes = plan.across
        else:
            routes = plan.routes
        fars = [lax.ppermute(s, axes, route) for s, route in zip(sends, routes)]
        after = sends if plan.paired else []
        if product == 0:
            ins = [index, row_slots, offset_slots, current, near, row_basis, near_tiles, *after]
            acc, dense, row_wide = call(
                functools.partial(first_own_kernel, plan),
                "first_own",
                ins,
                [IN_SMEM] * 3 + [IN_VMEM] * 2 + [PREFETCHED] * 2 + [ANYWHERE] * len(after),
                [
                    acc_out,
                    pltpu.VMEM((plan.cells, plan.size, plan.size), BF16),
                    pltpu.VMEM((2 * width, shard_len), BF16),
                ],
            )
        else:
            ins = [index, current, near, dense, *after] + ([krylov] if product > 1 else [])
            acc, krylov = call(
                functools.partial(own_kernel, plan, product - 1),
                "own",
                ins,
                [IN_SMEM] + [IN_VMEM] * 3 + [ANYWHERE] * (len(ins) - 4),
                [acc_out, krylov_out],
                [IN_VMEM, ANYWHERE],
                [pltpu.SemaphoreType.DMA],
                {len(ins) - 1: 1} if product > 1 else None,
            )
        (acc,) = call(
            functools.partial(halo_kernel, plan),
            "halo",
            [index, acc, over, dense],
            [IN_SMEM] + [IN_VMEM] * 3,
            [acc_out],
        )
        if product < PRODUCTS - 1:
            ins = [index, acc, row_wide, col_wide, coupled, *fars]
            current, *sends = call(
                functools.partial(finish_kernel, plan, len(fars)),
                "finish",
                ins,
                [IN_SMEM] + [IN_VMEM] * (len(ins) - 1),
                [block_out, *sends_out],
            )
        else:
            ins = [acc, row_wide, *fars, krylov]
            (krylov,) = call(
                functools.partial(last_kernel, plan, len(fars), product),
                "last",
                ins,
                [IN_VMEM] * (len(ins) - 1) + [ANYWHERE],
                [krylov_out],
                [ANYWHERE],
                [
                    pltpu.VMEM((rhs, shard_len), BF16),
                    pltpu.SemaphoreType.DMA((plan.per_device,)),
                ],
                {len(ins) - 1: 0},
            )
    return krylov


def solution(mesh):
    split = ("groups", "loop", "far")
    wide, narrow = P(split, None, None), P(split)
    in_specs = (P(None, split), wide, narrow, narrow, wide, wide, narrow, narrow, wide)
    return jax.shard_map(
        on_device, mesh=mesh, in_specs=in_specs, out_specs=P(None, None, split), check_vma=False
    )
```

```python
import functools

import jax
import jax.numpy as jnp
from jax import lax
from jax.experimental import pallas as pl
from jax.experimental.pallas import tpu as pltpu
from jax.sharding import PartitionSpec as P

PRODUCTS = 4
REACH = 4
LEVELS = 3
SPAN = 2 * REACH + 1

F32 = jnp.float32
BF16 = jnp.bfloat16
IN_VMEM = pl.BlockSpec(memory_space=pltpu.VMEM)
PREFETCHED = pl.BlockSpec(memory_space=pltpu.VMEM)
IN_SMEM = pl.BlockSpec(memory_space=pltpu.SMEM)
IN_HBM = pl.BlockSpec(memory_space=pltpu.HBM)
ANYWHERE = pl.BlockSpec(memory_space=pl.ANY)


def dot_nt(a, b):
    return lax.dot_general(a, b, (((1,), (1,)), ((), ())), preferred_element_type=F32)


def dot_nn(a, b):
    return lax.dot_general(a, b, (((1,), (0,)), ((), ())), preferred_element_type=F32)


def halves(value):
    upper = value.astype(BF16)
    return upper, (value - upper.astype(F32)).astype(BF16)


class Plan:
    def __init__(self, block_shape, tile_shape, coupling_shape, members, loop_size):
        self.rhs, self.shard_len = block_shape
        self.tiles, self.size, _ = tile_shape
        self.slots, self.rank, _ = coupling_shape
        self.members, self.loop_size = members, loop_size
        self.per_device = self.shard_len // self.size
        self.width = self.per_device * self.rank
        self.cells = self.per_device * SPAN
        self.block_clusters = self.per_device * members
        distances = [d % loop_size for d in (2, loop_size - 2, loop_size // 2)]
        self.hops = sorted(set(distances))
        self.set_of = [self.hops.index(d) for d in distances]
        self.paired = len(self.hops) == 1 and 2 * self.hops[0] == loop_size and members == 4
        devices = members * loop_size
        self.near = [(i, i ^ 1) for i in range(devices)]
        self.over = [(i, (i + 1 if i % 2 else i - 1) % devices) for i in range(devices)]
        places = [(l, m) for l in range(loop_size) for m in range(members)]
        self.across = [
            [
                (l * members + m, (l + self.hops[0]) % loop_size * members + self.far_target(m, other))
                for l, m in places
            ]
            for other in (1, 0)
        ]
        self.routes = [
            [(l * members + m, (l + hop) % loop_size * members + (m + step) % members) for l, m in places]
            for hop in self.hops
            for step in range(members)
        ]

    def far_target(self, member, other):
        pair, core = divmod(member, 2)
        return 2 * (pair ^ core) + (pair ^ other)

    def panel(self, ref, c):
        return ref[:, c * self.size : (c + 1) * self.size]

    def member(self, index_ref):
        return lax.rem(index_ref[0], self.members)

    def send_far(self, index_ref, x, cb_ref, g_ref, out_refs):
        coeffs = dot_nt(x, cb_ref[...]).astype(BF16)
        twice = jnp.concatenate([coeffs, coeffs], axis=1)
        totals = [dot_nt(twice, g_ref[index]) for index in range(len(self.hops))]
        if not self.paired:
            for i, out_ref in enumerate(out_refs):
                step = i % self.members * self.width
                out_ref[...] = totals[i // self.members][:, step : step + self.width].astype(BF16)
            return
        message_ref, keep_ref = out_refs
        (total,) = totals
        member = self.member(index_ref)
        second = lax.rem(member, 2) != lax.div(member, 2)
        first, last = total[:, : 2 * self.width], total[:, 2 * self.width :]
        keep_ref[...] = jnp.where(second, last, first)
        upper, lower = halves(jnp.where(second, first, last))
        message_ref[:, : self.shard_len] = x
        message_ref[:, self.shard_len : self.shard_len + 2 * self.width] = upper
        message_ref[:, self.shard_len + 2 * self.width :] = lower

    def relay_far(self, index_ref, keep_ref, message_ref, out_refs):
        upper = message_ref[:, self.shard_len : self.shard_len + 2 * self.width].astype(F32)
        lower = message_ref[:, self.shard_len + 2 * self.width :].astype(F32)
        total = (keep_ref[...] + (upper + lower)).astype(BF16)
        second = self.member(index_ref) >= 2
        first, last = total[:, : self.width], total[:, self.width :]
        out_refs[0][...] = jnp.where(second, first, last)
        out_refs[1][...] = jnp.where(second, last, first)

    def far_sum(self, far_refs):
        return sum(ref[...].astype(F32) for ref in far_refs)

    def near_sums(self, x_ref, d_ref, acc_ref, first, start_ref=None):
        panels = [self.panel(x_ref, c) for c in range(self.per_device)]
        for r in range(self.per_device):
            value = None if start_ref is None else self.panel(start_ref, r)
            for c in range(self.per_device):
                offset = first + c - r
                if -REACH <= offset <= REACH:
                    term = dot_nt(panels[c], d_ref[r * SPAN + offset + REACH])
                    value = term if value is None else value + term
            acc_ref[:, r * self.size : (r + 1) * self.size] = value

    def halo_sums(self, below, x_ref, d_ref, acc_ref, start_ref):
        @pl.when(below)
        def _():
            self.near_sums(x_ref, d_ref, acc_ref, -self.per_device, start_ref)

        @pl.when(jnp.logical_not(below))
        def _():
            self.near_sums(x_ref, d_ref, acc_ref, self.per_device, start_ref)

    def far_halves(self, far_refs):
        return jnp.concatenate(halves(self.far_sum(far_refs)), axis=1)

    def next_panel(self, acc_ref, rb_ref, both, c):
        return (self.panel(acc_ref, c) + dot_nn(both, self.panel(rb_ref, c))).astype(BF16)

    def next_block(self, acc_ref, rb_ref, far_refs):
        both = self.far_halves(far_refs)
        panels = [self.next_panel(acc_ref, rb_ref, both, c) for c in range(self.per_device)]
        return jnp.concatenate(panels, axis=1)


def prepare_kernel(plan, index_ref, *refs):
    sources, refs = refs[:7], refs[7:]
    x_ref, g_ref, cb_ref, near_ref, offsets_ref = refs[:5]
    sends, (rows_ref, cols_ref, col_ref, coup_ref, sum_ref, sems) = refs[5:-6], refs[-6:]
    targets = (near_ref, offsets_ref, rows_ref, cols_ref, x_ref, col_ref, coup_ref)
    copies = [
        pltpu.make_async_copy(source, target, sems.at[i])
        for i, (source, target) in enumerate(zip(sources, targets))
    ]
    for copy in copies:
        copy.start()
    rank, size = plan.rank, plan.size
    cb_ref[...] = jnp.zeros_like(cb_ref)
    sum_ref[...] = jnp.zeros_like(sum_ref)
    for copy in copies:
        copy.wait()
    for c in range(plan.per_device):
        cb_ref[c * rank : (c + 1) * rank, c * size : (c + 1) * size] = col_ref[c]
    column = lax.broadcasted_iota(jnp.int32, (rank, plan.width), 1) // rank
    shift = 0 if plan.paired else plan.member(index_ref)
    for s in range(plan.slots):
        row = lax.rem(rows_ref[s], plan.block_clusters)
        step = lax.rem(lax.div(row, plan.per_device) - shift + plan.members, plan.members)
        place = step * plan.per_device + lax.rem(row, plan.per_device)
        if len(plan.hops) > 1:
            level = lax.div(rows_ref[s], plan.block_clusters)
            index = sum(jnp.where(level == i, index, 0) for i, index in enumerate(plan.set_of))
        else:
            index = 0
        where = (index, pl.ds(pl.multiple_of(place * rank, rank), rank), slice(None))
        tile = coup_ref[s].astype(F32)
        wide = jnp.where(column == cols_ref[s], jnp.concatenate([tile] * plan.per_device, axis=1), 0.0)
        sum_ref[where] = sum_ref[where] + wide
    for index in range(len(plan.hops)):
        g_ref[index] = jnp.concatenate(halves(sum_ref[index]), axis=1)
    plan.send_far(index_ref, x_ref[...], cb_ref, g_ref, sends)


def relay_kernel(plan, index_ref, keep_ref, message_ref, *out_refs):
    plan.relay_far(index_ref, keep_ref, message_ref, out_refs)


def first_own_kernel(plan, *refs):
    index_ref, rows_ref, offsets_ref, x_ref, near_ref, row_ref, tiles_ref = refs[:7]
    acc_ref, d_ref, rb_ref = refs[-3:]
    rank, size = plan.rank, plan.size
    for cell in range(plan.cells):
        d_ref[cell] = jnp.zeros(d_ref.shape[1:], d_ref.dtype)
    for s in range(plan.tiles):
        d_ref[rows_ref[s] * SPAN + offsets_ref[s] + REACH] = tiles_ref[s]
    rb_ref[...] = jnp.zeros_like(rb_ref)
    for c in range(plan.per_device):
        for start in (c * rank, plan.width + c * rank):
            rb_ref[start : start + rank, c * size : (c + 1) * size] = row_ref[c]
    plan.near_sums(x_ref, d_ref, acc_ref, 0)
    plan.halo_sums(lax.rem(index_ref[0], 2) == 1, near_ref, d_ref, acc_ref, acc_ref)


def own_kernel(plan, slot, *refs):
    index_ref, x_ref, near_ref, d_ref = refs[:4]
    acc_ref, krylov_ref, sem = refs[-3:]
    copy = pltpu.make_async_copy(x_ref, krylov_ref.at[slot], sem)
    copy.start()
    plan.near_sums(x_ref, d_ref, acc_ref, 0)
    plan.halo_sums(lax.rem(index_ref[0], 2) == 1, near_ref, d_ref, acc_ref, acc_ref)
    copy.wait()


def halo_kernel(plan, index_ref, acc_ref, over_ref, d_ref, *refs):
    plan.halo_sums(lax.rem(index_ref[0], 2) == 0, over_ref, d_ref, refs[-1], acc_ref)


def finish_kernel(plan, fars, *refs):
    index_ref, acc_ref, rb_ref, cb_ref, g_ref = refs[:5]
    far_refs, (x_ref, *sends) = refs[5 : 5 + fars], refs[5 + fars :]
    x = plan.next_block(acc_ref, rb_ref, far_refs)
    x_ref[...] = x
    plan.send_far(index_ref, x, cb_ref, g_ref, sends)


def last_kernel(plan, fars, slot, *refs):
    acc_ref, rb_ref = refs[:2]
    far_refs, (_, krylov_ref, x_ref, sem) = refs[2 : 2 + fars], refs[2 + fars :]
    both = plan.far_halves(far_refs)
    copies = []
    for c in range(plan.per_device):
        columns = pl.ds(c * plan.size, plan.size)
        x_ref[:, columns] = plan.next_panel(acc_ref, rb_ref, both, c)
        copies.append(
            pltpu.make_async_copy(x_ref.at[:, columns], krylov_ref.at[slot, :, columns], sem.at[c])
        )
        copies[-1].start()
    for copy in copies:
        copy.wait()


def call(kernel, name, ins, specs, outs, out_specs=None, scratch=(), aliases=None):
    spaces = {id(IN_VMEM): pltpu.VMEM, id(IN_HBM): pltpu.HBM}
    ins = [
        pltpu.with_memory_space_constraint(v, spaces[id(spec)]) if id(spec) in spaces else v
        for v, spec in zip(ins, specs)
    ]
    return pl.pallas_call(
        kernel,
        in_specs=list(specs),
        out_specs=out_specs or [IN_VMEM] * len(outs),
        out_shape=list(outs),
        scratch_shapes=list(scratch),
        input_output_aliases=aliases or {},
        compiler_params=pltpu.CompilerParams(vmem_limit_bytes=16 * 2**20),
        cost_estimate=pl.CostEstimate(flops=10**9, bytes_accessed=2**22, transcendentals=0),
        name=name,
    )(*ins)


def on_device(
    block, near_tiles, near_rows, near_offsets, col_basis, couplings, far_rows, far_cols, row_basis
):
    axes = ("loop", "far")
    plan = Plan(
        block.shape, near_tiles.shape, couplings.shape, lax.axis_size("far"), lax.axis_size("loop")
    )
    rhs, shard_len, width = plan.rhs, plan.shard_len, plan.width
    block_out = pltpu.VMEM((rhs, shard_len), BF16)
    acc_out = pltpu.VMEM((rhs, shard_len), F32)
    relay_out = pltpu.VMEM((rhs, width), BF16)
    krylov_out = jax.ShapeDtypeStruct((PRODUCTS, rhs, shard_len), BF16)
    if plan.paired:
        sends_out = [
            pltpu.VMEM((rhs, shard_len + 4 * width), BF16),
            pltpu.VMEM((rhs, 2 * width), F32),
        ]
    else:
        sends_out = [pltpu.VMEM((rhs, width), BF16)] * len(plan.routes)
    index = lax.axis_index(axes).astype(jnp.int32).reshape(1)

    def scratch_for(*arrays):
        return [
            pltpu.SMEM(v.shape, v.dtype) if v.dtype == jnp.int32 else pltpu.VMEM(v.shape, v.dtype)
            for v in arrays
        ]

    current, sends, krylov = block, None, None
    for product in range(PRODUCTS):
        if product == 0:
            ins = [near_rows, near_offsets, far_rows, far_cols, block, col_basis, couplings]
            matrix = (len(plan.hops), plan.members * width, 2 * width)
            current, coupled, col_wide, row_slots, offset_slots, *sends = call(
                functools.partial(prepare_kernel, plan),
                "prepare",
                [index, *ins],
                [IN_SMEM] + [IN_HBM] * 7,
                [
                    block_out,
                    pltpu.VMEM(matrix, BF16),
                    pltpu.VMEM((width, shard_len), BF16),
                    *scratch_for(near_rows, near_offsets),
                    *sends_out,
                ],
                [IN_VMEM] * 3 + [IN_SMEM] * 2 + [IN_VMEM] * len(sends_out),
                scratch=scratch_for(far_rows, far_cols, col_basis, couplings)
                + [pltpu.VMEM(matrix[:2] + (width,), F32), pltpu.SemaphoreType.DMA((7,))],
            )
        over = lax.ppermute(block if product == 0 else current, axes, plan.over)
        near = lax.ppermute(sends[0] if plan.paired else current, axes, plan.near)
        if plan.paired:
            sends = call(
                functools.partial(relay_kernel, plan),
                "relay",
                [index, sends[1], near],
                [IN_SMEM] + [IN_VMEM] * 2,
                [relay_out] * 2,
            )
            routes = plan.across
        else:
            routes = plan.routes
        fars = [lax.ppermute(s, axes, route) for s, route in zip(sends, routes)]
        after = sends if plan.paired else []
        if product == 0:
            ins = [index, row_slots, offset_slots, current, near, row_basis, near_tiles, *after]
            acc, dense, row_wide = call(
                functools.partial(first_own_kernel, plan),
                "first_own",
                ins,
                [IN_SMEM] * 3 + [IN_VMEM] * 2 + [PREFETCHED] * 2 + [ANYWHERE] * len(after),
                [
                    acc_out,
                    pltpu.VMEM((plan.cells, plan.size, plan.size), BF16),
                    pltpu.VMEM((2 * width, shard_len), BF16),
                ],
            )
        else:
            ins = [index, current, near, dense, *after] + ([krylov] if product > 1 else [])
            acc, krylov = call(
                functools.partial(own_kernel, plan, product - 1),
                "own",
                ins,
                [IN_SMEM] + [IN_VMEM] * 3 + [ANYWHERE] * (len(ins) - 4),
                [acc_out, krylov_out],
                [IN_VMEM, ANYWHERE],
                [pltpu.SemaphoreType.DMA],
                {len(ins) - 1: 1} if product > 1 else None,
            )
        (acc,) = call(
            functools.partial(halo_kernel, plan),
            "halo",
            [index, acc, over, dense],
            [IN_SMEM] + [IN_VMEM] * 3,
            [acc_out],
        )
        if product < PRODUCTS - 1:
            ins = [index, acc, row_wide, col_wide, coupled, *fars]
            current, *sends = call(
                functools.partial(finish_kernel, plan, len(fars)),
                "finish",
                ins,
                [IN_SMEM] + [IN_VMEM] * (len(ins) - 1),
                [block_out, *sends_out],
            )
        else:
            ins = [acc, row_wide, *fars, krylov]
            (krylov,) = call(
                functools.partial(last_kernel, plan, len(fars), product),
                "last",
                ins,
                [IN_VMEM] * (len(ins) - 1) + [ANYWHERE],
                [krylov_out],
                [ANYWHERE],
                [
                    pltpu.VMEM((rhs, shard_len), BF16),
                    pltpu.SemaphoreType.DMA((plan.per_device,)),
                ],
                {len(ins) - 1: 0},
            )
    return krylov


def solution(mesh):
    split = ("groups", "loop", "far")
    wide, narrow = P(split, None, None), P(split)
    in_specs = (P(None, split), wide, narrow, narrow, wide, wide, narrow, narrow, wide)
    return jax.shard_map(
        on_device, mesh=mesh, in_specs=in_specs, out_specs=P(None, None, split), check_vma=False
    )
```

```python
import functools

import jax
import jax.numpy as jnp
from jax import lax
from jax.experimental import pallas as pl
from jax.experimental.pallas import tpu as pltpu
from jax.sharding import PartitionSpec as P

PRODUCTS = 4
REACH = 4
LEVELS = 3
SPAN = 2 * REACH + 1

F32 = jnp.float32
BF16 = jnp.bfloat16
IN_VMEM = pl.BlockSpec(memory_space=pltpu.VMEM)
PREFETCHED = pl.BlockSpec(memory_space=pltpu.VMEM)
IN_SMEM = pl.BlockSpec(memory_space=pltpu.SMEM)
IN_HBM = pl.BlockSpec(memory_space=pltpu.HBM)
ANYWHERE = pl.BlockSpec(memory_space=pl.ANY)


def dot_nt(a, b):
    return lax.dot_general(a, b, (((1,), (1,)), ((), ())), preferred_element_type=F32)


def dot_nn(a, b):
    return lax.dot_general(a, b, (((1,), (0,)), ((), ())), preferred_element_type=F32)


def halves(value):
    upper = value.astype(BF16)
    return upper, (value - upper.astype(F32)).astype(BF16)


class Plan:
    def __init__(self, block_shape, tile_shape, coupling_shape, members, loop_size):
        self.rhs, self.shard_len = block_shape
        self.tiles, self.size, _ = tile_shape
        self.slots, self.rank, _ = coupling_shape
        self.members, self.loop_size = members, loop_size
        self.per_device = self.shard_len // self.size
        self.width = self.per_device * self.rank
        self.cells = self.per_device * SPAN
        self.block_clusters = self.per_device * members
        distances = [d % loop_size for d in (2, loop_size - 2, loop_size // 2)]
        self.hops = sorted(set(distances))
        self.set_of = [self.hops.index(d) for d in distances]
        self.paired = len(self.hops) == 1 and 2 * self.hops[0] == loop_size and members == 4
        devices = members * loop_size
        self.near = [(i, i ^ 1) for i in range(devices)]
        self.over = [(i, (i + 1 if i % 2 else i - 1) % devices) for i in range(devices)]
        places = [(l, m) for l in range(loop_size) for m in range(members)]
        self.across = [
            [
                (l * members + m, (l + self.hops[0]) % loop_size * members + (m ^ other))
                for l, m in places
            ]
            for other in (2, 0)
        ]
        self.routes = [
            [(l * members + m, (l + hop) % loop_size * members + (m + step) % members) for l, m in places]
            for hop in self.hops
            for step in range(members)
        ]

    def panel(self, ref, c):
        return ref[:, c * self.size : (c + 1) * self.size]

    def member(self, index_ref):
        return lax.rem(index_ref[0], self.members)

    def send_far(self, index_ref, x, cb_ref, g_ref, out_refs):
        coeffs = dot_nt(x, cb_ref[...]).astype(BF16)
        twice = jnp.concatenate([coeffs, coeffs], axis=1)
        totals = [dot_nt(twice, g_ref[index]) for index in range(len(self.hops))]
        if not self.paired:
            for i, out_ref in enumerate(out_refs):
                step = i % self.members * self.width
                out_ref[...] = totals[i // self.members][:, step : step + self.width].astype(BF16)
            return
        message_ref, keep_ref = out_refs
        (total,) = totals
        pieces = [total[:, i * self.width : (i + 1) * self.width] for i in range(self.members)]
        even = jnp.concatenate(pieces[0::2], axis=1)
        odd = jnp.concatenate(pieces[1::2], axis=1)
        second = lax.rem(index_ref[0], 2) == 1
        keep_ref[...] = jnp.where(second, odd, even)
        upper, lower = halves(jnp.where(second, even, odd))
        message_ref[:, : self.shard_len] = x
        message_ref[:, self.shard_len : self.shard_len + 2 * self.width] = upper
        message_ref[:, self.shard_len + 2 * self.width :] = lower

    def relay_far(self, index_ref, keep_ref, message_ref, out_refs):
        upper = message_ref[:, self.shard_len : self.shard_len + 2 * self.width].astype(F32)
        lower = message_ref[:, self.shard_len + 2 * self.width :].astype(F32)
        total = (keep_ref[...] + (upper + lower)).astype(BF16)
        second = self.member(index_ref) >= 2
        first, last = total[:, : self.width], total[:, self.width :]
        out_refs[0][...] = jnp.where(second, first, last)
        out_refs[1][...] = jnp.where(second, last, first)

    def far_sum(self, far_refs):
        return sum(ref[...].astype(F32) for ref in far_refs)

    def near_sums(self, x_ref, d_ref, acc_ref, first, start_ref=None):
        panels = [self.panel(x_ref, c) for c in range(self.per_device)]
        for r in range(self.per_device):
            value = None if start_ref is None else self.panel(start_ref, r)
            for c in range(self.per_device):
                offset = first + c - r
                if -REACH <= offset <= REACH:
                    term = dot_nt(panels[c], d_ref[r * SPAN + offset + REACH])
                    value = term if value is None else value + term
            acc_ref[:, r * self.size : (r + 1) * self.size] = value

    def halo_sums(self, below, x_ref, d_ref, acc_ref, start_ref):
        @pl.when(below)
        def _():
            self.near_sums(x_ref, d_ref, acc_ref, -self.per_device, start_ref)

        @pl.when(jnp.logical_not(below))
        def _():
            self.near_sums(x_ref, d_ref, acc_ref, self.per_device, start_ref)

    def far_halves(self, far_refs):
        return jnp.concatenate(halves(self.far_sum(far_refs)), axis=1)

    def next_panel(self, acc_ref, rb_ref, both, c):
        return (self.panel(acc_ref, c) + dot_nn(both, self.panel(rb_ref, c))).astype(BF16)

    def next_block(self, acc_ref, rb_ref, far_refs):
        both = self.far_halves(far_refs)
        panels = [self.next_panel(acc_ref, rb_ref, both, c) for c in range(self.per_device)]
        return jnp.concatenate(panels, axis=1)


def prepare_kernel(plan, index_ref, *refs):
    sources, refs = refs[:7], refs[7:]
    x_ref, g_ref, cb_ref, near_ref, offsets_ref = refs[:5]
    sends, (rows_ref, cols_ref, col_ref, coup_ref, sum_ref, sems) = refs[5:-6], refs[-6:]
    targets = (near_ref, offsets_ref, rows_ref, cols_ref, x_ref, col_ref, coup_ref)
    copies = [
        pltpu.make_async_copy(source, target, sems.at[i])
        for i, (source, target) in enumerate(zip(sources, targets))
    ]
    for copy in copies:
        copy.start()
    rank, size = plan.rank, plan.size
    cb_ref[...] = jnp.zeros_like(cb_ref)
    sum_ref[...] = jnp.zeros_like(sum_ref)
    for copy in copies:
        copy.wait()
    for c in range(plan.per_device):
        cb_ref[c * rank : (c + 1) * rank, c * size : (c + 1) * size] = col_ref[c]
    column = lax.broadcasted_iota(jnp.int32, (rank, plan.width), 1) // rank
    shift = 0 if plan.paired else plan.member(index_ref)
    for s in range(plan.slots):
        row = lax.rem(rows_ref[s], plan.block_clusters)
        step = lax.rem(lax.div(row, plan.per_device) - shift + plan.members, plan.members)
        place = step * plan.per_device + lax.rem(row, plan.per_device)
        if len(plan.hops) > 1:
            level = lax.div(rows_ref[s], plan.block_clusters)
            index = sum(jnp.where(level == i, index, 0) for i, index in enumerate(plan.set_of))
        else:
            index = 0
        where = (index, pl.ds(pl.multiple_of(place * rank, rank), rank), slice(None))
        tile = coup_ref[s].astype(F32)
        wide = jnp.where(column == cols_ref[s], jnp.concatenate([tile] * plan.per_device, axis=1), 0.0)
        sum_ref[where] = sum_ref[where] + wide
    for index in range(len(plan.hops)):
        g_ref[index] = jnp.concatenate(halves(sum_ref[index]), axis=1)
    plan.send_far(index_ref, x_ref[...], cb_ref, g_ref, sends)


def relay_kernel(plan, index_ref, keep_ref, message_ref, *out_refs):
    plan.relay_far(index_ref, keep_ref, message_ref, out_refs)


def first_own_kernel(plan, *refs):
    index_ref, rows_ref, offsets_ref, x_ref, near_ref, row_ref, tiles_ref = refs[:7]
    acc_ref, d_ref, rb_ref = refs[-3:]
    rank, size = plan.rank, plan.size
    for cell in range(plan.cells):
        d_ref[cell] = jnp.zeros(d_ref.shape[1:], d_ref.dtype)
    for s in range(plan.tiles):
        d_ref[rows_ref[s] * SPAN + offsets_ref[s] + REACH] = tiles_ref[s]
    rb_ref[...] = jnp.zeros_like(rb_ref)
    for c in range(plan.per_device):
        for start in (c * rank, plan.width + c * rank):
            rb_ref[start : start + rank, c * size : (c + 1) * size] = row_ref[c]
    plan.near_sums(x_ref, d_ref, acc_ref, 0)
    plan.halo_sums(lax.rem(index_ref[0], 2) == 1, near_ref, d_ref, acc_ref, acc_ref)


def own_kernel(plan, slot, *refs):
    index_ref, x_ref, near_ref, d_ref = refs[:4]
    acc_ref, krylov_ref, sem = refs[-3:]
    copy = pltpu.make_async_copy(x_ref, krylov_ref.at[slot], sem)
    copy.start()
    plan.near_sums(x_ref, d_ref, acc_ref, 0)
    plan.halo_sums(lax.rem(index_ref[0], 2) == 1, near_ref, d_ref, acc_ref, acc_ref)
    copy.wait()


def halo_kernel(plan, index_ref, acc_ref, over_ref, d_ref, *refs):
    plan.halo_sums(lax.rem(index_ref[0], 2) == 0, over_ref, d_ref, refs[-1], acc_ref)


def finish_kernel(plan, fars, *refs):
    index_ref, acc_ref, rb_ref, cb_ref, g_ref = refs[:5]
    far_refs, (x_ref, *sends) = refs[5 : 5 + fars], refs[5 + fars :]
    x = plan.next_block(acc_ref, rb_ref, far_refs)
    x_ref[...] = x
    plan.send_far(index_ref, x, cb_ref, g_ref, sends)


def last_kernel(plan, fars, slot, *refs):
    acc_ref, rb_ref = refs[:2]
    far_refs, (_, krylov_ref, x_ref, sem) = refs[2 : 2 + fars], refs[2 + fars :]
    both = plan.far_halves(far_refs)
    copies = []
    for c in range(plan.per_device):
        columns = pl.ds(c * plan.size, plan.size)
        x_ref[:, columns] = plan.next_panel(acc_ref, rb_ref, both, c)
        copies.append(
            pltpu.make_async_copy(x_ref.at[:, columns], krylov_ref.at[slot, :, columns], sem.at[c])
        )
        copies[-1].start()
    for copy in copies:
        copy.wait()


def call(kernel, name, ins, specs, outs, out_specs=None, scratch=(), aliases=None):
    spaces = {id(IN_VMEM): pltpu.VMEM, id(IN_HBM): pltpu.HBM}
    ins = [
        pltpu.with_memory_space_constraint(v, spaces[id(spec)]) if id(spec) in spaces else v
        for v, spec in zip(ins, specs)
    ]
    return pl.pallas_call(
        kernel,
        in_specs=list(specs),
        out_specs=out_specs or [IN_VMEM] * len(outs),
        out_shape=list(outs),
        scratch_shapes=list(scratch),
        input_output_aliases=aliases or {},
        compiler_params=pltpu.CompilerParams(vmem_limit_bytes=16 * 2**20),
        cost_estimate=pl.CostEstimate(flops=10**9, bytes_accessed=2**22, transcendentals=0),
        name=name,
    )(*ins)


def on_device(
    block, near_tiles, near_rows, near_offsets, col_basis, couplings, far_rows, far_cols, row_basis
):
    axes = ("loop", "far")
    plan = Plan(
        block.shape, near_tiles.shape, couplings.shape, lax.axis_size("far"), lax.axis_size("loop")
    )
    rhs, shard_len, width = plan.rhs, plan.shard_len, plan.width
    block_out = pltpu.VMEM((rhs, shard_len), BF16)
    acc_out = pltpu.VMEM((rhs, shard_len), F32)
    relay_out = pltpu.VMEM((rhs, width), BF16)
    krylov_out = jax.ShapeDtypeStruct((PRODUCTS, rhs, shard_len), BF16)
    if plan.paired:
        sends_out = [
            pltpu.VMEM((rhs, shard_len + 4 * width), BF16),
            pltpu.VMEM((rhs, 2 * width), F32),
        ]
    else:
        sends_out = [pltpu.VMEM((rhs, width), BF16)] * len(plan.routes)
    index = lax.axis_index(axes).astype(jnp.int32).reshape(1)

    def scratch_for(*arrays):
        return [
            pltpu.SMEM(v.shape, v.dtype) if v.dtype == jnp.int32 else pltpu.VMEM(v.shape, v.dtype)
            for v in arrays
        ]

    current, sends, krylov = block, None, None
    for product in range(PRODUCTS):
        if product == 0:
            ins = [near_rows, near_offsets, far_rows, far_cols, block, col_basis, couplings]
            matrix = (len(plan.hops), plan.members * width, 2 * width)
            current, coupled, col_wide, row_slots, offset_slots, *sends = call(
                functools.partial(prepare_kernel, plan),
                "prepare",
                [index, *ins],
                [IN_SMEM] + [IN_HBM] * 7,
                [
                    block_out,
                    pltpu.VMEM(matrix, BF16),
                    pltpu.VMEM((width, shard_len), BF16),
                    *scratch_for(near_rows, near_offsets),
                    *sends_out,
                ],
                [IN_VMEM] * 3 + [IN_SMEM] * 2 + [IN_VMEM] * len(sends_out),
                scratch=scratch_for(far_rows, far_cols, col_basis, couplings)
                + [pltpu.VMEM(matrix[:2] + (width,), F32), pltpu.SemaphoreType.DMA((7,))],
            )
        over = lax.ppermute(block if product == 0 else current, axes, plan.over)
        near = lax.ppermute(sends[0] if plan.paired else current, axes, plan.near)
        if plan.paired:
            sends = call(
                functools.partial(relay_kernel, plan),
                "relay",
                [index, sends[1], near],
                [IN_SMEM] + [IN_VMEM] * 2,
                [relay_out] * 2,
            )
            routes = plan.across
        else:
            routes = plan.routes
        fars = [lax.ppermute(s, axes, route) for s, route in zip(sends, routes)]
        after = sends if plan.paired else []
        if product == 0:
            ins = [index, row_slots, offset_slots, current, near, row_basis, near_tiles, *after]
            acc, dense, row_wide = call(
                functools.partial(first_own_kernel, plan),
                "first_own",
                ins,
                [IN_SMEM] * 3 + [IN_VMEM] * 2 + [PREFETCHED] * 2 + [ANYWHERE] * len(after),
                [
                    acc_out,
                    pltpu.VMEM((plan.cells, plan.size, plan.size), BF16),
                    pltpu.VMEM((2 * width, shard_len), BF16),
                ],
            )
        else:
            ins = [index, current, near, dense, *after] + ([krylov] if product > 1 else [])
            acc, krylov = call(
                functools.partial(own_kernel, plan, product - 1),
                "own",
                ins,
                [IN_SMEM] + [IN_VMEM] * 3 + [ANYWHERE] * (len(ins) - 4),
                [acc_out, krylov_out],
                [IN_VMEM, ANYWHERE],
                [pltpu.SemaphoreType.DMA],
                {len(ins) - 1: 1} if product > 1 else None,
            )
        (acc,) = call(
            functools.partial(halo_kernel, plan),
            "halo",
            [index, acc, over, dense],
            [IN_SMEM] + [IN_VMEM] * 3,
            [acc_out],
        )
        if product < PRODUCTS - 1:
            ins = [index, acc, row_wide, col_wide, coupled, *fars]
            current, *sends = call(
                functools.partial(finish_kernel, plan, len(fars)),
                "finish",
                ins,
                [IN_SMEM] + [IN_VMEM] * (len(ins) - 1),
                [block_out, *sends_out],
            )
        else:
            ins = [acc, row_wide, *fars, krylov]
            (krylov,) = call(
                functools.partial(last_kernel, plan, len(fars), product),
                "last",
                ins,
                [IN_VMEM] * (len(ins) - 1) + [ANYWHERE],
                [krylov_out],
                [ANYWHERE],
                [
                    pltpu.VMEM((rhs, shard_len), BF16),
                    pltpu.SemaphoreType.DMA((plan.per_device,)),
                ],
                {len(ins) - 1: 0},
            )
    return krylov


def solution(mesh):
    split = ("groups", "loop", "far")
    wide, narrow = P(split, None, None), P(split)
    in_specs = (P(None, split), wide, narrow, narrow, wide, wide, narrow, narrow, wide)
    return jax.shard_map(
        on_device, mesh=mesh, in_specs=in_specs, out_specs=P(None, None, split), check_vma=False
    )
```

```python
import functools

import jax
import jax.numpy as jnp
from jax import lax
from jax.experimental import pallas as pl
from jax.experimental.pallas import tpu as pltpu
from jax.sharding import PartitionSpec as P

PRODUCTS = 4
REACH = 4
LEVELS = 3
SPAN = 2 * REACH + 1
OTHER_CORE_FIRST = 0b11011111

F32 = jnp.float32
BF16 = jnp.bfloat16
IN_VMEM = pl.BlockSpec(memory_space=pltpu.VMEM)
PREFETCHED = pl.BlockSpec(memory_space=pltpu.VMEM)
IN_SMEM = pl.BlockSpec(memory_space=pltpu.SMEM)
IN_HBM = pl.BlockSpec(memory_space=pltpu.HBM)
ANYWHERE = pl.BlockSpec(memory_space=pl.ANY)


def dot_nt(a, b):
    return lax.dot_general(a, b, (((1,), (1,)), ((), ())), preferred_element_type=F32)


def dot_nn(a, b):
    return lax.dot_general(a, b, (((1,), (0,)), ((), ())), preferred_element_type=F32)


def halves(value):
    upper = value.astype(BF16)
    return upper, (value - upper.astype(F32)).astype(BF16)


class Plan:
    def __init__(self, block_shape, tile_shape, coupling_shape, members, loop_size):
        self.rhs, self.shard_len = block_shape
        self.tiles, self.size, _ = tile_shape
        self.slots, self.rank, _ = coupling_shape
        self.members, self.loop_size = members, loop_size
        self.per_device = self.shard_len // self.size
        self.width = self.per_device * self.rank
        self.cells = self.per_device * SPAN
        self.block_clusters = self.per_device * members
        distances = [d % loop_size for d in (2, loop_size - 2, loop_size // 2)]
        self.hops = sorted(set(distances))
        self.set_of = [self.hops.index(d) for d in distances]
        self.paired = len(self.hops) == 1 and 2 * self.hops[0] == loop_size and members == 4
        devices = members * loop_size
        self.near = [(i, i ^ 1) for i in range(devices)]
        self.over = [(i, (i + 1 if i % 2 else i - 1) % devices) for i in range(devices)]
        places = [(l, m) for l in range(loop_size) for m in range(members)]
        self.across = [
            [
                (l * members + m, self.far_target(l, m)[turn])
                for l, m in places
            ]
            for turn in range(2)
        ]
        self.routes = [
            [(l * members + m, (l + hop) % loop_size * members + (m + step) % members) for l, m in places]
            for hop in self.hops
            for step in range(members)
        ]

    def far_target(self, loop_index, member):
        block = (loop_index + self.hops[0]) % self.loop_size
        pair, core = divmod(member, 2)
        chip = block * 2 + (pair ^ core)
        first = core ^ (OTHER_CORE_FIRST >> chip & 1)
        return 2 * chip + first, 2 * chip + (first ^ 1)

    def first_is_odd(self, index_ref):
        index = index_ref[0]
        block = lax.rem(lax.div(index, self.members) + self.hops[0], self.loop_size)
        pair, core = lax.div(self.member(index_ref), 2), lax.rem(index, 2)
        chip = block * 2 + lax.bitwise_xor(pair, core)
        swapped = lax.bitwise_and(lax.shift_right_logical(jnp.int32(OTHER_CORE_FIRST), chip), 1)
        return lax.bitwise_xor(core, swapped) == 1

    def panel(self, ref, c):
        return ref[:, c * self.size : (c + 1) * self.size]

    def member(self, index_ref):
        return lax.rem(index_ref[0], self.members)

    def send_far(self, index_ref, x, cb_ref, g_ref, out_refs):
        coeffs = dot_nt(x, cb_ref[...]).astype(BF16)
        twice = jnp.concatenate([coeffs, coeffs], axis=1)
        totals = [dot_nt(twice, g_ref[index]) for index in range(len(self.hops))]
        if not self.paired:
            for i, out_ref in enumerate(out_refs):
                step = i % self.members * self.width
                out_ref[...] = totals[i // self.members][:, step : step + self.width].astype(BF16)
            return
        message_ref, keep_ref = out_refs
        (total,) = totals
        member = self.member(index_ref)
        second = lax.rem(member, 2) != lax.div(member, 2)
        first, last = total[:, : 2 * self.width], total[:, 2 * self.width :]
        keep_ref[...] = jnp.where(second, last, first)
        upper, lower = halves(jnp.where(second, first, last))
        message_ref[:, : self.shard_len] = x
        message_ref[:, self.shard_len : self.shard_len + 2 * self.width] = upper
        message_ref[:, self.shard_len + 2 * self.width :] = lower

    def relay_far(self, index_ref, keep_ref, message_ref, out_refs):
        upper = message_ref[:, self.shard_len : self.shard_len + 2 * self.width].astype(F32)
        lower = message_ref[:, self.shard_len + 2 * self.width :].astype(F32)
        total = (keep_ref[...] + (upper + lower)).astype(BF16)
        odd = self.first_is_odd(index_ref)
        first, last = total[:, : self.width], total[:, self.width :]
        out_refs[0][...] = jnp.where(odd, last, first)
        out_refs[1][...] = jnp.where(odd, first, last)

    def far_sum(self, far_refs):
        return sum(ref[...].astype(F32) for ref in far_refs)

    def near_sums(self, x_ref, d_ref, acc_ref, first, start_ref=None):
        panels = [self.panel(x_ref, c) for c in range(self.per_device)]
        for r in range(self.per_device):
            value = None if start_ref is None else self.panel(start_ref, r)
            for c in range(self.per_device):
                offset = first + c - r
                if -REACH <= offset <= REACH:
                    term = dot_nt(panels[c], d_ref[r * SPAN + offset + REACH])
                    value = term if value is None else value + term
            acc_ref[:, r * self.size : (r + 1) * self.size] = value

    def halo_sums(self, below, x_ref, d_ref, acc_ref, start_ref):
        @pl.when(below)
        def _():
            self.near_sums(x_ref, d_ref, acc_ref, -self.per_device, start_ref)

        @pl.when(jnp.logical_not(below))
        def _():
            self.near_sums(x_ref, d_ref, acc_ref, self.per_device, start_ref)

    def far_halves(self, far_refs):
        return jnp.concatenate(halves(self.far_sum(far_refs)), axis=1)

    def next_panel(self, acc_ref, rb_ref, both, c):
        return (self.panel(acc_ref, c) + dot_nn(both, self.panel(rb_ref, c))).astype(BF16)

    def next_block(self, acc_ref, rb_ref, far_refs):
        both = self.far_halves(far_refs)
        panels = [self.next_panel(acc_ref, rb_ref, both, c) for c in range(self.per_device)]
        return jnp.concatenate(panels, axis=1)


def prepare_kernel(plan, index_ref, *refs):
    sources, refs = refs[:7], refs[7:]
    x_ref, g_ref, cb_ref, near_ref, offsets_ref = refs[:5]
    sends, (rows_ref, cols_ref, col_ref, coup_ref, sum_ref, sems) = refs[5:-6], refs[-6:]
    targets = (near_ref, offsets_ref, rows_ref, cols_ref, x_ref, col_ref, coup_ref)
    copies = [
        pltpu.make_async_copy(source, target, sems.at[i])
        for i, (source, target) in enumerate(zip(sources, targets))
    ]
    for copy in copies:
        copy.start()
    rank, size = plan.rank, plan.size
    cb_ref[...] = jnp.zeros_like(cb_ref)
    sum_ref[...] = jnp.zeros_like(sum_ref)
    for copy in copies:
        copy.wait()
    for c in range(plan.per_device):
        cb_ref[c * rank : (c + 1) * rank, c * size : (c + 1) * size] = col_ref[c]
    column = lax.broadcasted_iota(jnp.int32, (rank, plan.width), 1) // rank
    shift = 0 if plan.paired else plan.member(index_ref)
    for s in range(plan.slots):
        row = lax.rem(rows_ref[s], plan.block_clusters)
        step = lax.rem(lax.div(row, plan.per_device) - shift + plan.members, plan.members)
        place = step * plan.per_device + lax.rem(row, plan.per_device)
        if len(plan.hops) > 1:
            level = lax.div(rows_ref[s], plan.block_clusters)
            index = sum(jnp.where(level == i, index, 0) for i, index in enumerate(plan.set_of))
        else:
            index = 0
        where = (index, pl.ds(pl.multiple_of(place * rank, rank), rank), slice(None))
        tile = coup_ref[s].astype(F32)
        wide = jnp.where(column == cols_ref[s], jnp.concatenate([tile] * plan.per_device, axis=1), 0.0)
        sum_ref[where] = sum_ref[where] + wide
    for index in range(len(plan.hops)):
        g_ref[index] = jnp.concatenate(halves(sum_ref[index]), axis=1)
    plan.send_far(index_ref, x_ref[...], cb_ref, g_ref, sends)


def relay_kernel(plan, index_ref, keep_ref, message_ref, *out_refs):
    plan.relay_far(index_ref, keep_ref, message_ref, out_refs)


def first_own_kernel(plan, *refs):
    index_ref, rows_ref, offsets_ref, x_ref, near_ref, row_ref, tiles_ref = refs[:7]
    acc_ref, d_ref, rb_ref = refs[-3:]
    rank, size = plan.rank, plan.size
    for cell in range(plan.cells):
        d_ref[cell] = jnp.zeros(d_ref.shape[1:], d_ref.dtype)
    for s in range(plan.tiles):
        d_ref[rows_ref[s] * SPAN + offsets_ref[s] + REACH] = tiles_ref[s]
    rb_ref[...] = jnp.zeros_like(rb_ref)
    for c in range(plan.per_device):
        for start in (c * rank, plan.width + c * rank):
            rb_ref[start : start + rank, c * size : (c + 1) * size] = row_ref[c]
    plan.near_sums(x_ref, d_ref, acc_ref, 0)
    plan.halo_sums(lax.rem(index_ref[0], 2) == 1, near_ref, d_ref, acc_ref, acc_ref)


def own_kernel(plan, slot, *refs):
    index_ref, x_ref, near_ref, d_ref = refs[:4]
    acc_ref, krylov_ref, sem = refs[-3:]
    copy = pltpu.make_async_copy(x_ref, krylov_ref.at[slot], sem)
    copy.start()
    plan.near_sums(x_ref, d_ref, acc_ref, 0)
    plan.halo_sums(lax.rem(index_ref[0], 2) == 1, near_ref, d_ref, acc_ref, acc_ref)
    copy.wait()


def halo_kernel(plan, index_ref, acc_ref, over_ref, d_ref, *refs):
    plan.halo_sums(lax.rem(index_ref[0], 2) == 0, over_ref, d_ref, refs[-1], acc_ref)


def finish_kernel(plan, fars, *refs):
    index_ref, acc_ref, rb_ref, cb_ref, g_ref = refs[:5]
    far_refs, (x_ref, *sends) = refs[5 : 5 + fars], refs[5 + fars :]
    x = plan.next_block(acc_ref, rb_ref, far_refs)
    x_ref[...] = x
    plan.send_far(index_ref, x, cb_ref, g_ref, sends)


def last_kernel(plan, fars, slot, *refs):
    acc_ref, rb_ref = refs[:2]
    far_refs, (_, krylov_ref, x_ref, sem) = refs[2 : 2 + fars], refs[2 + fars :]
    both = plan.far_halves(far_refs)
    copies = []
    for c in range(plan.per_device):
        columns = pl.ds(c * plan.size, plan.size)
        x_ref[:, columns] = plan.next_panel(acc_ref, rb_ref, both, c)
        copies.append(
            pltpu.make_async_copy(x_ref.at[:, columns], krylov_ref.at[slot, :, columns], sem.at[c])
        )
        copies[-1].start()
    for copy in copies:
        copy.wait()


def call(kernel, name, ins, specs, outs, out_specs=None, scratch=(), aliases=None):
    spaces = {id(IN_VMEM): pltpu.VMEM, id(IN_HBM): pltpu.HBM}
    ins = [
        pltpu.with_memory_space_constraint(v, spaces[id(spec)]) if id(spec) in spaces else v
        for v, spec in zip(ins, specs)
    ]
    return pl.pallas_call(
        kernel,
        in_specs=list(specs),
        out_specs=out_specs or [IN_VMEM] * len(outs),
        out_shape=list(outs),
        scratch_shapes=list(scratch),
        input_output_aliases=aliases or {},
        compiler_params=pltpu.CompilerParams(vmem_limit_bytes=16 * 2**20),
        cost_estimate=pl.CostEstimate(flops=10**9, bytes_accessed=2**22, transcendentals=0),
        name=name,
    )(*ins)


def on_device(
    block, near_tiles, near_rows, near_offsets, col_basis, couplings, far_rows, far_cols, row_basis
):
    axes = ("loop", "far")
    plan = Plan(
        block.shape, near_tiles.shape, couplings.shape, lax.axis_size("far"), lax.axis_size("loop")
    )
    rhs, shard_len, width = plan.rhs, plan.shard_len, plan.width
    block_out = pltpu.VMEM((rhs, shard_len), BF16)
    acc_out = pltpu.VMEM((rhs, shard_len), F32)
    relay_out = pltpu.VMEM((rhs, width), BF16)
    krylov_out = jax.ShapeDtypeStruct((PRODUCTS, rhs, shard_len), BF16)
    if plan.paired:
        sends_out = [
            pltpu.VMEM((rhs, shard_len + 4 * width), BF16),
            pltpu.VMEM((rhs, 2 * width), F32),
        ]
    else:
        sends_out = [pltpu.VMEM((rhs, width), BF16)] * len(plan.routes)
    index = lax.axis_index(axes).astype(jnp.int32).reshape(1)

    def scratch_for(*arrays):
        return [
            pltpu.SMEM(v.shape, v.dtype) if v.dtype == jnp.int32 else pltpu.VMEM(v.shape, v.dtype)
            for v in arrays
        ]

    current, sends, krylov = block, None, None
    for product in range(PRODUCTS):
        if product == 0:
            ins = [near_rows, near_offsets, far_rows, far_cols, block, col_basis, couplings]
            matrix = (len(plan.hops), plan.members * width, 2 * width)
            current, coupled, col_wide, row_slots, offset_slots, *sends = call(
                functools.partial(prepare_kernel, plan),
                "prepare",
                [index, *ins],
                [IN_SMEM] + [IN_HBM] * 7,
                [
                    block_out,
                    pltpu.VMEM(matrix, BF16),
                    pltpu.VMEM((width, shard_len), BF16),
                    *scratch_for(near_rows, near_offsets),
                    *sends_out,
                ],
                [IN_VMEM] * 3 + [IN_SMEM] * 2 + [IN_VMEM] * len(sends_out),
                scratch=scratch_for(far_rows, far_cols, col_basis, couplings)
                + [pltpu.VMEM(matrix[:2] + (width,), F32), pltpu.SemaphoreType.DMA((7,))],
            )
        over = lax.ppermute(block if product == 0 else current, axes, plan.over)
        near = lax.ppermute(sends[0] if plan.paired else current, axes, plan.near)
        if plan.paired:
            sends = call(
                functools.partial(relay_kernel, plan),
                "relay",
                [index, sends[1], near],
                [IN_SMEM] + [IN_VMEM] * 2,
                [relay_out] * 2,
            )
            routes = plan.across
        else:
            routes = plan.routes
        fars = [lax.ppermute(s, axes, route) for s, route in zip(sends, routes)]
        after = sends if plan.paired else []
        if product == 0:
            ins = [index, row_slots, offset_slots, current, near, row_basis, near_tiles, *after]
            acc, dense, row_wide = call(
                functools.partial(first_own_kernel, plan),
                "first_own",
                ins,
                [IN_SMEM] * 3 + [IN_VMEM] * 2 + [PREFETCHED] * 2 + [ANYWHERE] * len(after),
                [
                    acc_out,
                    pltpu.VMEM((plan.cells, plan.size, plan.size), BF16),
                    pltpu.VMEM((2 * width, shard_len), BF16),
                ],
            )
        else:
            ins = [index, current, near, dense, *after] + ([krylov] if product > 1 else [])
            acc, krylov = call(
                functools.partial(own_kernel, plan, product - 1),
                "own",
                ins,
                [IN_SMEM] + [IN_VMEM] * 3 + [ANYWHERE] * (len(ins) - 4),
                [acc_out, krylov_out],
                [IN_VMEM, ANYWHERE],
                [pltpu.SemaphoreType.DMA],
                {len(ins) - 1: 1} if product > 1 else None,
            )
        (acc,) = call(
            functools.partial(halo_kernel, plan),
            "halo",
            [index, acc, over, dense],
            [IN_SMEM] + [IN_VMEM] * 3,
            [acc_out],
        )
        if product < PRODUCTS - 1:
            ins = [index, acc, row_wide, col_wide, coupled, *fars]
            current, *sends = call(
                functools.partial(finish_kernel, plan, len(fars)),
                "finish",
                ins,
                [IN_SMEM] + [IN_VMEM] * (len(ins) - 1),
                [block_out, *sends_out],
            )
        else:
            ins = [acc, row_wide, *fars, krylov]
            (krylov,) = call(
                functools.partial(last_kernel, plan, len(fars), product),
                "last",
                ins,
                [IN_VMEM] * (len(ins) - 1) + [ANYWHERE],
                [krylov_out],
                [ANYWHERE],
                [
                    pltpu.VMEM((rhs, shard_len), BF16),
                    pltpu.SemaphoreType.DMA((plan.per_device,)),
                ],
                {len(ins) - 1: 0},
            )
    return krylov


def solution(mesh):
    split = ("groups", "loop", "far")
    wide, narrow = P(split, None, None), P(split)
    in_specs = (P(None, split), wide, narrow, narrow, wide, wide, narrow, narrow, wide)
    return jax.shard_map(
        on_device, mesh=mesh, in_specs=in_specs, out_specs=P(None, None, split), check_vma=False
    )
```

```python
import functools

import jax
import jax.numpy as jnp
from jax import lax
from jax.experimental import pallas as pl
from jax.experimental.pallas import tpu as pltpu
from jax.sharding import PartitionSpec as P

PRODUCTS = 4
REACH = 4
LEVELS = 3
SPAN = 2 * REACH + 1

F32 = jnp.float32
BF16 = jnp.bfloat16
IN_VMEM = pl.BlockSpec(memory_space=pltpu.VMEM)
PREFETCHED = pl.BlockSpec(memory_space=pltpu.VMEM)
IN_SMEM = pl.BlockSpec(memory_space=pltpu.SMEM)
IN_HBM = pl.BlockSpec(memory_space=pltpu.HBM)
ANYWHERE = pl.BlockSpec(memory_space=pl.ANY)


def dot_nt(a, b):
    return lax.dot_general(a, b, (((1,), (1,)), ((), ())), preferred_element_type=F32)


def dot_nn(a, b):
    return lax.dot_general(a, b, (((1,), (0,)), ((), ())), preferred_element_type=F32)


def halves(value):
    upper = value.astype(BF16)
    return upper, (value - upper.astype(F32)).astype(BF16)


class Plan:
    def __init__(self, block_shape, tile_shape, coupling_shape, members, loop_size):
        self.rhs, self.shard_len = block_shape
        self.tiles, self.size, _ = tile_shape
        self.slots, self.rank, _ = coupling_shape
        self.members, self.loop_size = members, loop_size
        self.per_device = self.shard_len // self.size
        self.width = self.per_device * self.rank
        self.cells = self.per_device * SPAN
        self.block_clusters = self.per_device * members
        distances = [d % loop_size for d in (2, loop_size - 2, loop_size // 2)]
        self.hops = sorted(set(distances))
        self.set_of = [self.hops.index(d) for d in distances]
        self.paired = len(self.hops) == 1 and 2 * self.hops[0] == loop_size and members == 4
        devices = members * loop_size
        self.near = [(i, i ^ 1) for i in range(devices)]
        self.over = [(i, (i + 1 if i % 2 else i - 1) % devices) for i in range(devices)]
        places = [(l, m) for l in range(loop_size) for m in range(members)]
        self.across = [
            [
                (l * members + m, (l + self.hops[0]) % loop_size * members + (m ^ (m % 2 * 2) ^ other))
                for l, m in places
            ]
            for other in (1, 0)
        ]
        self.routes = [
            [(l * members + m, (l + hop) % loop_size * members + (m + step) % members) for l, m in places]
            for hop in self.hops
            for step in range(members)
        ]

    def panel(self, ref, c):
        return ref[:, c * self.size : (c + 1) * self.size]

    def member(self, index_ref):
        return lax.rem(index_ref[0], self.members)

    def send_far(self, index_ref, x, cb_ref, g_ref, out_refs):
        coeffs = dot_nt(x, cb_ref[...]).astype(BF16)
        twice = jnp.concatenate([coeffs, coeffs], axis=1)
        totals = [dot_nt(twice, g_ref[index]) for index in range(len(self.hops))]
        if not self.paired:
            for i, out_ref in enumerate(out_refs):
                step = i % self.members * self.width
                out_ref[...] = totals[i // self.members][:, step : step + self.width].astype(BF16)
            return
        message_ref, keep_ref = out_refs
        (total,) = totals
        member = self.member(index_ref)
        second = lax.rem(member, 2) != lax.div(member, 2)
        first, last = total[:, : 2 * self.width], total[:, 2 * self.width :]
        keep_ref[...] = jnp.where(second, last, first)
        upper, lower = halves(jnp.where(second, first, last))
        message_ref[:, : self.shard_len] = x
        message_ref[:, self.shard_len : self.shard_len + 2 * self.width] = upper
        message_ref[:, self.shard_len + 2 * self.width :] = lower

    def relay_far(self, index_ref, keep_ref, message_ref, out_refs):
        upper = message_ref[:, self.shard_len : self.shard_len + 2 * self.width].astype(F32)
        lower = message_ref[:, self.shard_len + 2 * self.width :].astype(F32)
        total = (keep_ref[...] + (upper + lower)).astype(BF16)
        second = lax.rem(index_ref[0], 2) == 1
        first, last = total[:, : self.width], total[:, self.width :]
        out_refs[0][...] = jnp.where(second, first, last)
        out_refs[1][...] = jnp.where(second, last, first)

    def far_sum(self, far_refs):
        return sum(ref[...].astype(F32) for ref in far_refs)

    def near_sums(self, x_ref, d_ref, acc_ref, first, start_ref=None):
        panels = [self.panel(x_ref, c) for c in range(self.per_device)]
        for r in range(self.per_device):
            value = None if start_ref is None else self.panel(start_ref, r)
            for c in range(self.per_device):
                offset = first + c - r
                if -REACH <= offset <= REACH:
                    term = dot_nt(panels[c], d_ref[r * SPAN + offset + REACH])
                    value = term if value is None else value + term
            acc_ref[:, r * self.size : (r + 1) * self.size] = value

    def halo_sums(self, below, x_ref, d_ref, acc_ref, start_ref):
        @pl.when(below)
        def _():
            self.near_sums(x_ref, d_ref, acc_ref, -self.per_device, start_ref)

        @pl.when(jnp.logical_not(below))
        def _():
            self.near_sums(x_ref, d_ref, acc_ref, self.per_device, start_ref)

    def far_halves(self, far_refs):
        return jnp.concatenate(halves(self.far_sum(far_refs)), axis=1)

    def next_panel(self, acc_ref, rb_ref, both, c):
        return (self.panel(acc_ref, c) + dot_nn(both, self.panel(rb_ref, c))).astype(BF16)

    def next_block(self, acc_ref, rb_ref, far_refs):
        both = self.far_halves(far_refs)
        panels = [self.next_panel(acc_ref, rb_ref, both, c) for c in range(self.per_device)]
        return jnp.concatenate(panels, axis=1)


def prepare_kernel(plan, index_ref, *refs):
    sources, refs = refs[:7], refs[7:]
    x_ref, g_ref, cb_ref, near_ref, offsets_ref = refs[:5]
    sends, (rows_ref, cols_ref, col_ref, coup_ref, sum_ref, sems) = refs[5:-6], refs[-6:]
    targets = (near_ref, offsets_ref, rows_ref, cols_ref, x_ref, col_ref, coup_ref)
    copies = [
        pltpu.make_async_copy(source, target, sems.at[i])
        for i, (source, target) in enumerate(zip(sources, targets))
    ]
    for copy in copies:
        copy.start()
    rank, size = plan.rank, plan.size
    cb_ref[...] = jnp.zeros_like(cb_ref)
    sum_ref[...] = jnp.zeros_like(sum_ref)
    for copy in copies:
        copy.wait()
    for c in range(plan.per_device):
        cb_ref[c * rank : (c + 1) * rank, c * size : (c + 1) * size] = col_ref[c]
    column = lax.broadcasted_iota(jnp.int32, (rank, plan.width), 1) // rank
    wide = jnp.concatenate([coup_ref[...].astype(F32)] * plan.per_device, axis=2)
    shift = 0 if plan.paired else plan.member(index_ref)
    for s in range(plan.slots):
        row = lax.rem(rows_ref[s], plan.block_clusters)
        step = lax.rem(lax.div(row, plan.per_device) - shift + plan.members, plan.members)
        place = step * plan.per_device + lax.rem(row, plan.per_device)
        if len(plan.hops) > 1:
            level = lax.div(rows_ref[s], plan.block_clusters)
            index = sum(jnp.where(level == i, index, 0) for i, index in enumerate(plan.set_of))
        else:
            index = 0
        where = (index, pl.ds(pl.multiple_of(place * rank, rank), rank), slice(None))
        sum_ref[where] = sum_ref[where] + jnp.where(column == cols_ref[s], wide[s], 0.0)
    for index in range(len(plan.hops)):
        g_ref[index] = jnp.concatenate(halves(sum_ref[index]), axis=1)
    plan.send_far(index_ref, x_ref[...], cb_ref, g_ref, sends)


def relay_kernel(plan, index_ref, keep_ref, message_ref, *out_refs):
    plan.relay_far(index_ref, keep_ref, message_ref, out_refs)


def first_own_kernel(plan, *refs):
    index_ref, rows_ref, offsets_ref, x_ref, near_ref, row_ref, tiles_ref = refs[:7]
    acc_ref, d_ref, rb_ref = refs[-3:]
    rank, size = plan.rank, plan.size
    for cell in range(plan.cells):
        d_ref[cell] = jnp.zeros(d_ref.shape[1:], d_ref.dtype)
    for s in range(plan.tiles):
        d_ref[rows_ref[s] * SPAN + offsets_ref[s] + REACH] = tiles_ref[s]
    rb_ref[...] = jnp.zeros_like(rb_ref)
    for c in range(plan.per_device):
        for start in (c * rank, plan.width + c * rank):
            rb_ref[start : start + rank, c * size : (c + 1) * size] = row_ref[c]
    plan.near_sums(x_ref, d_ref, acc_ref, 0)
    plan.halo_sums(lax.rem(index_ref[0], 2) == 1, near_ref, d_ref, acc_ref, acc_ref)


def own_kernel(plan, slot, *refs):
    index_ref, x_ref, near_ref, d_ref = refs[:4]
    acc_ref, krylov_ref, sem = refs[-3:]
    copy = pltpu.make_async_copy(x_ref, krylov_ref.at[slot], sem)
    copy.start()
    plan.near_sums(x_ref, d_ref, acc_ref, 0)
    plan.halo_sums(lax.rem(index_ref[0], 2) == 1, near_ref, d_ref, acc_ref, acc_ref)
    copy.wait()


def halo_kernel(plan, index_ref, acc_ref, over_ref, d_ref, *refs):
    plan.halo_sums(lax.rem(index_ref[0], 2) == 0, over_ref, d_ref, refs[-1], acc_ref)


def finish_kernel(plan, fars, *refs):
    index_ref, acc_ref, rb_ref, cb_ref, g_ref = refs[:5]
    far_refs, (x_ref, *sends) = refs[5 : 5 + fars], refs[5 + fars :]
    x = plan.next_block(acc_ref, rb_ref, far_refs)
    x_ref[...] = x
    plan.send_far(index_ref, x, cb_ref, g_ref, sends)


def last_kernel(plan, fars, slot, *refs):
    acc_ref, rb_ref = refs[:2]
    far_refs, (_, krylov_ref, x_ref, sem) = refs[2 : 2 + fars], refs[2 + fars :]
    both = plan.far_halves(far_refs)
    copies = []
    for c in range(plan.per_device):
        columns = pl.ds(c * plan.size, plan.size)
        x_ref[:, columns] = plan.next_panel(acc_ref, rb_ref, both, c)
        copies.append(
            pltpu.make_async_copy(x_ref.at[:, columns], krylov_ref.at[slot, :, columns], sem.at[c])
        )
        copies[-1].start()
    for copy in copies:
        copy.wait()


def call(kernel, name, ins, specs, outs, out_specs=None, scratch=(), aliases=None):
    spaces = {id(IN_VMEM): pltpu.VMEM, id(IN_HBM): pltpu.HBM}
    ins = [
        pltpu.with_memory_space_constraint(v, spaces[id(spec)]) if id(spec) in spaces else v
        for v, spec in zip(ins, specs)
    ]
    return pl.pallas_call(
        kernel,
        in_specs=list(specs),
        out_specs=out_specs or [IN_VMEM] * len(outs),
        out_shape=list(outs),
        scratch_shapes=list(scratch),
        input_output_aliases=aliases or {},
        compiler_params=pltpu.CompilerParams(vmem_limit_bytes=16 * 2**20),
        cost_estimate=pl.CostEstimate(flops=10**9, bytes_accessed=2**22, transcendentals=0),
        name=name,
    )(*ins)


def on_device(
    block, near_tiles, near_rows, near_offsets, col_basis, couplings, far_rows, far_cols, row_basis
):
    axes = ("loop", "far")
    plan = Plan(
        block.shape, near_tiles.shape, couplings.shape, lax.axis_size("far"), lax.axis_size("loop")
    )
    rhs, shard_len, width = plan.rhs, plan.shard_len, plan.width
    block_out = pltpu.VMEM((rhs, shard_len), BF16)
    acc_out = pltpu.VMEM((rhs, shard_len), F32)
    relay_out = pltpu.VMEM((rhs, width), BF16)
    krylov_out = jax.ShapeDtypeStruct((PRODUCTS, rhs, shard_len), BF16)
    if plan.paired:
        sends_out = [
            pltpu.VMEM((rhs, shard_len + 4 * width), BF16),
            pltpu.VMEM((rhs, 2 * width), F32),
        ]
    else:
        sends_out = [pltpu.VMEM((rhs, width), BF16)] * len(plan.routes)
    index = lax.axis_index(axes).astype(jnp.int32).reshape(1)

    def scratch_for(*arrays):
        return [
            pltpu.SMEM(v.shape, v.dtype) if v.dtype == jnp.int32 else pltpu.VMEM(v.shape, v.dtype)
            for v in arrays
        ]

    current, sends, krylov = block, None, None
    for product in range(PRODUCTS):
        if product == 0:
            ins = [near_rows, near_offsets, far_rows, far_cols, block, col_basis, couplings]
            matrix = (len(plan.hops), plan.members * width, 2 * width)
            current, coupled, col_wide, row_slots, offset_slots, *sends = call(
                functools.partial(prepare_kernel, plan),
                "prepare",
                [index, *ins],
                [IN_SMEM] + [IN_HBM] * 7,
                [
                    block_out,
                    pltpu.VMEM(matrix, BF16),
                    pltpu.VMEM((width, shard_len), BF16),
                    *scratch_for(near_rows, near_offsets),
                    *sends_out,
                ],
                [IN_VMEM] * 3 + [IN_SMEM] * 2 + [IN_VMEM] * len(sends_out),
                scratch=scratch_for(far_rows, far_cols, col_basis, couplings)
                + [pltpu.VMEM(matrix[:2] + (width,), F32), pltpu.SemaphoreType.DMA((7,))],
            )
        over = lax.ppermute(current, axes, plan.over)
        near = lax.ppermute(sends[0] if plan.paired else current, axes, plan.near)
        if plan.paired:
            sends = call(
                functools.partial(relay_kernel, plan),
                "relay",
                [index, sends[1], near],
                [IN_SMEM] + [IN_VMEM] * 2,
                [relay_out] * 2,
            )
            routes = plan.across
        else:
            routes = plan.routes
        fars = [lax.ppermute(s, axes, route) for s, route in zip(sends, routes)]
        after = sends if plan.paired else []
        if product == 0:
            ins = [index, row_slots, offset_slots, current, near, row_basis, near_tiles, *after]
            acc, dense, row_wide = call(
                functools.partial(first_own_kernel, plan),
                "first_own",
                ins,
                [IN_SMEM] * 3 + [IN_VMEM] * 2 + [PREFETCHED] * 2 + [ANYWHERE] * len(after),
                [
                    acc_out,
                    pltpu.VMEM((plan.cells, plan.size, plan.size), BF16),
                    pltpu.VMEM((2 * width, shard_len), BF16),
                ],
            )
        else:
            ins = [index, current, near, dense, *after] + ([krylov] if product > 1 else [])
            acc, krylov = call(
                functools.partial(own_kernel, plan, product - 1),
                "own",
                ins,
                [IN_SMEM] + [IN_VMEM] * 3 + [ANYWHERE] * (len(ins) - 4),
                [acc_out, krylov_out],
                [IN_VMEM, ANYWHERE],
                [pltpu.SemaphoreType.DMA],
                {len(ins) - 1: 1} if product > 1 else None,
            )
        (acc,) = call(
            functools.partial(halo_kernel, plan),
            "halo",
            [index, acc, over, dense],
            [IN_SMEM] + [IN_VMEM] * 3,
            [acc_out],
        )
        if product < PRODUCTS - 1:
            ins = [index, acc, row_wide, col_wide, coupled, *fars]
            current, *sends = call(
                functools.partial(finish_kernel, plan, len(fars)),
                "finish",
                ins,
                [IN_SMEM] + [IN_VMEM] * (len(ins) - 1),
                [block_out, *sends_out],
            )
        else:
            ins = [acc, row_wide, *fars, krylov]
            (krylov,) = call(
                functools.partial(last_kernel, plan, len(fars), product),
                "last",
                ins,
                [IN_VMEM] * (len(ins) - 1) + [ANYWHERE],
                [krylov_out],
                [ANYWHERE],
                [
                    pltpu.VMEM((rhs, shard_len), BF16),
                    pltpu.SemaphoreType.DMA((plan.per_device,)),
                ],
                {len(ins) - 1: 0},
            )
    return krylov


def solution(mesh):
    split = ("groups", "loop", "far")
    wide, narrow = P(split, None, None), P(split)
    in_specs = (P(None, split), wide, narrow, narrow, wide, wide, narrow, narrow, wide)
    return jax.shard_map(
        on_device, mesh=mesh, in_specs=in_specs, out_specs=P(None, None, split), check_vma=False
    )
```

```python
import functools

import jax
import jax.numpy as jnp
from jax import lax
from jax.experimental import pallas as pl
from jax.experimental.pallas import tpu as pltpu
from jax.sharding import PartitionSpec as P

PRODUCTS = 4
REACH = 4
LEVELS = 3
SPAN = 2 * REACH + 1
TURNED = 0b00011000

F32 = jnp.float32
BF16 = jnp.bfloat16
IN_VMEM = pl.BlockSpec(memory_space=pltpu.VMEM)
PREFETCHED = pl.BlockSpec(memory_space=pltpu.VMEM)
IN_SMEM = pl.BlockSpec(memory_space=pltpu.SMEM)
IN_HBM = pl.BlockSpec(memory_space=pltpu.HBM)
ANYWHERE = pl.BlockSpec(memory_space=pl.ANY)


def dot_nt(a, b):
    return lax.dot_general(a, b, (((1,), (1,)), ((), ())), preferred_element_type=F32)


def dot_nn(a, b):
    return lax.dot_general(a, b, (((1,), (0,)), ((), ())), preferred_element_type=F32)


def halves(value):
    upper = value.astype(BF16)
    return upper, (value - upper.astype(F32)).astype(BF16)


class Plan:
    def __init__(self, block_shape, tile_shape, coupling_shape, members, loop_size):
        self.rhs, self.shard_len = block_shape
        self.tiles, self.size, _ = tile_shape
        self.slots, self.rank, _ = coupling_shape
        self.members, self.loop_size = members, loop_size
        self.per_device = self.shard_len // self.size
        self.width = self.per_device * self.rank
        self.cells = self.per_device * SPAN
        self.block_clusters = self.per_device * members
        distances = [d % loop_size for d in (2, loop_size - 2, loop_size // 2)]
        self.hops = sorted(set(distances))
        self.set_of = [self.hops.index(d) for d in distances]
        self.paired = len(self.hops) == 1 and 2 * self.hops[0] == loop_size and members == 4
        devices = members * loop_size
        self.near = [(i, i ^ 1) for i in range(devices)]
        self.over = [(i, (i + 1 if i % 2 else i - 1) % devices) for i in range(devices)]
        places = [(l, m) for l in range(loop_size) for m in range(members)]
        self.across = [
            [
                (l * members + m, (l + self.hops[0]) % loop_size * members + self.far_target(l, m)[turn])
                for l, m in places
            ]
            for turn in range(2)
        ]
        self.routes = [
            [(l * members + m, (l + hop) % loop_size * members + (m + step) % members) for l, m in places]
            for hop in self.hops
            for step in range(members)
        ]

    def far_target(self, loop_index, member):
        block = (loop_index + self.hops[0]) % self.loop_size
        pair, core = divmod(member, 2)
        chip = block * 2 + core
        first = pair ^ (TURNED >> chip & 1)
        return 2 * chip % self.members + first, 2 * chip % self.members + (first ^ 1)

    def first_is_odd(self, index_ref):
        index = index_ref[0]
        block = lax.rem(lax.div(index, self.members) + self.hops[0], self.loop_size)
        pair, core = lax.div(self.member(index_ref), 2), lax.rem(index, 2)
        turned = lax.bitwise_and(lax.shift_right_logical(jnp.int32(TURNED), block * 2 + core), 1)
        return lax.bitwise_xor(pair, turned) == 1

    def panel(self, ref, c):
        return ref[:, c * self.size : (c + 1) * self.size]

    def member(self, index_ref):
        return lax.rem(index_ref[0], self.members)

    def send_far(self, index_ref, x, cb_ref, g_ref, out_refs):
        coeffs = dot_nt(x, cb_ref[...]).astype(BF16)
        twice = jnp.concatenate([coeffs, coeffs], axis=1)
        totals = [dot_nt(twice, g_ref[index]) for index in range(len(self.hops))]
        if not self.paired:
            for i, out_ref in enumerate(out_refs):
                step = i % self.members * self.width
                out_ref[...] = totals[i // self.members][:, step : step + self.width].astype(BF16)
            return
        message_ref, keep_ref = out_refs
        (total,) = totals
        member = self.member(index_ref)
        second = lax.rem(member, 2) == 1
        first, last = total[:, : 2 * self.width], total[:, 2 * self.width :]
        keep_ref[...] = jnp.where(second, last, first)
        upper, lower = halves(jnp.where(second, first, last))
        message_ref[:, : self.shard_len] = x
        message_ref[:, self.shard_len : self.shard_len + 2 * self.width] = upper
        message_ref[:, self.shard_len + 2 * self.width :] = lower

    def relay_far(self, index_ref, keep_ref, message_ref, out_refs):
        upper = message_ref[:, self.shard_len : self.shard_len + 2 * self.width].astype(F32)
        lower = message_ref[:, self.shard_len + 2 * self.width :].astype(F32)
        total = (keep_ref[...] + (upper + lower)).astype(BF16)
        odd = self.first_is_odd(index_ref)
        first, last = total[:, : self.width], total[:, self.width :]
        out_refs[0][...] = jnp.where(odd, last, first)
        out_refs[1][...] = jnp.where(odd, first, last)

    def far_sum(self, far_refs):
        return sum(ref[...].astype(F32) for ref in far_refs)

    def near_sums(self, x_ref, d_ref, acc_ref, first, start_ref=None):
        panels = [self.panel(x_ref, c) for c in range(self.per_device)]
        for r in range(self.per_device):
            value = None if start_ref is None else self.panel(start_ref, r)
            for c in range(self.per_device):
                offset = first + c - r
                if -REACH <= offset <= REACH:
                    term = dot_nt(panels[c], d_ref[r * SPAN + offset + REACH])
                    value = term if value is None else value + term
            acc_ref[:, r * self.size : (r + 1) * self.size] = value

    def halo_sums(self, below, x_ref, d_ref, acc_ref, start_ref):
        @pl.when(below)
        def _():
            self.near_sums(x_ref, d_ref, acc_ref, -self.per_device, start_ref)

        @pl.when(jnp.logical_not(below))
        def _():
            self.near_sums(x_ref, d_ref, acc_ref, self.per_device, start_ref)

    def far_halves(self, far_refs):
        return jnp.concatenate(halves(self.far_sum(far_refs)), axis=1)

    def next_panel(self, acc_ref, rb_ref, both, c):
        return (self.panel(acc_ref, c) + dot_nn(both, self.panel(rb_ref, c))).astype(BF16)

    def next_block(self, acc_ref, rb_ref, far_refs):
        both = self.far_halves(far_refs)
        panels = [self.next_panel(acc_ref, rb_ref, both, c) for c in range(self.per_device)]
        return jnp.concatenate(panels, axis=1)


def prepare_kernel(plan, index_ref, *refs):
    sources, refs = refs[:7], refs[7:]
    x_ref, g_ref, cb_ref, near_ref, offsets_ref = refs[:5]
    sends, (rows_ref, cols_ref, col_ref, coup_ref, sum_ref, sems) = refs[5:-6], refs[-6:]
    targets = (near_ref, offsets_ref, rows_ref, cols_ref, x_ref, col_ref, coup_ref)
    copies = [
        pltpu.make_async_copy(source, target, sems.at[i])
        for i, (source, target) in enumerate(zip(sources, targets))
    ]
    for copy in copies:
        copy.start()
    rank, size = plan.rank, plan.size
    cb_ref[...] = jnp.zeros_like(cb_ref)
    sum_ref[...] = jnp.zeros_like(sum_ref)
    for copy in copies:
        copy.wait()
    for c in range(plan.per_device):
        cb_ref[c * rank : (c + 1) * rank, c * size : (c + 1) * size] = col_ref[c]
    column = lax.broadcasted_iota(jnp.int32, (rank, plan.width), 1) // rank
    shift = 0 if plan.paired else plan.member(index_ref)
    for s in range(plan.slots):
        row = lax.rem(rows_ref[s], plan.block_clusters)
        step = lax.rem(lax.div(row, plan.per_device) - shift + plan.members, plan.members)
        place = step * plan.per_device + lax.rem(row, plan.per_device)
        if len(plan.hops) > 1:
            level = lax.div(rows_ref[s], plan.block_clusters)
            index = sum(jnp.where(level == i, index, 0) for i, index in enumerate(plan.set_of))
        else:
            index = 0
        where = (index, pl.ds(pl.multiple_of(place * rank, rank), rank), slice(None))
        tile = coup_ref[s].astype(F32)
        wide = jnp.where(column == cols_ref[s], jnp.concatenate([tile] * plan.per_device, axis=1), 0.0)
        sum_ref[where] = sum_ref[where] + wide
    for index in range(len(plan.hops)):
        g_ref[index] = jnp.concatenate(halves(sum_ref[index]), axis=1)
    plan.send_far(index_ref, x_ref[...], cb_ref, g_ref, sends)


def relay_kernel(plan, index_ref, keep_ref, message_ref, *out_refs):
    plan.relay_far(index_ref, keep_ref, message_ref, out_refs)


def first_own_kernel(plan, *refs):
    index_ref, rows_ref, offsets_ref, x_ref, near_ref, row_ref, tiles_ref = refs[:7]
    acc_ref, d_ref, rb_ref = refs[-3:]
    rank, size = plan.rank, plan.size
    for cell in range(plan.cells):
        d_ref[cell] = jnp.zeros(d_ref.shape[1:], d_ref.dtype)
    for s in range(plan.tiles):
        d_ref[rows_ref[s] * SPAN + offsets_ref[s] + REACH] = tiles_ref[s]
    rb_ref[...] = jnp.zeros_like(rb_ref)
    for c in range(plan.per_device):
        for start in (c * rank, plan.width + c * rank):
            rb_ref[start : start + rank, c * size : (c + 1) * size] = row_ref[c]
    plan.near_sums(x_ref, d_ref, acc_ref, 0)
    plan.halo_sums(lax.rem(index_ref[0], 2) == 1, near_ref, d_ref, acc_ref, acc_ref)


def own_kernel(plan, slot, *refs):
    index_ref, x_ref, near_ref, d_ref = refs[:4]
    acc_ref, krylov_ref, sem = refs[-3:]
    copy = pltpu.make_async_copy(x_ref, krylov_ref.at[slot], sem)
    copy.start()
    plan.near_sums(x_ref, d_ref, acc_ref, 0)
    plan.halo_sums(lax.rem(index_ref[0], 2) == 1, near_ref, d_ref, acc_ref, acc_ref)
    copy.wait()


def halo_kernel(plan, index_ref, acc_ref, over_ref, d_ref, *refs):
    plan.halo_sums(lax.rem(index_ref[0], 2) == 0, over_ref, d_ref, refs[-1], acc_ref)


def finish_kernel(plan, fars, *refs):
    index_ref, acc_ref, rb_ref, cb_ref, g_ref = refs[:5]
    far_refs, (x_ref, *sends) = refs[5 : 5 + fars], refs[5 + fars :]
    x = plan.next_block(acc_ref, rb_ref, far_refs)
    x_ref[...] = x
    plan.send_far(index_ref, x, cb_ref, g_ref, sends)


def last_kernel(plan, fars, slot, *refs):
    acc_ref, rb_ref = refs[:2]
    far_refs, (_, krylov_ref, x_ref, sem) = refs[2 : 2 + fars], refs[2 + fars :]
    both = plan.far_halves(far_refs)
    copies = []
    for c in range(plan.per_device):
        columns = pl.ds(c * plan.size, plan.size)
        x_ref[:, columns] = plan.next_panel(acc_ref, rb_ref, both, c)
        copies.append(
            pltpu.make_async_copy(x_ref.at[:, columns], krylov_ref.at[slot, :, columns], sem.at[c])
        )
        copies[-1].start()
    for copy in copies:
        copy.wait()


def call(kernel, name, ins, specs, outs, out_specs=None, scratch=(), aliases=None):
    spaces = {id(IN_VMEM): pltpu.VMEM, id(IN_HBM): pltpu.HBM}
    ins = [
        pltpu.with_memory_space_constraint(v, spaces[id(spec)]) if id(spec) in spaces else v
        for v, spec in zip(ins, specs)
    ]
    return pl.pallas_call(
        kernel,
        in_specs=list(specs),
        out_specs=out_specs or [IN_VMEM] * len(outs),
        out_shape=list(outs),
        scratch_shapes=list(scratch),
        input_output_aliases=aliases or {},
        compiler_params=pltpu.CompilerParams(vmem_limit_bytes=16 * 2**20),
        cost_estimate=pl.CostEstimate(flops=10**9, bytes_accessed=2**22, transcendentals=0),
        name=name,
    )(*ins)


def on_device(
    block, near_tiles, near_rows, near_offsets, col_basis, couplings, far_rows, far_cols, row_basis
):
    axes = ("loop", "far")
    plan = Plan(
        block.shape, near_tiles.shape, couplings.shape, lax.axis_size("far"), lax.axis_size("loop")
    )
    rhs, shard_len, width = plan.rhs, plan.shard_len, plan.width
    block_out = pltpu.VMEM((rhs, shard_len), BF16)
    acc_out = pltpu.VMEM((rhs, shard_len), F32)
    relay_out = pltpu.VMEM((rhs, width), BF16)
    krylov_out = jax.ShapeDtypeStruct((PRODUCTS, rhs, shard_len), BF16)
    if plan.paired:
        sends_out = [
            pltpu.VMEM((rhs, shard_len + 4 * width), BF16),
            pltpu.VMEM((rhs, 2 * width), F32),
        ]
    else:
        sends_out = [pltpu.VMEM((rhs, width), BF16)] * len(plan.routes)
    index = lax.axis_index(axes).astype(jnp.int32).reshape(1)

    def scratch_for(*arrays):
        return [
            pltpu.SMEM(v.shape, v.dtype) if v.dtype == jnp.int32 else pltpu.VMEM(v.shape, v.dtype)
            for v in arrays
        ]

    current, sends, krylov = block, None, None
    for product in range(PRODUCTS):
        if product == 0:
            ins = [near_rows, near_offsets, far_rows, far_cols, block, col_basis, couplings]
            matrix = (len(plan.hops), plan.members * width, 2 * width)
            current, coupled, col_wide, row_slots, offset_slots, *sends = call(
                functools.partial(prepare_kernel, plan),
                "prepare",
                [index, *ins],
                [IN_SMEM] + [IN_HBM] * 7,
                [
                    block_out,
                    pltpu.VMEM(matrix, BF16),
                    pltpu.VMEM((width, shard_len), BF16),
                    *scratch_for(near_rows, near_offsets),
                    *sends_out,
                ],
                [IN_VMEM] * 3 + [IN_SMEM] * 2 + [IN_VMEM] * len(sends_out),
                scratch=scratch_for(far_rows, far_cols, col_basis, couplings)
                + [pltpu.VMEM(matrix[:2] + (width,), F32), pltpu.SemaphoreType.DMA((7,))],
            )
        over = lax.ppermute(current, axes, plan.over)
        near = lax.ppermute(sends[0] if plan.paired else current, axes, plan.near)
        if plan.paired:
            sends = call(
                functools.partial(relay_kernel, plan),
                "relay",
                [index, sends[1], near],
                [IN_SMEM] + [IN_VMEM] * 2,
                [relay_out] * 2,
            )
            routes = plan.across
        else:
            routes = plan.routes
        fars = [lax.ppermute(s, axes, route) for s, route in zip(sends, routes)]
        after = sends if plan.paired else []
        if product == 0:
            ins = [index, row_slots, offset_slots, current, near, row_basis, near_tiles, *after]
            acc, dense, row_wide = call(
                functools.partial(first_own_kernel, plan),
                "first_own",
                ins,
                [IN_SMEM] * 3 + [IN_VMEM] * 2 + [PREFETCHED] * 2 + [ANYWHERE] * len(after),
                [
                    acc_out,
                    pltpu.VMEM((plan.cells, plan.size, plan.size), BF16),
                    pltpu.VMEM((2 * width, shard_len), BF16),
                ],
            )
        else:
            ins = [index, current, near, dense, *after] + ([krylov] if product > 1 else [])
            acc, krylov = call(
                functools.partial(own_kernel, plan, product - 1),
                "own",
                ins,
                [IN_SMEM] + [IN_VMEM] * 3 + [ANYWHERE] * (len(ins) - 4),
                [acc_out, krylov_out],
                [IN_VMEM, ANYWHERE],
                [pltpu.SemaphoreType.DMA],
                {len(ins) - 1: 1} if product > 1 else None,
            )
        (acc,) = call(
            functools.partial(halo_kernel, plan),
            "halo",
            [index, acc, over, dense],
            [IN_SMEM] + [IN_VMEM] * 3,
            [acc_out],
        )
        if product < PRODUCTS - 1:
            ins = [index, acc, row_wide, col_wide, coupled, *fars]
            current, *sends = call(
                functools.partial(finish_kernel, plan, len(fars)),
                "finish",
                ins,
                [IN_SMEM] + [IN_VMEM] * (len(ins) - 1),
                [block_out, *sends_out],
            )
        else:
            ins = [acc, row_wide, *fars, krylov]
            (krylov,) = call(
                functools.partial(last_kernel, plan, len(fars), product),
                "last",
                ins,
                [IN_VMEM] * (len(ins) - 1) + [ANYWHERE],
                [krylov_out],
                [ANYWHERE],
                [
                    pltpu.VMEM((rhs, shard_len), BF16),
                    pltpu.SemaphoreType.DMA((plan.per_device,)),
                ],
                {len(ins) - 1: 0},
            )
    return krylov


def solution(mesh):
    split = ("groups", "loop", "far")
    wide, narrow = P(split, None, None), P(split)
    in_specs = (P(None, split), wide, narrow, narrow, wide, wide, narrow, narrow, wide)
    return jax.shard_map(
        on_device, mesh=mesh, in_specs=in_specs, out_specs=P(None, None, split), check_vma=False
    )
```

```python
import functools

import jax
import jax.numpy as jnp
from jax import lax
from jax.experimental import pallas as pl
from jax.experimental.pallas import tpu as pltpu
from jax.sharding import PartitionSpec as P

PRODUCTS = 4
REACH = 4
LEVELS = 3
SPAN = 2 * REACH + 1
TURNED = 0b10000001

F32 = jnp.float32
BF16 = jnp.bfloat16
IN_VMEM = pl.BlockSpec(memory_space=pltpu.VMEM)
PREFETCHED = pl.BlockSpec(memory_space=pltpu.VMEM)
IN_SMEM = pl.BlockSpec(memory_space=pltpu.SMEM)
IN_HBM = pl.BlockSpec(memory_space=pltpu.HBM)
ANYWHERE = pl.BlockSpec(memory_space=pl.ANY)


def dot_nt(a, b):
    return lax.dot_general(a, b, (((1,), (1,)), ((), ())), preferred_element_type=F32)


def dot_nn(a, b):
    return lax.dot_general(a, b, (((1,), (0,)), ((), ())), preferred_element_type=F32)


def halves(value):
    upper = value.astype(BF16)
    return upper, (value - upper.astype(F32)).astype(BF16)


class Plan:
    def __init__(self, block_shape, tile_shape, coupling_shape, members, loop_size):
        self.rhs, self.shard_len = block_shape
        self.tiles, self.size, _ = tile_shape
        self.slots, self.rank, _ = coupling_shape
        self.members, self.loop_size = members, loop_size
        self.per_device = self.shard_len // self.size
        self.width = self.per_device * self.rank
        self.cells = self.per_device * SPAN
        self.block_clusters = self.per_device * members
        distances = [d % loop_size for d in (2, loop_size - 2, loop_size // 2)]
        self.hops = sorted(set(distances))
        self.set_of = [self.hops.index(d) for d in distances]
        self.paired = len(self.hops) == 1 and 2 * self.hops[0] == loop_size and members == 4
        devices = members * loop_size
        self.near = [(i, i ^ 1) for i in range(devices)]
        self.over = [(i, (i + 1 if i % 2 else i - 1) % devices) for i in range(devices)]
        places = [(l, m) for l in range(loop_size) for m in range(members)]
        self.across = [
            [
                (l * members + m, (l + self.hops[0]) % loop_size * members + self.far_target(l, m)[turn])
                for l, m in places
            ]
            for turn in range(2)
        ]
        self.routes = [
            [(l * members + m, (l + hop) % loop_size * members + (m + step) % members) for l, m in places]
            for hop in self.hops
            for step in range(members)
        ]

    def far_target(self, loop_index, member):
        block = (loop_index + self.hops[0]) % self.loop_size
        pair, core = divmod(member, 2)
        chip = block * 2 + core
        first = pair ^ (TURNED >> chip & 1)
        return 2 * chip % self.members + first, 2 * chip % self.members + (first ^ 1)

    def first_is_odd(self, index_ref):
        index = index_ref[0]
        block = lax.rem(lax.div(index, self.members) + self.hops[0], self.loop_size)
        pair, core = lax.div(self.member(index_ref), 2), lax.rem(index, 2)
        turned = lax.bitwise_and(lax.shift_right_logical(jnp.int32(TURNED), block * 2 + core), 1)
        return lax.bitwise_xor(pair, turned) == 1

    def panel(self, ref, c):
        return ref[:, c * self.size : (c + 1) * self.size]

    def member(self, index_ref):
        return lax.rem(index_ref[0], self.members)

    def send_far(self, index_ref, x, cb_ref, g_ref, out_refs):
        coeffs = dot_nt(x, cb_ref[...]).astype(BF16)
        twice = jnp.concatenate([coeffs, coeffs], axis=1)
        totals = [dot_nt(twice, g_ref[index]) for index in range(len(self.hops))]
        if not self.paired:
            for i, out_ref in enumerate(out_refs):
                step = i % self.members * self.width
                out_ref[...] = totals[i // self.members][:, step : step + self.width].astype(BF16)
            return
        message_ref, keep_ref = out_refs
        (total,) = totals
        member = self.member(index_ref)
        second = lax.rem(member, 2) == 1
        first, last = total[:, : 2 * self.width], total[:, 2 * self.width :]
        keep_ref[...] = jnp.where(second, last, first)
        upper, lower = halves(jnp.where(second, first, last))
        message_ref[:, : self.shard_len] = x
        message_ref[:, self.shard_len : self.shard_len + 2 * self.width] = upper
        message_ref[:, self.shard_len + 2 * self.width :] = lower

    def relay_far(self, index_ref, keep_ref, message_ref, out_refs):
        upper = message_ref[:, self.shard_len : self.shard_len + 2 * self.width].astype(F32)
        lower = message_ref[:, self.shard_len + 2 * self.width :].astype(F32)
        total = (keep_ref[...] + (upper + lower)).astype(BF16)
        odd = self.first_is_odd(index_ref)
        first, last = total[:, : self.width], total[:, self.width :]
        out_refs[0][...] = jnp.where(odd, last, first)
        out_refs[1][...] = jnp.where(odd, first, last)

    def far_sum(self, far_refs):
        return sum(ref[...].astype(F32) for ref in far_refs)

    def near_sums(self, x_ref, d_ref, acc_ref, first, start_ref=None):
        panels = [self.panel(x_ref, c) for c in range(self.per_device)]
        for r in range(self.per_device):
            value = None if start_ref is None else self.panel(start_ref, r)
            for c in range(self.per_device):
                offset = first + c - r
                if -REACH <= offset <= REACH:
                    term = dot_nt(panels[c], d_ref[r * SPAN + offset + REACH])
                    value = term if value is None else value + term
            acc_ref[:, r * self.size : (r + 1) * self.size] = value

    def halo_sums(self, below, x_ref, d_ref, acc_ref, start_ref):
        @pl.when(below)
        def _():
            self.near_sums(x_ref, d_ref, acc_ref, -self.per_device, start_ref)

        @pl.when(jnp.logical_not(below))
        def _():
            self.near_sums(x_ref, d_ref, acc_ref, self.per_device, start_ref)

    def far_halves(self, far_refs):
        return jnp.concatenate(halves(self.far_sum(far_refs)), axis=1)

    def next_panel(self, acc_ref, rb_ref, both, c):
        return (self.panel(acc_ref, c) + dot_nn(both, self.panel(rb_ref, c))).astype(BF16)

    def next_block(self, acc_ref, rb_ref, far_refs):
        both = self.far_halves(far_refs)
        panels = [self.next_panel(acc_ref, rb_ref, both, c) for c in range(self.per_device)]
        return jnp.concatenate(panels, axis=1)


def prepare_kernel(plan, index_ref, *refs):
    sources, refs = refs[:7], refs[7:]
    x_ref, g_ref, cb_ref, near_ref, offsets_ref = refs[:5]
    sends, (rows_ref, cols_ref, col_ref, coup_ref, sum_ref, sems) = refs[5:-6], refs[-6:]
    targets = (near_ref, offsets_ref, rows_ref, cols_ref, x_ref, col_ref, coup_ref)
    copies = [
        pltpu.make_async_copy(source, target, sems.at[i])
        for i, (source, target) in enumerate(zip(sources, targets))
    ]
    for copy in copies:
        copy.start()
    rank, size = plan.rank, plan.size
    cb_ref[...] = jnp.zeros_like(cb_ref)
    sum_ref[...] = jnp.zeros_like(sum_ref)
    for copy in copies:
        copy.wait()
    for c in range(plan.per_device):
        cb_ref[c * rank : (c + 1) * rank, c * size : (c + 1) * size] = col_ref[c]
    column = lax.broadcasted_iota(jnp.int32, (rank, plan.width), 1) // rank
    shift = 0 if plan.paired else plan.member(index_ref)
    for s in range(plan.slots):
        row = lax.rem(rows_ref[s], plan.block_clusters)
        step = lax.rem(lax.div(row, plan.per_device) - shift + plan.members, plan.members)
        place = step * plan.per_device + lax.rem(row, plan.per_device)
        if len(plan.hops) > 1:
            level = lax.div(rows_ref[s], plan.block_clusters)
            index = sum(jnp.where(level == i, index, 0) for i, index in enumerate(plan.set_of))
        else:
            index = 0
        where = (index, pl.ds(pl.multiple_of(place * rank, rank), rank), slice(None))
        tile = coup_ref[s].astype(F32)
        wide = jnp.where(column == cols_ref[s], jnp.concatenate([tile] * plan.per_device, axis=1), 0.0)
        sum_ref[where] = sum_ref[where] + wide
    for index in range(len(plan.hops)):
        g_ref[index] = jnp.concatenate(halves(sum_ref[index]), axis=1)
    plan.send_far(index_ref, x_ref[...], cb_ref, g_ref, sends)


def relay_kernel(plan, index_ref, keep_ref, message_ref, *out_refs):
    plan.relay_far(index_ref, keep_ref, message_ref, out_refs)


def first_own_kernel(plan, *refs):
    index_ref, rows_ref, offsets_ref, x_ref, near_ref, row_ref, tiles_ref = refs[:7]
    acc_ref, d_ref, rb_ref = refs[-3:]
    rank, size = plan.rank, plan.size
    for cell in range(plan.cells):
        d_ref[cell] = jnp.zeros(d_ref.shape[1:], d_ref.dtype)
    for s in range(plan.tiles):
        d_ref[rows_ref[s] * SPAN + offsets_ref[s] + REACH] = tiles_ref[s]
    rb_ref[...] = jnp.zeros_like(rb_ref)
    for c in range(plan.per_device):
        for start in (c * rank, plan.width + c * rank):
            rb_ref[start : start + rank, c * size : (c + 1) * size] = row_ref[c]
    plan.near_sums(x_ref, d_ref, acc_ref, 0)
    plan.halo_sums(lax.rem(index_ref[0], 2) == 1, near_ref, d_ref, acc_ref, acc_ref)


def own_kernel(plan, slot, *refs):
    index_ref, x_ref, near_ref, d_ref = refs[:4]
    acc_ref, krylov_ref, sem = refs[-3:]
    copy = pltpu.make_async_copy(x_ref, krylov_ref.at[slot], sem)
    copy.start()
    plan.near_sums(x_ref, d_ref, acc_ref, 0)
    plan.halo_sums(lax.rem(index_ref[0], 2) == 1, near_ref, d_ref, acc_ref, acc_ref)
    copy.wait()


def halo_kernel(plan, index_ref, acc_ref, over_ref, d_ref, *refs):
    plan.halo_sums(lax.rem(index_ref[0], 2) == 0, over_ref, d_ref, refs[-1], acc_ref)


def finish_kernel(plan, fars, *refs):
    index_ref, acc_ref, rb_ref, cb_ref, g_ref = refs[:5]
    far_refs, (x_ref, *sends) = refs[5 : 5 + fars], refs[5 + fars :]
    x = plan.next_block(acc_ref, rb_ref, far_refs)
    x_ref[...] = x
    plan.send_far(index_ref, x, cb_ref, g_ref, sends)


def last_kernel(plan, fars, slot, *refs):
    acc_ref, rb_ref = refs[:2]
    far_refs, (_, krylov_ref, x_ref, sem) = refs[2 : 2 + fars], refs[2 + fars :]
    both = plan.far_halves(far_refs)
    copies = []
    for c in range(plan.per_device):
        columns = pl.ds(c * plan.size, plan.size)
        x_ref[:, columns] = plan.next_panel(acc_ref, rb_ref, both, c)
        copies.append(
            pltpu.make_async_copy(x_ref.at[:, columns], krylov_ref.at[slot, :, columns], sem.at[c])
        )
        copies[-1].start()
    for copy in copies:
        copy.wait()


def call(kernel, name, ins, specs, outs, out_specs=None, scratch=(), aliases=None):
    spaces = {id(IN_VMEM): pltpu.VMEM, id(IN_HBM): pltpu.HBM}
    ins = [
        pltpu.with_memory_space_constraint(v, spaces[id(spec)]) if id(spec) in spaces else v
        for v, spec in zip(ins, specs)
    ]
    return pl.pallas_call(
        kernel,
        in_specs=list(specs),
        out_specs=out_specs or [IN_VMEM] * len(outs),
        out_shape=list(outs),
        scratch_shapes=list(scratch),
        input_output_aliases=aliases or {},
        compiler_params=pltpu.CompilerParams(vmem_limit_bytes=16 * 2**20),
        cost_estimate=pl.CostEstimate(flops=10**9, bytes_accessed=2**22, transcendentals=0),
        name=name,
    )(*ins)


def on_device(
    block, near_tiles, near_rows, near_offsets, col_basis, couplings, far_rows, far_cols, row_basis
):
    axes = ("loop", "far")
    plan = Plan(
        block.shape, near_tiles.shape, couplings.shape, lax.axis_size("far"), lax.axis_size("loop")
    )
    rhs, shard_len, width = plan.rhs, plan.shard_len, plan.width
    block_out = pltpu.VMEM((rhs, shard_len), BF16)
    acc_out = pltpu.VMEM((rhs, shard_len), F32)
    relay_out = pltpu.VMEM((rhs, width), BF16)
    krylov_out = jax.ShapeDtypeStruct((PRODUCTS, rhs, shard_len), BF16)
    if plan.paired:
        sends_out = [
            pltpu.VMEM((rhs, shard_len + 4 * width), BF16),
            pltpu.VMEM((rhs, 2 * width), F32),
        ]
    else:
        sends_out = [pltpu.VMEM((rhs, width), BF16)] * len(plan.routes)
    index = lax.axis_index(axes).astype(jnp.int32).reshape(1)

    def scratch_for(*arrays):
        return [
            pltpu.SMEM(v.shape, v.dtype) if v.dtype == jnp.int32 else pltpu.VMEM(v.shape, v.dtype)
            for v in arrays
        ]

    current, sends, krylov = block, None, None
    for product in range(PRODUCTS):
        if product == 0:
            ins = [near_rows, near_offsets, far_rows, far_cols, block, col_basis, couplings]
            matrix = (len(plan.hops), plan.members * width, 2 * width)
            current, coupled, col_wide, row_slots, offset_slots, *sends = call(
                functools.partial(prepare_kernel, plan),
                "prepare",
                [index, *ins],
                [IN_SMEM] + [IN_HBM] * 7,
                [
                    block_out,
                    pltpu.VMEM(matrix, BF16),
                    pltpu.VMEM((width, shard_len), BF16),
                    *scratch_for(near_rows, near_offsets),
                    *sends_out,
                ],
                [IN_VMEM] * 3 + [IN_SMEM] * 2 + [IN_VMEM] * len(sends_out),
                scratch=scratch_for(far_rows, far_cols, col_basis, couplings)
                + [pltpu.VMEM(matrix[:2] + (width,), F32), pltpu.SemaphoreType.DMA((7,))],
            )
        over = lax.ppermute(current, axes, plan.over)
        near = lax.ppermute(sends[0] if plan.paired else current, axes, plan.near)
        if plan.paired:
            sends = call(
                functools.partial(relay_kernel, plan),
                "relay",
                [index, sends[1], near],
                [IN_SMEM] + [IN_VMEM] * 2,
                [relay_out] * 2,
            )
            routes = plan.across
        else:
            routes = plan.routes
        fars = [lax.ppermute(s, axes, route) for s, route in zip(sends, routes)]
        after = sends if plan.paired else []
        if product == 0:
            ins = [index, row_slots, offset_slots, current, near, row_basis, near_tiles, *after]
            acc, dense, row_wide = call(
                functools.partial(first_own_kernel, plan),
                "first_own",
                ins,
                [IN_SMEM] * 3 + [IN_VMEM] * 2 + [PREFETCHED] * 2 + [ANYWHERE] * len(after),
                [
                    acc_out,
                    pltpu.VMEM((plan.cells, plan.size, plan.size), BF16),
                    pltpu.VMEM((2 * width, shard_len), BF16),
                ],
            )
        else:
            ins = [index, current, near, dense, *after] + ([krylov] if product > 1 else [])
            acc, krylov = call(
                functools.partial(own_kernel, plan, product - 1),
                "own",
                ins,
                [IN_SMEM] + [IN_VMEM] * 3 + [ANYWHERE] * (len(ins) - 4),
                [acc_out, krylov_out],
                [IN_VMEM, ANYWHERE],
                [pltpu.SemaphoreType.DMA],
                {len(ins) - 1: 1} if product > 1 else None,
            )
        (acc,) = call(
            functools.partial(halo_kernel, plan),
            "halo",
            [index, acc, over, dense],
            [IN_SMEM] + [IN_VMEM] * 3,
            [acc_out],
        )
        if product < PRODUCTS - 1:
            ins = [index, acc, row_wide, col_wide, coupled, *fars]
            current, *sends = call(
                functools.partial(finish_kernel, plan, len(fars)),
                "finish",
                ins,
                [IN_SMEM] + [IN_VMEM] * (len(ins) - 1),
                [block_out, *sends_out],
            )
        else:
            ins = [acc, row_wide, *fars, krylov]
            (krylov,) = call(
                functools.partial(last_kernel, plan, len(fars), product),
                "last",
                ins,
                [IN_VMEM] * (len(ins) - 1) + [ANYWHERE],
                [krylov_out],
                [ANYWHERE],
                [
                    pltpu.VMEM((rhs, shard_len), BF16),
                    pltpu.SemaphoreType.DMA((plan.per_device,)),
                ],
                {len(ins) - 1: 0},
            )
    return krylov


def solution(mesh):
    split = ("groups", "loop", "far")
    wide, narrow = P(split, None, None), P(split)
    in_specs = (P(None, split), wide, narrow, narrow, wide, wide, narrow, narrow, wide)
    return jax.shard_map(
        on_device, mesh=mesh, in_specs=in_specs, out_specs=P(None, None, split), check_vma=False
    )
```

```python
import functools

import jax
import jax.numpy as jnp
from jax import lax
from jax.experimental import pallas as pl
from jax.experimental.pallas import tpu as pltpu
from jax.sharding import PartitionSpec as P

PRODUCTS = 4
REACH = 4
LEVELS = 3
SPAN = 2 * REACH + 1
TURNED = 0

F32 = jnp.float32
BF16 = jnp.bfloat16
IN_VMEM = pl.BlockSpec(memory_space=pltpu.VMEM)
PREFETCHED = pl.BlockSpec(memory_space=pltpu.VMEM)
IN_SMEM = pl.BlockSpec(memory_space=pltpu.SMEM)
IN_HBM = pl.BlockSpec(memory_space=pltpu.HBM)
ANYWHERE = pl.BlockSpec(memory_space=pl.ANY)


def dot_nt(a, b):
    return lax.dot_general(a, b, (((1,), (1,)), ((), ())), preferred_element_type=F32)


def dot_nn(a, b):
    return lax.dot_general(a, b, (((1,), (0,)), ((), ())), preferred_element_type=F32)


def halves(value):
    upper = value.astype(BF16)
    return upper, (value - upper.astype(F32)).astype(BF16)


class Plan:
    def __init__(self, block_shape, tile_shape, coupling_shape, members, loop_size):
        self.rhs, self.shard_len = block_shape
        self.tiles, self.size, _ = tile_shape
        self.slots, self.rank, _ = coupling_shape
        self.members, self.loop_size = members, loop_size
        self.per_device = self.shard_len // self.size
        self.width = self.per_device * self.rank
        self.cells = self.per_device * SPAN
        self.block_clusters = self.per_device * members
        distances = [d % loop_size for d in (2, loop_size - 2, loop_size // 2)]
        self.hops = sorted(set(distances))
        self.set_of = [self.hops.index(d) for d in distances]
        self.paired = len(self.hops) == 1 and 2 * self.hops[0] == loop_size and members == 4
        devices = members * loop_size
        self.near = [(i, i ^ 1) for i in range(devices)]
        self.over = [(i, (i + 1 if i % 2 else i - 1) % devices) for i in range(devices)]
        places = [(l, m) for l in range(loop_size) for m in range(members)]
        self.across = [
            [
                (l * members + m, (l + self.hops[0]) % loop_size * members + self.far_target(l, m)[turn])
                for l, m in places
            ]
            for turn in range(2)
        ]
        self.routes = [
            [(l * members + m, (l + hop) % loop_size * members + (m + step) % members) for l, m in places]
            for hop in self.hops
            for step in range(members)
        ]

    def far_target(self, loop_index, member):
        block = (loop_index + self.hops[0]) % self.loop_size
        pair, core = divmod(member, 2)
        chip = block * 2 + core
        first = pair ^ (TURNED >> chip & 1)
        return 2 * chip % self.members + first, 2 * chip % self.members + (first ^ 1)

    def first_is_odd(self, index_ref):
        index = index_ref[0]
        block = lax.rem(lax.div(index, self.members) + self.hops[0], self.loop_size)
        pair, core = lax.div(self.member(index_ref), 2), lax.rem(index, 2)
        turned = lax.bitwise_and(lax.shift_right_logical(jnp.int32(TURNED), block * 2 + core), 1)
        return lax.bitwise_xor(pair, turned) == 1

    def panel(self, ref, c):
        return ref[:, c * self.size : (c + 1) * self.size]

    def member(self, index_ref):
        return lax.rem(index_ref[0], self.members)

    def send_far(self, index_ref, x, cb_ref, g_ref, out_refs):
        coeffs = dot_nt(x, cb_ref[...]).astype(BF16)
        twice = jnp.concatenate([coeffs, coeffs], axis=1)
        totals = [dot_nt(twice, g_ref[index]) for index in range(len(self.hops))]
        if not self.paired:
            for i, out_ref in enumerate(out_refs):
                step = i % self.members * self.width
                out_ref[...] = totals[i // self.members][:, step : step + self.width].astype(BF16)
            return
        message_ref, keep_ref = out_refs
        (total,) = totals
        member = self.member(index_ref)
        second = lax.rem(member, 2) == 1
        first, last = total[:, : 2 * self.width], total[:, 2 * self.width :]
        keep_ref[...] = jnp.where(second, last, first)
        upper, lower = halves(jnp.where(second, first, last))
        message_ref[:, : self.shard_len] = x
        message_ref[:, self.shard_len : self.shard_len + 2 * self.width] = upper
        message_ref[:, self.shard_len + 2 * self.width :] = lower

    def relay_far(self, index_ref, keep_ref, message_ref, out_refs):
        upper = message_ref[:, self.shard_len : self.shard_len + 2 * self.width].astype(F32)
        lower = message_ref[:, self.shard_len + 2 * self.width :].astype(F32)
        total = (keep_ref[...] + (upper + lower)).astype(BF16)
        odd = self.first_is_odd(index_ref)
        first, last = total[:, : self.width], total[:, self.width :]
        out_refs[0][...] = jnp.where(odd, last, first)
        out_refs[1][...] = jnp.where(odd, first, last)

    def far_sum(self, far_refs):
        return sum(ref[...].astype(F32) for ref in far_refs)

    def near_sums(self, x_ref, d_ref, acc_ref, first, start_ref=None):
        panels = [self.panel(x_ref, c) for c in range(self.per_device)]
        for r in range(self.per_device):
            value = None if start_ref is None else self.panel(start_ref, r)
            for c in range(self.per_device):
                offset = first + c - r
                if -REACH <= offset <= REACH:
                    term = dot_nt(panels[c], d_ref[r * SPAN + offset + REACH])
                    value = term if value is None else value + term
            acc_ref[:, r * self.size : (r + 1) * self.size] = value

    def halo_sums(self, below, x_ref, d_ref, acc_ref, start_ref):
        @pl.when(below)
        def _():
            self.near_sums(x_ref, d_ref, acc_ref, -self.per_device, start_ref)

        @pl.when(jnp.logical_not(below))
        def _():
            self.near_sums(x_ref, d_ref, acc_ref, self.per_device, start_ref)

    def far_halves(self, far_refs):
        return jnp.concatenate(halves(self.far_sum(far_refs)), axis=1)

    def next_panel(self, acc_ref, rb_ref, both, c):
        return (self.panel(acc_ref, c) + dot_nn(both, self.panel(rb_ref, c))).astype(BF16)

    def next_block(self, acc_ref, rb_ref, far_refs):
        both = self.far_halves(far_refs)
        panels = [self.next_panel(acc_ref, rb_ref, both, c) for c in range(self.per_device)]
        return jnp.concatenate(panels, axis=1)


def prepare_kernel(plan, index_ref, *refs):
    sources, refs = refs[:7], refs[7:]
    x_ref, g_ref, cb_ref, near_ref, offsets_ref = refs[:5]
    sends, (rows_ref, cols_ref, col_ref, coup_ref, sum_ref, sems) = refs[5:-6], refs[-6:]
    targets = (near_ref, offsets_ref, rows_ref, cols_ref, x_ref, col_ref, coup_ref)
    copies = [
        pltpu.make_async_copy(source, target, sems.at[i])
        for i, (source, target) in enumerate(zip(sources, targets))
    ]
    for copy in copies:
        copy.start()
    rank, size = plan.rank, plan.size
    cb_ref[...] = jnp.zeros_like(cb_ref)
    sum_ref[...] = jnp.zeros_like(sum_ref)
    for copy in copies:
        copy.wait()
    for c in range(plan.per_device):
        cb_ref[c * rank : (c + 1) * rank, c * size : (c + 1) * size] = col_ref[c]
    column = lax.broadcasted_iota(jnp.int32, (rank, plan.width), 1) // rank
    shift = 0 if plan.paired else plan.member(index_ref)
    for s in range(plan.slots):
        row = lax.rem(rows_ref[s], plan.block_clusters)
        step = lax.rem(lax.div(row, plan.per_device) - shift + plan.members, plan.members)
        place = step * plan.per_device + lax.rem(row, plan.per_device)
        if len(plan.hops) > 1:
            level = lax.div(rows_ref[s], plan.block_clusters)
            index = sum(jnp.where(level == i, index, 0) for i, index in enumerate(plan.set_of))
        else:
            index = 0
        where = (index, pl.ds(pl.multiple_of(place * rank, rank), rank), slice(None))
        tile = coup_ref[s].astype(F32)
        wide = jnp.where(column == cols_ref[s], jnp.concatenate([tile] * plan.per_device, axis=1), 0.0)
        sum_ref[where] = sum_ref[where] + wide
    for index in range(len(plan.hops)):
        g_ref[index] = jnp.concatenate(halves(sum_ref[index]), axis=1)
    plan.send_far(index_ref, x_ref[...], cb_ref, g_ref, sends)


def relay_kernel(plan, index_ref, keep_ref, message_ref, *out_refs):
    plan.relay_far(index_ref, keep_ref, message_ref, out_refs)


def first_own_kernel(plan, *refs):
    index_ref, rows_ref, offsets_ref, x_ref, near_ref, row_ref, tiles_ref = refs[:7]
    acc_ref, d_ref, rb_ref = refs[-3:]
    rank, size = plan.rank, plan.size
    for cell in range(plan.cells):
        d_ref[cell] = jnp.zeros(d_ref.shape[1:], d_ref.dtype)
    for s in range(plan.tiles):
        d_ref[rows_ref[s] * SPAN + offsets_ref[s] + REACH] = tiles_ref[s]
    rb_ref[...] = jnp.zeros_like(rb_ref)
    for c in range(plan.per_device):
        for start in (c * rank, plan.width + c * rank):
            rb_ref[start : start + rank, c * size : (c + 1) * size] = row_ref[c]
    plan.near_sums(x_ref, d_ref, acc_ref, 0)
    plan.halo_sums(lax.rem(index_ref[0], 2) == 1, near_ref, d_ref, acc_ref, acc_ref)


def own_kernel(plan, slot, *refs):
    index_ref, x_ref, near_ref, d_ref = refs[:4]
    acc_ref, krylov_ref, sem = refs[-3:]
    copy = pltpu.make_async_copy(x_ref, krylov_ref.at[slot], sem)
    copy.start()
    plan.near_sums(x_ref, d_ref, acc_ref, 0)
    plan.halo_sums(lax.rem(index_ref[0], 2) == 1, near_ref, d_ref, acc_ref, acc_ref)
    copy.wait()


def halo_kernel(plan, index_ref, acc_ref, over_ref, d_ref, *refs):
    plan.halo_sums(lax.rem(index_ref[0], 2) == 0, over_ref, d_ref, refs[-1], acc_ref)


def finish_kernel(plan, fars, *refs):
    index_ref, acc_ref, rb_ref, cb_ref, g_ref = refs[:5]
    far_refs, (x_ref, *sends) = refs[5 : 5 + fars], refs[5 + fars :]
    x = plan.next_block(acc_ref, rb_ref, far_refs)
    x_ref[...] = x
    plan.send_far(index_ref, x, cb_ref, g_ref, sends)


def last_kernel(plan, fars, slot, *refs):
    acc_ref, rb_ref = refs[:2]
    far_refs, (_, krylov_ref, x_ref, sem) = refs[2 : 2 + fars], refs[2 + fars :]
    both = plan.far_halves(far_refs)
    copies = []
    for c in range(plan.per_device):
        columns = pl.ds(c * plan.size, plan.size)
        x_ref[:, columns] = plan.next_panel(acc_ref, rb_ref, both, c)
        copies.append(
            pltpu.make_async_copy(x_ref.at[:, columns], krylov_ref.at[slot, :, columns], sem.at[c])
        )
        copies[-1].start()
    for copy in copies:
        copy.wait()


def call(kernel, name, ins, specs, outs, out_specs=None, scratch=(), aliases=None):
    spaces = {id(IN_VMEM): pltpu.VMEM, id(IN_HBM): pltpu.HBM}
    ins = [
        pltpu.with_memory_space_constraint(v, spaces[id(spec)]) if id(spec) in spaces else v
        for v, spec in zip(ins, specs)
    ]
    return pl.pallas_call(
        kernel,
        in_specs=list(specs),
        out_specs=out_specs or [IN_VMEM] * len(outs),
        out_shape=list(outs),
        scratch_shapes=list(scratch),
        input_output_aliases=aliases or {},
        compiler_params=pltpu.CompilerParams(vmem_limit_bytes=16 * 2**20),
        cost_estimate=pl.CostEstimate(flops=10**9, bytes_accessed=2**22, transcendentals=0),
        name=name,
    )(*ins)


def on_device(
    block, near_tiles, near_rows, near_offsets, col_basis, couplings, far_rows, far_cols, row_basis
):
    axes = ("loop", "far")
    plan = Plan(
        block.shape, near_tiles.shape, couplings.shape, lax.axis_size("far"), lax.axis_size("loop")
    )
    rhs, shard_len, width = plan.rhs, plan.shard_len, plan.width
    block_out = pltpu.VMEM((rhs, shard_len), BF16)
    acc_out = pltpu.VMEM((rhs, shard_len), F32)
    relay_out = pltpu.VMEM((rhs, width), BF16)
    krylov_out = jax.ShapeDtypeStruct((PRODUCTS, rhs, shard_len), BF16)
    if plan.paired:
        sends_out = [
            pltpu.VMEM((rhs, shard_len + 4 * width), BF16),
            pltpu.VMEM((rhs, 2 * width), F32),
        ]
    else:
        sends_out = [pltpu.VMEM((rhs, width), BF16)] * len(plan.routes)
    index = lax.axis_index(axes).astype(jnp.int32).reshape(1)

    def scratch_for(*arrays):
        return [
            pltpu.SMEM(v.shape, v.dtype) if v.dtype == jnp.int32 else pltpu.VMEM(v.shape, v.dtype)
            for v in arrays
        ]

    current, sends, krylov = block, None, None
    for product in range(PRODUCTS):
        if product == 0:
            ins = [near_rows, near_offsets, far_rows, far_cols, block, col_basis, couplings]
            matrix = (len(plan.hops), plan.members * width, 2 * width)
            current, coupled, col_wide, row_slots, offset_slots, *sends = call(
                functools.partial(prepare_kernel, plan),
                "prepare",
                [index, *ins],
                [IN_SMEM] + [IN_HBM] * 7,
                [
                    block_out,
                    pltpu.VMEM(matrix, BF16),
                    pltpu.VMEM((width, shard_len), BF16),
                    *scratch_for(near_rows, near_offsets),
                    *sends_out,
                ],
                [IN_VMEM] * 3 + [IN_SMEM] * 2 + [IN_VMEM] * len(sends_out),
                scratch=scratch_for(far_rows, far_cols, col_basis, couplings)
                + [pltpu.VMEM(matrix[:2] + (width,), F32), pltpu.SemaphoreType.DMA((7,))],
            )
        over = lax.ppermute(current, axes, plan.over)
        near = lax.ppermute(sends[0] if plan.paired else current, axes, plan.near)
        if plan.paired:
            sends = call(
                functools.partial(relay_kernel, plan),
                "relay",
                [index, sends[1], near],
                [IN_SMEM] + [IN_VMEM] * 2,
                [relay_out] * 2,
            )
            routes = plan.across
        else:
            routes = plan.routes
        fars = [lax.ppermute(s, axes, route) for s, route in zip(sends, routes)]
        after = sends if plan.paired else []
        if product == 0:
            ins = [index, row_slots, offset_slots, current, near, row_basis, near_tiles, *after]
            acc, dense, row_wide = call(
                functools.partial(first_own_kernel, plan),
                "first_own",
                ins,
                [IN_SMEM] * 3 + [IN_VMEM] * 2 + [PREFETCHED] * 2 + [ANYWHERE] * len(after),
                [
                    acc_out,
                    pltpu.VMEM((plan.cells, plan.size, plan.size), BF16),
                    pltpu.VMEM((2 * width, shard_len), BF16),
                ],
            )
        else:
            ins = [index, current, near, dense, *after] + ([krylov] if product > 1 else [])
            acc, krylov = call(
                functools.partial(own_kernel, plan, product - 1),
                "own",
                ins,
                [IN_SMEM] + [IN_VMEM] * 3 + [ANYWHERE] * (len(ins) - 4),
                [acc_out, krylov_out],
                [IN_VMEM, ANYWHERE],
                [pltpu.SemaphoreType.DMA],
                {len(ins) - 1: 1} if product > 1 else None,
            )
        (acc,) = call(
            functools.partial(halo_kernel, plan),
            "halo",
            [index, acc, over, dense],
            [IN_SMEM] + [IN_VMEM] * 3,
            [acc_out],
        )
        if product < PRODUCTS - 1:
            ins = [index, acc, row_wide, col_wide, coupled, *fars]
            current, *sends = call(
                functools.partial(finish_kernel, plan, len(fars)),
                "finish",
                ins,
                [IN_SMEM] + [IN_VMEM] * (len(ins) - 1),
                [block_out, *sends_out],
            )
        else:
            ins = [acc, row_wide, *fars, krylov]
            (krylov,) = call(
                functools.partial(last_kernel, plan, len(fars), product),
                "last",
                ins,
                [IN_VMEM] * (len(ins) - 1) + [ANYWHERE],
                [krylov_out],
                [ANYWHERE],
                [
                    pltpu.VMEM((rhs, shard_len), BF16),
                    pltpu.SemaphoreType.DMA((plan.per_device,)),
                ],
                {len(ins) - 1: 0},
            )
    return krylov


def solution(mesh):
    split = ("groups", "loop", "far")
    wide, narrow = P(split, None, None), P(split)
    in_specs = (P(None, split), wide, narrow, narrow, wide, wide, narrow, narrow, wide)
    return jax.shard_map(
        on_device, mesh=mesh, in_specs=in_specs, out_specs=P(None, None, split), check_vma=False
    )
```

```python
import functools

import jax
import jax.numpy as jnp
from jax import lax
from jax.experimental import pallas as pl
from jax.experimental.pallas import tpu as pltpu
from jax.sharding import PartitionSpec as P

PRODUCTS = 4
REACH = 4
LEVELS = 3
SPAN = 2 * REACH + 1
OTHER_CORE_FIRST = 0b11011011

F32 = jnp.float32
BF16 = jnp.bfloat16
IN_VMEM = pl.BlockSpec(memory_space=pltpu.VMEM)
PREFETCHED = pl.BlockSpec(memory_space=pltpu.VMEM)
IN_SMEM = pl.BlockSpec(memory_space=pltpu.SMEM)
IN_HBM = pl.BlockSpec(memory_space=pltpu.HBM)
ANYWHERE = pl.BlockSpec(memory_space=pl.ANY)


def dot_nt(a, b):
    return lax.dot_general(a, b, (((1,), (1,)), ((), ())), preferred_element_type=F32)


def dot_nn(a, b):
    return lax.dot_general(a, b, (((1,), (0,)), ((), ())), preferred_element_type=F32)


def halves(value):
    upper = value.astype(BF16)
    return upper, (value - upper.astype(F32)).astype(BF16)


class Plan:
    def __init__(self, block_shape, tile_shape, coupling_shape, members, loop_size):
        self.rhs, self.shard_len = block_shape
        self.tiles, self.size, _ = tile_shape
        self.slots, self.rank, _ = coupling_shape
        self.members, self.loop_size = members, loop_size
        self.per_device = self.shard_len // self.size
        self.width = self.per_device * self.rank
        self.cells = self.per_device * SPAN
        self.block_clusters = self.per_device * members
        distances = [d % loop_size for d in (2, loop_size - 2, loop_size // 2)]
        self.hops = sorted(set(distances))
        self.set_of = [self.hops.index(d) for d in distances]
        self.paired = len(self.hops) == 1 and 2 * self.hops[0] == loop_size and members == 4
        devices = members * loop_size
        self.near = [(i, i ^ 1) for i in range(devices)]
        self.over = [(i, (i + 1 if i % 2 else i - 1) % devices) for i in range(devices)]
        places = [(l, m) for l in range(loop_size) for m in range(members)]
        self.across = [
            [
                (l * members + m, self.far_target(l, m)[turn])
                for l, m in places
            ]
            for turn in range(2)
        ]
        self.routes = [
            [(l * members + m, (l + hop) % loop_size * members + (m + step) % members) for l, m in places]
            for hop in self.hops
            for step in range(members)
        ]

    def far_target(self, loop_index, member):
        block = (loop_index + self.hops[0]) % self.loop_size
        pair, core = divmod(member, 2)
        chip = block * 2 + (pair ^ core)
        first = core ^ (OTHER_CORE_FIRST >> chip & 1)
        return 2 * chip + first, 2 * chip + (first ^ 1)

    def first_is_odd(self, index_ref):
        index = index_ref[0]
        block = lax.rem(lax.div(index, self.members) + self.hops[0], self.loop_size)
        pair, core = lax.div(self.member(index_ref), 2), lax.rem(index, 2)
        chip = block * 2 + lax.bitwise_xor(pair, core)
        swapped = lax.bitwise_and(lax.shift_right_logical(jnp.int32(OTHER_CORE_FIRST), chip), 1)
        return lax.bitwise_xor(core, swapped) == 1

    def panel(self, ref, c):
        return ref[:, c * self.size : (c + 1) * self.size]

    def member(self, index_ref):
        return lax.rem(index_ref[0], self.members)

    def send_far(self, index_ref, x, cb_ref, g_ref, out_refs):
        coeffs = dot_nt(x, cb_ref[...]).astype(BF16)
        twice = jnp.concatenate([coeffs, coeffs], axis=1)
        totals = [dot_nt(twice, g_ref[index]) for index in range(len(self.hops))]
        if not self.paired:
            for i, out_ref in enumerate(out_refs):
                step = i % self.members * self.width
                out_ref[...] = totals[i // self.members][:, step : step + self.width].astype(BF16)
            return
        message_ref, keep_ref = out_refs
        (total,) = totals
        member = self.member(index_ref)
        second = lax.rem(member, 2) != lax.div(member, 2)
        first, last = total[:, : 2 * self.width], total[:, 2 * self.width :]
        keep_ref[...] = jnp.where(second, last, first)
        upper, lower = halves(jnp.where(second, first, last))
        message_ref[:, : self.shard_len] = x
        message_ref[:, self.shard_len : self.shard_len + 2 * self.width] = upper
        message_ref[:, self.shard_len + 2 * self.width :] = lower

    def relay_far(self, index_ref, keep_ref, message_ref, out_refs):
        upper = message_ref[:, self.shard_len : self.shard_len + 2 * self.width].astype(F32)
        lower = message_ref[:, self.shard_len + 2 * self.width :].astype(F32)
        total = (keep_ref[...] + (upper + lower)).astype(BF16)
        odd = self.first_is_odd(index_ref)
        first, last = total[:, : self.width], total[:, self.width :]
        out_refs[0][...] = jnp.where(odd, last, first)
        out_refs[1][...] = jnp.where(odd, first, last)

    def far_sum(self, far_refs):
        return sum(ref[...].astype(F32) for ref in far_refs)

    def near_sums(self, x_ref, d_ref, acc_ref, first, start_ref=None):
        panels = [self.panel(x_ref, c) for c in range(self.per_device)]
        for r in range(self.per_device):
            value = None if start_ref is None else self.panel(start_ref, r)
            for c in range(self.per_device):
                offset = first + c - r
                if -REACH <= offset <= REACH:
                    term = dot_nt(panels[c], d_ref[r * SPAN + offset + REACH])
                    value = term if value is None else value + term
            acc_ref[:, r * self.size : (r + 1) * self.size] = value

    def halo_sums(self, below, x_ref, d_ref, acc_ref, start_ref):
        @pl.when(below)
        def _():
            self.near_sums(x_ref, d_ref, acc_ref, -self.per_device, start_ref)

        @pl.when(jnp.logical_not(below))
        def _():
            self.near_sums(x_ref, d_ref, acc_ref, self.per_device, start_ref)

    def far_halves(self, far_refs):
        return jnp.concatenate(halves(self.far_sum(far_refs)), axis=1)

    def next_panel(self, acc_ref, rb_ref, both, c):
        return (self.panel(acc_ref, c) + dot_nn(both, self.panel(rb_ref, c))).astype(BF16)

    def next_block(self, acc_ref, rb_ref, far_refs):
        both = self.far_halves(far_refs)
        panels = [self.next_panel(acc_ref, rb_ref, both, c) for c in range(self.per_device)]
        return jnp.concatenate(panels, axis=1)


def prepare_kernel(plan, index_ref, *refs):
    sources, refs = refs[:7], refs[7:]
    x_ref, g_ref, cb_ref, near_ref, offsets_ref = refs[:5]
    sends, (rows_ref, cols_ref, col_ref, coup_ref, sum_ref, sems) = refs[5:-6], refs[-6:]
    targets = (near_ref, offsets_ref, rows_ref, cols_ref, x_ref, col_ref, coup_ref)
    copies = [
        pltpu.make_async_copy(source, target, sems.at[i])
        for i, (source, target) in enumerate(zip(sources, targets))
    ]
    for copy in copies:
        copy.start()
    rank, size = plan.rank, plan.size
    cb_ref[...] = jnp.zeros_like(cb_ref)
    sum_ref[...] = jnp.zeros_like(sum_ref)
    for copy in copies:
        copy.wait()
    for c in range(plan.per_device):
        cb_ref[c * rank : (c + 1) * rank, c * size : (c + 1) * size] = col_ref[c]
    column = lax.broadcasted_iota(jnp.int32, (rank, plan.width), 1) // rank
    shift = 0 if plan.paired else plan.member(index_ref)
    for s in range(plan.slots):
        row = lax.rem(rows_ref[s], plan.block_clusters)
        step = lax.rem(lax.div(row, plan.per_device) - shift + plan.members, plan.members)
        place = step * plan.per_device + lax.rem(row, plan.per_device)
        if len(plan.hops) > 1:
            level = lax.div(rows_ref[s], plan.block_clusters)
            index = sum(jnp.where(level == i, index, 0) for i, index in enumerate(plan.set_of))
        else:
            index = 0
        where = (index, pl.ds(pl.multiple_of(place * rank, rank), rank), slice(None))
        tile = coup_ref[s].astype(F32)
        wide = jnp.where(column == cols_ref[s], jnp.concatenate([tile] * plan.per_device, axis=1), 0.0)
        sum_ref[where] = sum_ref[where] + wide
    for index in range(len(plan.hops)):
        g_ref[index] = jnp.concatenate(halves(sum_ref[index]), axis=1)
    plan.send_far(index_ref, x_ref[...], cb_ref, g_ref, sends)


def relay_kernel(plan, index_ref, keep_ref, message_ref, *out_refs):
    plan.relay_far(index_ref, keep_ref, message_ref, out_refs)


def first_own_kernel(plan, *refs):
    index_ref, rows_ref, offsets_ref, x_ref, near_ref, row_ref, tiles_ref = refs[:7]
    acc_ref, d_ref, rb_ref = refs[-3:]
    rank, size = plan.rank, plan.size
    for cell in range(plan.cells):
        d_ref[cell] = jnp.zeros(d_ref.shape[1:], d_ref.dtype)
    for s in range(plan.tiles):
        d_ref[rows_ref[s] * SPAN + offsets_ref[s] + REACH] = tiles_ref[s]
    rb_ref[...] = jnp.zeros_like(rb_ref)
    for c in range(plan.per_device):
        for start in (c * rank, plan.width + c * rank):
            rb_ref[start : start + rank, c * size : (c + 1) * size] = row_ref[c]
    plan.near_sums(x_ref, d_ref, acc_ref, 0)
    plan.halo_sums(lax.rem(index_ref[0], 2) == 1, near_ref, d_ref, acc_ref, acc_ref)


def own_kernel(plan, slot, *refs):
    index_ref, x_ref, near_ref, d_ref = refs[:4]
    acc_ref, krylov_ref, sem = refs[-3:]
    copy = pltpu.make_async_copy(x_ref, krylov_ref.at[slot], sem)
    copy.start()
    plan.near_sums(x_ref, d_ref, acc_ref, 0)
    plan.halo_sums(lax.rem(index_ref[0], 2) == 1, near_ref, d_ref, acc_ref, acc_ref)
    copy.wait()


def halo_kernel(plan, index_ref, acc_ref, over_ref, d_ref, *refs):
    plan.halo_sums(lax.rem(index_ref[0], 2) == 0, over_ref, d_ref, refs[-1], acc_ref)


def finish_kernel(plan, fars, *refs):
    index_ref, acc_ref, rb_ref, cb_ref, g_ref = refs[:5]
    far_refs, (x_ref, *sends) = refs[5 : 5 + fars], refs[5 + fars :]
    x = plan.next_block(acc_ref, rb_ref, far_refs)
    x_ref[...] = x
    plan.send_far(index_ref, x, cb_ref, g_ref, sends)


def last_kernel(plan, fars, slot, *refs):
    acc_ref, rb_ref = refs[:2]
    far_refs, (_, krylov_ref, x_ref, sem) = refs[2 : 2 + fars], refs[2 + fars :]
    both = plan.far_halves(far_refs)
    copies = []
    for c in range(plan.per_device):
        columns = pl.ds(c * plan.size, plan.size)
        x_ref[:, columns] = plan.next_panel(acc_ref, rb_ref, both, c)
        copies.append(
            pltpu.make_async_copy(x_ref.at[:, columns], krylov_ref.at[slot, :, columns], sem.at[c])
        )
        copies[-1].start()
    for copy in copies:
        copy.wait()


def call(kernel, name, ins, specs, outs, out_specs=None, scratch=(), aliases=None):
    spaces = {id(IN_VMEM): pltpu.VMEM, id(IN_HBM): pltpu.HBM}
    ins = [
        pltpu.with_memory_space_constraint(v, spaces[id(spec)]) if id(spec) in spaces else v
        for v, spec in zip(ins, specs)
    ]
    return pl.pallas_call(
        kernel,
        in_specs=list(specs),
        out_specs=out_specs or [IN_VMEM] * len(outs),
        out_shape=list(outs),
        scratch_shapes=list(scratch),
        input_output_aliases=aliases or {},
        compiler_params=pltpu.CompilerParams(vmem_limit_bytes=16 * 2**20),
        cost_estimate=pl.CostEstimate(flops=10**9, bytes_accessed=2**22, transcendentals=0),
        name=name,
    )(*ins)


def on_device(
    block, near_tiles, near_rows, near_offsets, col_basis, couplings, far_rows, far_cols, row_basis
):
    axes = ("loop", "far")
    plan = Plan(
        block.shape, near_tiles.shape, couplings.shape, lax.axis_size("far"), lax.axis_size("loop")
    )
    rhs, shard_len, width = plan.rhs, plan.shard_len, plan.width
    block_out = pltpu.VMEM((rhs, shard_len), BF16)
    acc_out = pltpu.VMEM((rhs, shard_len), F32)
    relay_out = pltpu.VMEM((rhs, width), BF16)
    krylov_out = jax.ShapeDtypeStruct((PRODUCTS, rhs, shard_len), BF16)
    if plan.paired:
        sends_out = [
            pltpu.VMEM((rhs, shard_len + 4 * width), BF16),
            pltpu.VMEM((rhs, 2 * width), F32),
        ]
    else:
        sends_out = [pltpu.VMEM((rhs, width), BF16)] * len(plan.routes)
    index = lax.axis_index(axes).astype(jnp.int32).reshape(1)

    def scratch_for(*arrays):
        return [
            pltpu.SMEM(v.shape, v.dtype) if v.dtype == jnp.int32 else pltpu.VMEM(v.shape, v.dtype)
            for v in arrays
        ]

    current, sends, krylov = block, None, None
    for product in range(PRODUCTS):
        if product == 0:
            ins = [near_rows, near_offsets, far_rows, far_cols, block, col_basis, couplings]
            matrix = (len(plan.hops), plan.members * width, 2 * width)
            current, coupled, col_wide, row_slots, offset_slots, *sends = call(
                functools.partial(prepare_kernel, plan),
                "prepare",
                [index, *ins],
                [IN_SMEM] + [IN_HBM] * 7,
                [
                    block_out,
                    pltpu.VMEM(matrix, BF16),
                    pltpu.VMEM((width, shard_len), BF16),
                    *scratch_for(near_rows, near_offsets),
                    *sends_out,
                ],
                [IN_VMEM] * 3 + [IN_SMEM] * 2 + [IN_VMEM] * len(sends_out),
                scratch=scratch_for(far_rows, far_cols, col_basis, couplings)
                + [pltpu.VMEM(matrix[:2] + (width,), F32), pltpu.SemaphoreType.DMA((7,))],
            )
        over = lax.ppermute(current, axes, plan.over)
        near = lax.ppermute(sends[0] if plan.paired else current, axes, plan.near)
        if plan.paired:
            sends = call(
                functools.partial(relay_kernel, plan),
                "relay",
                [index, sends[1], near],
                [IN_SMEM] + [IN_VMEM] * 2,
                [relay_out] * 2,
            )
            routes = plan.across
        else:
            routes = plan.routes
        fars = [lax.ppermute(s, axes, route) for s, route in zip(sends, routes)]
        after = sends if plan.paired else []
        if product == 0:
            ins = [index, row_slots, offset_slots, current, near, row_basis, near_tiles, *after]
            acc, dense, row_wide = call(
                functools.partial(first_own_kernel, plan),
                "first_own",
                ins,
                [IN_SMEM] * 3 + [IN_VMEM] * 2 + [PREFETCHED] * 2 + [ANYWHERE] * len(after),
                [
                    acc_out,
                    pltpu.VMEM((plan.cells, plan.size, plan.size), BF16),
                    pltpu.VMEM((2 * width, shard_len), BF16),
                ],
            )
        else:
            ins = [index, current, near, dense, *after] + ([krylov] if product > 1 else [])
            acc, krylov = call(
                functools.partial(own_kernel, plan, product - 1),
                "own",
                ins,
                [IN_SMEM] + [IN_VMEM] * 3 + [ANYWHERE] * (len(ins) - 4),
                [acc_out, krylov_out],
                [IN_VMEM, ANYWHERE],
                [pltpu.SemaphoreType.DMA],
                {len(ins) - 1: 1} if product > 1 else None,
            )
        (acc,) = call(
            functools.partial(halo_kernel, plan),
            "halo",
            [index, acc, over, dense],
            [IN_SMEM] + [IN_VMEM] * 3,
            [acc_out],
        )
        if product < PRODUCTS - 1:
            ins = [index, acc, row_wide, col_wide, coupled, *fars]
            current, *sends = call(
                functools.partial(finish_kernel, plan, len(fars)),
                "finish",
                ins,
                [IN_SMEM] + [IN_VMEM] * (len(ins) - 1),
                [block_out, *sends_out],
            )
        else:
            ins = [acc, row_wide, *fars, krylov]
            (krylov,) = call(
                functools.partial(last_kernel, plan, len(fars), product),
                "last",
                ins,
                [IN_VMEM] * (len(ins) - 1) + [ANYWHERE],
                [krylov_out],
                [ANYWHERE],
                [
                    pltpu.VMEM((rhs, shard_len), BF16),
                    pltpu.SemaphoreType.DMA((plan.per_device,)),
                ],
                {len(ins) - 1: 0},
            )
    return krylov


def solution(mesh):
    split = ("groups", "loop", "far")
    wide, narrow = P(split, None, None), P(split)
    in_specs = (P(None, split), wide, narrow, narrow, wide, wide, narrow, narrow, wide)
    return jax.shard_map(
        on_device, mesh=mesh, in_specs=in_specs, out_specs=P(None, None, split), check_vma=False
    )
```

```python
import functools

import jax
import jax.numpy as jnp
from jax import lax
from jax.experimental import pallas as pl
from jax.experimental.pallas import tpu as pltpu
from jax.sharding import PartitionSpec as P

PRODUCTS = 4
REACH = 4
LEVELS = 3
SPAN = 2 * REACH + 1

F32 = jnp.float32
BF16 = jnp.bfloat16
IN_VMEM = pl.BlockSpec(memory_space=pltpu.VMEM)
PREFETCHED = pl.BlockSpec(memory_space=pltpu.VMEM)
IN_SMEM = pl.BlockSpec(memory_space=pltpu.SMEM)
IN_HBM = pl.BlockSpec(memory_space=pltpu.HBM)
ANYWHERE = pl.BlockSpec(memory_space=pl.ANY)


def dot_nt(a, b):
    return lax.dot_general(a, b, (((1,), (1,)), ((), ())), preferred_element_type=F32)


def dot_nn(a, b):
    return lax.dot_general(a, b, (((1,), (0,)), ((), ())), preferred_element_type=F32)


def halves(value):
    upper = value.astype(BF16)
    return upper, (value - upper.astype(F32)).astype(BF16)


class Plan:
    def __init__(self, block_shape, tile_shape, coupling_shape, members, loop_size):
        self.rhs, self.shard_len = block_shape
        self.tiles, self.size, _ = tile_shape
        self.slots, self.rank, _ = coupling_shape
        self.members, self.loop_size = members, loop_size
        self.per_device = self.shard_len // self.size
        self.width = self.per_device * self.rank
        self.cells = self.per_device * SPAN
        self.block_clusters = self.per_device * members
        distances = [d % loop_size for d in (2, loop_size - 2, loop_size // 2)]
        self.hops = sorted(set(distances))
        self.set_of = [self.hops.index(d) for d in distances]
        self.paired = len(self.hops) == 1 and 2 * self.hops[0] == loop_size and members == 4
        devices = members * loop_size
        self.near = [(i, i ^ 1) for i in range(devices)]
        self.over = [(i, (i + 1 if i % 2 else i - 1) % devices) for i in range(devices)]
        places = [(l, m) for l in range(loop_size) for m in range(members)]
        self.across = [
            [
                (l * members + m, (l + self.hops[0]) % loop_size * members + (m ^ 2 ^ (m % 2 * 2) ^ other))
                for l, m in places
            ]
            for other in (0, 1)
        ]
        self.routes = [
            [(l * members + m, (l + hop) % loop_size * members + (m + step) % members) for l, m in places]
            for hop in self.hops
            for step in range(members)
        ]

    def panel(self, ref, c):
        return ref[:, c * self.size : (c + 1) * self.size]

    def member(self, index_ref):
        return lax.rem(index_ref[0], self.members)

    def send_far(self, index_ref, x, cb_ref, g_ref, out_refs):
        coeffs = dot_nt(x, cb_ref[...]).astype(BF16)
        twice = jnp.concatenate([coeffs, coeffs], axis=1)
        totals = [dot_nt(twice, g_ref[index]) for index in range(len(self.hops))]
        if not self.paired:
            for i, out_ref in enumerate(out_refs):
                step = i % self.members * self.width
                out_ref[...] = totals[i // self.members][:, step : step + self.width].astype(BF16)
            return
        message_ref, keep_ref = out_refs
        (total,) = totals
        member = self.member(index_ref)
        second = lax.rem(member, 2) == lax.div(member, 2)
        first, last = total[:, : 2 * self.width], total[:, 2 * self.width :]
        keep_ref[...] = jnp.where(second, last, first)
        upper, lower = halves(jnp.where(second, first, last))
        message_ref[:, : self.shard_len] = x
        message_ref[:, self.shard_len : self.shard_len + 2 * self.width] = upper
        message_ref[:, self.shard_len + 2 * self.width :] = lower

    def relay_far(self, index_ref, keep_ref, message_ref, out_refs):
        upper = message_ref[:, self.shard_len : self.shard_len + 2 * self.width].astype(F32)
        lower = message_ref[:, self.shard_len + 2 * self.width :].astype(F32)
        total = (keep_ref[...] + (upper + lower)).astype(BF16)
        second = lax.rem(index_ref[0], 2) == 1
        first, last = total[:, : self.width], total[:, self.width :]
        out_refs[0][...] = jnp.where(second, last, first)
        out_refs[1][...] = jnp.where(second, first, last)

    def far_sum(self, far_refs):
        return sum(ref[...].astype(F32) for ref in far_refs)

    def near_sums(self, x_ref, d_ref, acc_ref, first, start_ref=None):
        panels = [self.panel(x_ref, c) for c in range(self.per_device)]
        for r in range(self.per_device):
            value = None if start_ref is None else self.panel(start_ref, r)
            for c in range(self.per_device):
                offset = first + c - r
                if -REACH <= offset <= REACH:
                    term = dot_nt(panels[c], d_ref[r * SPAN + offset + REACH])
                    value = term if value is None else value + term
            acc_ref[:, r * self.size : (r + 1) * self.size] = value

    def halo_sums(self, below, x_ref, d_ref, acc_ref, start_ref):
        @pl.when(below)
        def _():
            self.near_sums(x_ref, d_ref, acc_ref, -self.per_device, start_ref)

        @pl.when(jnp.logical_not(below))
        def _():
            self.near_sums(x_ref, d_ref, acc_ref, self.per_device, start_ref)

    def far_halves(self, far_refs):
        return jnp.concatenate(halves(self.far_sum(far_refs)), axis=1)

    def next_panel(self, acc_ref, rb_ref, both, c):
        return (self.panel(acc_ref, c) + dot_nn(both, self.panel(rb_ref, c))).astype(BF16)

    def next_block(self, acc_ref, rb_ref, far_refs):
        both = self.far_halves(far_refs)
        panels = [self.next_panel(acc_ref, rb_ref, both, c) for c in range(self.per_device)]
        return jnp.concatenate(panels, axis=1)


def prepare_kernel(plan, index_ref, *refs):
    sources, refs = refs[:7], refs[7:]
    x_ref, g_ref, cb_ref, near_ref, offsets_ref = refs[:5]
    sends, (rows_ref, cols_ref, col_ref, coup_ref, sum_ref, sems) = refs[5:-6], refs[-6:]
    targets = (near_ref, offsets_ref, rows_ref, cols_ref, x_ref, col_ref, coup_ref)
    copies = [
        pltpu.make_async_copy(source, target, sems.at[i])
        for i, (source, target) in enumerate(zip(sources, targets))
    ]
    for copy in copies:
        copy.start()
    rank, size = plan.rank, plan.size
    cb_ref[...] = jnp.zeros_like(cb_ref)
    sum_ref[...] = jnp.zeros_like(sum_ref)
    for copy in copies:
        copy.wait()
    for c in range(plan.per_device):
        cb_ref[c * rank : (c + 1) * rank, c * size : (c + 1) * size] = col_ref[c]
    column = lax.broadcasted_iota(jnp.int32, (rank, plan.width), 1) // rank
    shift = 0 if plan.paired else plan.member(index_ref)
    for s in range(plan.slots):
        row = lax.rem(rows_ref[s], plan.block_clusters)
        step = lax.rem(lax.div(row, plan.per_device) - shift + plan.members, plan.members)
        place = step * plan.per_device + lax.rem(row, plan.per_device)
        if len(plan.hops) > 1:
            level = lax.div(rows_ref[s], plan.block_clusters)
            index = sum(jnp.where(level == i, index, 0) for i, index in enumerate(plan.set_of))
        else:
            index = 0
        where = (index, pl.ds(pl.multiple_of(place * rank, rank), rank), slice(None))
        tile = coup_ref[s].astype(F32)
        wide = jnp.where(column == cols_ref[s], jnp.concatenate([tile] * plan.per_device, axis=1), 0.0)
        sum_ref[where] = sum_ref[where] + wide
    for index in range(len(plan.hops)):
        g_ref[index] = jnp.concatenate(halves(sum_ref[index]), axis=1)
    plan.send_far(index_ref, x_ref[...], cb_ref, g_ref, sends)


def relay_kernel(plan, index_ref, keep_ref, message_ref, *out_refs):
    plan.relay_far(index_ref, keep_ref, message_ref, out_refs)


def first_own_kernel(plan, *refs):
    index_ref, rows_ref, offsets_ref, x_ref, near_ref, row_ref, tiles_ref = refs[:7]
    acc_ref, d_ref, rb_ref = refs[-3:]
    rank, size = plan.rank, plan.size
    for cell in range(plan.cells):
        d_ref[cell] = jnp.zeros(d_ref.shape[1:], d_ref.dtype)
    for s in range(plan.tiles):
        d_ref[rows_ref[s] * SPAN + offsets_ref[s] + REACH] = tiles_ref[s]
    rb_ref[...] = jnp.zeros_like(rb_ref)
    for c in range(plan.per_device):
        for start in (c * rank, plan.width + c * rank):
            rb_ref[start : start + rank, c * size : (c + 1) * size] = row_ref[c]
    plan.near_sums(x_ref, d_ref, acc_ref, 0)
    plan.halo_sums(lax.rem(index_ref[0], 2) == 1, near_ref, d_ref, acc_ref, acc_ref)


def own_kernel(plan, slot, *refs):
    index_ref, x_ref, near_ref, d_ref = refs[:4]
    acc_ref, krylov_ref, sem = refs[-3:]
    copy = pltpu.make_async_copy(x_ref, krylov_ref.at[slot], sem)
    copy.start()
    plan.near_sums(x_ref, d_ref, acc_ref, 0)
    plan.halo_sums(lax.rem(index_ref[0], 2) == 1, near_ref, d_ref, acc_ref, acc_ref)
    copy.wait()


def halo_kernel(plan, index_ref, acc_ref, over_ref, d_ref, *refs):
    plan.halo_sums(lax.rem(index_ref[0], 2) == 0, over_ref, d_ref, refs[-1], acc_ref)


def finish_kernel(plan, fars, *refs):
    index_ref, acc_ref, rb_ref, cb_ref, g_ref = refs[:5]
    far_refs, (x_ref, *sends) = refs[5 : 5 + fars], refs[5 + fars :]
    x = plan.next_block(acc_ref, rb_ref, far_refs)
    x_ref[...] = x
    plan.send_far(index_ref, x, cb_ref, g_ref, sends)


def last_kernel(plan, fars, slot, *refs):
    acc_ref, rb_ref = refs[:2]
    far_refs, (_, krylov_ref, x_ref, sem) = refs[2 : 2 + fars], refs[2 + fars :]
    both = plan.far_halves(far_refs)
    copies = []
    for c in range(plan.per_device):
        columns = pl.ds(c * plan.size, plan.size)
        x_ref[:, columns] = plan.next_panel(acc_ref, rb_ref, both, c)
        copies.append(
            pltpu.make_async_copy(x_ref.at[:, columns], krylov_ref.at[slot, :, columns], sem.at[c])
        )
        copies[-1].start()
    for copy in copies:
        copy.wait()


def call(kernel, name, ins, specs, outs, out_specs=None, scratch=(), aliases=None):
    spaces = {id(IN_VMEM): pltpu.VMEM, id(IN_HBM): pltpu.HBM}
    ins = [
        pltpu.with_memory_space_constraint(v, spaces[id(spec)]) if id(spec) in spaces else v
        for v, spec in zip(ins, specs)
    ]
    return pl.pallas_call(
        kernel,
        in_specs=list(specs),
        out_specs=out_specs or [IN_VMEM] * len(outs),
        out_shape=list(outs),
        scratch_shapes=list(scratch),
        input_output_aliases=aliases or {},
        compiler_params=pltpu.CompilerParams(vmem_limit_bytes=16 * 2**20),
        cost_estimate=pl.CostEstimate(flops=10**9, bytes_accessed=2**22, transcendentals=0),
        name=name,
    )(*ins)


def on_device(
    block, near_tiles, near_rows, near_offsets, col_basis, couplings, far_rows, far_cols, row_basis
):
    axes = ("loop", "far")
    plan = Plan(
        block.shape, near_tiles.shape, couplings.shape, lax.axis_size("far"), lax.axis_size("loop")
    )
    rhs, shard_len, width = plan.rhs, plan.shard_len, plan.width
    block_out = pltpu.VMEM((rhs, shard_len), BF16)
    acc_out = pltpu.VMEM((rhs, shard_len), F32)
    relay_out = pltpu.VMEM((rhs, width), BF16)
    krylov_out = jax.ShapeDtypeStruct((PRODUCTS, rhs, shard_len), BF16)
    if plan.paired:
        sends_out = [
            pltpu.VMEM((rhs, shard_len + 4 * width), BF16),
            pltpu.VMEM((rhs, 2 * width), F32),
        ]
    else:
        sends_out = [pltpu.VMEM((rhs, width), BF16)] * len(plan.routes)
    index = lax.axis_index(axes).astype(jnp.int32).reshape(1)

    def scratch_for(*arrays):
        return [
            pltpu.SMEM(v.shape, v.dtype) if v.dtype == jnp.int32 else pltpu.VMEM(v.shape, v.dtype)
            for v in arrays
        ]

    current, sends, krylov = block, None, None
    for product in range(PRODUCTS):
        if product == 0:
            ins = [near_rows, near_offsets, far_rows, far_cols, block, col_basis, couplings]
            matrix = (len(plan.hops), plan.members * width, 2 * width)
            current, coupled, col_wide, row_slots, offset_slots, *sends = call(
                functools.partial(prepare_kernel, plan),
                "prepare",
                [index, *ins],
                [IN_SMEM] + [IN_HBM] * 7,
                [
                    block_out,
                    pltpu.VMEM(matrix, BF16),
                    pltpu.VMEM((width, shard_len), BF16),
                    *scratch_for(near_rows, near_offsets),
                    *sends_out,
                ],
                [IN_VMEM] * 3 + [IN_SMEM] * 2 + [IN_VMEM] * len(sends_out),
                scratch=scratch_for(far_rows, far_cols, col_basis, couplings)
                + [pltpu.VMEM(matrix[:2] + (width,), F32), pltpu.SemaphoreType.DMA((7,))],
            )
        over = lax.ppermute(current, axes, plan.over)
        near = lax.ppermute(sends[0] if plan.paired else current, axes, plan.near)
        if plan.paired:
            sends = call(
                functools.partial(relay_kernel, plan),
                "relay",
                [index, sends[1], near],
                [IN_SMEM] + [IN_VMEM] * 2,
                [relay_out] * 2,
            )
            routes = plan.across
        else:
            routes = plan.routes
        fars = [lax.ppermute(s, axes, route) for s, route in zip(sends, routes)]
        after = sends if plan.paired else []
        if product == 0:
            ins = [index, row_slots, offset_slots, current, near, row_basis, near_tiles, *after]
            acc, dense, row_wide = call(
                functools.partial(first_own_kernel, plan),
                "first_own",
                ins,
                [IN_SMEM] * 3 + [IN_VMEM] * 2 + [PREFETCHED] * 2 + [ANYWHERE] * len(after),
                [
                    acc_out,
                    pltpu.VMEM((plan.cells, plan.size, plan.size), BF16),
                    pltpu.VMEM((2 * width, shard_len), BF16),
                ],
            )
        else:
            ins = [index, current, near, dense, *after] + ([krylov] if product > 1 else [])
            acc, krylov = call(
                functools.partial(own_kernel, plan, product - 1),
                "own",
                ins,
                [IN_SMEM] + [IN_VMEM] * 3 + [ANYWHERE] * (len(ins) - 4),
                [acc_out, krylov_out],
                [IN_VMEM, ANYWHERE],
                [pltpu.SemaphoreType.DMA],
                {len(ins) - 1: 1} if product > 1 else None,
            )
        (acc,) = call(
            functools.partial(halo_kernel, plan),
            "halo",
            [index, acc, over, dense],
            [IN_SMEM] + [IN_VMEM] * 3,
            [acc_out],
        )
        if product < PRODUCTS - 1:
            ins = [index, acc, row_wide, col_wide, coupled, *fars]
            current, *sends = call(
                functools.partial(finish_kernel, plan, len(fars)),
                "finish",
                ins,
                [IN_SMEM] + [IN_VMEM] * (len(ins) - 1),
                [block_out, *sends_out],
            )
        else:
            ins = [acc, row_wide, *fars, krylov]
            (krylov,) = call(
                functools.partial(last_kernel, plan, len(fars), product),
                "last",
                ins,
                [IN_VMEM] * (len(ins) - 1) + [ANYWHERE],
                [krylov_out],
                [ANYWHERE],
                [
                    pltpu.VMEM((rhs, shard_len), BF16),
                    pltpu.SemaphoreType.DMA((plan.per_device,)),
                ],
                {len(ins) - 1: 0},
            )
    return krylov


def solution(mesh):
    split = ("groups", "loop", "far")
    wide, narrow = P(split, None, None), P(split)
    in_specs = (P(None, split), wide, narrow, narrow, wide, wide, narrow, narrow, wide)
    return jax.shard_map(
        on_device, mesh=mesh, in_specs=in_specs, out_specs=P(None, None, split), check_vma=False
    )
```

```python
import functools

import jax
import jax.numpy as jnp
from jax import lax
from jax.experimental import pallas as pl
from jax.experimental.pallas import tpu as pltpu
from jax.sharding import PartitionSpec as P

PRODUCTS = 4
REACH = 4
LEVELS = 3
SPAN = 2 * REACH + 1

F32 = jnp.float32
BF16 = jnp.bfloat16
IN_VMEM = pl.BlockSpec(memory_space=pltpu.VMEM)
PREFETCHED = pl.BlockSpec(memory_space=pltpu.VMEM)
IN_SMEM = pl.BlockSpec(memory_space=pltpu.SMEM)
IN_HBM = pl.BlockSpec(memory_space=pltpu.HBM)
ANYWHERE = pl.BlockSpec(memory_space=pl.ANY)


def dot_nt(a, b):
    return lax.dot_general(a, b, (((1,), (1,)), ((), ())), preferred_element_type=F32)


def dot_nn(a, b):
    return lax.dot_general(a, b, (((1,), (0,)), ((), ())), preferred_element_type=F32)


def halves(value):
    upper = value.astype(BF16)
    return upper, (value - upper.astype(F32)).astype(BF16)


class Plan:
    def __init__(self, block_shape, tile_shape, coupling_shape, members, loop_size):
        self.rhs, self.shard_len = block_shape
        self.tiles, self.size, _ = tile_shape
        self.slots, self.rank, _ = coupling_shape
        self.members, self.loop_size = members, loop_size
        self.per_device = self.shard_len // self.size
        self.width = self.per_device * self.rank
        self.cells = self.per_device * SPAN
        self.block_clusters = self.per_device * members
        distances = [d % loop_size for d in (2, loop_size - 2, loop_size // 2)]
        self.hops = sorted(set(distances))
        self.set_of = [self.hops.index(d) for d in distances]
        self.paired = len(self.hops) == 1 and 2 * self.hops[0] == loop_size and members == 4
        devices = members * loop_size
        self.near = [(i, i ^ 1) for i in range(devices)]
        self.over = [(i, (i + 1 if i % 2 else i - 1) % devices) for i in range(devices)]
        places = [(l, m) for l in range(loop_size) for m in range(members)]
        self.across = [
            [
                (l * members + m, (l + self.hops[0]) % loop_size * members + (m ^ (m % 2 * 2) ^ other))
                for l, m in places
            ]
            for other in (1, 0)
        ]
        self.routes = [
            [(l * members + m, (l + hop) % loop_size * members + (m + step) % members) for l, m in places]
            for hop in self.hops
            for step in range(members)
        ]

    def panel(self, ref, c):
        return ref[:, c * self.size : (c + 1) * self.size]

    def member(self, index_ref):
        return lax.rem(index_ref[0], self.members)

    def send_far(self, index_ref, x, cb_ref, g_ref, out_refs):
        coeffs = dot_nt(x, cb_ref[...]).astype(BF16)
        twice = jnp.concatenate([coeffs, coeffs], axis=1)
        totals = [dot_nt(twice, g_ref[index]) for index in range(len(self.hops))]
        if not self.paired:
            for i, out_ref in enumerate(out_refs):
                step = i % self.members * self.width
                out_ref[...] = totals[i // self.members][:, step : step + self.width].astype(BF16)
            return
        message_ref, keep_ref = out_refs
        (total,) = totals
        member = self.member(index_ref)
        second = lax.rem(member, 2) != lax.div(member, 2)
        first, last = total[:, : 2 * self.width], total[:, 2 * self.width :]
        keep_ref[...] = jnp.where(second, last, first)
        upper, lower = halves(jnp.where(second, first, last))
        message_ref[:, : self.shard_len] = x
        message_ref[:, self.shard_len : self.shard_len + 2 * self.width] = upper
        message_ref[:, self.shard_len + 2 * self.width :] = lower

    def relay_far(self, index_ref, keep_ref, message_ref, out_refs):
        upper = message_ref[:, self.shard_len : self.shard_len + 2 * self.width].astype(F32)
        lower = message_ref[:, self.shard_len + 2 * self.width :].astype(F32)
        total = (keep_ref[...] + (upper + lower)).astype(BF16)
        second = lax.rem(index_ref[0], 2) == 1
        first, last = total[:, : self.width], total[:, self.width :]
        out_refs[0][...] = jnp.where(second, first, last)
        out_refs[1][...] = jnp.where(second, last, first)

    def far_sum(self, far_refs):
        return sum(ref[...].astype(F32) for ref in far_refs)

    def near_sums(self, x_ref, d_ref, acc_ref, first, start_ref=None):
        panels = [self.panel(x_ref, c) for c in range(self.per_device)]
        for r in range(self.per_device):
            value = None if start_ref is None else self.panel(start_ref, r)
            for c in range(self.per_device):
                offset = first + c - r
                if -REACH <= offset <= REACH:
                    term = dot_nt(panels[c], d_ref[r * SPAN + offset + REACH])
                    value = term if value is None else value + term
            acc_ref[:, r * self.size : (r + 1) * self.size] = value

    def halo_sums(self, below, x_ref, d_ref, acc_ref, start_ref):
        @pl.when(below)
        def _():
            self.near_sums(x_ref, d_ref, acc_ref, -self.per_device, start_ref)

        @pl.when(jnp.logical_not(below))
        def _():
            self.near_sums(x_ref, d_ref, acc_ref, self.per_device, start_ref)

    def far_halves(self, far_refs):
        return jnp.concatenate(halves(self.far_sum(far_refs)), axis=1)

    def next_panel(self, acc_ref, rb_ref, both, c):
        return (self.panel(acc_ref, c) + dot_nn(both, self.panel(rb_ref, c))).astype(BF16)

    def next_block(self, acc_ref, rb_ref, far_refs):
        both = self.far_halves(far_refs)
        panels = [self.next_panel(acc_ref, rb_ref, both, c) for c in range(self.per_device)]
        return jnp.concatenate(panels, axis=1)


def prepare_kernel(plan, index_ref, *refs):
    sources, refs = refs[:7], refs[7:]
    x_ref, g_ref, cb_ref, near_ref, offsets_ref = refs[:5]
    sends, (rows_ref, cols_ref, col_ref, coup_ref, sum_ref, sems) = refs[5:-6], refs[-6:]
    targets = (near_ref, offsets_ref, rows_ref, cols_ref, x_ref, col_ref, coup_ref)
    copies = [
        pltpu.make_async_copy(source, target, sems.at[i])
        for i, (source, target) in enumerate(zip(sources, targets))
    ]
    for copy in copies:
        copy.start()
    rank, size = plan.rank, plan.size
    cb_ref[...] = jnp.zeros_like(cb_ref)
    sum_ref[...] = jnp.zeros_like(sum_ref)
    for copy in copies:
        copy.wait()
    for c in range(plan.per_device):
        cb_ref[c * rank : (c + 1) * rank, c * size : (c + 1) * size] = col_ref[c]
    column = lax.broadcasted_iota(jnp.int32, (rank, plan.width), 1) // rank
    shift = 0 if plan.paired else plan.member(index_ref)
    for s in range(plan.slots):
        row = lax.rem(rows_ref[s], plan.block_clusters)
        step = lax.rem(lax.div(row, plan.per_device) - shift + plan.members, plan.members)
        place = step * plan.per_device + lax.rem(row, plan.per_device)
        if len(plan.hops) > 1:
            level = lax.div(rows_ref[s], plan.block_clusters)
            index = sum(jnp.where(level == i, index, 0) for i, index in enumerate(plan.set_of))
        else:
            index = 0
        where = (index, pl.ds(pl.multiple_of(place * rank, rank), rank), slice(None))
        tile = coup_ref[s].astype(F32)
        wide = jnp.where(column == cols_ref[s], jnp.concatenate([tile] * plan.per_device, axis=1), 0.0)
        sum_ref[where] = sum_ref[where] + wide
    for index in range(len(plan.hops)):
        g_ref[index] = jnp.concatenate(halves(sum_ref[index]), axis=1)
    plan.send_far(index_ref, x_ref[...], cb_ref, g_ref, sends)


def relay_kernel(plan, index_ref, keep_ref, message_ref, *out_refs):
    plan.relay_far(index_ref, keep_ref, message_ref, out_refs)


def first_own_kernel(plan, *refs):
    index_ref, rows_ref, offsets_ref, x_ref, near_ref, row_ref, tiles_ref = refs[:7]
    acc_ref, d_ref, rb_ref = refs[-3:]
    rank, size = plan.rank, plan.size
    for cell in range(plan.cells):
        d_ref[cell] = jnp.zeros(d_ref.shape[1:], d_ref.dtype)
    for s in range(plan.tiles):
        d_ref[rows_ref[s] * SPAN + offsets_ref[s] + REACH] = tiles_ref[s]
    rb_ref[...] = jnp.zeros_like(rb_ref)
    for c in range(plan.per_device):
        for start in (c * rank, plan.width + c * rank):
            rb_ref[start : start + rank, c * size : (c + 1) * size] = row_ref[c]
    plan.near_sums(x_ref, d_ref, acc_ref, 0)
    plan.halo_sums(lax.rem(index_ref[0], 2) == 1, near_ref, d_ref, acc_ref, acc_ref)


def own_kernel(plan, slot, *refs):
    index_ref, x_ref, near_ref, d_ref = refs[:4]
    acc_ref, krylov_ref, sem = refs[-3:]
    copy = pltpu.make_async_copy(x_ref, krylov_ref.at[slot], sem)
    copy.start()
    plan.near_sums(x_ref, d_ref, acc_ref, 0)
    plan.halo_sums(lax.rem(index_ref[0], 2) == 1, near_ref, d_ref, acc_ref, acc_ref)
    copy.wait()


def halo_kernel(plan, index_ref, acc_ref, over_ref, d_ref, *refs):
    plan.halo_sums(lax.rem(index_ref[0], 2) == 0, over_ref, d_ref, refs[-1], acc_ref)


def finish_kernel(plan, fars, *refs):
    index_ref, acc_ref, rb_ref, cb_ref, g_ref = refs[:5]
    far_refs, (x_ref, *sends) = refs[5 : 5 + fars], refs[5 + fars :]
    x = plan.next_block(acc_ref, rb_ref, far_refs)
    x_ref[...] = x
    plan.send_far(index_ref, x, cb_ref, g_ref, sends)


def last_kernel(plan, fars, slot, *refs):
    index_ref, acc_ref, over_ref, d_ref, rb_ref = refs[:5]
    far_refs, (_, krylov_ref, x_ref, sem) = refs[5 : 5 + fars], refs[5 + fars :]
    both = plan.far_halves(far_refs)
    over = [plan.panel(over_ref, c) for c in range(plan.per_device)]

    def copy(r):
        columns = pl.ds(r * plan.size, plan.size)
        return pltpu.make_async_copy(x_ref.at[:, columns], krylov_ref.at[slot, :, columns], sem.at[r])

    def sums(first):
        for r in range(plan.per_device):
            value = plan.panel(acc_ref, r) + dot_nn(both, plan.panel(rb_ref, r))
            for c in range(plan.per_device):
                offset = first + c - r
                if -REACH <= offset <= REACH:
                    value = value + dot_nt(over[c], d_ref[r * SPAN + offset + REACH])
            x_ref[:, r * plan.size : (r + 1) * plan.size] = value.astype(BF16)
            copy(r).start()

    below = lax.rem(index_ref[0], 2) == 0

    @pl.when(below)
    def _():
        sums(-plan.per_device)

    @pl.when(jnp.logical_not(below))
    def _():
        sums(plan.per_device)

    for r in range(plan.per_device):
        copy(r).wait()


def call(kernel, name, ins, specs, outs, out_specs=None, scratch=(), aliases=None):
    spaces = {id(IN_VMEM): pltpu.VMEM, id(IN_HBM): pltpu.HBM}
    ins = [
        pltpu.with_memory_space_constraint(v, spaces[id(spec)]) if id(spec) in spaces else v
        for v, spec in zip(ins, specs)
    ]
    return pl.pallas_call(
        kernel,
        in_specs=list(specs),
        out_specs=out_specs or [IN_VMEM] * len(outs),
        out_shape=list(outs),
        scratch_shapes=list(scratch),
        input_output_aliases=aliases or {},
        compiler_params=pltpu.CompilerParams(vmem_limit_bytes=16 * 2**20),
        cost_estimate=pl.CostEstimate(flops=10**9, bytes_accessed=2**22, transcendentals=0),
        name=name,
    )(*ins)


def on_device(
    block, near_tiles, near_rows, near_offsets, col_basis, couplings, far_rows, far_cols, row_basis
):
    axes = ("loop", "far")
    plan = Plan(
        block.shape, near_tiles.shape, couplings.shape, lax.axis_size("far"), lax.axis_size("loop")
    )
    rhs, shard_len, width = plan.rhs, plan.shard_len, plan.width
    block_out = pltpu.VMEM((rhs, shard_len), BF16)
    acc_out = pltpu.VMEM((rhs, shard_len), F32)
    relay_out = pltpu.VMEM((rhs, width), BF16)
    krylov_out = jax.ShapeDtypeStruct((PRODUCTS, rhs, shard_len), BF16)
    if plan.paired:
        sends_out = [
            pltpu.VMEM((rhs, shard_len + 4 * width), BF16),
            pltpu.VMEM((rhs, 2 * width), F32),
        ]
    else:
        sends_out = [pltpu.VMEM((rhs, width), BF16)] * len(plan.routes)
    index = lax.axis_index(axes).astype(jnp.int32).reshape(1)

    def scratch_for(*arrays):
        return [
            pltpu.SMEM(v.shape, v.dtype) if v.dtype == jnp.int32 else pltpu.VMEM(v.shape, v.dtype)
            for v in arrays
        ]

    current, sends, krylov = block, None, None
    for product in range(PRODUCTS):
        if product == 0:
            ins = [near_rows, near_offsets, far_rows, far_cols, block, col_basis, couplings]
            matrix = (len(plan.hops), plan.members * width, 2 * width)
            current, coupled, col_wide, row_slots, offset_slots, *sends = call(
                functools.partial(prepare_kernel, plan),
                "prepare",
                [index, *ins],
                [IN_SMEM] + [IN_HBM] * 7,
                [
                    block_out,
                    pltpu.VMEM(matrix, BF16),
                    pltpu.VMEM((width, shard_len), BF16),
                    *scratch_for(near_rows, near_offsets),
                    *sends_out,
                ],
                [IN_VMEM] * 3 + [IN_SMEM] * 2 + [IN_VMEM] * len(sends_out),
                scratch=scratch_for(far_rows, far_cols, col_basis, couplings)
                + [pltpu.VMEM(matrix[:2] + (width,), F32), pltpu.SemaphoreType.DMA((7,))],
            )
        over = lax.ppermute(block if product == 0 else current, axes, plan.over)
        near = lax.ppermute(sends[0] if plan.paired else current, axes, plan.near)
        if plan.paired:
            sends = call(
                functools.partial(relay_kernel, plan),
                "relay",
                [index, sends[1], near],
                [IN_SMEM] + [IN_VMEM] * 2,
                [relay_out] * 2,
            )
            routes = plan.across
        else:
            routes = plan.routes
        fars = [lax.ppermute(s, axes, route) for s, route in zip(sends, routes)]
        after = sends if plan.paired else []
        if product == 0:
            ins = [index, row_slots, offset_slots, current, near, row_basis, near_tiles, *after]
            acc, dense, row_wide = call(
                functools.partial(first_own_kernel, plan),
                "first_own",
                ins,
                [IN_SMEM] * 3 + [IN_VMEM] * 2 + [PREFETCHED] * 2 + [ANYWHERE] * len(after),
                [
                    acc_out,
                    pltpu.VMEM((plan.cells, plan.size, plan.size), BF16),
                    pltpu.VMEM((2 * width, shard_len), BF16),
                ],
            )
        else:
            ins = [index, current, near, dense, *after] + ([krylov] if product > 1 else [])
            acc, krylov = call(
                functools.partial(own_kernel, plan, product - 1),
                "own",
                ins,
                [IN_SMEM] + [IN_VMEM] * 3 + [ANYWHERE] * (len(ins) - 4),
                [acc_out, krylov_out],
                [IN_VMEM, ANYWHERE],
                [pltpu.SemaphoreType.DMA],
                {len(ins) - 1: 1} if product > 1 else None,
            )
        if product < PRODUCTS - 1:
            (acc,) = call(
                functools.partial(halo_kernel, plan),
                "halo",
                [index, acc, over, dense],
                [IN_SMEM] + [IN_VMEM] * 3,
                [acc_out],
            )
            ins = [index, acc, row_wide, col_wide, coupled, *fars]
            current, *sends = call(
                functools.partial(finish_kernel, plan, len(fars)),
                "finish",
                ins,
                [IN_SMEM] + [IN_VMEM] * (len(ins) - 1),
                [block_out, *sends_out],
            )
        else:
            ins = [index, acc, over, dense, row_wide, *fars, krylov]
            (krylov,) = call(
                functools.partial(last_kernel, plan, len(fars), product),
                "last",
                ins,
                [IN_SMEM] + [IN_VMEM] * (len(ins) - 2) + [ANYWHERE],
                [krylov_out],
                [ANYWHERE],
                [
                    pltpu.VMEM((rhs, shard_len), BF16),
                    pltpu.SemaphoreType.DMA((plan.per_device,)),
                ],
                {len(ins) - 1: 0},
            )
    return krylov


def solution(mesh):
    split = ("groups", "loop", "far")
    wide, narrow = P(split, None, None), P(split)
    in_specs = (P(None, split), wide, narrow, narrow, wide, wide, narrow, narrow, wide)
    return jax.shard_map(
        on_device, mesh=mesh, in_specs=in_specs, out_specs=P(None, None, split), check_vma=False
    )
```

```python
import functools

import jax
import jax.numpy as jnp
from jax import lax
from jax.experimental import pallas as pl
from jax.experimental.pallas import tpu as pltpu
from jax.sharding import PartitionSpec as P

PRODUCTS = 4
REACH = 4
LEVELS = 3
SPAN = 2 * REACH + 1
OTHER_CORE_FIRST = 0b11101111

F32 = jnp.float32
BF16 = jnp.bfloat16
IN_VMEM = pl.BlockSpec(memory_space=pltpu.VMEM)
PREFETCHED = pl.BlockSpec(memory_space=pltpu.VMEM)
IN_SMEM = pl.BlockSpec(memory_space=pltpu.SMEM)
IN_HBM = pl.BlockSpec(memory_space=pltpu.HBM)
ANYWHERE = pl.BlockSpec(memory_space=pl.ANY)


def dot_nt(a, b):
    return lax.dot_general(a, b, (((1,), (1,)), ((), ())), preferred_element_type=F32)


def dot_nn(a, b):
    return lax.dot_general(a, b, (((1,), (0,)), ((), ())), preferred_element_type=F32)


def halves(value):
    upper = value.astype(BF16)
    return upper, (value - upper.astype(F32)).astype(BF16)


class Plan:
    def __init__(self, block_shape, tile_shape, coupling_shape, members, loop_size):
        self.rhs, self.shard_len = block_shape
        self.tiles, self.size, _ = tile_shape
        self.slots, self.rank, _ = coupling_shape
        self.members, self.loop_size = members, loop_size
        self.per_device = self.shard_len // self.size
        self.width = self.per_device * self.rank
        self.cells = self.per_device * SPAN
        self.block_clusters = self.per_device * members
        distances = [d % loop_size for d in (2, loop_size - 2, loop_size // 2)]
        self.hops = sorted(set(distances))
        self.set_of = [self.hops.index(d) for d in distances]
        self.paired = len(self.hops) == 1 and 2 * self.hops[0] == loop_size and members == 4
        devices = members * loop_size
        self.near = [(i, i ^ 1) for i in range(devices)]
        self.over = [(i, (i + 1 if i % 2 else i - 1) % devices) for i in range(devices)]
        places = [(l, m) for l in range(loop_size) for m in range(members)]
        self.across = [
            [
                (l * members + m, self.far_target(l, m)[turn])
                for l, m in places
            ]
            for turn in range(2)
        ]
        self.routes = [
            [(l * members + m, (l + hop) % loop_size * members + (m + step) % members) for l, m in places]
            for hop in self.hops
            for step in range(members)
        ]

    def far_target(self, loop_index, member):
        block = (loop_index + self.hops[0]) % self.loop_size
        pair, core = divmod(member, 2)
        chip = block * 2 + (pair ^ core)
        first = core ^ (OTHER_CORE_FIRST >> chip & 1)
        return 2 * chip + first, 2 * chip + (first ^ 1)

    def first_is_odd(self, index_ref):
        index = index_ref[0]
        block = lax.rem(lax.div(index, self.members) + self.hops[0], self.loop_size)
        pair, core = lax.div(self.member(index_ref), 2), lax.rem(index, 2)
        chip = block * 2 + lax.bitwise_xor(pair, core)
        swapped = lax.bitwise_and(lax.shift_right_logical(jnp.int32(OTHER_CORE_FIRST), chip), 1)
        return lax.bitwise_xor(core, swapped) == 1

    def panel(self, ref, c):
        return ref[:, c * self.size : (c + 1) * self.size]

    def member(self, index_ref):
        return lax.rem(index_ref[0], self.members)

    def send_far(self, index_ref, x, cb_ref, g_ref, out_refs):
        coeffs = dot_nt(x, cb_ref[...]).astype(BF16)
        twice = jnp.concatenate([coeffs, coeffs], axis=1)
        totals = [dot_nt(twice, g_ref[index]) for index in range(len(self.hops))]
        if not self.paired:
            for i, out_ref in enumerate(out_refs):
                step = i % self.members * self.width
                out_ref[...] = totals[i // self.members][:, step : step + self.width].astype(BF16)
            return
        message_ref, keep_ref = out_refs
        (total,) = totals
        member = self.member(index_ref)
        second = lax.rem(member, 2) != lax.div(member, 2)
        first, last = total[:, : 2 * self.width], total[:, 2 * self.width :]
        keep_ref[...] = jnp.where(second, last, first)
        upper, lower = halves(jnp.where(second, first, last))
        message_ref[:, : self.shard_len] = x
        message_ref[:, self.shard_len : self.shard_len + 2 * self.width] = upper
        message_ref[:, self.shard_len + 2 * self.width :] = lower

    def relay_far(self, index_ref, keep_ref, message_ref, out_refs):
        upper = message_ref[:, self.shard_len : self.shard_len + 2 * self.width].astype(F32)
        lower = message_ref[:, self.shard_len + 2 * self.width :].astype(F32)
        total = (keep_ref[...] + (upper + lower)).astype(BF16)
        odd = self.first_is_odd(index_ref)
        first, last = total[:, : self.width], total[:, self.width :]
        out_refs[0][...] = jnp.where(odd, last, first)
        out_refs[1][...] = jnp.where(odd, first, last)

    def far_sum(self, far_refs):
        return sum(ref[...].astype(F32) for ref in far_refs)

    def near_sums(self, x_ref, d_ref, acc_ref, first, start_ref=None):
        panels = [self.panel(x_ref, c) for c in range(self.per_device)]
        for r in range(self.per_device):
            value = None if start_ref is None else self.panel(start_ref, r)
            for c in range(self.per_device):
                offset = first + c - r
                if -REACH <= offset <= REACH:
                    term = dot_nt(panels[c], d_ref[r * SPAN + offset + REACH])
                    value = term if value is None else value + term
            acc_ref[:, r * self.size : (r + 1) * self.size] = value

    def halo_sums(self, below, x_ref, d_ref, acc_ref, start_ref):
        @pl.when(below)
        def _():
            self.near_sums(x_ref, d_ref, acc_ref, -self.per_device, start_ref)

        @pl.when(jnp.logical_not(below))
        def _():
            self.near_sums(x_ref, d_ref, acc_ref, self.per_device, start_ref)

    def far_halves(self, far_refs):
        return jnp.concatenate(halves(self.far_sum(far_refs)), axis=1)

    def next_panel(self, acc_ref, rb_ref, both, c):
        return (self.panel(acc_ref, c) + dot_nn(both, self.panel(rb_ref, c))).astype(BF16)

    def next_block(self, acc_ref, rb_ref, far_refs):
        both = self.far_halves(far_refs)
        panels = [self.next_panel(acc_ref, rb_ref, both, c) for c in range(self.per_device)]
        return jnp.concatenate(panels, axis=1)


def prepare_kernel(plan, index_ref, *refs):
    sources, refs = refs[:7], refs[7:]
    x_ref, g_ref, cb_ref, near_ref, offsets_ref = refs[:5]
    sends, (rows_ref, cols_ref, col_ref, coup_ref, sum_ref, sems) = refs[5:-6], refs[-6:]
    targets = (near_ref, offsets_ref, rows_ref, cols_ref, x_ref, col_ref, coup_ref)
    copies = [
        pltpu.make_async_copy(source, target, sems.at[i])
        for i, (source, target) in enumerate(zip(sources, targets))
    ]
    for copy in copies:
        copy.start()
    rank, size = plan.rank, plan.size
    cb_ref[...] = jnp.zeros_like(cb_ref)
    sum_ref[...] = jnp.zeros_like(sum_ref)
    for copy in copies:
        copy.wait()
    for c in range(plan.per_device):
        cb_ref[c * rank : (c + 1) * rank, c * size : (c + 1) * size] = col_ref[c]
    column = lax.broadcasted_iota(jnp.int32, (rank, plan.width), 1) // rank
    shift = 0 if plan.paired else plan.member(index_ref)
    for s in range(plan.slots):
        row = lax.rem(rows_ref[s], plan.block_clusters)
        step = lax.rem(lax.div(row, plan.per_device) - shift + plan.members, plan.members)
        place = step * plan.per_device + lax.rem(row, plan.per_device)
        if len(plan.hops) > 1:
            level = lax.div(rows_ref[s], plan.block_clusters)
            index = sum(jnp.where(level == i, index, 0) for i, index in enumerate(plan.set_of))
        else:
            index = 0
        where = (index, pl.ds(pl.multiple_of(place * rank, rank), rank), slice(None))
        tile = coup_ref[s].astype(F32)
        wide = jnp.where(column == cols_ref[s], jnp.concatenate([tile] * plan.per_device, axis=1), 0.0)
        sum_ref[where] = sum_ref[where] + wide
    for index in range(len(plan.hops)):
        g_ref[index] = jnp.concatenate(halves(sum_ref[index]), axis=1)
    plan.send_far(index_ref, x_ref[...], cb_ref, g_ref, sends)


def relay_kernel(plan, index_ref, keep_ref, message_ref, *out_refs):
    plan.relay_far(index_ref, keep_ref, message_ref, out_refs)


def first_own_kernel(plan, *refs):
    index_ref, rows_ref, offsets_ref, x_ref, near_ref, row_ref, tiles_ref = refs[:7]
    acc_ref, d_ref, rb_ref = refs[-3:]
    rank, size = plan.rank, plan.size
    for cell in range(plan.cells):
        d_ref[cell] = jnp.zeros(d_ref.shape[1:], d_ref.dtype)
    for s in range(plan.tiles):
        d_ref[rows_ref[s] * SPAN + offsets_ref[s] + REACH] = tiles_ref[s]
    rb_ref[...] = jnp.zeros_like(rb_ref)
    for c in range(plan.per_device):
        for start in (c * rank, plan.width + c * rank):
            rb_ref[start : start + rank, c * size : (c + 1) * size] = row_ref[c]
    plan.near_sums(x_ref, d_ref, acc_ref, 0)
    plan.halo_sums(lax.rem(index_ref[0], 2) == 1, near_ref, d_ref, acc_ref, acc_ref)


def own_kernel(plan, slot, *refs):
    index_ref, x_ref, near_ref, d_ref = refs[:4]
    acc_ref, krylov_ref, sem = refs[-3:]
    copy = pltpu.make_async_copy(x_ref, krylov_ref.at[slot], sem)
    copy.start()
    plan.near_sums(x_ref, d_ref, acc_ref, 0)
    plan.halo_sums(lax.rem(index_ref[0], 2) == 1, near_ref, d_ref, acc_ref, acc_ref)
    copy.wait()


def halo_kernel(plan, index_ref, acc_ref, over_ref, d_ref, *refs):
    plan.halo_sums(lax.rem(index_ref[0], 2) == 0, over_ref, d_ref, refs[-1], acc_ref)


def finish_kernel(plan, fars, *refs):
    index_ref, acc_ref, rb_ref, cb_ref, g_ref = refs[:5]
    far_refs, (x_ref, *sends) = refs[5 : 5 + fars], refs[5 + fars :]
    x = plan.next_block(acc_ref, rb_ref, far_refs)
    x_ref[...] = x
    plan.send_far(index_ref, x, cb_ref, g_ref, sends)


def last_kernel(plan, fars, slot, *refs):
    acc_ref, rb_ref = refs[:2]
    far_refs, (_, krylov_ref, x_ref, sem) = refs[2 : 2 + fars], refs[2 + fars :]
    both = plan.far_halves(far_refs)
    copies = []
    for c in range(plan.per_device):
        columns = pl.ds(c * plan.size, plan.size)
        x_ref[:, columns] = plan.next_panel(acc_ref, rb_ref, both, c)
        copies.append(
            pltpu.make_async_copy(x_ref.at[:, columns], krylov_ref.at[slot, :, columns], sem.at[c])
        )
        copies[-1].start()
    for copy in copies:
        copy.wait()


def call(kernel, name, ins, specs, outs, out_specs=None, scratch=(), aliases=None):
    spaces = {id(IN_VMEM): pltpu.VMEM, id(IN_HBM): pltpu.HBM}
    ins = [
        pltpu.with_memory_space_constraint(v, spaces[id(spec)]) if id(spec) in spaces else v
        for v, spec in zip(ins, specs)
    ]
    return pl.pallas_call(
        kernel,
        in_specs=list(specs),
        out_specs=out_specs or [IN_VMEM] * len(outs),
        out_shape=list(outs),
        scratch_shapes=list(scratch),
        input_output_aliases=aliases or {},
        compiler_params=pltpu.CompilerParams(vmem_limit_bytes=16 * 2**20),
        cost_estimate=pl.CostEstimate(flops=10**9, bytes_accessed=2**22, transcendentals=0),
        name=name,
    )(*ins)


def on_device(
    block, near_tiles, near_rows, near_offsets, col_basis, couplings, far_rows, far_cols, row_basis
):
    axes = ("loop", "far")
    plan = Plan(
        block.shape, near_tiles.shape, couplings.shape, lax.axis_size("far"), lax.axis_size("loop")
    )
    rhs, shard_len, width = plan.rhs, plan.shard_len, plan.width
    block_out = pltpu.VMEM((rhs, shard_len), BF16)
    acc_out = pltpu.VMEM((rhs, shard_len), F32)
    relay_out = pltpu.VMEM((rhs, width), BF16)
    krylov_out = jax.ShapeDtypeStruct((PRODUCTS, rhs, shard_len), BF16)
    if plan.paired:
        sends_out = [
            pltpu.VMEM((rhs, shard_len + 4 * width), BF16),
            pltpu.VMEM((rhs, 2 * width), F32),
        ]
    else:
        sends_out = [pltpu.VMEM((rhs, width), BF16)] * len(plan.routes)
    index = lax.axis_index(axes).astype(jnp.int32).reshape(1)

    def scratch_for(*arrays):
        return [
            pltpu.SMEM(v.shape, v.dtype) if v.dtype == jnp.int32 else pltpu.VMEM(v.shape, v.dtype)
            for v in arrays
        ]

    current, sends, krylov = block, None, None
    for product in range(PRODUCTS):
        if product == 0:
            ins = [near_rows, near_offsets, far_rows, far_cols, block, col_basis, couplings]
            matrix = (len(plan.hops), plan.members * width, 2 * width)
            current, coupled, col_wide, row_slots, offset_slots, *sends = call(
                functools.partial(prepare_kernel, plan),
                "prepare",
                [index, *ins],
                [IN_SMEM] + [IN_HBM] * 7,
                [
                    block_out,
                    pltpu.VMEM(matrix, BF16),
                    pltpu.VMEM((width, shard_len), BF16),
                    *scratch_for(near_rows, near_offsets),
                    *sends_out,
                ],
                [IN_VMEM] * 3 + [IN_SMEM] * 2 + [IN_VMEM] * len(sends_out),
                scratch=scratch_for(far_rows, far_cols, col_basis, couplings)
                + [pltpu.VMEM(matrix[:2] + (width,), F32), pltpu.SemaphoreType.DMA((7,))],
            )
        over = lax.ppermute(block if product == 0 else current, axes, plan.over)
        near = lax.ppermute(sends[0] if plan.paired else current, axes, plan.near)
        if plan.paired:
            sends = call(
                functools.partial(relay_kernel, plan),
                "relay",
                [index, sends[1], near],
                [IN_SMEM] + [IN_VMEM] * 2,
                [relay_out] * 2,
            )
            routes = plan.across
        else:
            routes = plan.routes
        fars = [lax.ppermute(s, axes, route) for s, route in zip(sends, routes)]
        after = sends if plan.paired else []
        if product == 0:
            ins = [index, row_slots, offset_slots, current, near, row_basis, near_tiles, *after]
            acc, dense, row_wide = call(
                functools.partial(first_own_kernel, plan),
                "first_own",
                ins,
                [IN_SMEM] * 3 + [IN_VMEM] * 2 + [PREFETCHED] * 2 + [ANYWHERE] * len(after),
                [
                    acc_out,
                    pltpu.VMEM((plan.cells, plan.size, plan.size), BF16),
                    pltpu.VMEM((2 * width, shard_len), BF16),
                ],
            )
        else:
            ins = [index, current, near, dense, *after] + ([krylov] if product > 1 else [])
            acc, krylov = call(
                functools.partial(own_kernel, plan, product - 1),
                "own",
                ins,
                [IN_SMEM] + [IN_VMEM] * 3 + [ANYWHERE] * (len(ins) - 4),
                [acc_out, krylov_out],
                [IN_VMEM, ANYWHERE],
                [pltpu.SemaphoreType.DMA],
                {len(ins) - 1: 1} if product > 1 else None,
            )
        (acc,) = call(
            functools.partial(halo_kernel, plan),
            "halo",
            [index, acc, over, dense],
            [IN_SMEM] + [IN_VMEM] * 3,
            [acc_out],
        )
        if product < PRODUCTS - 1:
            ins = [index, acc, row_wide, col_wide, coupled, *fars]
            current, *sends = call(
                functools.partial(finish_kernel, plan, len(fars)),
                "finish",
                ins,
                [IN_SMEM] + [IN_VMEM] * (len(ins) - 1),
                [block_out, *sends_out],
            )
        else:
            ins = [acc, row_wide, *fars, krylov]
            (krylov,) = call(
                functools.partial(last_kernel, plan, len(fars), product),
                "last",
                ins,
                [IN_VMEM] * (len(ins) - 1) + [ANYWHERE],
                [krylov_out],
                [ANYWHERE],
                [
                    pltpu.VMEM((rhs, shard_len), BF16),
                    pltpu.SemaphoreType.DMA((plan.per_device,)),
                ],
                {len(ins) - 1: 0},
            )
    return krylov


def solution(mesh):
    split = ("groups", "loop", "far")
    wide, narrow = P(split, None, None), P(split)
    in_specs = (P(None, split), wide, narrow, narrow, wide, wide, narrow, narrow, wide)
    return jax.shard_map(
        on_device, mesh=mesh, in_specs=in_specs, out_specs=P(None, None, split), check_vma=False
    )
```

```python
import functools

import jax
import jax.numpy as jnp
from jax import lax
from jax.experimental import pallas as pl
from jax.experimental.pallas import tpu as pltpu
from jax.sharding import PartitionSpec as P

PRODUCTS = 4
REACH = 4
LEVELS = 3
SPAN = 2 * REACH + 1
OTHER_CORE_FIRST = 0b11001111

F32 = jnp.float32
BF16 = jnp.bfloat16
IN_VMEM = pl.BlockSpec(memory_space=pltpu.VMEM)
PREFETCHED = pl.BlockSpec(memory_space=pltpu.VMEM)
IN_SMEM = pl.BlockSpec(memory_space=pltpu.SMEM)
IN_HBM = pl.BlockSpec(memory_space=pltpu.HBM)
ANYWHERE = pl.BlockSpec(memory_space=pl.ANY)


def dot_nt(a, b):
    return lax.dot_general(a, b, (((1,), (1,)), ((), ())), preferred_element_type=F32)


def dot_nn(a, b):
    return lax.dot_general(a, b, (((1,), (0,)), ((), ())), preferred_element_type=F32)


def halves(value):
    upper = value.astype(BF16)
    return upper, (value - upper.astype(F32)).astype(BF16)


class Plan:
    def __init__(self, block_shape, tile_shape, coupling_shape, members, loop_size):
        self.rhs, self.shard_len = block_shape
        self.tiles, self.size, _ = tile_shape
        self.slots, self.rank, _ = coupling_shape
        self.members, self.loop_size = members, loop_size
        self.per_device = self.shard_len // self.size
        self.width = self.per_device * self.rank
        self.cells = self.per_device * SPAN
        self.block_clusters = self.per_device * members
        distances = [d % loop_size for d in (2, loop_size - 2, loop_size // 2)]
        self.hops = sorted(set(distances))
        self.set_of = [self.hops.index(d) for d in distances]
        self.paired = len(self.hops) == 1 and 2 * self.hops[0] == loop_size and members == 4
        devices = members * loop_size
        self.near = [(i, i ^ 1) for i in range(devices)]
        self.over = [(i, (i + 1 if i % 2 else i - 1) % devices) for i in range(devices)]
        places = [(l, m) for l in range(loop_size) for m in range(members)]
        self.across = [
            [
                (l * members + m, self.far_target(l, m)[turn])
                for l, m in places
            ]
            for turn in range(2)
        ]
        self.routes = [
            [(l * members + m, (l + hop) % loop_size * members + (m + step) % members) for l, m in places]
            for hop in self.hops
            for step in range(members)
        ]

    def far_target(self, loop_index, member):
        block = (loop_index + self.hops[0]) % self.loop_size
        pair, core = divmod(member, 2)
        chip = block * 2 + (pair ^ core)
        first = core ^ (OTHER_CORE_FIRST >> chip & 1)
        return 2 * chip + first, 2 * chip + (first ^ 1)

    def first_is_odd(self, index_ref):
        index = index_ref[0]
        block = lax.rem(lax.div(index, self.members) + self.hops[0], self.loop_size)
        pair, core = lax.div(self.member(index_ref), 2), lax.rem(index, 2)
        chip = block * 2 + lax.bitwise_xor(pair, core)
        swapped = lax.bitwise_and(lax.shift_right_logical(jnp.int32(OTHER_CORE_FIRST), chip), 1)
        return lax.bitwise_xor(core, swapped) == 1

    def panel(self, ref, c):
        return ref[:, c * self.size : (c + 1) * self.size]

    def member(self, index_ref):
        return lax.rem(index_ref[0], self.members)

    def send_far(self, index_ref, x, cb_ref, g_ref, out_refs):
        coeffs = dot_nt(x, cb_ref[...]).astype(BF16)
        twice = jnp.concatenate([coeffs, coeffs], axis=1)
        totals = [dot_nt(twice, g_ref[index]) for index in range(len(self.hops))]
        if not self.paired:
            for i, out_ref in enumerate(out_refs):
                step = i % self.members * self.width
                out_ref[...] = totals[i // self.members][:, step : step + self.width].astype(BF16)
            return
        message_ref, keep_ref = out_refs
        (total,) = totals
        member = self.member(index_ref)
        second = lax.rem(member, 2) != lax.div(member, 2)
        first, last = total[:, : 2 * self.width], total[:, 2 * self.width :]
        keep_ref[...] = jnp.where(second, last, first)
        upper, lower = halves(jnp.where(second, first, last))
        message_ref[:, : self.shard_len] = x
        message_ref[:, self.shard_len : self.shard_len + 2 * self.width] = upper
        message_ref[:, self.shard_len + 2 * self.width :] = lower

    def relay_far(self, index_ref, keep_ref, message_ref, out_refs):
        upper = message_ref[:, self.shard_len : self.shard_len + 2 * self.width].astype(F32)
        lower = message_ref[:, self.shard_len + 2 * self.width :].astype(F32)
        total = (keep_ref[...] + (upper + lower)).astype(BF16)
        odd = self.first_is_odd(index_ref)
        first, last = total[:, : self.width], total[:, self.width :]
        out_refs[0][...] = jnp.where(odd, last, first)
        out_refs[1][...] = jnp.where(odd, first, last)

    def far_sum(self, far_refs):
        return sum(ref[...].astype(F32) for ref in far_refs)

    def near_sums(self, x_ref, d_ref, acc_ref, first, start_ref=None):
        panels = [self.panel(x_ref, c) for c in range(self.per_device)]
        for r in range(self.per_device):
            value = None if start_ref is None else self.panel(start_ref, r)
            for c in range(self.per_device):
                offset = first + c - r
                if -REACH <= offset <= REACH:
                    term = dot_nt(panels[c], d_ref[r * SPAN + offset + REACH])
                    value = term if value is None else value + term
            acc_ref[:, r * self.size : (r + 1) * self.size] = value

    def halo_sums(self, below, x_ref, d_ref, acc_ref, start_ref):
        @pl.when(below)
        def _():
            self.near_sums(x_ref, d_ref, acc_ref, -self.per_device, start_ref)

        @pl.when(jnp.logical_not(below))
        def _():
            self.near_sums(x_ref, d_ref, acc_ref, self.per_device, start_ref)

    def far_halves(self, far_refs):
        return jnp.concatenate(halves(self.far_sum(far_refs)), axis=1)

    def next_panel(self, acc_ref, rb_ref, both, c):
        return (self.panel(acc_ref, c) + dot_nn(both, self.panel(rb_ref, c))).astype(BF16)

    def next_block(self, acc_ref, rb_ref, far_refs):
        both = self.far_halves(far_refs)
        panels = [self.next_panel(acc_ref, rb_ref, both, c) for c in range(self.per_device)]
        return jnp.concatenate(panels, axis=1)


def prepare_kernel(plan, index_ref, *refs):
    sources, refs = refs[:7], refs[7:]
    x_ref, g_ref, cb_ref, near_ref, offsets_ref = refs[:5]
    sends, (rows_ref, cols_ref, col_ref, coup_ref, sum_ref, sems) = refs[5:-6], refs[-6:]
    targets = (near_ref, offsets_ref, rows_ref, cols_ref, x_ref, col_ref, coup_ref)
    copies = [
        pltpu.make_async_copy(source, target, sems.at[i])
        for i, (source, target) in enumerate(zip(sources, targets))
    ]
    for copy in copies:
        copy.start()
    rank, size = plan.rank, plan.size
    cb_ref[...] = jnp.zeros_like(cb_ref)
    sum_ref[...] = jnp.zeros_like(sum_ref)
    for copy in copies:
        copy.wait()
    for c in range(plan.per_device):
        cb_ref[c * rank : (c + 1) * rank, c * size : (c + 1) * size] = col_ref[c]
    column = lax.broadcasted_iota(jnp.int32, (rank, plan.width), 1) // rank
    shift = 0 if plan.paired else plan.member(index_ref)
    for s in range(plan.slots):
        row = lax.rem(rows_ref[s], plan.block_clusters)
        step = lax.rem(lax.div(row, plan.per_device) - shift + plan.members, plan.members)
        place = step * plan.per_device + lax.rem(row, plan.per_device)
        if len(plan.hops) > 1:
            level = lax.div(rows_ref[s], plan.block_clusters)
            index = sum(jnp.where(level == i, index, 0) for i, index in enumerate(plan.set_of))
        else:
            index = 0
        where = (index, pl.ds(pl.multiple_of(place * rank, rank), rank), slice(None))
        tile = coup_ref[s].astype(F32)
        wide = jnp.where(column == cols_ref[s], jnp.concatenate([tile] * plan.per_device, axis=1), 0.0)
        sum_ref[where] = sum_ref[where] + wide
    for index in range(len(plan.hops)):
        g_ref[index] = jnp.concatenate(halves(sum_ref[index]), axis=1)
    plan.send_far(index_ref, x_ref[...], cb_ref, g_ref, sends)


def relay_kernel(plan, index_ref, keep_ref, message_ref, *out_refs):
    plan.relay_far(index_ref, keep_ref, message_ref, out_refs)


def first_own_kernel(plan, *refs):
    index_ref, rows_ref, offsets_ref, x_ref, near_ref, row_ref, tiles_ref = refs[:7]
    acc_ref, d_ref, rb_ref = refs[-3:]
    rank, size = plan.rank, plan.size
    for cell in range(plan.cells):
        d_ref[cell] = jnp.zeros(d_ref.shape[1:], d_ref.dtype)
    for s in range(plan.tiles):
        d_ref[rows_ref[s] * SPAN + offsets_ref[s] + REACH] = tiles_ref[s]
    rb_ref[...] = jnp.zeros_like(rb_ref)
    for c in range(plan.per_device):
        for start in (c * rank, plan.width + c * rank):
            rb_ref[start : start + rank, c * size : (c + 1) * size] = row_ref[c]
    plan.near_sums(x_ref, d_ref, acc_ref, 0)
    plan.halo_sums(lax.rem(index_ref[0], 2) == 1, near_ref, d_ref, acc_ref, acc_ref)


def own_kernel(plan, slot, *refs):
    index_ref, x_ref, near_ref, d_ref = refs[:4]
    acc_ref, krylov_ref, sem = refs[-3:]
    copy = pltpu.make_async_copy(x_ref, krylov_ref.at[slot], sem)
    copy.start()
    plan.near_sums(x_ref, d_ref, acc_ref, 0)
    plan.halo_sums(lax.rem(index_ref[0], 2) == 1, near_ref, d_ref, acc_ref, acc_ref)
    copy.wait()


def halo_kernel(plan, index_ref, acc_ref, over_ref, d_ref, *refs):
    plan.halo_sums(lax.rem(index_ref[0], 2) == 0, over_ref, d_ref, refs[-1], acc_ref)


def finish_kernel(plan, fars, *refs):
    index_ref, acc_ref, rb_ref, cb_ref, g_ref = refs[:5]
    far_refs, (x_ref, *sends) = refs[5 : 5 + fars], refs[5 + fars :]
    x = plan.next_block(acc_ref, rb_ref, far_refs)
    x_ref[...] = x
    plan.send_far(index_ref, x, cb_ref, g_ref, sends)


def last_kernel(plan, fars, slot, *refs):
    acc_ref, rb_ref = refs[:2]
    far_refs, (_, krylov_ref, x_ref, sem) = refs[2 : 2 + fars], refs[2 + fars :]
    both = plan.far_halves(far_refs)
    copies = []
    for c in range(plan.per_device):
        columns = pl.ds(c * plan.size, plan.size)
        x_ref[:, columns] = plan.next_panel(acc_ref, rb_ref, both, c)
        copies.append(
            pltpu.make_async_copy(x_ref.at[:, columns], krylov_ref.at[slot, :, columns], sem.at[c])
        )
        copies[-1].start()
    for copy in copies:
        copy.wait()


def call(kernel, name, ins, specs, outs, out_specs=None, scratch=(), aliases=None):
    spaces = {id(IN_VMEM): pltpu.VMEM, id(IN_HBM): pltpu.HBM}
    ins = [
        pltpu.with_memory_space_constraint(v, spaces[id(spec)]) if id(spec) in spaces else v
        for v, spec in zip(ins, specs)
    ]
    return pl.pallas_call(
        kernel,
        in_specs=list(specs),
        out_specs=out_specs or [IN_VMEM] * len(outs),
        out_shape=list(outs),
        scratch_shapes=list(scratch),
        input_output_aliases=aliases or {},
        compiler_params=pltpu.CompilerParams(vmem_limit_bytes=16 * 2**20),
        cost_estimate=pl.CostEstimate(flops=10**9, bytes_accessed=2**22, transcendentals=0),
        name=name,
    )(*ins)


def on_device(
    block, near_tiles, near_rows, near_offsets, col_basis, couplings, far_rows, far_cols, row_basis
):
    axes = ("loop", "far")
    plan = Plan(
        block.shape, near_tiles.shape, couplings.shape, lax.axis_size("far"), lax.axis_size("loop")
    )
    rhs, shard_len, width = plan.rhs, plan.shard_len, plan.width
    block_out = pltpu.VMEM((rhs, shard_len), BF16)
    acc_out = pltpu.VMEM((rhs, shard_len), F32)
    relay_out = pltpu.VMEM((rhs, width), BF16)
    krylov_out = jax.ShapeDtypeStruct((PRODUCTS, rhs, shard_len), BF16)
    if plan.paired:
        sends_out = [
            pltpu.VMEM((rhs, shard_len + 4 * width), BF16),
            pltpu.VMEM((rhs, 2 * width), F32),
        ]
    else:
        sends_out = [pltpu.VMEM((rhs, width), BF16)] * len(plan.routes)
    index = lax.axis_index(axes).astype(jnp.int32).reshape(1)

    def scratch_for(*arrays):
        return [
            pltpu.SMEM(v.shape, v.dtype) if v.dtype == jnp.int32 else pltpu.VMEM(v.shape, v.dtype)
            for v in arrays
        ]

    current, sends, krylov = block, None, None
    for product in range(PRODUCTS):
        if product == 0:
            ins = [near_rows, near_offsets, far_rows, far_cols, block, col_basis, couplings]
            matrix = (len(plan.hops), plan.members * width, 2 * width)
            current, coupled, col_wide, row_slots, offset_slots, *sends = call(
                functools.partial(prepare_kernel, plan),
                "prepare",
                [index, *ins],
                [IN_SMEM] + [IN_HBM] * 7,
                [
                    block_out,
                    pltpu.VMEM(matrix, BF16),
                    pltpu.VMEM((width, shard_len), BF16),
                    *scratch_for(near_rows, near_offsets),
                    *sends_out,
                ],
                [IN_VMEM] * 3 + [IN_SMEM] * 2 + [IN_VMEM] * len(sends_out),
                scratch=scratch_for(far_rows, far_cols, col_basis, couplings)
                + [pltpu.VMEM(matrix[:2] + (width,), F32), pltpu.SemaphoreType.DMA((7,))],
            )
        over = lax.ppermute(block if product == 0 else current, axes, plan.over)
        near = lax.ppermute(sends[0] if plan.paired else current, axes, plan.near)
        if plan.paired:
            sends = call(
                functools.partial(relay_kernel, plan),
                "relay",
                [index, sends[1], near],
                [IN_SMEM] + [IN_VMEM] * 2,
                [relay_out] * 2,
            )
            routes = plan.across
        else:
            routes = plan.routes
        fars = [lax.ppermute(s, axes, route) for s, route in zip(sends, routes)]
        after = sends if plan.paired else []
        if product == 0:
            ins = [index, row_slots, offset_slots, current, near, row_basis, near_tiles, *after]
            acc, dense, row_wide = call(
                functools.partial(first_own_kernel, plan),
                "first_own",
                ins,
                [IN_SMEM] * 3 + [IN_VMEM] * 2 + [PREFETCHED] * 2 + [ANYWHERE] * len(after),
                [
                    acc_out,
                    pltpu.VMEM((plan.cells, plan.size, plan.size), BF16),
                    pltpu.VMEM((2 * width, shard_len), BF16),
                ],
            )
        else:
            ins = [index, current, near, dense, *after] + ([krylov] if product > 1 else [])
            acc, krylov = call(
                functools.partial(own_kernel, plan, product - 1),
                "own",
                ins,
                [IN_SMEM] + [IN_VMEM] * 3 + [ANYWHERE] * (len(ins) - 4),
                [acc_out, krylov_out],
                [IN_VMEM, ANYWHERE],
                [pltpu.SemaphoreType.DMA],
                {len(ins) - 1: 1} if product > 1 else None,
            )
        (acc,) = call(
            functools.partial(halo_kernel, plan),
            "halo",
            [index, acc, over, dense],
            [IN_SMEM] + [IN_VMEM] * 3,
            [acc_out],
        )
        if product < PRODUCTS - 1:
            ins = [index, acc, row_wide, col_wide, coupled, *fars]
            current, *sends = call(
                functools.partial(finish_kernel, plan, len(fars)),
                "finish",
                ins,
                [IN_SMEM] + [IN_VMEM] * (len(ins) - 1),
                [block_out, *sends_out],
            )
        else:
            ins = [acc, row_wide, *fars, krylov]
            (krylov,) = call(
                functools.partial(last_kernel, plan, len(fars), product),
                "last",
                ins,
                [IN_VMEM] * (len(ins) - 1) + [ANYWHERE],
                [krylov_out],
                [ANYWHERE],
                [
                    pltpu.VMEM((rhs, shard_len), BF16),
                    pltpu.SemaphoreType.DMA((plan.per_device,)),
                ],
                {len(ins) - 1: 0},
            )
    return krylov


def solution(mesh):
    split = ("groups", "loop", "far")
    wide, narrow = P(split, None, None), P(split)
    in_specs = (P(None, split), wide, narrow, narrow, wide, wide, narrow, narrow, wide)
    return jax.shard_map(
        on_device, mesh=mesh, in_specs=in_specs, out_specs=P(None, None, split), check_vma=False
    )
```

```python
import functools

import jax
import jax.numpy as jnp
from jax import lax
from jax.experimental import pallas as pl
from jax.experimental.pallas import tpu as pltpu
from jax.sharding import PartitionSpec as P

PRODUCTS = 4
REACH = 4
LEVELS = 3
SPAN = 2 * REACH + 1
OTHER_CORE_FIRST = 0b11110111

F32 = jnp.float32
BF16 = jnp.bfloat16
IN_VMEM = pl.BlockSpec(memory_space=pltpu.VMEM)
PREFETCHED = pl.BlockSpec(memory_space=pltpu.VMEM)
IN_SMEM = pl.BlockSpec(memory_space=pltpu.SMEM)
IN_HBM = pl.BlockSpec(memory_space=pltpu.HBM)
ANYWHERE = pl.BlockSpec(memory_space=pl.ANY)


def dot_nt(a, b):
    return lax.dot_general(a, b, (((1,), (1,)), ((), ())), preferred_element_type=F32)


def dot_nn(a, b):
    return lax.dot_general(a, b, (((1,), (0,)), ((), ())), preferred_element_type=F32)


def halves(value):
    upper = value.astype(BF16)
    return upper, (value - upper.astype(F32)).astype(BF16)


class Plan:
    def __init__(self, block_shape, tile_shape, coupling_shape, members, loop_size):
        self.rhs, self.shard_len = block_shape
        self.tiles, self.size, _ = tile_shape
        self.slots, self.rank, _ = coupling_shape
        self.members, self.loop_size = members, loop_size
        self.per_device = self.shard_len // self.size
        self.width = self.per_device * self.rank
        self.cells = self.per_device * SPAN
        self.block_clusters = self.per_device * members
        distances = [d % loop_size for d in (2, loop_size - 2, loop_size // 2)]
        self.hops = sorted(set(distances))
        self.set_of = [self.hops.index(d) for d in distances]
        self.paired = len(self.hops) == 1 and 2 * self.hops[0] == loop_size and members == 4
        devices = members * loop_size
        self.near = [(i, i ^ 1) for i in range(devices)]
        self.over = [(i, (i + 1 if i % 2 else i - 1) % devices) for i in range(devices)]
        places = [(l, m) for l in range(loop_size) for m in range(members)]
        self.across = [
            [
                (l * members + m, self.far_target(l, m)[turn])
                for l, m in places
            ]
            for turn in range(2)
        ]
        self.routes = [
            [(l * members + m, (l + hop) % loop_size * members + (m + step) % members) for l, m in places]
            for hop in self.hops
            for step in range(members)
        ]

    def far_target(self, loop_index, member):
        block = (loop_index + self.hops[0]) % self.loop_size
        pair, core = divmod(member, 2)
        chip = block * 2 + (pair ^ core)
        first = core ^ (OTHER_CORE_FIRST >> chip & 1)
        return 2 * chip + first, 2 * chip + (first ^ 1)

    def first_is_odd(self, index_ref):
        index = index_ref[0]
        block = lax.rem(lax.div(index, self.members) + self.hops[0], self.loop_size)
        pair, core = lax.div(self.member(index_ref), 2), lax.rem(index, 2)
        chip = block * 2 + lax.bitwise_xor(pair, core)
        swapped = lax.bitwise_and(lax.shift_right_logical(jnp.int32(OTHER_CORE_FIRST), chip), 1)
        return lax.bitwise_xor(core, swapped) == 1

    def panel(self, ref, c):
        return ref[:, c * self.size : (c + 1) * self.size]

    def member(self, index_ref):
        return lax.rem(index_ref[0], self.members)

    def send_far(self, index_ref, x, cb_ref, g_ref, out_refs):
        coeffs = dot_nt(x, cb_ref[...]).astype(BF16)
        twice = jnp.concatenate([coeffs, coeffs], axis=1)
        totals = [dot_nt(twice, g_ref[index]) for index in range(len(self.hops))]
        if not self.paired:
            for i, out_ref in enumerate(out_refs):
                step = i % self.members * self.width
                out_ref[...] = totals[i // self.members][:, step : step + self.width].astype(BF16)
            return
        message_ref, keep_ref = out_refs
        (total,) = totals
        member = self.member(index_ref)
        second = lax.rem(member, 2) != lax.div(member, 2)
        first, last = total[:, : 2 * self.width], total[:, 2 * self.width :]
        keep_ref[...] = jnp.where(second, last, first)
        upper, lower = halves(jnp.where(second, first, last))
        message_ref[:, : self.shard_len] = x
        message_ref[:, self.shard_len : self.shard_len + 2 * self.width] = upper
        message_ref[:, self.shard_len + 2 * self.width :] = lower

    def relay_far(self, index_ref, keep_ref, message_ref, out_refs):
        upper = message_ref[:, self.shard_len : self.shard_len + 2 * self.width].astype(F32)
        lower = message_ref[:, self.shard_len + 2 * self.width :].astype(F32)
        total = (keep_ref[...] + (upper + lower)).astype(BF16)
        odd = self.first_is_odd(index_ref)
        first, last = total[:, : self.width], total[:, self.width :]
        out_refs[0][...] = jnp.where(odd, last, first)
        out_refs[1][...] = jnp.where(odd, first, last)

    def far_sum(self, far_refs):
        return sum(ref[...].astype(F32) for ref in far_refs)

    def near_sums(self, x_ref, d_ref, acc_ref, first, start_ref=None):
        panels = [self.panel(x_ref, c) for c in range(self.per_device)]
        for r in range(self.per_device):
            value = None if start_ref is None else self.panel(start_ref, r)
            for c in range(self.per_device):
                offset = first + c - r
                if -REACH <= offset <= REACH:
                    term = dot_nt(panels[c], d_ref[r * SPAN + offset + REACH])
                    value = term if value is None else value + term
            acc_ref[:, r * self.size : (r + 1) * self.size] = value

    def halo_sums(self, below, x_ref, d_ref, acc_ref, start_ref):
        @pl.when(below)
        def _():
            self.near_sums(x_ref, d_ref, acc_ref, -self.per_device, start_ref)

        @pl.when(jnp.logical_not(below))
        def _():
            self.near_sums(x_ref, d_ref, acc_ref, self.per_device, start_ref)

    def far_halves(self, far_refs):
        return jnp.concatenate(halves(self.far_sum(far_refs)), axis=1)

    def next_panel(self, acc_ref, rb_ref, both, c):
        return (self.panel(acc_ref, c) + dot_nn(both, self.panel(rb_ref, c))).astype(BF16)

    def next_block(self, acc_ref, rb_ref, far_refs):
        both = self.far_halves(far_refs)
        panels = [self.next_panel(acc_ref, rb_ref, both, c) for c in range(self.per_device)]
        return jnp.concatenate(panels, axis=1)


def prepare_kernel(plan, index_ref, *refs):
    sources, refs = refs[:7], refs[7:]
    x_ref, g_ref, cb_ref, near_ref, offsets_ref = refs[:5]
    sends, (rows_ref, cols_ref, col_ref, coup_ref, sum_ref, sems) = refs[5:-6], refs[-6:]
    targets = (near_ref, offsets_ref, rows_ref, cols_ref, x_ref, col_ref, coup_ref)
    copies = [
        pltpu.make_async_copy(source, target, sems.at[i])
        for i, (source, target) in enumerate(zip(sources, targets))
    ]
    for copy in copies:
        copy.start()
    rank, size = plan.rank, plan.size
    cb_ref[...] = jnp.zeros_like(cb_ref)
    sum_ref[...] = jnp.zeros_like(sum_ref)
    for copy in copies:
        copy.wait()
    for c in range(plan.per_device):
        cb_ref[c * rank : (c + 1) * rank, c * size : (c + 1) * size] = col_ref[c]
    column = lax.broadcasted_iota(jnp.int32, (rank, plan.width), 1) // rank
    shift = 0 if plan.paired else plan.member(index_ref)
    for s in range(plan.slots):
        row = lax.rem(rows_ref[s], plan.block_clusters)
        step = lax.rem(lax.div(row, plan.per_device) - shift + plan.members, plan.members)
        place = step * plan.per_device + lax.rem(row, plan.per_device)
        if len(plan.hops) > 1:
            level = lax.div(rows_ref[s], plan.block_clusters)
            index = sum(jnp.where(level == i, index, 0) for i, index in enumerate(plan.set_of))
        else:
            index = 0
        where = (index, pl.ds(pl.multiple_of(place * rank, rank), rank), slice(None))
        tile = coup_ref[s].astype(F32)
        wide = jnp.where(column == cols_ref[s], jnp.concatenate([tile] * plan.per_device, axis=1), 0.0)
        sum_ref[where] = sum_ref[where] + wide
    for index in range(len(plan.hops)):
        g_ref[index] = jnp.concatenate(halves(sum_ref[index]), axis=1)
    plan.send_far(index_ref, x_ref[...], cb_ref, g_ref, sends)


def relay_kernel(plan, index_ref, keep_ref, message_ref, *out_refs):
    plan.relay_far(index_ref, keep_ref, message_ref, out_refs)


def first_own_kernel(plan, *refs):
    index_ref, rows_ref, offsets_ref, x_ref, near_ref, row_ref, tiles_ref = refs[:7]
    acc_ref, d_ref, rb_ref = refs[-3:]
    rank, size = plan.rank, plan.size
    for cell in range(plan.cells):
        d_ref[cell] = jnp.zeros(d_ref.shape[1:], d_ref.dtype)
    for s in range(plan.tiles):
        d_ref[rows_ref[s] * SPAN + offsets_ref[s] + REACH] = tiles_ref[s]
    rb_ref[...] = jnp.zeros_like(rb_ref)
    for c in range(plan.per_device):
        for start in (c * rank, plan.width + c * rank):
            rb_ref[start : start + rank, c * size : (c + 1) * size] = row_ref[c]
    plan.near_sums(x_ref, d_ref, acc_ref, 0)
    plan.halo_sums(lax.rem(index_ref[0], 2) == 1, near_ref, d_ref, acc_ref, acc_ref)


def own_kernel(plan, slot, *refs):
    index_ref, x_ref, near_ref, d_ref = refs[:4]
    acc_ref, krylov_ref, sem = refs[-3:]
    copy = pltpu.make_async_copy(x_ref, krylov_ref.at[slot], sem)
    copy.start()
    plan.near_sums(x_ref, d_ref, acc_ref, 0)
    plan.halo_sums(lax.rem(index_ref[0], 2) == 1, near_ref, d_ref, acc_ref, acc_ref)
    copy.wait()


def halo_kernel(plan, index_ref, acc_ref, over_ref, d_ref, *refs):
    plan.halo_sums(lax.rem(index_ref[0], 2) == 0, over_ref, d_ref, refs[-1], acc_ref)


def finish_kernel(plan, fars, *refs):
    index_ref, acc_ref, rb_ref, cb_ref, g_ref = refs[:5]
    far_refs, (x_ref, *sends) = refs[5 : 5 + fars], refs[5 + fars :]
    x = plan.next_block(acc_ref, rb_ref, far_refs)
    x_ref[...] = x
    plan.send_far(index_ref, x, cb_ref, g_ref, sends)


def last_kernel(plan, fars, slot, *refs):
    acc_ref, rb_ref = refs[:2]
    far_refs, (_, krylov_ref, x_ref, sem) = refs[2 : 2 + fars], refs[2 + fars :]
    both = plan.far_halves(far_refs)
    copies = []
    for c in range(plan.per_device):
        columns = pl.ds(c * plan.size, plan.size)
        x_ref[:, columns] = plan.next_panel(acc_ref, rb_ref, both, c)
        copies.append(
            pltpu.make_async_copy(x_ref.at[:, columns], krylov_ref.at[slot, :, columns], sem.at[c])
        )
        copies[-1].start()
    for copy in copies:
        copy.wait()


def call(kernel, name, ins, specs, outs, out_specs=None, scratch=(), aliases=None):
    spaces = {id(IN_VMEM): pltpu.VMEM, id(IN_HBM): pltpu.HBM}
    ins = [
        pltpu.with_memory_space_constraint(v, spaces[id(spec)]) if id(spec) in spaces else v
        for v, spec in zip(ins, specs)
    ]
    return pl.pallas_call(
        kernel,
        in_specs=list(specs),
        out_specs=out_specs or [IN_VMEM] * len(outs),
        out_shape=list(outs),
        scratch_shapes=list(scratch),
        input_output_aliases=aliases or {},
        compiler_params=pltpu.CompilerParams(vmem_limit_bytes=16 * 2**20),
        cost_estimate=pl.CostEstimate(flops=10**9, bytes_accessed=2**22, transcendentals=0),
        name=name,
    )(*ins)


def on_device(
    block, near_tiles, near_rows, near_offsets, col_basis, couplings, far_rows, far_cols, row_basis
):
    axes = ("loop", "far")
    plan = Plan(
        block.shape, near_tiles.shape, couplings.shape, lax.axis_size("far"), lax.axis_size("loop")
    )
    rhs, shard_len, width = plan.rhs, plan.shard_len, plan.width
    block_out = pltpu.VMEM((rhs, shard_len), BF16)
    acc_out = pltpu.VMEM((rhs, shard_len), F32)
    relay_out = pltpu.VMEM((rhs, width), BF16)
    krylov_out = jax.ShapeDtypeStruct((PRODUCTS, rhs, shard_len), BF16)
    if plan.paired:
        sends_out = [
            pltpu.VMEM((rhs, shard_len + 4 * width), BF16),
            pltpu.VMEM((rhs, 2 * width), F32),
        ]
    else:
        sends_out = [pltpu.VMEM((rhs, width), BF16)] * len(plan.routes)
    index = lax.axis_index(axes).astype(jnp.int32).reshape(1)

    def scratch_for(*arrays):
        return [
            pltpu.SMEM(v.shape, v.dtype) if v.dtype == jnp.int32 else pltpu.VMEM(v.shape, v.dtype)
            for v in arrays
        ]

    current, sends, krylov = block, None, None
    for product in range(PRODUCTS):
        if product == 0:
            ins = [near_rows, near_offsets, far_rows, far_cols, block, col_basis, couplings]
            matrix = (len(plan.hops), plan.members * width, 2 * width)
            current, coupled, col_wide, row_slots, offset_slots, *sends = call(
                functools.partial(prepare_kernel, plan),
                "prepare",
                [index, *ins],
                [IN_SMEM] + [IN_HBM] * 7,
                [
                    block_out,
                    pltpu.VMEM(matrix, BF16),
                    pltpu.VMEM((width, shard_len), BF16),
                    *scratch_for(near_rows, near_offsets),
                    *sends_out,
                ],
                [IN_VMEM] * 3 + [IN_SMEM] * 2 + [IN_VMEM] * len(sends_out),
                scratch=scratch_for(far_rows, far_cols, col_basis, couplings)
                + [pltpu.VMEM(matrix[:2] + (width,), F32), pltpu.SemaphoreType.DMA((7,))],
            )
        over = lax.ppermute(block if product == 0 else current, axes, plan.over)
        near = lax.ppermute(sends[0] if plan.paired else current, axes, plan.near)
        if plan.paired:
            sends = call(
                functools.partial(relay_kernel, plan),
                "relay",
                [index, sends[1], near],
                [IN_SMEM] + [IN_VMEM] * 2,
                [relay_out] * 2,
            )
            routes = plan.across
        else:
            routes = plan.routes
        fars = [lax.ppermute(s, axes, route) for s, route in zip(sends, routes)]
        after = sends if plan.paired else []
        if product == 0:
            ins = [index, row_slots, offset_slots, current, near, row_basis, near_tiles, *after]
            acc, dense, row_wide = call(
                functools.partial(first_own_kernel, plan),
                "first_own",
                ins,
                [IN_SMEM] * 3 + [IN_VMEM] * 2 + [PREFETCHED] * 2 + [ANYWHERE] * len(after),
                [
                    acc_out,
                    pltpu.VMEM((plan.cells, plan.size, plan.size), BF16),
                    pltpu.VMEM((2 * width, shard_len), BF16),
                ],
            )
        else:
            ins = [index, current, near, dense, *after] + ([krylov] if product > 1 else [])
            acc, krylov = call(
                functools.partial(own_kernel, plan, product - 1),
                "own",
                ins,
                [IN_SMEM] + [IN_VMEM] * 3 + [ANYWHERE] * (len(ins) - 4),
                [acc_out, krylov_out],
                [IN_VMEM, ANYWHERE],
                [pltpu.SemaphoreType.DMA],
                {len(ins) - 1: 1} if product > 1 else None,
            )
        (acc,) = call(
            functools.partial(halo_kernel, plan),
            "halo",
            [index, acc, over, dense],
            [IN_SMEM] + [IN_VMEM] * 3,
            [acc_out],
        )
        if product < PRODUCTS - 1:
            ins = [index, acc, row_wide, col_wide, coupled, *fars]
            current, *sends = call(
                functools.partial(finish_kernel, plan, len(fars)),
                "finish",
                ins,
                [IN_SMEM] + [IN_VMEM] * (len(ins) - 1),
                [block_out, *sends_out],
            )
        else:
            ins = [acc, row_wide, *fars, krylov]
            (krylov,) = call(
                functools.partial(last_kernel, plan, len(fars), product),
                "last",
                ins,
                [IN_VMEM] * (len(ins) - 1) + [ANYWHERE],
                [krylov_out],
                [ANYWHERE],
                [
                    pltpu.VMEM((rhs, shard_len), BF16),
                    pltpu.SemaphoreType.DMA((plan.per_device,)),
                ],
                {len(ins) - 1: 0},
            )
    return krylov


def solution(mesh):
    split = ("groups", "loop", "far")
    wide, narrow = P(split, None, None), P(split)
    in_specs = (P(None, split), wide, narrow, narrow, wide, wide, narrow, narrow, wide)
    return jax.shard_map(
        on_device, mesh=mesh, in_specs=in_specs, out_specs=P(None, None, split), check_vma=False
    )
```

```python
import functools

import jax
import jax.numpy as jnp
from jax import lax
from jax.experimental import pallas as pl
from jax.experimental.pallas import tpu as pltpu
from jax.sharding import PartitionSpec as P

PRODUCTS = 4
REACH = 4
LEVELS = 3
SPAN = 2 * REACH + 1
OTHER_CORE_FIRST = 0b11100111

F32 = jnp.float32
BF16 = jnp.bfloat16
IN_VMEM = pl.BlockSpec(memory_space=pltpu.VMEM)
PREFETCHED = pl.BlockSpec(memory_space=pltpu.VMEM)
IN_SMEM = pl.BlockSpec(memory_space=pltpu.SMEM)
IN_HBM = pl.BlockSpec(memory_space=pltpu.HBM)
ANYWHERE = pl.BlockSpec(memory_space=pl.ANY)


def dot_nt(a, b):
    return lax.dot_general(a, b, (((1,), (1,)), ((), ())), preferred_element_type=F32)


def dot_nn(a, b):
    return lax.dot_general(a, b, (((1,), (0,)), ((), ())), preferred_element_type=F32)


def halves(value):
    upper = value.astype(BF16)
    return upper, (value - upper.astype(F32)).astype(BF16)


class Plan:
    def __init__(self, block_shape, tile_shape, coupling_shape, members, loop_size):
        self.rhs, self.shard_len = block_shape
        self.tiles, self.size, _ = tile_shape
        self.slots, self.rank, _ = coupling_shape
        self.members, self.loop_size = members, loop_size
        self.per_device = self.shard_len // self.size
        self.width = self.per_device * self.rank
        self.cells = self.per_device * SPAN
        self.block_clusters = self.per_device * members
        distances = [d % loop_size for d in (2, loop_size - 2, loop_size // 2)]
        self.hops = sorted(set(distances))
        self.set_of = [self.hops.index(d) for d in distances]
        self.paired = len(self.hops) == 1 and 2 * self.hops[0] == loop_size and members == 4
        devices = members * loop_size
        self.near = [(i, i ^ 1) for i in range(devices)]
        self.over = [(i, (i + 1 if i % 2 else i - 1) % devices) for i in range(devices)]
        places = [(l, m) for l in range(loop_size) for m in range(members)]
        self.across = [
            [
                (l * members + m, self.far_target(l, m)[turn])
                for l, m in places
            ]
            for turn in range(2)
        ]
        self.routes = [
            [(l * members + m, (l + hop) % loop_size * members + (m + step) % members) for l, m in places]
            for hop in self.hops
            for step in range(members)
        ]

    def far_target(self, loop_index, member):
        block = (loop_index + self.hops[0]) % self.loop_size
        pair, core = divmod(member, 2)
        chip = block * 2 + (pair ^ core)
        first = core ^ (OTHER_CORE_FIRST >> chip & 1)
        return 2 * chip + first, 2 * chip + (first ^ 1)

    def first_is_odd(self, index_ref):
        index = index_ref[0]
        block = lax.rem(lax.div(index, self.members) + self.hops[0], self.loop_size)
        pair, core = lax.div(self.member(index_ref), 2), lax.rem(index, 2)
        chip = block * 2 + lax.bitwise_xor(pair, core)
        swapped = lax.bitwise_and(lax.shift_right_logical(jnp.int32(OTHER_CORE_FIRST), chip), 1)
        return lax.bitwise_xor(core, swapped) == 1

    def panel(self, ref, c):
        return ref[:, c * self.size : (c + 1) * self.size]

    def member(self, index_ref):
        return lax.rem(index_ref[0], self.members)

    def send_far(self, index_ref, x, cb_ref, g_ref, out_refs):
        coeffs = dot_nt(x, cb_ref[...]).astype(BF16)
        twice = jnp.concatenate([coeffs, coeffs], axis=1)
        totals = [dot_nt(twice, g_ref[index]) for index in range(len(self.hops))]
        if not self.paired:
            for i, out_ref in enumerate(out_refs):
                step = i % self.members * self.width
                out_ref[...] = totals[i // self.members][:, step : step + self.width].astype(BF16)
            return
        message_ref, keep_ref = out_refs
        (total,) = totals
        member = self.member(index_ref)
        second = lax.rem(member, 2) != lax.div(member, 2)
        first, last = total[:, : 2 * self.width], total[:, 2 * self.width :]
        keep_ref[...] = jnp.where(second, last, first)
        upper, lower = halves(jnp.where(second, first, last))
        message_ref[:, : self.shard_len] = x
        message_ref[:, self.shard_len : self.shard_len + 2 * self.width] = upper
        message_ref[:, self.shard_len + 2 * self.width :] = lower

    def relay_far(self, index_ref, keep_ref, message_ref, out_refs):
        upper = message_ref[:, self.shard_len : self.shard_len + 2 * self.width].astype(F32)
        lower = message_ref[:, self.shard_len + 2 * self.width :].astype(F32)
        total = (keep_ref[...] + (upper + lower)).astype(BF16)
        odd = self.first_is_odd(index_ref)
        first, last = total[:, : self.width], total[:, self.width :]
        out_refs[0][...] = jnp.where(odd, last, first)
        out_refs[1][...] = jnp.where(odd, first, last)

    def far_sum(self, far_refs):
        return sum(ref[...].astype(F32) for ref in far_refs)

    def near_sums(self, x_ref, d_ref, acc_ref, first, start_ref=None):
        panels = [self.panel(x_ref, c) for c in range(self.per_device)]
        for r in range(self.per_device):
            value = None if start_ref is None else self.panel(start_ref, r)
            for c in range(self.per_device):
                offset = first + c - r
                if -REACH <= offset <= REACH:
                    term = dot_nt(panels[c], d_ref[r * SPAN + offset + REACH])
                    value = term if value is None else value + term
            acc_ref[:, r * self.size : (r + 1) * self.size] = value

    def halo_sums(self, below, x_ref, d_ref, acc_ref, start_ref):
        @pl.when(below)
        def _():
            self.near_sums(x_ref, d_ref, acc_ref, -self.per_device, start_ref)

        @pl.when(jnp.logical_not(below))
        def _():
            self.near_sums(x_ref, d_ref, acc_ref, self.per_device, start_ref)

    def far_halves(self, far_refs):
        return jnp.concatenate(halves(self.far_sum(far_refs)), axis=1)

    def next_panel(self, acc_ref, rb_ref, both, c):
        return (self.panel(acc_ref, c) + dot_nn(both, self.panel(rb_ref, c))).astype(BF16)

    def next_block(self, acc_ref, rb_ref, far_refs):
        both = self.far_halves(far_refs)
        panels = [self.next_panel(acc_ref, rb_ref, both, c) for c in range(self.per_device)]
        return jnp.concatenate(panels, axis=1)


def prepare_kernel(plan, index_ref, *refs):
    sources, refs = refs[:7], refs[7:]
    x_ref, g_ref, cb_ref, near_ref, offsets_ref = refs[:5]
    sends, (rows_ref, cols_ref, col_ref, coup_ref, sum_ref, sems) = refs[5:-6], refs[-6:]
    targets = (near_ref, offsets_ref, rows_ref, cols_ref, x_ref, col_ref, coup_ref)
    copies = [
        pltpu.make_async_copy(source, target, sems.at[i])
        for i, (source, target) in enumerate(zip(sources, targets))
    ]
    for copy in copies:
        copy.start()
    rank, size = plan.rank, plan.size
    cb_ref[...] = jnp.zeros_like(cb_ref)
    sum_ref[...] = jnp.zeros_like(sum_ref)
    for copy in copies:
        copy.wait()
    for c in range(plan.per_device):
        cb_ref[c * rank : (c + 1) * rank, c * size : (c + 1) * size] = col_ref[c]
    column = lax.broadcasted_iota(jnp.int32, (rank, plan.width), 1) // rank
    shift = 0 if plan.paired else plan.member(index_ref)
    for s in range(plan.slots):
        row = lax.rem(rows_ref[s], plan.block_clusters)
        step = lax.rem(lax.div(row, plan.per_device) - shift + plan.members, plan.members)
        place = step * plan.per_device + lax.rem(row, plan.per_device)
        if len(plan.hops) > 1:
            level = lax.div(rows_ref[s], plan.block_clusters)
            index = sum(jnp.where(level == i, index, 0) for i, index in enumerate(plan.set_of))
        else:
            index = 0
        where = (index, pl.ds(pl.multiple_of(place * rank, rank), rank), slice(None))
        tile = coup_ref[s].astype(F32)
        wide = jnp.where(column == cols_ref[s], jnp.concatenate([tile] * plan.per_device, axis=1), 0.0)
        sum_ref[where] = sum_ref[where] + wide
    for index in range(len(plan.hops)):
        g_ref[index] = jnp.concatenate(halves(sum_ref[index]), axis=1)
    plan.send_far(index_ref, x_ref[...], cb_ref, g_ref, sends)


def relay_kernel(plan, index_ref, keep_ref, message_ref, *out_refs):
    plan.relay_far(index_ref, keep_ref, message_ref, out_refs)


def first_own_kernel(plan, *refs):
    index_ref, rows_ref, offsets_ref, x_ref, near_ref, row_ref, tiles_ref = refs[:7]
    acc_ref, d_ref, rb_ref = refs[-3:]
    rank, size = plan.rank, plan.size
    for cell in range(plan.cells):
        d_ref[cell] = jnp.zeros(d_ref.shape[1:], d_ref.dtype)
    for s in range(plan.tiles):
        d_ref[rows_ref[s] * SPAN + offsets_ref[s] + REACH] = tiles_ref[s]
    rb_ref[...] = jnp.zeros_like(rb_ref)
    for c in range(plan.per_device):
        for start in (c * rank, plan.width + c * rank):
            rb_ref[start : start + rank, c * size : (c + 1) * size] = row_ref[c]
    plan.near_sums(x_ref, d_ref, acc_ref, 0)
    plan.halo_sums(lax.rem(index_ref[0], 2) == 1, near_ref, d_ref, acc_ref, acc_ref)


def own_kernel(plan, slot, *refs):
    index_ref, x_ref, near_ref, d_ref = refs[:4]
    acc_ref, krylov_ref, sem = refs[-3:]
    copy = pltpu.make_async_copy(x_ref, krylov_ref.at[slot], sem)
    copy.start()
    plan.near_sums(x_ref, d_ref, acc_ref, 0)
    plan.halo_sums(lax.rem(index_ref[0], 2) == 1, near_ref, d_ref, acc_ref, acc_ref)
    copy.wait()


def halo_kernel(plan, index_ref, acc_ref, over_ref, d_ref, *refs):
    plan.halo_sums(lax.rem(index_ref[0], 2) == 0, over_ref, d_ref, refs[-1], acc_ref)


def finish_kernel(plan, fars, *refs):
    index_ref, acc_ref, rb_ref, cb_ref, g_ref = refs[:5]
    far_refs, (x_ref, *sends) = refs[5 : 5 + fars], refs[5 + fars :]
    x = plan.next_block(acc_ref, rb_ref, far_refs)
    x_ref[...] = x
    plan.send_far(index_ref, x, cb_ref, g_ref, sends)


def last_kernel(plan, fars, slot, *refs):
    acc_ref, rb_ref = refs[:2]
    far_refs, (_, krylov_ref, x_ref, sem) = refs[2 : 2 + fars], refs[2 + fars :]
    both = plan.far_halves(far_refs)
    copies = []
    for c in range(plan.per_device):
        columns = pl.ds(c * plan.size, plan.size)
        x_ref[:, columns] = plan.next_panel(acc_ref, rb_ref, both, c)
        copies.append(
            pltpu.make_async_copy(x_ref.at[:, columns], krylov_ref.at[slot, :, columns], sem.at[c])
        )
        copies[-1].start()
    for copy in copies:
        copy.wait()


def call(kernel, name, ins, specs, outs, out_specs=None, scratch=(), aliases=None):
    spaces = {id(IN_VMEM): pltpu.VMEM, id(IN_HBM): pltpu.HBM}
    ins = [
        pltpu.with_memory_space_constraint(v, spaces[id(spec)]) if id(spec) in spaces else v
        for v, spec in zip(ins, specs)
    ]
    return pl.pallas_call(
        kernel,
        in_specs=list(specs),
        out_specs=out_specs or [IN_VMEM] * len(outs),
        out_shape=list(outs),
        scratch_shapes=list(scratch),
        input_output_aliases=aliases or {},
        compiler_params=pltpu.CompilerParams(vmem_limit_bytes=16 * 2**20),
        cost_estimate=pl.CostEstimate(flops=10**9, bytes_accessed=2**22, transcendentals=0),
        name=name,
    )(*ins)


def on_device(
    block, near_tiles, near_rows, near_offsets, col_basis, couplings, far_rows, far_cols, row_basis
):
    axes = ("loop", "far")
    plan = Plan(
        block.shape, near_tiles.shape, couplings.shape, lax.axis_size("far"), lax.axis_size("loop")
    )
    rhs, shard_len, width = plan.rhs, plan.shard_len, plan.width
    block_out = pltpu.VMEM((rhs, shard_len), BF16)
    acc_out = pltpu.VMEM((rhs, shard_len), F32)
    relay_out = pltpu.VMEM((rhs, width), BF16)
    krylov_out = jax.ShapeDtypeStruct((PRODUCTS, rhs, shard_len), BF16)
    if plan.paired:
        sends_out = [
            pltpu.VMEM((rhs, shard_len + 4 * width), BF16),
            pltpu.VMEM((rhs, 2 * width), F32),
        ]
    else:
        sends_out = [pltpu.VMEM((rhs, width), BF16)] * len(plan.routes)
    index = lax.axis_index(axes).astype(jnp.int32).reshape(1)

    def scratch_for(*arrays):
        return [
            pltpu.SMEM(v.shape, v.dtype) if v.dtype == jnp.int32 else pltpu.VMEM(v.shape, v.dtype)
            for v in arrays
        ]

    current, sends, krylov = block, None, None
    for product in range(PRODUCTS):
        if product == 0:
            ins = [near_rows, near_offsets, far_rows, far_cols, block, col_basis, couplings]
            matrix = (len(plan.hops), plan.members * width, 2 * width)
            current, coupled, col_wide, row_slots, offset_slots, *sends = call(
                functools.partial(prepare_kernel, plan),
                "prepare",
                [index, *ins],
                [IN_SMEM] + [IN_HBM] * 7,
                [
                    block_out,
                    pltpu.VMEM(matrix, BF16),
                    pltpu.VMEM((width, shard_len), BF16),
                    *scratch_for(near_rows, near_offsets),
                    *sends_out,
                ],
                [IN_VMEM] * 3 + [IN_SMEM] * 2 + [IN_VMEM] * len(sends_out),
                scratch=scratch_for(far_rows, far_cols, col_basis, couplings)
                + [pltpu.VMEM(matrix[:2] + (width,), F32), pltpu.SemaphoreType.DMA((7,))],
            )
        over = lax.ppermute(block if product == 0 else current, axes, plan.over)
        near = lax.ppermute(sends[0] if plan.paired else current, axes, plan.near)
        if plan.paired:
            sends = call(
                functools.partial(relay_kernel, plan),
                "relay",
                [index, sends[1], near],
                [IN_SMEM] + [IN_VMEM] * 2,
                [relay_out] * 2,
            )
            routes = plan.across
        else:
            routes = plan.routes
        fars = [lax.ppermute(s, axes, route) for s, route in zip(sends, routes)]
        after = sends if plan.paired else []
        if product == 0:
            ins = [index, row_slots, offset_slots, current, near, row_basis, near_tiles, *after]
            acc, dense, row_wide = call(
                functools.partial(first_own_kernel, plan),
                "first_own",
                ins,
                [IN_SMEM] * 3 + [IN_VMEM] * 2 + [PREFETCHED] * 2 + [ANYWHERE] * len(after),
                [
                    acc_out,
                    pltpu.VMEM((plan.cells, plan.size, plan.size), BF16),
                    pltpu.VMEM((2 * width, shard_len), BF16),
                ],
            )
        else:
            ins = [index, current, near, dense, *after] + ([krylov] if product > 1 else [])
            acc, krylov = call(
                functools.partial(own_kernel, plan, product - 1),
                "own",
                ins,
                [IN_SMEM] + [IN_VMEM] * 3 + [ANYWHERE] * (len(ins) - 4),
                [acc_out, krylov_out],
                [IN_VMEM, ANYWHERE],
                [pltpu.SemaphoreType.DMA],
                {len(ins) - 1: 1} if product > 1 else None,
            )
        (acc,) = call(
            functools.partial(halo_kernel, plan),
            "halo",
            [index, acc, over, dense],
            [IN_SMEM] + [IN_VMEM] * 3,
            [acc_out],
        )
        if product < PRODUCTS - 1:
            ins = [index, acc, row_wide, col_wide, coupled, *fars]
            current, *sends = call(
                functools.partial(finish_kernel, plan, len(fars)),
                "finish",
                ins,
                [IN_SMEM] + [IN_VMEM] * (len(ins) - 1),
                [block_out, *sends_out],
            )
        else:
            ins = [acc, row_wide, *fars, krylov]
            (krylov,) = call(
                functools.partial(last_kernel, plan, len(fars), product),
                "last",
                ins,
                [IN_VMEM] * (len(ins) - 1) + [ANYWHERE],
                [krylov_out],
                [ANYWHERE],
                [
                    pltpu.VMEM((rhs, shard_len), BF16),
                    pltpu.SemaphoreType.DMA((plan.per_device,)),
                ],
                {len(ins) - 1: 0},
            )
    return krylov


def solution(mesh):
    split = ("groups", "loop", "far")
    wide, narrow = P(split, None, None), P(split)
    in_specs = (P(None, split), wide, narrow, narrow, wide, wide, narrow, narrow, wide)
    return jax.shard_map(
        on_device, mesh=mesh, in_specs=in_specs, out_specs=P(None, None, split), check_vma=False
    )
```
